32 devices in a mesh: dp: 8 (over z, y), tensor: 4 (over x, core).
Axes of the slice: x: 2, y: 2, z: 4, core: 2. Of those that a mesh axis runs over, the one named last changes fastest.
Arguments:
- tokens: bfloat16 [16384, 1024], P(('dp', 'tensor')), may hold values from -6 to 6
- lengths: int32 [8, 2], P('dp'), may hold values from 64 to 1984, as said below
- attn_gain: bfloat16 [1024], replicated, may hold values from 0.5 to 1.5
- qkv_weight: bfloat16 [1024, 3, 1024], P(None, None, 'tensor'), may hold values from -0.1875 to 0.1875
- beta_weight: bfloat16 [1024, 8], P(None, 'tensor'), may hold values from -0.1875 to 0.1875
- conv_weight: bfloat16 [4, 3, 1024], P(None, None, 'tensor'), may hold values from -3 to 3
- head_gain: bfloat16 [128], replicated, may hold values from 0.5 to 1.5
- out_weight: bfloat16 [1024, 1024], P('tensor'), may hold values from -0.1875 to 0.1875
- mlp_gain: bfloat16 [1024], replicated, may hold values from 0.5 to 1.5
- gate_up_weight: bfloat16 [1024, 2, 2816], P(None, None, 'tensor'), may hold values from -0.1875 to 0.1875
- down_weight: bfloat16 [2816, 1024], P('tensor'), may hold values from -0.109375 to 0.109375
- cotangent: bfloat16 [16384, 1024], P(('dp', 'tensor')), may hold values from -6 to 6
Outputs:
- output: bfloat16 [16384, 1024], P(('dp', 'tensor'))
- input_grad: float32 [16384, 1024], P(('dp', 'tensor'))
- attn_gain_grad: float32 [1024], replicated
- qkv_grad: float32 [1024, 3, 1024], P(None, None, 'tensor')
- beta_grad: float32 [1024, 8], P(None, 'tensor')
- conv_grad: float32 [4, 3, 1024], P(None, None, 'tensor')
- head_gain_grad: float32 [128], replicated
- out_grad: float32 [1024, 1024], P('tensor')
- mlp_gain_grad: float32 [1024], replicated
- gate_up_grad: float32 [1024, 2, 2816], P(None, None, 'tensor')
- down_grad: float32 [2816, 1024], P('tensor')
The draws below stay inside these ranges and needn't reach their ends.
Inputs may be any that keep to these rules, and one draw needn't show every extreme that they name: Each row holds the lengths of the two sequences of one group, in order; both are multiples of 64, they sum to 2048, and the shorter is at most 448.
All inputs are finite; a program needn't handle non-finite values.
Results may differ from the reference program's by a relative error of at most 0.017.
Values may be sent and summed in bfloat16 or wider, within the bound.
A program may use at most 256 MiB of HBM per device.

```python
import jax
import jax.numpy as jnp
from jax import lax

D = 1024
HEADS = 8
HEAD_DIM = 128
FF = 2816
WIDTH = 4
SPAN = 64
TOK_DEV = 512
GROUP = 2048
GROUPS = 8
TOKENS = 16384


def draw_lengths(key, part):
    key = jax.random.fold_in(key, 7)
    first_key, pick_key, order_key = jax.random.split(key, 3)
    longest_short = TOK_DEV // SPAN - 1
    shorts = jax.random.randint(first_key, (GROUPS,), 1, longest_short + 1)
    picked = jax.random.randint(pick_key, (), 0, GROUPS)
    shorts = jnp.where(jnp.arange(GROUPS) == picked, 1, shorts)
    orders = jax.random.randint(order_key, (GROUPS,), 0, 2)
    short_len = shorts * SPAN
    long_len = GROUP - short_len
    first_len = jnp.where(orders == 1, short_len, long_len)
    return jnp.stack([first_len, GROUP - first_len], axis=1).astype(jnp.int32)


def block_scale(own_key, extent, cuts, smallest, largest):
    factor_of, own = 1.0, jax.random.fold_in(own_key, 6)
    for dim, shards_of in cuts:
        heights = jnp.exp(jax.random.uniform(jax.random.fold_in(own, dim), (shards_of,), jnp.float32, smallest / len(cuts), largest / len(cuts)))
        factor_of = factor_of * jnp.repeat(heights, extent[dim] // shards_of).reshape([-1 if axis == dim else 1 for axis in range(len(extent))])
    return factor_of


def normal_values(rng, extent, scale, limit, shards=(), kind=jnp.bfloat16):
    drawn = scale * jax.random.normal(rng, extent, jnp.float32)
    if shards:
        drawn = drawn * block_scale(rng, extent, shards, -0.22, 0.18)
    return jnp.clip(drawn, -limit, limit).astype(kind)


def setup_inputs(seed: int = 0) -> dict:
    seeds = jax.random.split(jax.random.key(seed), 13)
    tokens = normal_values(seeds[0], (TOKENS, D), 1.0, 6.0, ((0, 32),))
    lengths = draw_lengths(jax.random.fold_in(seeds[12], 71), 0)
    attn_gain = jnp.clip(1.0 + 0.1 * jax.random.normal(seeds[2], (D,), jnp.float32), 0.5, 1.5).astype(jnp.bfloat16)
    qkv_weight = normal_values(seeds[3], (D, 3, D), D ** -0.5, 0.1875, ((2, 4),))
    beta_weight = normal_values(seeds[4], (D, HEADS), D ** -0.5, 0.1875, ((1, 4),))
    conv_weight = normal_values(seeds[5], (WIDTH, 3, D), 0.5, 3.0, ((2, 4),))
    head_gain = jnp.clip(1.0 + 0.1 * jax.random.normal(seeds[6], (HEAD_DIM,), jnp.float32), 0.5, 1.5).astype(jnp.bfloat16)
    out_weight = normal_values(seeds[7], (D, D), D ** -0.5, 0.1875, ((0, 4),))
    mlp_gain = jnp.clip(1.0 + 0.1 * jax.random.normal(seeds[8], (D,), jnp.float32), 0.5, 1.5).astype(jnp.bfloat16)
    gate_up_weight = normal_values(seeds[9], (D, 2, FF), D ** -0.5, 0.1875, ((2, 4),))
    down_weight = normal_values(seeds[10], (FF, D), FF ** -0.5, 0.109375, ((0, 4),))
    cotangent = normal_values(seeds[11], (TOKENS, D), 1.0, 6.0, ((0, 32),))
    return {"tokens": tokens, "lengths": lengths, "attn_gain": attn_gain, "qkv_weight": qkv_weight, "beta_weight": beta_weight, "conv_weight": conv_weight, "head_gain": head_gain, "out_weight": out_weight, "mlp_gain": mlp_gain, "gate_up_weight": gate_up_weight, "down_weight": down_weight, "cotangent": cotangent}


precise = lax.Precision.HIGHEST

@jax.custom_vjp
def low(v):
    return lax.optimization_barrier(v.astype(jnp.bfloat16)).astype(jnp.float32)

@jax.custom_vjp
def low_back(v):
    return v

def low_keep(v):
    return (low(v), None)

def low_pass(kept, grad):
    return (grad,)

def back_keep(v):
    return (v, None)

def back_low(kept, grad):
    return (low(grad),)
low.defvjp(low_keep, low_pass)
low_back.defvjp(back_keep, back_low)

def rms_norm(values, scales):
    inverse = lax.rsqrt(lax.optimization_barrier(jnp.mean(values * values, axis=-1, keepdims=True)) + 1e-05)
    return values * inverse * scales

def doc_layout(first_len, group_rows, block_len):
    row_index = jnp.arange(group_rows, dtype=jnp.int32)
    doc_start = jnp.where(row_index >= first_len, first_len, 0).astype(jnp.int32)
    position = row_index - doc_start
    block_start = jnp.arange(group_rows // block_len, dtype=jnp.int32) * block_len
    reset_flags = jnp.where((block_start == 0) | (block_start == first_len), 1.0, 0.0).astype(jnp.float32)
    return (position, reset_flags)

def short_conv(projected, kernel, position):
    total_rows = projected.shape[0]
    summed = jnp.zeros_like(projected)
    for offset in range(kernel.shape[0]):
        shifted = jnp.pad(projected, ((offset, 0), (0, 0)))[:total_rows]
        usable = (position >= offset)[:, None]
        summed = summed + jnp.where(usable, shifted * kernel[offset], 0.0)
    return jax.nn.silu(summed)

def delta_rule(query_rows, key_rows, value_rows, beta_rows, reset_flags, block_len):
    total_rows, head_count, head_size = query_rows.shape
    block_count = total_rows // block_len

    def blocked(values):
        return jnp.swapaxes(values.reshape((block_count, block_len) + values.shape[1:]), 1, 2)
    query_all = blocked(query_rows)
    key_all = blocked(key_rows)
    value_all = blocked(value_rows)
    beta_all = blocked(beta_rows)
    index = jnp.arange(block_len)
    strict = index[:, None] > index[None, :]
    causal = index[:, None] >= index[None, :]
    identity = jnp.eye(block_len, dtype=jnp.float32)
    key_gram = jnp.einsum('nhid,nhjd->nhij', key_all, key_all, precision=precise)
    system = identity + jnp.where(strict, beta_all[..., None] * key_gram, 0.0)
    right_hand = beta_all[..., None] * jnp.concatenate([key_all, value_all], axis=-1)
    solved = jax.scipy.linalg.solve_triangular(system, right_hand, lower=True, unit_diagonal=True)
    solved_keys = solved[..., :head_size]
    solved_values = solved[..., head_size:]
    scores_all = jnp.where(causal, jnp.einsum('nhid,nhjd->nhij', query_all, key_all, precision=precise), 0.0)

    def advance(memory, inputs):
        query_block, key_block, keys_solved, values_solved, scores, reset_flag = inputs
        memory = memory * (1.0 - reset_flag)
        residual = values_solved - jnp.einsum('hcd,hde->hce', keys_solved, memory, precision=precise)
        outputs = jnp.einsum('hcd,hde->hce', query_block, memory, precision=precise)
        outputs = outputs + jnp.einsum('hij,hje->hie', scores, residual, precision=precise)
        memory = memory + jnp.einsum('hcd,hce->hde', key_block, residual, precision=precise)
        return (memory, outputs)
    initial = jnp.zeros((head_count, head_size, head_size), jnp.float32)
    inputs = (query_all, key_all, solved_keys, solved_values, scores_all, reset_flags)
    _, outputs = lax.scan(jax.checkpoint(advance), initial, inputs)
    return jnp.swapaxes(outputs, 1, 2).reshape(total_rows, head_count, head_size)

def mixer(projected, beta_pre, kernel, head_scale, position, reset_flags):
    conved = short_conv(projected, kernel, position)
    total_rows = projected.shape[0]
    channels = projected.shape[1] // 3
    head_size = head_scale.shape[0]
    head_count = channels // head_size
    shaped = conved.reshape(total_rows, 3, head_count, head_size)
    query_rows = shaped[:, 0]
    key_rows = shaped[:, 1]
    value_rows = shaped[:, 2]
    query_rows = query_rows * lax.rsqrt(lax.optimization_barrier(jnp.sum(query_rows * query_rows, axis=-1, keepdims=True)) + 1e-06)
    key_rows = key_rows * lax.rsqrt(lax.optimization_barrier(jnp.sum(key_rows * key_rows, axis=-1, keepdims=True)) + 1e-06)
    mixed = delta_rule(query_rows, key_rows, value_rows, jax.nn.sigmoid(beta_pre), reset_flags, SPAN)
    return rms_norm(mixed, head_scale).reshape(total_rows, channels)

def block_forward(tokens, attn_gain, qkv_weight, beta_weight, conv_weight, head_gain, out_weight, mlp_gain, gate_up_weight, down_weight, position, reset_flags):
    model_width = tokens.shape[1]
    attn_in = low(rms_norm(tokens, attn_gain))
    projected = low_back(jnp.dot(attn_in, qkv_weight.reshape(model_width, -1), precision=precise))
    beta_pre = low_back(jnp.dot(attn_in, beta_weight, precision=precise))
    kernel = conv_weight.reshape(conv_weight.shape[0], -1)
    headed = low(mixer(projected, beta_pre, kernel, head_gain, position, reset_flags))
    hidden_res = tokens + low_back(jnp.dot(headed, out_weight, precision=precise))
    mlp_in = low(rms_norm(hidden_res, mlp_gain))
    gate_up = low_back(jnp.dot(mlp_in, gate_up_weight.reshape(model_width, -1), precision=precise))
    hidden_units = gate_up.shape[1] // 2
    activated = low(jax.nn.silu(gate_up[:, :hidden_units]) * gate_up[:, hidden_units:])
    return hidden_res + jnp.dot(activated, down_weight, precision=precise)

def reference(tokens, lengths, attn_gain, qkv_weight, beta_weight, conv_weight, head_gain, out_weight, mlp_gain, gate_up_weight, down_weight, cotangent):
    weights = tuple((matrix.astype(jnp.float32) for matrix in (attn_gain, qkv_weight, beta_weight, conv_weight, head_gain, out_weight, mlp_gain, gate_up_weight, down_weight)))
    group_count = lengths.shape[0]
    model_width = tokens.shape[1]
    group_rows = tokens.shape[0] // group_count
    grouped = tokens.astype(jnp.float32).reshape(group_count, group_rows, model_width)
    grouped_cot = cotangent.astype(jnp.float32).reshape(group_count, group_rows, model_width)

    def per_group(running, inputs):
        group_tokens, group_cot, group_lengths = inputs
        position, reset_flags = doc_layout(group_lengths[0], group_rows, SPAN)

        def forward(group_in, *params):
            return block_forward(group_in, *params, position, reset_flags)
        result, backward = jax.vjp(forward, group_tokens, *weights)
        grads = backward(group_cot)
        running = tuple((total + update for total, update in zip(running, grads[1:])))
        return (running, (result.astype(jnp.bfloat16), grads[0]))
    initial = tuple((jnp.zeros_like(matrix) for matrix in weights))
    totals, (results, input_grads) = lax.scan(per_group, initial, (grouped, grouped_cot, lengths))
    return (results.reshape(-1, model_width), input_grads.reshape(-1, model_width), totals[0], totals[1], totals[2], totals[3], totals[4], totals[5], totals[6], totals[7], totals[8])
```

```python
import functools
import jax
import jax.numpy as jnp
from jax import lax
from jax.experimental import pallas as pl
from jax.experimental.pallas import tpu as pltpu
from jax.sharding import PartitionSpec as P

HEAD = 128
STEP = 128
SPAN = 64
STEPS = 4
ROWS = STEP * STEPS
NN = (((1,), (0,)), ((), ()))
NT = (((1,), (1,)), ((), ()))
TN = (((0,), (0,)), ((), ()))
f32 = jnp.float32
bf16 = jnp.bfloat16


def mm(a, b, dims=NN):
    return lax.dot_general(a.astype(bf16), b.astype(bf16), dims, preferred_element_type=f32)


def split(a):
    high = a.astype(bf16)
    return high, (a - high.astype(f32)).astype(bf16)


def stack(x):
    return jnp.concatenate([x[:, :HEAD], x[:, HEAD:]], axis=0)


def unstack(x):
    return jnp.concatenate([x[:STEP], x[STEP:]], axis=1)


def pair_masks():
    i = lax.broadcasted_iota(jnp.int32, (2 * STEP, 2 * STEP), 0)
    j = lax.broadcasted_iota(jnp.int32, (2 * STEP, 2 * STEP), 1)
    same = (i // STEP) == (j // STEP)
    cross = ((i % STEP) >= SPAN) & ((j % STEP) < SPAN)
    levels = []
    size = 1
    while size < STEP:
        levels.append(((i // (2 * size)) == (j // (2 * size))) & ((i // size) % 2 == 1) & ((j // size) % 2 == 0))
        size *= 2
    return same & (i > j), same & (i >= j), cross, levels, i == j


def tri_inverse(a, levels, eye):
    inv = jnp.where(eye, 1.0, jnp.where(levels[0], -a, 0.0))
    for level in levels[1:]:
        low = inv.astype(bf16)
        part = jnp.where(level, a, 0.0).astype(bf16)
        inv = inv - mm(mm(low, part), low)
    return inv


def row_masks(start_reset, mid_reset):
    r = lax.broadcasted_iota(jnp.int32, (2 * STEP, HEAD), 0) % STEP
    upper = r < SPAN
    enter = jnp.where(upper, 1.0 - start_reset, (1.0 - start_reset) * (1.0 - mid_reset))
    leave = jnp.where(upper, 1.0 - mid_reset, 1.0)
    keep = (1.0 - start_reset) * (1.0 - mid_reset)
    return enter, leave, keep


def resets(step_start, first):
    start = jnp.where((step_start == 0) | (step_start == first), 1.0, 0.0).astype(f32)
    mid = jnp.where(step_start + SPAN == first, 1.0, 0.0).astype(f32)
    return start, mid


def conv_masks(base, first, rows):
    r = lax.broadcasted_iota(jnp.int32, (rows, HEAD), 0) + base
    pos = jnp.where(r >= first, r - first, r)
    return [pos >= j for j in range(4)]


def mixer_fwd_kernel(first_ref, proj_ref, conv_ref, gain_ref, headed_ref, mixed_ref, state_out, res_out, wu_out, inv_out, state, buf):
    g = pl.program_id(0)
    first = first_ref[0]

    @pl.when(g == 0)
    def _():
        state[...] = jnp.zeros_like(state)
        buf[0:8, :] = jnp.zeros((8, buf.shape[1]), f32)

    width = buf.shape[1]
    buf[8:, :] = proj_ref[:, :width]
    valid = conv_masks(g * ROWS, first, ROWS)
    cols = []
    for c in range(width // HEAD):
        cs = slice(c * HEAD, (c + 1) * HEAD)
        total = buf[8:8 + ROWS, cs] * conv_ref[0:1, cs]
        for j in range(1, 4):
            total = total + jnp.where(valid[j], buf[8 - j:8 - j + ROWS, cs] * conv_ref[j:j + 1, cs], 0.0)
        cols.append(total * jax.nn.sigmoid(total))
    buf[0:8, :] = buf[ROWS:ROWS + 8, :]
    betas = jax.nn.sigmoid(proj_ref[:, width:])
    strict, causal, cross, levels, eye = pair_masks()
    mem = [state[0], state[1]]
    for s in range(STEPS):
        rs = slice(s * STEP, (s + 1) * STEP)
        start_reset, mid_reset = resets(g * ROWS + s * STEP, first)
        enter, leave, keep = row_masks(start_reset, mid_reset)
        gate = jnp.where(cross, 1.0 - mid_reset, 1.0)
        two = lambda n: jnp.concatenate([cols[2 * n][rs], cols[2 * n + 1][rs]], axis=0)
        q, k, v = two(0), two(1), two(2)
        q = q * lax.rsqrt(jnp.sum(q * q, axis=-1, keepdims=True) + 1e-6)
        k = k * lax.rsqrt(jnp.sum(k * k, axis=-1, keepdims=True) + 1e-6)
        b = jnp.concatenate([betas[rs, 0:1], betas[rs, 1:2]], axis=0)
        gp = mm(jnp.concatenate([k, q], axis=0), k, NT)
        a = jnp.where(strict, gate * gp[:2 * STEP], 0.0) * b
        p = jnp.where(causal, gate * gp[2 * STEP:], 0.0)
        inv = tri_inverse(a, levels, eye)
        wu = mm(inv, jnp.concatenate([b * k, b * v], axis=1))
        inv_out[s] = inv.astype(bf16)
        wu_out[s] = wu.astype(bf16)
        state_out[s, :HEAD] = mem[0].astype(bf16)
        state_out[s, HEAD:] = mem[1].astype(bf16)
        w = wu[:, :HEAD] * enter
        qe = q * enter
        ws, qs = [], []
        for h in range(2):
            hs = slice(h * STEP, (h + 1) * STEP)
            both = mm(jnp.concatenate([w[hs], qe[hs]], axis=0), mem[h])
            ws.append(both[:STEP])
            qs.append(both[STEP:])
        res = wu[:, HEAD:] - jnp.concatenate(ws, axis=0)
        res_out[s] = res.astype(bf16)
        ke = k * leave
        for h in range(2):
            hs = slice(h * STEP, (h + 1) * STEP)
            mem[h] = keep * mem[h] + mm(ke[hs], res[hs], TN)
        o = jnp.concatenate(qs, axis=0) + mm(p, res)
        mixed_ref[rs, :] = unstack(o)
        headed = o * lax.rsqrt(jnp.mean(o * o, axis=-1, keepdims=True) + 1e-5) * gain_ref[...]
        headed_ref[rs, :] = unstack(headed).astype(bf16)
    state[0] = mem[0]
    state[1] = mem[1]


def mixer_fwd(first, proj, conv, gain):
    rows, total = proj.shape
    width = conv.shape[1]
    n = rows // ROWS
    steps = rows // STEP
    return pl.pallas_call(
        mixer_fwd_kernel,
        grid_spec=pltpu.PrefetchScalarGridSpec(
            num_scalar_prefetch=1, grid=(n,),
            in_specs=[pl.BlockSpec((ROWS, total), lambda g, f: (g, 0)), pl.BlockSpec((4, width), lambda g, f: (0, 0)), pl.BlockSpec((1, HEAD), lambda g, f: (0, 0))],
            out_specs=[pl.BlockSpec((ROWS, 2 * HEAD), lambda g, f: (g, 0)), pl.BlockSpec((ROWS, 2 * HEAD), lambda g, f: (g, 0)),
                       pl.BlockSpec((STEPS, 2 * HEAD, HEAD), lambda g, f: (g, 0, 0)), pl.BlockSpec((STEPS, 2 * STEP, HEAD), lambda g, f: (g, 0, 0)),
                       pl.BlockSpec((STEPS, 2 * STEP, 2 * HEAD), lambda g, f: (g, 0, 0)), pl.BlockSpec((STEPS, 2 * STEP, 2 * STEP), lambda g, f: (g, 0, 0))],
            scratch_shapes=[pltpu.VMEM((2, HEAD, HEAD), f32), pltpu.VMEM((ROWS + 8, width), f32)]),
        out_shape=[jax.ShapeDtypeStruct((rows, 2 * HEAD), bf16), jax.ShapeDtypeStruct((rows, 2 * HEAD), f32),
                   jax.ShapeDtypeStruct((steps, 2 * HEAD, HEAD), bf16), jax.ShapeDtypeStruct((steps, 2 * STEP, HEAD), bf16),
                   jax.ShapeDtypeStruct((steps, 2 * STEP, 2 * HEAD), bf16), jax.ShapeDtypeStruct((steps, 2 * STEP, 2 * STEP), bf16)],
        compiler_params=pltpu.CompilerParams(dimension_semantics=("arbitrary",), vmem_limit_bytes=48 * 2**20),
    )(first, proj, conv, gain)


def mixer_bwd_kernel(first_ref, proj_ref, prev_ref, conv_ref, gain_ref, dh_ref, mixed_ref, state_in, res_in, wu_in, inv_in,
                     dcat_ref, dconv_ref, dgain_ref, dstate, buf, dbuf, cacc, gacc):
    g = pl.program_id(0)
    n = pl.num_programs(0)
    blk = n - 1 - g
    first = first_ref[0]
    width = buf.shape[1]

    @pl.when(g == 0)
    def _():
        dstate[...] = jnp.zeros_like(dstate)
        dbuf[ROWS:, :] = jnp.zeros((8, width), f32)
        cacc[...] = jnp.zeros_like(cacc)
        gacc[...] = jnp.zeros_like(gacc)

    buf[0:8, :] = prev_ref[:, :width]
    buf[8:, :] = proj_ref[:, :width]
    valid = conv_masks(blk * ROWS, first, ROWS + 8)
    cols, slopes = [], []
    for c in range(width // HEAD):
        cs = slice(c * HEAD, (c + 1) * HEAD)
        total = buf[8:8 + ROWS, cs] * conv_ref[0:1, cs]
        for j in range(1, 4):
            total = total + jnp.where(valid[j][:ROWS], buf[8 - j:8 - j + ROWS, cs] * conv_ref[j:j + 1, cs], 0.0)
        sig = jax.nn.sigmoid(total)
        cols.append(total * sig)
        slopes.append(sig * (1.0 + total * (1.0 - sig)))
    betas = jax.nn.sigmoid(proj_ref[:, width:])
    strict, causal, cross, _, _ = pair_masks()
    lane = lax.broadcasted_iota(jnp.int32, (STEP, HEAD), 1)
    dmem = [dstate[0], dstate[1]]
    for s in reversed(range(STEPS)):
        rs = slice(s * STEP, (s + 1) * STEP)
        start_reset, mid_reset = resets(blk * ROWS + s * STEP, first)
        enter, leave, keep = row_masks(start_reset, mid_reset)
        gate = jnp.where(cross, 1.0 - mid_reset, 1.0)
        two = lambda n: jnp.concatenate([cols[2 * n][rs], cols[2 * n + 1][rs]], axis=0)
        q, k, v = two(0), two(1), two(2)
        rq = lax.rsqrt(jnp.sum(q * q, axis=-1, keepdims=True) + 1e-6)
        rk = lax.rsqrt(jnp.sum(k * k, axis=-1, keepdims=True) + 1e-6)
        q = q * rq
        k = k * rk
        b = jnp.concatenate([betas[rs, 0:1], betas[rs, 1:2]], axis=0)
        gp = mm(jnp.concatenate([k, q], axis=0), k, NT)
        gram = jnp.where(strict, gate * gp[:2 * STEP], 0.0)
        p = jnp.where(causal, gate * gp[2 * STEP:], 0.0)
        o = stack(mixed_ref[rs, :])
        dh = stack(dh_ref[rs, :].astype(f32))
        ro = lax.rsqrt(jnp.mean(o * o, axis=-1, keepdims=True) + 1e-5)
        on = o * ro
        gacc[...] += jnp.sum((dh * on).reshape(2 * STEP // 8, 8, HEAD), axis=0)
        dn = dh * gain_ref[...]
        do = ro * (dn - on * jnp.mean(dn * on, axis=-1, keepdims=True))
        mem = state_in[s]
        res = res_in[s]
        wu = wu_in[s]
        inv = inv_in[s]
        do16 = do.astype(bf16)
        doe = (do * enter).astype(bf16)
        q16 = q.astype(bf16)
        k16 = k.astype(bf16)
        ke16 = (k * leave).astype(bf16)
        we = (wu[:, :HEAD].astype(f32) * enter).astype(bf16)
        dres = mm(p, do16, TN)
        hs = [slice(h * STEP, (h + 1) * STEP) for h in range(2)]
        dres = dres + jnp.concatenate([mm(ke16[hs[h]], dmem[h]) for h in range(2)], axis=0)
        dres16 = dres.astype(bf16)
        dke = jnp.concatenate([mm(res[hs[h]], dmem[h], NT) for h in range(2)], axis=0)
        for h in range(2):
            dmem[h] = keep * dmem[h] + mm(q16[hs[h]], doe[hs[h]], TN) - mm(we[hs[h]], dres16[hs[h]], TN)
        dp = jnp.where(causal, gate * mm(do16, res, NT), 0.0).astype(bf16)
        both = [mm(jnp.concatenate([do16[hs[h]], dres16[hs[h]]], axis=0), mem[h * HEAD:(h + 1) * HEAD], NT) for h in range(2)]
        dq = enter * jnp.concatenate([both[0][:STEP], both[1][:STEP]], axis=0) + mm(dp, k16)
        dw = -enter * jnp.concatenate([both[0][STEP:], both[1][STEP:]], axis=0)
        dk = mm(dp, q16, TN) + leave * dke
        db_kv = mm(inv, jnp.concatenate([dw, dres], axis=1), TN)
        da = -jnp.where(strict, gate * mm(db_kv, wu, NT), 0.0)
        dbk, dbv = db_kv[:, :HEAD], db_kv[:, HEAD:]
        dbeta = jnp.sum(da * gram, axis=-1, keepdims=True) + jnp.sum(dbk * k + dbv * v, axis=-1, keepdims=True)
        dg = (da * b).astype(bf16)
        dk = dk + mm(dg, k16) + mm(dg, k16, TN) + b * dbk
        dv = b * dbv
        dq = rq * (dq - q * jnp.sum(dq * q, axis=-1, keepdims=True))
        dk = rk * (dk - k * jnp.sum(dk * k, axis=-1, keepdims=True))
        dpre = dbeta * b * (1.0 - b)
        for i, x in enumerate((dq, dk, dv)):
            for h in range(2):
                c = 2 * i + h
                dbuf[rs, c * HEAD:(c + 1) * HEAD] = x[hs[h]] * slopes[c][rs]
        dcat_ref[rs, width:] = jnp.where(lane == 0, dpre[:STEP], jnp.where(lane == 1, dpre[STEP:], 0.0)).astype(bf16)
    dstate[0] = dmem[0]
    dstate[1] = dmem[1]
    for c in range(width // HEAD):
        cs = slice(c * HEAD, (c + 1) * HEAD)
        total = dbuf[:ROWS, cs] * conv_ref[0:1, cs]
        grads = [jnp.sum((buf[8:8 + ROWS, cs] * dbuf[:ROWS, cs]).reshape(ROWS // 8, 8, HEAD), axis=0)]
        for j in range(1, 4):
            total = total + jnp.where(shifted_valid(blk * ROWS, first, j), dbuf[j:j + ROWS, cs] * conv_ref[j:j + 1, cs], 0.0)
            grads.append(jnp.sum(jnp.where(valid[j][:ROWS], buf[8 - j:8 - j + ROWS, cs] * dbuf[:ROWS, cs], 0.0).reshape(ROWS // 8, 8, HEAD), axis=0))
        dcat_ref[:, cs] = total.astype(bf16)
        for j in range(4):
            cacc[j, :, cs] += grads[j]
    dbuf[ROWS:, :] = dbuf[0:8, :]

    @pl.when(g == n - 1)
    def _():
        for j in range(4):
            dconv_ref[j:j + 1, :] = jnp.sum(cacc[j], axis=0, keepdims=True)
        dgain_ref[...] = jnp.sum(gacc[...], axis=0, keepdims=True)


def shifted_valid(base, first, j):
    r = lax.broadcasted_iota(jnp.int32, (ROWS, HEAD), 0) + base + j
    pos = jnp.where(r >= first, r - first, r)
    return pos >= j


def mixer_bwd(first, proj, conv, gain, dheaded, saved):
    rows, total = proj.shape
    width = conv.shape[1]
    n = rows // ROWS
    mixed, st, res, wu, inv = saved
    m2 = lambda g, f: (n - 1 - g, 0)
    m3 = lambda g, f: (n - 1 - g, 0, 0)
    z2 = lambda g, f: (0, 0)
    return pl.pallas_call(
        mixer_bwd_kernel,
        grid_spec=pltpu.PrefetchScalarGridSpec(
            num_scalar_prefetch=1, grid=(n,),
            in_specs=[pl.BlockSpec((ROWS, total), m2),
                      pl.BlockSpec((8, total), lambda g, f: (jnp.maximum((n - 1 - g) * (ROWS // 8) - 1, 0), 0)),
                      pl.BlockSpec((4, width), z2), pl.BlockSpec((1, HEAD), z2),
                      pl.BlockSpec((ROWS, 2 * HEAD), m2), pl.BlockSpec((ROWS, 2 * HEAD), m2),
                      pl.BlockSpec((STEPS, 2 * HEAD, HEAD), m3), pl.BlockSpec((STEPS, 2 * STEP, HEAD), m3),
                      pl.BlockSpec((STEPS, 2 * STEP, 2 * HEAD), m3), pl.BlockSpec((STEPS, 2 * STEP, 2 * STEP), m3)],
            out_specs=[pl.BlockSpec((ROWS, total), m2), pl.BlockSpec((4, width), z2), pl.BlockSpec((1, HEAD), z2)],
            scratch_shapes=[pltpu.VMEM((2, HEAD, HEAD), f32), pltpu.VMEM((ROWS + 8, width), f32), pltpu.VMEM((ROWS + 8, width), f32),
                            pltpu.VMEM((4, 8, width), f32), pltpu.VMEM((8, HEAD), f32)]),
        out_shape=[jax.ShapeDtypeStruct((rows, total), bf16), jax.ShapeDtypeStruct((4, width), f32), jax.ShapeDtypeStruct((1, HEAD), f32)],
        compiler_params=pltpu.CompilerParams(dimension_semantics=("arbitrary",), vmem_limit_bytes=56 * 2**20),
    )(first, proj, proj, conv, gain, dheaded, mixed, st, res, wu, inv)


def rms_norm(values, scales):
    inverse = lax.rsqrt(jnp.mean(values * values, axis=-1, keepdims=True) + 1e-05)
    return values * inverse * scales


def gather(x):
    return lax.all_gather(x, "tensor", axis=0, tiled=True)


def scatter_sum(x):
    return lax.psum_scatter(x, "tensor", scatter_dimension=0, tiled=True)


def dot(a, b, dims=NN):
    return lax.dot_general(a, b, dims, preferred_element_type=f32)


def on_device(tokens, lengths, attn_gain, qkv_weight, beta_weight, conv_weight, head_gain, out_weight, mlp_gain, gate_up_weight, down_weight, cotangent):
    model_width = tokens.shape[1]
    width = qkv_weight.shape[1] * qkv_weight.shape[2]
    heads = beta_weight.shape[1]
    first = lengths[0, :1]
    local_in = tokens.astype(f32)
    first_scale = attn_gain.astype(f32)
    second_scale = mlp_gain.astype(f32)
    head_scale = head_gain.astype(f32)[None]
    conv = conv_weight.reshape(conv_weight.shape[0], -1).astype(f32)
    qkv_matrix = jnp.concatenate([qkv_weight.reshape(model_width, -1), jnp.pad(beta_weight, ((0, 0), (0, HEAD - heads)))], axis=1)
    out_all = gather(out_weight)
    attn_in = rms_norm(local_in, first_scale).astype(bf16)
    attn_all = gather(attn_in)
    proj = dot(attn_all, qkv_matrix)
    headed, *saved = mixer_fwd(first, proj, conv, head_scale)
    headed_rows = lax.all_to_all(headed, "tensor", split_axis=0, concat_axis=1, tiled=True)
    hidden_res = local_in + dot(headed_rows, out_all)
    mlp_in = rms_norm(hidden_res, second_scale).astype(bf16)
    mlp_all = gather(mlp_in)
    cot_all = gather(cotangent)
    gate_up_matrix = gate_up_weight.reshape(model_width, -1)
    gate_up = dot(mlp_all, gate_up_matrix)
    hidden_units = gate_up.shape[1] // 2
    gate_pre = gate_up[:, :hidden_units]
    up_pre = gate_up[:, hidden_units:]
    sigmoid_gate = jax.nn.sigmoid(gate_pre)
    silu_gate = gate_pre * sigmoid_gate
    activated = (silu_gate * up_pre).astype(bf16)
    d_activated = dot(cot_all, down_weight, NT)
    d_gate = (d_activated * up_pre * sigmoid_gate * (1.0 + gate_pre * (1.0 - sigmoid_gate))).astype(bf16)
    d_up = (d_activated * silu_gate).astype(bf16)
    d_gate_up = jnp.concatenate([d_gate, d_up], axis=1)
    d_mlp_in = scatter_sum(dot(d_gate_up, gate_up_matrix, NT).astype(bf16)).astype(f32)
    mlp_out = scatter_sum(dot(activated, down_weight).astype(bf16)).astype(f32)
    output = (hidden_res + mlp_out).astype(bf16)
    down_part = dot(activated, cot_all, TN).astype(bf16)
    gate_up_part = dot(mlp_all, d_gate_up, TN).astype(bf16)
    gate_up_sum, down_sum = lax.psum((gate_up_part, down_part), "dp")
    d_from_mlp, mlp_gain_part = jax.vjp(rms_norm, hidden_res, second_scale)[1](d_mlp_in)
    d_hidden = cotangent.astype(f32) + d_from_mlp
    d_attn = d_hidden.astype(bf16)
    d_headed_rows = dot(d_attn, out_all, NT).astype(bf16)
    d_headed = lax.all_to_all(d_headed_rows, "tensor", split_axis=1, concat_axis=0, tiled=True)
    d_attn_all = gather(d_attn)
    d_cat, conv_part, head_gain_part = mixer_bwd(first, proj, conv, head_scale, d_headed, saved)
    d_attn_in = scatter_sum(dot(d_cat, qkv_matrix, NT).astype(bf16)).astype(f32)
    d_from_attn, attn_gain_part = jax.vjp(rms_norm, local_in, first_scale)[1](d_attn_in)
    input_grad = d_hidden + d_from_attn
    d_cat, gate_up_sum, down_sum = lax.optimization_barrier((d_cat, gate_up_sum, down_sum))
    cat_part = dot(attn_all, d_cat, TN).astype(bf16)
    out_part = dot(headed, d_attn_all, TN).astype(bf16)
    cat_sum, out_sum, conv_sum = lax.psum((cat_part, out_part, conv_part.astype(bf16)), "dp")
    attn_gain_grad, head_gain_grad, mlp_gain_grad = lax.psum((attn_gain_part, head_gain_part[0], mlp_gain_part), ("dp", "tensor"))
    return (
        output,
        input_grad,
        attn_gain_grad,
        cat_sum[:, :width].astype(f32).reshape(qkv_weight.shape),
        cat_sum[:, width:width + heads].astype(f32),
        conv_sum.astype(f32).reshape(conv_weight.shape),
        head_gain_grad,
        out_sum.astype(f32),
        mlp_gain_grad,
        gate_up_sum.astype(f32).reshape(gate_up_weight.shape),
        down_sum.astype(f32),
    )


def solution(mesh):
    rows = P(("dp", "tensor"), None)
    last = P(None, None, "tensor")
    return jax.shard_map(
        on_device,
        mesh=mesh,
        in_specs=(rows, P("dp", None), P(), last, P(None, "tensor"), last, P(), P("tensor", None), P(), last, P("tensor", None), rows),
        out_specs=(rows, rows, P(), last, P(None, "tensor"), last, P(), P("tensor", None), P(), last, P("tensor", None)),
        check_vma=False,
    )
```

```python
import functools
import jax
import jax.numpy as jnp
from jax import lax
from jax.experimental import pallas as pl
from jax.experimental.pallas import tpu as pltpu
from jax.sharding import PartitionSpec as P

HEAD = 128
STEP = 128
SPAN = 64
STEPS = 4
ROWS = STEP * STEPS
NN = (((1,), (0,)), ((), ()))
NT = (((1,), (1,)), ((), ()))
TN = (((0,), (0,)), ((), ()))
f32 = jnp.float32
bf16 = jnp.bfloat16


def mm(a, b, dims=NN):
    return lax.dot_general(a.astype(bf16), b.astype(bf16), dims, preferred_element_type=f32)


def split(a):
    high = a.astype(bf16)
    return high, (a - high.astype(f32)).astype(bf16)


def stack(x):
    return jnp.concatenate([x[:, :HEAD], x[:, HEAD:]], axis=0)


def unstack(x):
    return jnp.concatenate([x[:STEP], x[STEP:]], axis=1)


def pair_masks():
    i = lax.broadcasted_iota(jnp.int32, (2 * STEP, 2 * STEP), 0)
    j = lax.broadcasted_iota(jnp.int32, (2 * STEP, 2 * STEP), 1)
    same = (i // STEP) == (j // STEP)
    cross = ((i % STEP) >= SPAN) & ((j % STEP) < SPAN)
    levels = []
    size = 1
    while size < STEP:
        levels.append(((i // (2 * size)) == (j // (2 * size))) & ((i // size) % 2 == 1) & ((j // size) % 2 == 0))
        size *= 2
    return same & (i > j), same & (i >= j), cross, levels, i == j


def tri_inverse(a, levels, eye):
    inv = jnp.where(eye, 1.0, jnp.where(levels[0], -a, 0.0))
    for level in levels[1:]:
        low = inv.astype(bf16)
        part = jnp.where(level, a, 0.0).astype(bf16)
        inv = inv - mm(mm(low, part), low)
    return inv


def row_masks(start_reset, mid_reset):
    r = lax.broadcasted_iota(jnp.int32, (2 * STEP, HEAD), 0) % STEP
    upper = r < SPAN
    enter = jnp.where(upper, 1.0 - start_reset, (1.0 - start_reset) * (1.0 - mid_reset))
    leave = jnp.where(upper, 1.0 - mid_reset, 1.0)
    keep = (1.0 - start_reset) * (1.0 - mid_reset)
    return enter, leave, keep


def resets(step_start, first):
    start = jnp.where((step_start == 0) | (step_start == first), 1.0, 0.0).astype(f32)
    mid = jnp.where(step_start + SPAN == first, 1.0, 0.0).astype(f32)
    return start, mid


def conv_masks(base, first, rows):
    r = lax.broadcasted_iota(jnp.int32, (rows, HEAD), 0) + base
    pos = jnp.where(r >= first, r - first, r)
    return [pos >= j for j in range(4)]


def mixer_fwd_kernel(first_ref, proj_ref, conv_ref, gain_ref, headed_ref, mixed_ref, state_out, res_out, wu_out, inv_out, state, buf):
    g = pl.program_id(0)
    first = first_ref[0]

    @pl.when(g == 0)
    def _():
        state[...] = jnp.zeros_like(state)
        buf[0:8, :] = jnp.zeros((8, buf.shape[1]), f32)

    width = buf.shape[1]
    buf[8:, :] = proj_ref[:, :width]
    valid = conv_masks(g * ROWS, first, ROWS)
    cols = []
    for c in range(width // HEAD):
        cs = slice(c * HEAD, (c + 1) * HEAD)
        total = buf[8:8 + ROWS, cs] * conv_ref[0:1, cs]
        for j in range(1, 4):
            total = total + jnp.where(valid[j], buf[8 - j:8 - j + ROWS, cs] * conv_ref[j:j + 1, cs], 0.0)
        cols.append(total * jax.nn.sigmoid(total))
    buf[0:8, :] = buf[ROWS:ROWS + 8, :]
    betas = jax.nn.sigmoid(proj_ref[:, width:])
    strict, causal, cross, levels, eye = pair_masks()
    mem = [state[0], state[1]]
    for s in range(STEPS):
        rs = slice(s * STEP, (s + 1) * STEP)
        start_reset, mid_reset = resets(g * ROWS + s * STEP, first)
        enter, leave, keep = row_masks(start_reset, mid_reset)
        gate = jnp.where(cross, 1.0 - mid_reset, 1.0)
        two = lambda n: jnp.concatenate([cols[2 * n][rs], cols[2 * n + 1][rs]], axis=0)
        q, k, v = two(0), two(1), two(2)
        q = q * lax.rsqrt(jnp.sum(q * q, axis=-1, keepdims=True) + 1e-6)
        k = k * lax.rsqrt(jnp.sum(k * k, axis=-1, keepdims=True) + 1e-6)
        b = jnp.concatenate([betas[rs, 0:1], betas[rs, 1:2]], axis=0)
        gp = mm(jnp.concatenate([k, q], axis=0), k, NT)
        a = jnp.where(strict, gate * gp[:2 * STEP], 0.0) * b
        p = jnp.where(causal, gate * gp[2 * STEP:], 0.0)
        inv = tri_inverse(a, levels, eye)
        wu = mm(inv, jnp.concatenate([b * k, b * v], axis=1))
        inv_out[s] = inv.astype(bf16)
        wu_out[s] = wu.astype(bf16)
        state_out[s, :HEAD] = mem[0].astype(bf16)
        state_out[s, HEAD:] = mem[1].astype(bf16)
        w = wu[:, :HEAD] * enter
        qe = q * enter
        ws, qs = [], []
        for h in range(2):
            hs = slice(h * STEP, (h + 1) * STEP)
            both = mm(jnp.concatenate([w[hs], qe[hs]], axis=0), mem[h])
            ws.append(both[:STEP])
            qs.append(both[STEP:])
        res = wu[:, HEAD:] - jnp.concatenate(ws, axis=0)
        res_out[s] = res.astype(bf16)
        ke = k * leave
        for h in range(2):
            hs = slice(h * STEP, (h + 1) * STEP)
            mem[h] = keep * mem[h] + mm(ke[hs], res[hs], TN)
        o = jnp.concatenate(qs, axis=0) + mm(p, res)
        mixed_ref[rs, :] = unstack(o)
        headed = o * lax.rsqrt(jnp.mean(o * o, axis=-1, keepdims=True) + 1e-5) * gain_ref[...]
        headed_ref[rs, :] = unstack(headed).astype(bf16)
    state[0] = mem[0]
    state[1] = mem[1]


def mixer_fwd(first, proj, conv, gain):
    rows, total = proj.shape
    width = conv.shape[1]
    n = rows // ROWS
    steps = rows // STEP
    return pl.pallas_call(
        mixer_fwd_kernel,
        grid_spec=pltpu.PrefetchScalarGridSpec(
            num_scalar_prefetch=1, grid=(n,),
            in_specs=[pl.BlockSpec((ROWS, total), lambda g, f: (g, 0)), pl.BlockSpec((4, width), lambda g, f: (0, 0)), pl.BlockSpec((1, HEAD), lambda g, f: (0, 0))],
            out_specs=[pl.BlockSpec((ROWS, 2 * HEAD), lambda g, f: (g, 0)), pl.BlockSpec((ROWS, 2 * HEAD), lambda g, f: (g, 0)),
                       pl.BlockSpec((STEPS, 2 * HEAD, HEAD), lambda g, f: (g, 0, 0)), pl.BlockSpec((STEPS, 2 * STEP, HEAD), lambda g, f: (g, 0, 0)),
                       pl.BlockSpec((STEPS, 2 * STEP, 2 * HEAD), lambda g, f: (g, 0, 0)), pl.BlockSpec((STEPS, 2 * STEP, 2 * STEP), lambda g, f: (g, 0, 0))],
            scratch_shapes=[pltpu.VMEM((2, HEAD, HEAD), f32), pltpu.VMEM((ROWS + 8, width), f32)]),
        out_shape=[jax.ShapeDtypeStruct((rows, 2 * HEAD), bf16), jax.ShapeDtypeStruct((rows, 2 * HEAD), f32),
                   jax.ShapeDtypeStruct((steps, 2 * HEAD, HEAD), bf16), jax.ShapeDtypeStruct((steps, 2 * STEP, HEAD), bf16),
                   jax.ShapeDtypeStruct((steps, 2 * STEP, 2 * HEAD), bf16), jax.ShapeDtypeStruct((steps, 2 * STEP, 2 * STEP), bf16)],
        compiler_params=pltpu.CompilerParams(dimension_semantics=("arbitrary",), vmem_limit_bytes=48 * 2**20),
    )(first, proj, conv, gain)


def mixer_bwd_kernel(first_ref, proj_ref, prev_ref, conv_ref, gain_ref, dh_ref, mixed_ref, state_in, res_in, wu_in, inv_in,
                     dcat_ref, dconv_ref, dgain_ref, dstate, buf, dbuf, cacc, gacc):
    g = pl.program_id(0)
    n = pl.num_programs(0)
    blk = n - 1 - g
    first = first_ref[0]
    width = buf.shape[1]

    @pl.when(g == 0)
    def _():
        dstate[...] = jnp.zeros_like(dstate)
        dbuf[ROWS:, :] = jnp.zeros((8, width), f32)
        cacc[...] = jnp.zeros_like(cacc)
        gacc[...] = jnp.zeros_like(gacc)

    buf[0:8, :] = prev_ref[:, :width]
    buf[8:, :] = proj_ref[:, :width]
    valid = conv_masks(blk * ROWS, first, ROWS + 8)
    cols, slopes = [], []
    for c in range(width // HEAD):
        cs = slice(c * HEAD, (c + 1) * HEAD)
        total = buf[8:8 + ROWS, cs] * conv_ref[0:1, cs]
        for j in range(1, 4):
            total = total + jnp.where(valid[j][:ROWS], buf[8 - j:8 - j + ROWS, cs] * conv_ref[j:j + 1, cs], 0.0)
        sig = jax.nn.sigmoid(total)
        cols.append(total * sig)
        slopes.append(sig * (1.0 + total * (1.0 - sig)))
    betas = jax.nn.sigmoid(proj_ref[:, width:])
    strict, causal, cross, _, _ = pair_masks()
    lane = lax.broadcasted_iota(jnp.int32, (STEP, HEAD), 1)
    dmem = [dstate[0], dstate[1]]
    for s in reversed(range(STEPS)):
        rs = slice(s * STEP, (s + 1) * STEP)
        start_reset, mid_reset = resets(blk * ROWS + s * STEP, first)
        enter, leave, keep = row_masks(start_reset, mid_reset)
        gate = jnp.where(cross, 1.0 - mid_reset, 1.0)
        two = lambda n: jnp.concatenate([cols[2 * n][rs], cols[2 * n + 1][rs]], axis=0)
        q, k, v = two(0), two(1), two(2)
        rq = lax.rsqrt(jnp.sum(q * q, axis=-1, keepdims=True) + 1e-6)
        rk = lax.rsqrt(jnp.sum(k * k, axis=-1, keepdims=True) + 1e-6)
        q = q * rq
        k = k * rk
        b = jnp.concatenate([betas[rs, 0:1], betas[rs, 1:2]], axis=0)
        gp = mm(jnp.concatenate([k, q], axis=0), k, NT)
        gram = jnp.where(strict, gate * gp[:2 * STEP], 0.0)
        p = jnp.where(causal, gate * gp[2 * STEP:], 0.0)
        o = stack(mixed_ref[rs, :])
        dh = stack(dh_ref[rs, :].astype(f32))
        ro = lax.rsqrt(jnp.mean(o * o, axis=-1, keepdims=True) + 1e-5)
        on = o * ro
        gacc[...] += jnp.sum((dh * on).reshape(2 * STEP // 8, 8, HEAD), axis=0)
        dn = dh * gain_ref[...]
        do = ro * (dn - on * jnp.mean(dn * on, axis=-1, keepdims=True))
        mem = state_in[s]
        res = res_in[s]
        wu = wu_in[s]
        inv = inv_in[s]
        do16 = do.astype(bf16)
        doe = (do * enter).astype(bf16)
        q16 = q.astype(bf16)
        k16 = k.astype(bf16)
        ke16 = (k * leave).astype(bf16)
        we = (wu[:, :HEAD].astype(f32) * enter).astype(bf16)
        dres = mm(p, do16, TN)
        hs = [slice(h * STEP, (h + 1) * STEP) for h in range(2)]
        dres = dres + jnp.concatenate([mm(ke16[hs[h]], dmem[h]) for h in range(2)], axis=0)
        dres16 = dres.astype(bf16)
        dke = jnp.concatenate([mm(res[hs[h]], dmem[h], NT) for h in range(2)], axis=0)
        for h in range(2):
            dmem[h] = keep * dmem[h] + mm(q16[hs[h]], doe[hs[h]], TN) - mm(we[hs[h]], dres16[hs[h]], TN)
        dp = jnp.where(causal, gate * mm(do16, res, NT), 0.0).astype(bf16)
        both = [mm(jnp.concatenate([do16[hs[h]], dres16[hs[h]]], axis=0), mem[h * HEAD:(h + 1) * HEAD], NT) for h in range(2)]
        dq = enter * jnp.concatenate([both[0][:STEP], both[1][:STEP]], axis=0) + mm(dp, k16)
        dw = -enter * jnp.concatenate([both[0][STEP:], both[1][STEP:]], axis=0)
        dk = mm(dp, q16, TN) + leave * dke
        db_kv = mm(inv, jnp.concatenate([dw, dres], axis=1), TN)
        da = -jnp.where(strict, gate * mm(db_kv, wu, NT), 0.0)
        dbk, dbv = db_kv[:, :HEAD], db_kv[:, HEAD:]
        dbeta = jnp.sum(da * gram, axis=-1, keepdims=True) + jnp.sum(dbk * k + dbv * v, axis=-1, keepdims=True)
        dg = (da * b).astype(bf16)
        dk = dk + mm(dg, k16) + mm(dg, k16, TN) + b * dbk
        dv = b * dbv
        dq = rq * (dq - q * jnp.sum(dq * q, axis=-1, keepdims=True))
        dk = rk * (dk - k * jnp.sum(dk * k, axis=-1, keepdims=True))
        dpre = dbeta * b * (1.0 - b)
        for i, x in enumerate((dq, dk, dv)):
            for h in range(2):
                c = 2 * i + h
                dbuf[rs, c * HEAD:(c + 1) * HEAD] = x[hs[h]] * slopes[c][rs]
        dcat_ref[rs, width:] = jnp.where(lane == 0, dpre[:STEP], jnp.where(lane == 1, dpre[STEP:], 0.0)).astype(bf16)
    dstate[0] = dmem[0]
    dstate[1] = dmem[1]
    for c in range(width // HEAD):
        cs = slice(c * HEAD, (c + 1) * HEAD)
        total = dbuf[:ROWS, cs] * conv_ref[0:1, cs]
        grads = [jnp.sum((buf[8:8 + ROWS, cs] * dbuf[:ROWS, cs]).reshape(ROWS // 8, 8, HEAD), axis=0)]
        for j in range(1, 4):
            total = total + jnp.where(shifted_valid(blk * ROWS, first, j), dbuf[j:j + ROWS, cs] * conv_ref[j:j + 1, cs], 0.0)
            grads.append(jnp.sum(jnp.where(valid[j][:ROWS], buf[8 - j:8 - j + ROWS, cs] * dbuf[:ROWS, cs], 0.0).reshape(ROWS // 8, 8, HEAD), axis=0))
        dcat_ref[:, cs] = total.astype(bf16)
        for j in range(4):
            cacc[j, :, cs] += grads[j]
    dbuf[ROWS:, :] = dbuf[0:8, :]

    @pl.when(g == n - 1)
    def _():
        for j in range(4):
            dconv_ref[j:j + 1, :] = jnp.sum(cacc[j], axis=0, keepdims=True)
        dgain_ref[...] = jnp.sum(gacc[...], axis=0, keepdims=True)


def shifted_valid(base, first, j):
    r = lax.broadcasted_iota(jnp.int32, (ROWS, HEAD), 0) + base + j
    pos = jnp.where(r >= first, r - first, r)
    return pos >= j


def mixer_bwd(first, proj, conv, gain, dheaded, saved):
    rows, total = proj.shape
    width = conv.shape[1]
    n = rows // ROWS
    mixed, st, res, wu, inv = saved
    m2 = lambda g, f: (n - 1 - g, 0)
    m3 = lambda g, f: (n - 1 - g, 0, 0)
    z2 = lambda g, f: (0, 0)
    return pl.pallas_call(
        mixer_bwd_kernel,
        grid_spec=pltpu.PrefetchScalarGridSpec(
            num_scalar_prefetch=1, grid=(n,),
            in_specs=[pl.BlockSpec((ROWS, total), m2),
                      pl.BlockSpec((8, total), lambda g, f: (jnp.maximum((n - 1 - g) * (ROWS // 8) - 1, 0), 0)),
                      pl.BlockSpec((4, width), z2), pl.BlockSpec((1, HEAD), z2),
                      pl.BlockSpec((ROWS, 2 * HEAD), m2), pl.BlockSpec((ROWS, 2 * HEAD), m2),
                      pl.BlockSpec((STEPS, 2 * HEAD, HEAD), m3), pl.BlockSpec((STEPS, 2 * STEP, HEAD), m3),
                      pl.BlockSpec((STEPS, 2 * STEP, 2 * HEAD), m3), pl.BlockSpec((STEPS, 2 * STEP, 2 * STEP), m3)],
            out_specs=[pl.BlockSpec((ROWS, total), m2), pl.BlockSpec((4, width), z2), pl.BlockSpec((1, HEAD), z2)],
            scratch_shapes=[pltpu.VMEM((2, HEAD, HEAD), f32), pltpu.VMEM((ROWS + 8, width), f32), pltpu.VMEM((ROWS + 8, width), f32),
                            pltpu.VMEM((4, 8, width), f32), pltpu.VMEM((8, HEAD), f32)]),
        out_shape=[jax.ShapeDtypeStruct((rows, total), bf16), jax.ShapeDtypeStruct((4, width), f32), jax.ShapeDtypeStruct((1, HEAD), f32)],
        compiler_params=pltpu.CompilerParams(dimension_semantics=("arbitrary",), vmem_limit_bytes=56 * 2**20),
    )(first, proj, proj, conv, gain, dheaded, mixed, st, res, wu, inv)


MESH_ID = pl.DeviceIdType.MESH
HALF = 2


def places():
    d = lax.axis_index("dp")
    t = lax.axis_index("tensor")
    beside = t + 1 - 2 * lax.rem(t, 2)
    across = lax.rem(t + 2, 4)
    corner = lax.rem(beside + 2, 4)
    return d, t, beside, across, corner


def push(src, dst, send, recv, device):
    copy = pltpu.make_async_remote_copy(src_ref=src, dst_ref=dst, send_sem=send, recv_sem=recv, device_id=device, device_id_type=MESH_ID)
    copy.start()
    return copy


def greet(devices):
    barrier = pltpu.get_barrier_semaphore()
    for device in devices:
        pl.semaphore_signal(barrier, inc=1, device_id=device, device_id_type=MESH_ID)
    pl.semaphore_wait(barrier, len(devices))


def row_block(owner, part, owner_rows, part_rows):
    return pl.ds(pl.multiple_of(owner * owner_rows + part * part_rows, part_rows), part_rows)


def mlp_kernel(x_ref, cot_ref, gate_w, up_w, down_w, all_ref, act_ref, dgate_ref, dup_ref, out_ref, sum_ref, mine, to_beside, from_beside, to_across, from_across, to_own, from_own, send, recv):
    d, t, beside, across, corner = places()
    rows = x_ref.shape[0]
    part = rows // HALF
    greet([(d, beside), (d, across)])
    copies = []
    arrive_beside, arrive_across = [], []
    for s in range(HALF):
        src = x_ref.at[pl.ds(s * part, part)]
        dst = all_ref.at[row_block(t, s, rows, part)]
        arrive_across.append(push(src, dst, send.at[0, s], recv.at[0, s], (d, across)))
        arrive_beside.append(push(src, dst, send.at[1, s], recv.at[1, s], (d, beside)))
    all_ref[pl.ds(pl.multiple_of(t * rows, rows), rows), :] = x_ref[...]
    copies += arrive_across + arrive_beside

    def work(owner, s):
        at = row_block(owner, s, rows, part)
        x = all_ref[at, :]
        gate = lax.dot_general(x, gate_w[...], NN, preferred_element_type=f32)
        up = lax.dot_general(x, up_w[...], NN, preferred_element_type=f32)
        sig = jax.nn.sigmoid(gate)
        silu = gate * sig
        act = (silu * up).astype(bf16)
        act_ref[at, :] = act
        d_act = lax.dot_general(cot_ref[at, :], down_w[...], NT, preferred_element_type=f32)
        d_gate = (d_act * up * sig * (1.0 + gate * (1.0 - sig))).astype(bf16)
        d_up = (d_act * silu).astype(bf16)
        dgate_ref[at, :] = d_gate
        dup_ref[at, :] = d_up
        out_ref[at, :] = lax.dot_general(act, down_w[...], NN, preferred_element_type=f32).astype(bf16)
        return lax.dot_general(d_gate, gate_w[...], NT, preferred_element_type=f32) + lax.dot_general(d_up, up_w[...], NT, preferred_element_type=f32)

    for s in range(HALF):
        mine[pl.ds(s * part, part), :] = work(t, s)
    own_copies = []
    for s in range(HALF):
        arrive_beside[s].wait_recv()
        at = pl.ds(s * part, part)
        to_own[at, :] = work(beside, s).astype(bf16)
        own_copies.append(push(to_own.at[at], from_own.at[at], send.at[2, s], recv.at[2, s], (d, beside)))
    passed, sums = [], []
    for s in range(HALF):
        at = pl.ds(s * part, part)
        arrive_across[s].wait_recv()
        block = all_ref.at[row_block(across, s, rows, part)]
        passed.append(push(block, block, send.at[3, s], recv.at[3, s], (d, beside)))
        passed[s].wait_recv()
        to_beside[at, :] = work(corner, s).astype(bf16)
        handed = push(to_beside.at[at], from_beside.at[at], send.at[4, s], recv.at[4, s], (d, beside))
        total = work(across, s)
        handed.wait_recv()
        to_across[at, :] = (total + from_beside[at, :].astype(f32)).astype(bf16)
        sums.append(push(to_across.at[at], from_across.at[at], send.at[5, s], recv.at[5, s], (d, across)))
        copies.append(handed)
    for s in range(HALF):
        at = pl.ds(s * part, part)
        own_copies[s].wait_recv()
        sums[s].wait_recv()
        sum_ref[at, :] = mine[at, :] + from_own[at, :].astype(f32) + from_across[at, :].astype(f32)
    for copy in copies + own_copies + passed + sums:
        copy.wait_send()


def mlp(x, cot, gate_w, up_w, down_w):
    rows, width = x.shape
    total = cot.shape[0]
    units = gate_w.shape[1]
    vmem = pl.BlockSpec(memory_space=pltpu.VMEM)
    half = lambda: pltpu.VMEM((rows, width), bf16)
    return pl.pallas_call(
        mlp_kernel,
        in_specs=[vmem] * 5,
        out_specs=[vmem] * 6,
        out_shape=[jax.ShapeDtypeStruct((total, width), bf16), jax.ShapeDtypeStruct((total, units), bf16), jax.ShapeDtypeStruct((total, units), bf16),
                   jax.ShapeDtypeStruct((total, units), bf16), jax.ShapeDtypeStruct((total, width), bf16), jax.ShapeDtypeStruct((rows, width), f32)],
        scratch_shapes=[pltpu.VMEM((rows, width), f32), half(), half(), half(), half(), half(), half(),
                        pltpu.SemaphoreType.DMA((6, HALF)), pltpu.SemaphoreType.DMA((6, HALF))],
        compiler_params=pltpu.CompilerParams(collective_id=1, has_side_effects=True, vmem_limit_bytes=60 * 2**20),
    )(x, cot, gate_w, up_w, down_w)


def final_kernel(n_dp, dcat_ref, w_ref, tok_ref, dhid_ref, gain_ref, small_ref, dx_ref, small_out, mine, to_beside, from_beside, to_across, from_across, to_own, from_own,
                 group_send, group_land, all_send, all_land, gain_acc, send, recv, send_g, recv_g, send_a, recv_a):
    d, t, beside, across, corner = places()
    rows = tok_ref.shape[0]
    part = rows // HALF
    others = [lax.rem(d + k, n_dp) for k in range(1, n_dp)]
    greet([(d, beside), (d, across), (d, corner)] + [(o, t) for o in others])

    def work(owner, s):
        return lax.dot_general(dcat_ref[row_block(owner, s, rows, part), :], w_ref[...], NT, preferred_element_type=f32)

    handed, sums, owns = [], [], []
    for s in range(HALF):
        at = pl.ds(s * part, part)
        to_beside[at, :] = work(corner, s).astype(bf16)
        handed.append(push(to_beside.at[at], from_beside.at[at], send.at[0, s], recv.at[0, s], (d, beside)))
        total = work(across, s)
        handed[s].wait_recv()
        to_across[at, :] = (total + from_beside[at, :].astype(f32)).astype(bf16)
        sums.append(push(to_across.at[at], from_across.at[at], send.at[1, s], recv.at[1, s], (d, across)))
    for s in range(HALF):
        at = pl.ds(s * part, part)
        to_own[at, :] = work(beside, s).astype(bf16)
        owns.append(push(to_own.at[at], from_own.at[at], send.at[2, s], recv.at[2, s], (d, beside)))
        mine[at, :] = work(t, s)
    gain_acc[...] = jnp.zeros_like(gain_acc)
    gain = gain_ref[...]
    piece = 64
    for s in range(HALF):
        owns[s].wait_recv()
        sums[s].wait_recv()

        def finish(i, carry, s=s):
            at = pl.ds(pl.multiple_of(s * part + i * piece, piece), piece)
            grad = mine[at, :] + from_own[at, :].astype(f32) + from_across[at, :].astype(f32)
            tok = tok_ref[at, :].astype(f32)
            r = lax.rsqrt(jnp.mean(tok * tok, axis=-1, keepdims=True) + 1e-5)
            scaled = gain * grad
            dx_ref[at, :] = dhid_ref[at, :] + r * scaled - tok * (r * r * r * jnp.mean(tok * scaled, axis=-1, keepdims=True))
            gain_acc[...] += jnp.sum((grad * tok * r).reshape(piece // 8, 8, grad.shape[1]), axis=0)
            return carry

        lax.fori_loop(0, part // piece, finish, 0)
    line = lax.broadcasted_iota(jnp.int32, small_ref.shape, 0)
    small = jnp.where(line == 0, jnp.sum(gain_acc[...], axis=0, keepdims=True), small_ref[...])
    group_send[...] = small
    grouped = [push(group_send, group_land.at[i], send_g.at[i], recv_g.at[i], (d, peer)) for i, peer in enumerate((beside, across, corner))]
    for copy in grouped:
        copy.wait_recv()
    both = small + group_land[0]
    both = both + (group_land[1] + group_land[2])
    small = jnp.where(line < 3, both, small)
    all_send[...] = small
    spread = [push(all_send, all_land.at[i], send_a.at[i], recv_a.at[i], (o, t)) for i, o in enumerate(others)]
    for i, copy in enumerate(spread):
        copy.wait_recv()
        small = small + all_land[i]
    small_out[...] = small
    for copy in handed + sums + owns + grouped + spread:
        copy.wait_send()


def final(n_dp, dcat, w, tokens, dhid, gain, small):
    rows, width = tokens.shape
    vmem = pl.BlockSpec(memory_space=pltpu.VMEM)
    half = lambda: pltpu.VMEM((rows, width), bf16)
    line = small.shape
    dma = pltpu.SemaphoreType.DMA
    return pl.pallas_call(
        functools.partial(final_kernel, n_dp),
        in_specs=[vmem] * 6,
        out_specs=[vmem] * 2,
        out_shape=[jax.ShapeDtypeStruct((rows, width), f32), jax.ShapeDtypeStruct(line, f32)],
        scratch_shapes=[pltpu.VMEM((rows, width), f32), half(), half(), half(), half(), half(), half(),
                        pltpu.VMEM(line, f32), pltpu.VMEM((3,) + line, f32), pltpu.VMEM(line, f32), pltpu.VMEM((n_dp - 1,) + line, f32), pltpu.VMEM((8, width), f32),
                        dma((3, HALF)), dma((3, HALF)), dma((3,)), dma((3,)), dma((n_dp - 1,)), dma((n_dp - 1,))],
        compiler_params=pltpu.CompilerParams(collective_id=2, has_side_effects=True, vmem_limit_bytes=48 * 2**20),
        cost_estimate=pl.CostEstimate(flops=2 * dcat.shape[0] * dcat.shape[1] * width, bytes_accessed=12 * 2**20, transcendentals=0),
    )(dcat, w, tokens, dhid, gain, small)


def rms_norm(values, scales):
    inverse = lax.rsqrt(jnp.mean(values * values, axis=-1, keepdims=True) + 1e-05)
    return values * inverse * scales


def gather(x):
    return lax.all_gather(x, "tensor", axis=0, tiled=True)


def dot(a, b, dims=NN):
    return lax.dot_general(a, b, dims, preferred_element_type=f32)


def on_device(tokens, lengths, attn_gain, qkv_weight, beta_weight, conv_weight, head_gain, out_weight, mlp_gain, gate_up_weight, down_weight, cotangent):
    model_width = tokens.shape[1]
    width = qkv_weight.shape[1] * qkv_weight.shape[2]
    heads = beta_weight.shape[1]
    first = lengths[0, :1]
    local_in = tokens.astype(f32)
    first_scale = attn_gain.astype(f32)
    second_scale = mlp_gain.astype(f32)
    head_scale = head_gain.astype(f32)[None]
    conv = conv_weight.reshape(conv_weight.shape[0], -1).astype(f32)
    qkv_matrix = jnp.concatenate([qkv_weight.reshape(model_width, -1), jnp.pad(beta_weight, ((0, 0), (0, HEAD - heads)))], axis=1)
    attn_in = rms_norm(local_in, first_scale).astype(bf16)
    attn_all = gather(attn_in)
    out_all = gather(out_weight)
    cot_all = gather(cotangent)
    proj = dot(attn_all, qkv_matrix)
    headed, *saved = mixer_fwd(first, proj, conv, head_scale)
    headed_rows = lax.all_to_all(headed, "tensor", split_axis=0, concat_axis=1, tiled=True)
    hidden_res = local_in + dot(headed_rows, out_all)
    mlp_in = rms_norm(hidden_res, second_scale).astype(bf16)
    gate_w, up_w = gate_up_weight[:, 0], gate_up_weight[:, 1]
    mlp_all, activated, d_gate, d_up, out_parts, d_mlp_in = mlp(mlp_in, cot_all, gate_w, up_w, down_weight)
    d_from_mlp, mlp_gain_part = jax.vjp(rms_norm, hidden_res, second_scale)[1](d_mlp_in)
    d_hidden = cotangent.astype(f32) + d_from_mlp
    d_attn_all = gather(d_hidden.astype(bf16))
    down_part = dot(activated, cot_all, TN).astype(bf16)
    gate_part = dot(mlp_all, d_gate, TN).astype(bf16)
    up_part = dot(mlp_all, d_up, TN).astype(bf16)
    d_attn_all, gate_part, up_part, down_part, out_parts = lax.optimization_barrier((d_attn_all, gate_part, up_part, down_part, out_parts))
    gate_sum, up_sum, down_sum = lax.psum((gate_part, up_part, down_part), "dp")
    d_headed = dot(d_attn_all, out_weight, NT).astype(bf16)
    d_cat, conv_part, head_gain_part = mixer_bwd(first, proj, conv, head_scale, d_headed, saved)
    cat_part = dot(attn_all, d_cat, TN).astype(bf16)
    out_part = dot(headed, d_attn_all, TN).astype(bf16)
    out_parts = lax.optimization_barrier((out_parts, d_cat))[0]
    mlp_out = lax.psum_scatter(out_parts, "tensor", scatter_dimension=0, tiled=True).astype(f32)
    output = (hidden_res + mlp_out).astype(bf16)
    cat_part, out_part, gate_sum, up_sum, down_sum = lax.optimization_barrier((cat_part, out_part, gate_sum, up_sum, down_sum))
    cat_sum, out_sum = lax.psum((cat_part, out_part), "dp")
    small = jnp.concatenate([
        jnp.zeros((1, model_width), f32), mlp_gain_part[None], jnp.pad(head_gain_part, ((0, 0), (0, model_width - HEAD))),
        conv_part.reshape(-1, model_width), jnp.zeros((5 - conv_part.size // model_width, model_width), f32)], axis=0)
    input_grad, small = final(lax.axis_size("dp"), d_cat, qkv_matrix, tokens, d_hidden, first_scale[None], small)
    conv_lines = conv_part.size // model_width
    return (
        output,
        input_grad,
        small[0],
        cat_sum[:, :width].astype(f32).reshape(qkv_weight.shape),
        cat_sum[:, width:width + heads].astype(f32),
        small[3:3 + conv_lines].reshape(conv_weight.shape),
        small[2, :HEAD],
        out_sum.astype(f32),
        small[1],
        jnp.stack([gate_sum, up_sum], axis=1).astype(f32),
        down_sum.astype(f32),
    )


def solution(mesh):
    rows = P(("dp", "tensor"), None)
    last = P(None, None, "tensor")
    return jax.shard_map(
        on_device,
        mesh=mesh,
        in_specs=(rows, P("dp", None), P(), last, P(None, "tensor"), last, P(), P("tensor", None), P(), last, P("tensor", None), rows),
        out_specs=(rows, rows, P(), last, P(None, "tensor"), last, P(), P("tensor", None), P(), last, P("tensor", None)),
        check_vma=False,
    )
```

```python
import functools
import jax
import jax.numpy as jnp
from jax import lax
from jax.experimental import pallas as pl
from jax.experimental.pallas import tpu as pltpu
from jax.sharding import PartitionSpec as P

HEAD = 128
STEP = 128
SPAN = 64
STEPS = 4
ROWS = STEP * STEPS
BACK_STEPS = 2
BACK_ROWS = STEP * BACK_STEPS
RING = 8
ROUNDS = 2 * RING - 2
NN = (((1,), (0,)), ((), ()))
NT = (((1,), (1,)), ((), ()))
TN = (((0,), (0,)), ((), ()))
f32 = jnp.float32
bf16 = jnp.bfloat16


def mm(a, b, dims=NN):
    return lax.dot_general(a.astype(bf16), b.astype(bf16), dims, preferred_element_type=f32)


def split(a):
    high = a.astype(bf16)
    return high, (a - high.astype(f32)).astype(bf16)


def stack(x):
    return jnp.concatenate([x[:, :HEAD], x[:, HEAD:]], axis=0)


def unstack(x):
    return jnp.concatenate([x[:STEP], x[STEP:]], axis=1)


def pair_masks():
    i = lax.broadcasted_iota(jnp.int32, (2 * STEP, 2 * STEP), 0)
    j = lax.broadcasted_iota(jnp.int32, (2 * STEP, 2 * STEP), 1)
    same = (i // STEP) == (j // STEP)
    cross = ((i % STEP) >= SPAN) & ((j % STEP) < SPAN)
    levels = []
    size = 1
    while size < STEP:
        levels.append(((i // (2 * size)) == (j // (2 * size))) & ((i // size) % 2 == 1) & ((j // size) % 2 == 0))
        size *= 2
    return same & (i > j), same & (i >= j), cross, levels, i == j


def tri_inverses(systems, levels, eye):
    invs = [jnp.where(eye, 1.0, jnp.where(levels[0], -a, 0.0)) for a in systems]
    for level in levels[1:]:
        lows = [inv.astype(bf16) for inv in invs]
        parts = [mm(low, jnp.where(level, a, 0.0)) for low, a in zip(lows, systems)]
        parts = [mm(part, low) for part, low in zip(parts, lows)]
        invs = [inv - part for inv, part in zip(invs, parts)]
    return invs


def row_masks(start_reset, mid_reset):
    r = lax.broadcasted_iota(jnp.int32, (2 * STEP, HEAD), 0) % STEP
    upper = r < SPAN
    enter = jnp.where(upper, 1.0 - start_reset, (1.0 - start_reset) * (1.0 - mid_reset))
    leave = jnp.where(upper, 1.0 - mid_reset, 1.0)
    keep = (1.0 - start_reset) * (1.0 - mid_reset)
    return enter, leave, keep


def resets(flags, step):
    return flags[2 * step], flags[2 * step + 1]


def sigmoid(x):
    return 0.5 * jnp.tanh(0.5 * x) + 0.5


def span_masks(flags, span, count):
    row = lax.broadcasted_iota(jnp.int32, (8, HEAD), 0)
    heads, tails = [], []
    for i in range(count):
        heads.append([None] + [jnp.where(row >= j, 1.0, 1.0 - flags[span + i]) for j in range(1, 4)])
        tails.append([None] + [jnp.where(row + j < 8, 1.0, 1.0 - flags[span + i + 1]) for j in range(1, 4)])
    return heads, tails


def conv_column(buf, conv_ref, heads, cs):
    out = []
    for i in range(len(heads)):
        at = 8 + i * SPAN
        total = buf[at:at + SPAN, cs] * conv_ref[0:1, cs]
        for j in range(1, 4):
            lead = buf[at - j:at - j + 8, cs] * heads[i][j]
            rest = buf[at - j + 8:at - j + SPAN, cs]
            total = total + jnp.concatenate([lead, rest], axis=0) * conv_ref[j:j + 1, cs]
        out.append(total)
    return jnp.concatenate(out, axis=0)


def conv_column_back(buf, dbuf, conv_ref, tails, cs):
    out, grads = [], [0.0] * 4
    for i in range(len(tails)):
        at = i * SPAN
        x = buf[8 + at:8 + at + SPAN, cs]
        for j in range(4):
            if j == 0:
                grad = dbuf[at:at + SPAN, cs]
                total = grad * conv_ref[0:1, cs]
            else:
                most = dbuf[at + j:at + j + SPAN - 8, cs]
                last = dbuf[at + j + SPAN - 8:at + j + SPAN, cs] * tails[i][j]
                grad = jnp.concatenate([most, last], axis=0)
                total = total + grad * conv_ref[j:j + 1, cs]
            grads[j] = grads[j] + jnp.sum((x * grad).reshape(SPAN // 8, 8, HEAD), axis=0)
        out.append(total)
    return jnp.concatenate(out, axis=0), grads


def mixer_fwd_kernel(flags, proj_ref, conv_ref, gain_ref, headed_ref, mixed_ref, state_out, res_out, wu_out, inv_out, state, buf):
    g = pl.program_id(0)

    @pl.when(g == 0)
    def _():
        state[...] = jnp.zeros_like(state)
        buf[0:8, :] = jnp.zeros((8, buf.shape[1]), f32)

    width = buf.shape[1]
    buf[8:, :] = proj_ref[:, :width]
    heads, _ = span_masks(flags, g * (ROWS // SPAN), ROWS // SPAN)
    cols = []
    for c in range(width // HEAD):
        total = conv_column(buf, conv_ref, heads, slice(c * HEAD, (c + 1) * HEAD))
        cols.append(total * sigmoid(total))
    buf[0:8, :] = buf[ROWS:ROWS + 8, :]
    betas = sigmoid(proj_ref[:, width:])
    strict, causal, cross, levels, eye = pair_masks()
    todo = []
    for s in range(STEPS):
        rs = slice(s * STEP, (s + 1) * STEP)
        start_reset, mid_reset = resets(flags, g * STEPS + s)
        gate = jnp.where(cross, 1.0 - mid_reset, 1.0)
        two = lambda n: jnp.concatenate([cols[2 * n][rs], cols[2 * n + 1][rs]], axis=0)
        q, k, v = two(0), two(1), two(2)
        q = q * lax.rsqrt(jnp.sum(q * q, axis=-1, keepdims=True) + 1e-6)
        k = k * lax.rsqrt(jnp.sum(k * k, axis=-1, keepdims=True) + 1e-6)
        b = jnp.concatenate([betas[rs, 0:1], betas[rs, 1:2]], axis=0)
        gp = mm(jnp.concatenate([k, q], axis=0), k, NT)
        a = jnp.where(strict, gate * gp[:2 * STEP], 0.0) * b
        p = jnp.where(causal, gate * gp[2 * STEP:], 0.0)
        todo.append((q, k, v, b, a, p, row_masks(start_reset, mid_reset)))
    invs = tri_inverses([x[4] for x in todo], levels, eye)
    wus = [mm(inv, jnp.concatenate([x[3] * x[1], x[3] * x[2]], axis=1)) for inv, x in zip(invs, todo)]
    mem = [state[0], state[1]]
    for s in range(STEPS):
        rs = slice(s * STEP, (s + 1) * STEP)
        q, k, v, b, a, p, (enter, leave, keep) = todo[s]
        wu = wus[s]
        inv_out[s] = invs[s].astype(bf16)
        wu_out[s] = wu.astype(bf16)
        state_out[s, :HEAD] = mem[0].astype(bf16)
        state_out[s, HEAD:] = mem[1].astype(bf16)
        w = wu[:, :HEAD] * enter
        qe = q * enter
        ws, qs = [], []
        for h in range(2):
            hs = slice(h * STEP, (h + 1) * STEP)
            both = mm(jnp.concatenate([w[hs], qe[hs]], axis=0), mem[h])
            ws.append(both[:STEP])
            qs.append(both[STEP:])
        res = wu[:, HEAD:] - jnp.concatenate(ws, axis=0)
        res_out[s] = res.astype(bf16)
        ke = k * leave
        for h in range(2):
            hs = slice(h * STEP, (h + 1) * STEP)
            mem[h] = keep * mem[h] + mm(ke[hs], res[hs], TN)
        o = jnp.concatenate(qs, axis=0) + mm(p, res)
        mixed_ref[rs, :] = unstack(o)
        headed = o * lax.rsqrt(jnp.mean(o * o, axis=-1, keepdims=True) + 1e-5) * gain_ref[...]
        headed_ref[rs, :] = unstack(headed).astype(bf16)
    state[0] = mem[0]
    state[1] = mem[1]


def mixer_fwd(flags, proj, conv, gain):
    rows, total = proj.shape
    width = conv.shape[1]
    n = rows // ROWS
    steps = rows // STEP
    return pl.pallas_call(
        mixer_fwd_kernel,
        grid_spec=pltpu.PrefetchScalarGridSpec(
            num_scalar_prefetch=1, grid=(n,),
            in_specs=[pl.BlockSpec((ROWS, total), lambda g, f: (g, 0)), pl.BlockSpec((4, width), lambda g, f: (0, 0)), pl.BlockSpec((1, HEAD), lambda g, f: (0, 0))],
            out_specs=[pl.BlockSpec((ROWS, 2 * HEAD), lambda g, f: (g, 0)), pl.BlockSpec((ROWS, 2 * HEAD), lambda g, f: (g, 0)),
                       pl.BlockSpec((STEPS, 2 * HEAD, HEAD), lambda g, f: (g, 0, 0)), pl.BlockSpec((STEPS, 2 * STEP, HEAD), lambda g, f: (g, 0, 0)),
                       pl.BlockSpec((STEPS, 2 * STEP, 2 * HEAD), lambda g, f: (g, 0, 0)), pl.BlockSpec((STEPS, 2 * STEP, 2 * STEP), lambda g, f: (g, 0, 0))],
            scratch_shapes=[pltpu.VMEM((2, HEAD, HEAD), f32), pltpu.VMEM((ROWS + 8, width), f32)]),
        out_shape=[jax.ShapeDtypeStruct((rows, 2 * HEAD), bf16), jax.ShapeDtypeStruct((rows, 2 * HEAD), f32),
                   jax.ShapeDtypeStruct((steps, 2 * HEAD, HEAD), bf16), jax.ShapeDtypeStruct((steps, 2 * STEP, HEAD), bf16),
                   jax.ShapeDtypeStruct((steps, 2 * STEP, 2 * HEAD), bf16), jax.ShapeDtypeStruct((steps, 2 * STEP, 2 * STEP), bf16)],
        compiler_params=pltpu.CompilerParams(dimension_semantics=("arbitrary",), vmem_limit_bytes=48 * 2**20),
    )(flags, proj, conv, gain)


MESH_ID = pl.DeviceIdType.MESH
HALF = 2


def places():
    d = lax.axis_index("dp")
    t = lax.axis_index("tensor")
    beside = t + 1 - 2 * lax.rem(t, 2)
    across = lax.rem(t + 2, 4)
    corner = lax.rem(beside + 2, 4)
    return d, t, beside, across, corner


def push(src, dst, send, recv, device):
    copy = pltpu.make_async_remote_copy(src_ref=src, dst_ref=dst, send_sem=send, recv_sem=recv, device_id=device, device_id_type=MESH_ID)
    copy.start()
    return copy


def greet(devices):
    barrier = pltpu.get_barrier_semaphore()
    for device in devices:
        pl.semaphore_signal(barrier, inc=1, device_id=device, device_id_type=MESH_ID)
    pl.semaphore_wait(barrier, len(devices))


def row_block(owner, part, owner_rows, part_rows):
    return pl.ds(pl.multiple_of(owner * owner_rows + part * part_rows, part_rows), part_rows)


def mlp_kernel(x_ref, cot_ref, gate_w, up_w, down_w, all_ref, act_ref, dgate_ref, dup_ref, out_ref, sum_ref, mine, to_beside, from_beside, to_across, from_across, to_own, from_own, send, recv):
    d, t, beside, across, corner = places()
    rows = x_ref.shape[0]
    part = rows // HALF
    greet([(d, beside), (d, across)])
    copies = []
    arrive_beside, arrive_across = [], []
    for s in range(HALF):
        src = x_ref.at[pl.ds(s * part, part)]
        dst = all_ref.at[row_block(t, s, rows, part)]
        arrive_across.append(push(src, dst, send.at[0, s], recv.at[0, s], (d, across)))
        arrive_beside.append(push(src, dst, send.at[1, s], recv.at[1, s], (d, beside)))
    all_ref[pl.ds(pl.multiple_of(t * rows, rows), rows), :] = x_ref[...]
    copies += arrive_across + arrive_beside

    def work(owner, s):
        at = row_block(owner, s, rows, part)
        x = all_ref[at, :]
        gate = lax.dot_general(x, gate_w[...], NN, preferred_element_type=f32)
        up = lax.dot_general(x, up_w[...], NN, preferred_element_type=f32)
        sig = jax.nn.sigmoid(gate)
        silu = gate * sig
        act = (silu * up).astype(bf16)
        act_ref[at, :] = act
        d_act = lax.dot_general(cot_ref[at, :], down_w[...], NT, preferred_element_type=f32)
        d_gate = (d_act * up * sig * (1.0 + gate * (1.0 - sig))).astype(bf16)
        d_up = (d_act * silu).astype(bf16)
        dgate_ref[at, :] = d_gate
        dup_ref[at, :] = d_up
        out_ref[at, :] = lax.dot_general(act, down_w[...], NN, preferred_element_type=f32).astype(bf16)
        return lax.dot_general(d_gate, gate_w[...], NT, preferred_element_type=f32) + lax.dot_general(d_up, up_w[...], NT, preferred_element_type=f32)

    for s in range(HALF):
        mine[pl.ds(s * part, part), :] = work(t, s)
    own_copies = []
    for s in range(HALF):
        arrive_beside[s].wait_recv()
        at = pl.ds(s * part, part)
        to_own[at, :] = work(beside, s).astype(bf16)
        own_copies.append(push(to_own.at[at], from_own.at[at], send.at[2, s], recv.at[2, s], (d, beside)))
    passed, sums = [], []
    for s in range(HALF):
        at = pl.ds(s * part, part)
        arrive_across[s].wait_recv()
        block = all_ref.at[row_block(across, s, rows, part)]
        passed.append(push(block, block, send.at[3, s], recv.at[3, s], (d, beside)))
        passed[s].wait_recv()
        to_beside[at, :] = work(corner, s).astype(bf16)
        handed = push(to_beside.at[at], from_beside.at[at], send.at[4, s], recv.at[4, s], (d, beside))
        total = work(across, s)
        handed.wait_recv()
        to_across[at, :] = (total + from_beside[at, :].astype(f32)).astype(bf16)
        sums.append(push(to_across.at[at], from_across.at[at], send.at[5, s], recv.at[5, s], (d, across)))
        copies.append(handed)
    for s in range(HALF):
        at = pl.ds(s * part, part)
        own_copies[s].wait_recv()
        sums[s].wait_recv()
        sum_ref[at, :] = mine[at, :] + from_own[at, :].astype(f32) + from_across[at, :].astype(f32)
    for copy in copies + own_copies + passed + sums:
        copy.wait_send()


def mlp(x, cot, gate_w, up_w, down_w):
    rows, width = x.shape
    total = cot.shape[0]
    units = gate_w.shape[1]
    vmem = pl.BlockSpec(memory_space=pltpu.VMEM)
    half = lambda: pltpu.VMEM((rows, width), bf16)
    return pl.pallas_call(
        mlp_kernel,
        in_specs=[vmem] * 5,
        out_specs=[vmem] * 6,
        out_shape=[jax.ShapeDtypeStruct((total, width), bf16), jax.ShapeDtypeStruct((total, units), bf16), jax.ShapeDtypeStruct((total, units), bf16),
                   jax.ShapeDtypeStruct((total, units), bf16), jax.ShapeDtypeStruct((total, width), bf16), jax.ShapeDtypeStruct((rows, width), f32)],
        scratch_shapes=[pltpu.VMEM((rows, width), f32), half(), half(), half(), half(), half(), half(),
                        pltpu.SemaphoreType.DMA((6, HALF)), pltpu.SemaphoreType.DMA((6, HALF))],
        compiler_params=pltpu.CompilerParams(collective_id=1, has_side_effects=True, vmem_limit_bytes=60 * 2**20),
    )(x, cot, gate_w, up_w, down_w)


def mixer_bwd_block(blk, width, flags, proj_ref, prev_ref, conv_ref, gain_ref, mixed_ref, state_in, res_in, wu_in, inv_in, dheaded, dcat, dstate, buf, dbuf, cacc, gacc):
    buf[0:8, :] = prev_ref[:, :width]
    buf[8:, :] = proj_ref[:, :width]
    heads, tails = span_masks(flags, blk * (BACK_ROWS // SPAN), BACK_ROWS // SPAN)
    cols, slopes = [], []
    for c in range(width // HEAD):
        total = conv_column(buf, conv_ref, heads, slice(c * HEAD, (c + 1) * HEAD))
        sig = sigmoid(total)
        cols.append(total * sig)
        slopes.append(sig * (1.0 + total * (1.0 - sig)))
    betas = sigmoid(proj_ref[:, width:])
    strict, causal, cross, _, _ = pair_masks()
    lane = lax.broadcasted_iota(jnp.int32, (STEP, HEAD), 1)
    order = list(reversed(range(BACK_STEPS)))
    hs = [slice(h * STEP, (h + 1) * STEP) for h in range(2)]
    spans = [slice(s * STEP, (s + 1) * STEP) for s in range(BACK_STEPS)]
    edge = [resets(flags, blk * BACK_STEPS + s) for s in range(BACK_STEPS)]
    enter, leave, keep = zip(*[row_masks(*e) for e in edge])
    gate = [jnp.where(cross, 1.0 - e[1], 1.0) for e in edge]
    both = lambda n: [jnp.concatenate([cols[2 * n][rs], cols[2 * n + 1][rs]], axis=0) for rs in spans]
    q, k, v = both(0), both(1), both(2)
    rq = [lax.rsqrt(jnp.sum(x * x, axis=-1, keepdims=True) + 1e-6) for x in q]
    rk = [lax.rsqrt(jnp.sum(x * x, axis=-1, keepdims=True) + 1e-6) for x in k]
    q = [x * r for x, r in zip(q, rq)]
    k = [x * r for x, r in zip(k, rk)]
    q16 = [x.astype(bf16) for x in q]
    k16 = [x.astype(bf16) for x in k]
    b = [jnp.concatenate([betas[rs, 0:1], betas[rs, 1:2]], axis=0) for rs in spans]
    gp = [mm(jnp.concatenate([x, y], axis=0), x, NT) for x, y in zip(k16, q16)]
    gram = [jnp.where(strict, m * x[:2 * STEP], 0.0) for m, x in zip(gate, gp)]
    p = [jnp.where(causal, m * x[2 * STEP:], 0.0).astype(bf16) for m, x in zip(gate, gp)]
    do = []
    for s in range(BACK_STEPS):
        o = stack(mixed_ref[spans[s], :])
        dh = stack(dheaded[pl.ds(pl.multiple_of(blk * BACK_ROWS + s * STEP, STEP), STEP), :].astype(f32))
        ro = lax.rsqrt(jnp.mean(o * o, axis=-1, keepdims=True) + 1e-5)
        on = o * ro
        gacc[...] += jnp.sum((dh * on).reshape(2 * STEP // 8, 8, HEAD), axis=0)
        dn = dh * gain_ref[...]
        do.append(ro * (dn - on * jnp.mean(dn * on, axis=-1, keepdims=True)))
    do16 = [x.astype(bf16) for x in do]
    doe = [(x * e).astype(bf16) for x, e in zip(do, enter)]
    ke16 = [(x * e).astype(bf16) for x, e in zip(k, leave)]
    we = [(wu_in[s][:, :HEAD].astype(f32) * enter[s]).astype(bf16) for s in range(BACK_STEPS)]
    dres = [mm(x, y, TN) for x, y in zip(p, do16)]
    qdo = [[mm(x[r], y[r], TN) for r in hs] for x, y in zip(q16, doe)]
    dmem = [dstate[0], dstate[1]]
    dres16, after = [None] * BACK_STEPS, [None] * BACK_STEPS
    for s in order:
        low = [m.astype(bf16) for m in dmem]
        after[s] = low
        dres[s] = dres[s] + jnp.concatenate([mm(ke16[s][hs[h]], low[h]) for h in range(2)], axis=0)
        dres16[s] = dres[s].astype(bf16)
        for h in range(2):
            dmem[h] = keep[s] * dmem[h] + qdo[s][h] - mm(we[s][hs[h]], dres16[s][hs[h]], TN)
    dp = [mm(do16[s], res_in[s], NT) for s in order]
    dke = [jnp.concatenate([mm(res_in[s, hs[h]], after[s][h], NT) for h in range(2)], axis=0) for s in order]
    ds = [[mm(jnp.concatenate([do16[s][hs[h]], dres16[s][hs[h]]], axis=0), state_in[s, h * HEAD:(h + 1) * HEAD], NT) for h in range(2)] for s in order]
    dp = [jnp.where(causal, gate[s] * x, 0.0).astype(bf16) for s, x in zip(order, dp)]
    dw = [-enter[s] * jnp.concatenate([x[0][STEP:], x[1][STEP:]], axis=0) for s, x in zip(order, ds)]
    db_kv = [mm(inv_in[s], jnp.concatenate([x, dres[s]], axis=1), TN) for s, x in zip(order, dw)]
    dq = [enter[s] * jnp.concatenate([x[0][:STEP], x[1][:STEP]], axis=0) + mm(y, k16[s]) for s, x, y in zip(order, ds, dp)]
    dk = [mm(y, q16[s], TN) + leave[s] * x for s, x, y in zip(order, dke, dp)]
    da = [-jnp.where(strict, gate[s] * mm(x, wu_in[s], NT), 0.0) for s, x in zip(order, db_kv)]
    dg = [(x * b[s]).astype(bf16) for s, x in zip(order, da)]
    dk = [x + mm(y, k16[s]) + mm(y, k16[s], TN) + b[s] * z[:, :HEAD] for s, x, y, z in zip(order, dk, dg, db_kv)]
    for i, s in enumerate(order):
        rs = spans[s]
        dbeta = jnp.sum(da[i] * gram[s], axis=-1, keepdims=True) + jnp.sum(db_kv[i][:, :HEAD] * k[s] + db_kv[i][:, HEAD:] * v[s], axis=-1, keepdims=True)
        dv = b[s] * db_kv[i][:, HEAD:]
        dqs = rq[s] * (dq[i] - q[s] * jnp.sum(dq[i] * q[s], axis=-1, keepdims=True))
        dks = rk[s] * (dk[i] - k[s] * jnp.sum(dk[i] * k[s], axis=-1, keepdims=True))
        dpre = dbeta * b[s] * (1.0 - b[s])
        for n, x in enumerate((dqs, dks, dv)):
            for h in range(2):
                c = 2 * n + h
                dbuf[rs, c * HEAD:(c + 1) * HEAD] = x[hs[h]] * slopes[c][rs]
        dcat[pl.ds(pl.multiple_of(blk * BACK_ROWS + s * STEP, STEP), STEP), width:] = jnp.where(lane == 0, dpre[:STEP], jnp.where(lane == 1, dpre[STEP:], 0.0)).astype(bf16)
    dstate[0] = dmem[0]
    dstate[1] = dmem[1]
    for c in range(width // HEAD):
        cs = slice(c * HEAD, (c + 1) * HEAD)
        total, grads = conv_column_back(buf, dbuf, conv_ref, tails, cs)
        dcat[pl.ds(pl.multiple_of(blk * BACK_ROWS, BACK_ROWS), BACK_ROWS), cs] = total.astype(bf16)
        for j in range(4):
            cacc[j, :, cs] += grads[j]
    dbuf[BACK_ROWS:, :] = dbuf[0:8, :]


class Ring:
    def __init__(self, here, after, before, sources, results, lands, by_rows, send, recv):
        self.here, self.targets = here, (after, before)
        self.sources, self.results, self.lands, self.by_rows, self.send, self.recv = sources, results, lands, by_rows, send, recv

    def shard(self, way, k):
        return lax.rem(self.here + (k if way else 2 * RING - k), RING)

    def view(self, ref, i, way, k):
        shard = self.shard(way, k)
        rows, cols = ref.shape
        if self.by_rows[i]:
            piece = rows // (2 * RING)
            return ref.at[pl.ds(pl.multiple_of((2 * shard + way) * piece, piece), piece)]
        piece = cols // RING
        return ref.at[pl.ds(way * (rows // 2), rows // 2), pl.ds(pl.multiple_of(shard * piece, piece), piece)]

    def copy(self, i, way, r):
        if r == 0:
            src, dst = self.view(self.sources[i], i, way, 0), self.lands[i].at[way, 0]
        elif r < RING - 1:
            src, dst = self.lands[i].at[way, r - 1], self.lands[i].at[way, r]
        else:
            src = dst = self.view(self.results[i], i, way, r)
        return pltpu.make_async_remote_copy(src_ref=src, dst_ref=dst, send_sem=self.send.at[i, way], recv_sem=self.recv.at[i, way, r], device_id=self.targets[way], device_id_type=MESH_ID)

    def round(self, r):
        for i in range(len(self.sources)):
            for way in range(2):
                if r > 0:
                    last = self.copy(i, way, r - 1)
                    last.wait_send()
                    last.wait_recv()
                if 0 < r < RING:
                    land = self.lands[i].at[way, r - 1]
                    total = (land[...].astype(f32) + self.view(self.sources[i], i, way, r)[...].astype(f32)).astype(bf16)
                    if r < RING - 1:
                        land[...] = total
                    else:
                        done = self.view(self.results[i], i, way, r)
                        done[...] = total
                if r < ROUNDS:
                    self.copy(i, way, r).start()


def ring_place(d):
    base = d // RING * RING
    inner = lax.rem(d, RING)
    line = inner // 2
    here = jnp.where(lax.rem(inner, 2) == 0, line, RING - 1 - line)

    def device(place):
        return base + jnp.where(place < RING // 2, 2 * place, 2 * (RING - 1 - place) + 1)

    return here, device(lax.rem(here + 1, RING)), device(lax.rem(here + RING - 1, RING))


def ring_lands(shapes, by_rows):
    pieces = [(s[0] // (2 * RING), s[1]) if rows else (s[0] // 2, s[1] // RING) for s, rows in zip(shapes, by_rows)]
    return [pltpu.VMEM((2, RING - 1) + p, bf16) for p in pieces]


def back_kernel(n_dp, flags, proj_ref, prev_ref, conv_ref, gain_ref, mixed_ref, state_in, res_in, wu_in, inv_in,
                headed_hbm, attn_hbm, dattn_hbm, out_w_hbm, w_hbm, tok_hbm, dhid_hbm, first_gain, small_ref, gate_hbm, up_hbm, down_hbm,
                dx_hbm, small_out, gate_out, up_out, down_out, cat_out, outw_out,
                headed, attn, dattn_all, out_w, w, tok, dhid, gate_src, up_src, down_src, cat_src, outw_src,
                gate_res, up_res, down_res, cat_res, outw_res, gate_land, up_land, down_land, cat_land, outw_land,
                dheaded, dcat, dstate, buf, dbuf, cacc, gacc, mine, to_beside, from_beside, to_across, from_across, to_own, from_own,
                group_send, group_land, all_send, all_land, gain_acc,
                load, store, send_m, recv_m, send_c, recv_c, send_x, recv_x, send_g, recv_g, send_a, recv_a):
    g = pl.program_id(0)
    n = pl.num_programs(0)
    d, t, beside, across, corner = places()
    here, after, before = ring_place(d)
    rows = tok.shape[0]
    part = rows // HALF
    width = buf.shape[1]
    others = [d // RING * RING + lax.rem(d + k, RING) for k in range(1, RING)]
    mlp_ring = Ring(here, (after, t), (before, t), [gate_src, up_src, down_src], [gate_res, up_res, down_res], [gate_land, up_land, down_land], [True, True, False], send_m, recv_m)
    cat_ring = Ring(here, (after, t), (before, t), [cat_src, outw_src], [cat_res, outw_res], [cat_land, outw_land], [True, True], send_c, recv_c)
    loads = [(gate_hbm, gate_src), (up_hbm, up_src), (down_hbm, down_src), (dattn_hbm, dattn_all.at[pl.ds(pl.multiple_of(t * rows, rows), rows)]), (out_w_hbm, out_w), (headed_hbm, headed), (attn_hbm, attn), (w_hbm, w), (tok_hbm, tok), (dhid_hbm, dhid)]
    stores = [(gate_res, gate_out), (up_res, up_out), (down_res, down_out), (mine, dx_hbm), (cat_res, cat_out), (outw_res, outw_out)]

    def loaded(i):
        return pltpu.make_async_copy(loads[i][0], loads[i][1], load.at[i])

    def stored(i):
        return pltpu.make_async_copy(stores[i][0], stores[i][1], store.at[i])

    def pushed(src, dst, i, s, peer):
        return pltpu.make_async_remote_copy(src_ref=src, dst_ref=dst, send_sem=send_x.at[i, s], recv_sem=recv_x.at[i, s], device_id=(d, peer), device_id_type=MESH_ID)

    def block_at(owner, s):
        return row_block(owner, s, rows, part)

    def rows_to(i, s, peer):
        block = dattn_all.at[block_at(t, s)]
        return pushed(block, block, i, s, peer)

    def passed(s):
        block = dattn_all.at[block_at(across, s)]
        return pushed(block, block, 2, s, beside)

    def head_grad(owner, s):
        at = block_at(owner, s)
        dheaded[at, :] = lax.dot_general(dattn_all[at, :], out_w[...], NT, preferred_element_type=f32).astype(bf16)

    @pl.when(g == 0)
    def _():
        for i in range(len(loads)):
            loaded(i).start()
        greet([(d, beside), (d, across), (d, corner)] + [(o, t) for o in others])
        for i in range(4):
            loaded(i).wait()
        for s in range(HALF):
            rows_to(0, s, across).start()
            rows_to(1, s, beside).start()
        mlp_ring.round(0)
        loaded(4).wait()
        dstate[...] = jnp.zeros_like(dstate)
        dbuf[BACK_ROWS:, :] = jnp.zeros((8, width), f32)
        cacc[...] = jnp.zeros_like(cacc)
        gacc[...] = jnp.zeros_like(gacc)
        gain_acc[...] = jnp.zeros_like(gain_acc)
        for s in range(HALF):
            head_grad(t, s)
        for s in range(HALF):
            rows_to(1, s, beside).wait_recv()
            head_grad(beside, s)
        mlp_ring.round(1)
        rows_to(0, 0, across).wait_recv()
        passed(0).start()
        head_grad(across, 0)
        mlp_ring.round(2)
        passed(0).wait_recv()
        head_grad(corner, 0)
        mlp_ring.round(3)
        rows_to(0, 1, across).wait_recv()
        passed(1).start()
        head_grad(across, 1)
        passed(1).wait_recv()
        head_grad(corner, 1)
        mlp_ring.round(4)

    for at, r in ((1, 5), (3, 6), (5, 7), (6, 8)):
        @pl.when(g == at)
        def _(r=r):
            mlp_ring.round(r)

    blk = n - 1 - g
    mixer_bwd_block(blk, width, flags, proj_ref, prev_ref, conv_ref, gain_ref, mixed_ref, state_in, res_in, wu_in, inv_in, dheaded, dcat, dstate, buf, dbuf, cacc, gacc)

    def work(owner, s):
        return lax.dot_general(dcat[block_at(owner, s), :], w[...], NT, preferred_element_type=f32)

    def handed(s):
        at = pl.ds(s * part, part)
        return pushed(to_beside.at[at], from_beside.at[at], 3, s, beside)

    def summed(s):
        at = pl.ds(s * part, part)
        return pushed(to_across.at[at], from_across.at[at], 4, s, across)

    def owned(s):
        at = pl.ds(s * part, part)
        return pushed(to_own.at[at], from_own.at[at], 5, s, beside)

    def grouped(i, peer):
        return pltpu.make_async_remote_copy(src_ref=group_send, dst_ref=group_land.at[i], send_sem=send_g.at[i], recv_sem=recv_g.at[i], device_id=(d, peer), device_id_type=MESH_ID)

    def spread(i, o):
        return pltpu.make_async_remote_copy(src_ref=all_send, dst_ref=all_land.at[i], send_sem=send_a.at[i], recv_sem=recv_a.at[i], device_id=(o, t), device_id_type=MESH_ID)

    piece = 64

    def finish(s):
        gain = first_gain[...]

        def chunk(i, carry):
            at = pl.ds(pl.multiple_of(s * part + i * piece, piece), piece)
            grad = mine[at, :] + from_own[at, :].astype(f32) + from_across[at, :].astype(f32)
            x = tok[at, :].astype(f32)
            r = lax.rsqrt(jnp.mean(x * x, axis=-1, keepdims=True) + 1e-5)
            scaled = gain * grad
            mine[at, :] = dhid[at, :] + r * scaled - x * (r * r * r * jnp.mean(x * scaled, axis=-1, keepdims=True))
            gain_acc[...] += jnp.sum((grad * x * r).reshape(piece // 8, 8, grad.shape[1]), axis=0)
            return carry

        lax.fori_loop(0, part // piece, chunk, 0)

    @pl.when(g == n - 1)
    def _():
        for i in range(5, len(loads)):
            loaded(i).wait()
        mlp_ring.round(9)

        def cat_chunk(i):
            at = pl.ds(i * 256, 256)
            cat_src[at, :] = lax.dot_general(attn[:, i * 256:(i + 1) * 256], dcat[...], TN, preferred_element_type=f32).astype(bf16)

        count = attn.shape[1] // 256
        for i in range(count):
            cat_chunk(i)
            if i == count // 2 - 1:
                mlp_ring.round(10)
        outw_src[...] = lax.dot_general(headed[...], dattn_all[...], TN, preferred_element_type=f32).astype(bf16)
        cat_ring.round(0)
        mlp_ring.round(11)
        for s in range(HALF):
            at = pl.ds(s * part, part)
            to_beside[at, :] = work(corner, s).astype(bf16)
            handed(s).start()
            total = work(across, s)
            handed(s).wait_recv()
            to_across[at, :] = (total + from_beside[at, :].astype(f32)).astype(bf16)
            summed(s).start()
        cat_ring.round(1)
        mlp_ring.round(12)
        for s in range(HALF):
            at = pl.ds(s * part, part)
            to_own[at, :] = work(beside, s).astype(bf16)
            owned(s).start()
            mine[at, :] = work(t, s)
        cat_ring.round(2)
        mlp_ring.round(13)
        cat_ring.round(3)
        cat_ring.round(4)
        mlp_ring.round(14)
        for i in range(3):
            stored(i).start()
        cat_ring.round(5)
        owned(0).wait_recv()
        summed(0).wait_recv()
        finish(0)
        cat_ring.round(6)
        cat_ring.round(7)
        owned(1).wait_recv()
        summed(1).wait_recv()
        finish(1)
        stored(3).start()
        cat_ring.round(8)
        line = lax.broadcasted_iota(jnp.int32, small_ref.shape, 0)
        small = jnp.where(line == 0, jnp.sum(gain_acc[...], axis=0, keepdims=True), small_ref[...])
        head_part = jnp.sum(gacc[...], axis=0, keepdims=True)
        small = jnp.where(line == 2, jnp.concatenate([head_part] + [jnp.zeros_like(head_part)] * (small.shape[1] // HEAD - 1), axis=1), small)
        group_send[...] = small
        for j in range(4):
            group_send[3 + j:4 + j, :width] = jnp.sum(cacc[j], axis=0, keepdims=True)
        for i, peer in enumerate((beside, across, corner)):
            grouped(i, peer).start()
        cat_ring.round(9)
        small = group_send[...]
        for i, peer in enumerate((beside, across, corner)):
            grouped(i, peer).wait_recv()
        both = (small + group_land[0]) + (group_land[1] + group_land[2])
        small = jnp.where(line < 3, both, small)
        all_send[...] = small
        for i, o in enumerate(others):
            spread(i, o).start()
        cat_ring.round(10)
        cat_ring.round(11)
        for i, o in enumerate(others):
            spread(i, o).wait_recv()
            small = small + all_land[i]
        small_out[...] = small
        cat_ring.round(12)
        cat_ring.round(13)
        cat_ring.round(14)
        for i in range(4, 6):
            stored(i).start()
        for s in range(HALF):
            for copy in (rows_to(0, s, across), rows_to(1, s, beside), passed(s), handed(s), summed(s), owned(s)):
                copy.wait_send()
        for i, peer in enumerate((beside, across, corner)):
            grouped(i, peer).wait_send()
        for i, o in enumerate(others):
            spread(i, o).wait_send()
        for i in range(len(stores)):
            stored(i).wait()


def backward(n_dp, flags, proj, conv, gain, saved, headed, attn_all, d_attn, out_w, w, tokens, d_hidden, first_gain, small, gate_part, up_part, down_part):
    mixed, states, res, wu, inv = saved
    total_rows, total = proj.shape
    width = conv.shape[1]
    rows, model = tokens.shape
    n = total_rows // BACK_ROWS
    m2 = lambda g: (n - 1 - g, 0)
    m3 = lambda g: (n - 1 - g, 0, 0)
    z2 = lambda g: (0, 0)
    hbm = pl.BlockSpec(memory_space=pl.ANY)
    dma = pltpu.SemaphoreType.DMA
    like = lambda x: pltpu.VMEM(x.shape, x.dtype)
    mlp_parts = (gate_part, up_part, down_part)
    cat_shapes = [(model, total), (headed.shape[1], model)]
    half = lambda: pltpu.VMEM((rows, model), bf16)
    line = small.shape
    out = lambda shape, kind: jax.ShapeDtypeStruct(shape, kind)
    return pl.pallas_call(
        functools.partial(back_kernel, n_dp),
        grid=(n,),
        in_specs=[pl.BlockSpec(memory_space=pltpu.SMEM), pl.BlockSpec((BACK_ROWS, total), m2),
                  pl.BlockSpec((8, total), lambda g: (jnp.maximum((n - 1 - g) * (BACK_ROWS // 8) - 1, 0), 0)),
                  pl.BlockSpec((4, width), z2), pl.BlockSpec((1, HEAD), z2), pl.BlockSpec((BACK_ROWS, 2 * HEAD), m2),
                  pl.BlockSpec((BACK_STEPS, 2 * HEAD, HEAD), m3), pl.BlockSpec((BACK_STEPS, 2 * STEP, HEAD), m3),
                  pl.BlockSpec((BACK_STEPS, 2 * STEP, 2 * HEAD), m3), pl.BlockSpec((BACK_STEPS, 2 * STEP, 2 * STEP), m3)]
        + [hbm] * 7 + [pl.BlockSpec((1, model), z2), pl.BlockSpec(line, z2)] + [hbm] * 3,
        out_specs=[hbm, pl.BlockSpec(line, z2)] + [hbm] * 5,
        out_shape=[out((rows, model), f32), out(line, f32)] + [out(x.shape, bf16) for x in mlp_parts] + [out(s, bf16) for s in cat_shapes],
        scratch_shapes=[like(headed), like(attn_all), like(attn_all), like(out_w), like(w), like(tokens), like(d_hidden)]
        + [like(x) for x in mlp_parts] + [pltpu.VMEM(s, bf16) for s in cat_shapes]
        + [like(x) for x in mlp_parts] + [pltpu.VMEM(s, bf16) for s in cat_shapes]
        + ring_lands([x.shape for x in mlp_parts], [True, True, False]) + ring_lands(cat_shapes, [True, True])
        + [pltpu.VMEM((total_rows, 2 * HEAD), bf16), pltpu.VMEM((total_rows, total), bf16), pltpu.VMEM((2, HEAD, HEAD), f32),
           pltpu.VMEM((BACK_ROWS + 8, width), f32), pltpu.VMEM((BACK_ROWS + 8, width), f32), pltpu.VMEM((4, 8, width), f32), pltpu.VMEM((8, HEAD), f32),
           pltpu.VMEM((rows, model), f32), half(), half(), half(), half(), half(), half(),
           pltpu.VMEM(line, f32), pltpu.VMEM((3,) + line, f32), pltpu.VMEM(line, f32), pltpu.VMEM((RING - 1,) + line, f32), pltpu.VMEM((8, model), f32),
           dma((10,)), dma((6,)), dma((3, 2)), dma((3, 2, ROUNDS)), dma((2, 2)), dma((2, 2, ROUNDS)), dma((6, HALF)), dma((6, HALF)),
           dma((3,)), dma((3,)), dma((RING - 1,)), dma((RING - 1,))],
        compiler_params=pltpu.CompilerParams(dimension_semantics=("arbitrary",), collective_id=2, has_side_effects=True, vmem_limit_bytes=62 * 2**20),
    )(flags, proj, proj, conv, gain, mixed, states, res, wu, inv, headed, attn_all, d_attn, out_w, w, tokens, d_hidden, first_gain, small, gate_part, up_part, down_part)


def rms_norm(values, scales):
    inverse = lax.rsqrt(jnp.mean(values * values, axis=-1, keepdims=True) + 1e-05)
    return values * inverse * scales


def gather(x):
    return lax.all_gather(x, "tensor", axis=0, tiled=True)


def dot(a, b, dims=NN):
    return lax.dot_general(a, b, dims, preferred_element_type=f32)


def on_device(tokens, lengths, attn_gain, qkv_weight, beta_weight, conv_weight, head_gain, out_weight, mlp_gain, gate_up_weight, down_weight, cotangent):
    model_width = tokens.shape[1]
    width = qkv_weight.shape[1] * qkv_weight.shape[2]
    heads = beta_weight.shape[1]
    group_rows = tokens.shape[0] * lax.axis_size("tensor")
    starts = jnp.arange(group_rows // SPAN + 8, dtype=jnp.int32) * SPAN
    flags = jnp.where((starts == 0) | (starts == lengths[0, 0]), 1.0, 0.0).astype(f32)
    local_in = tokens.astype(f32)
    first_scale = attn_gain.astype(f32)
    second_scale = mlp_gain.astype(f32)
    head_scale = head_gain.astype(f32)[None]
    conv = conv_weight.reshape(conv_weight.shape[0], -1).astype(f32)
    qkv_matrix = jnp.concatenate([qkv_weight.reshape(model_width, -1), jnp.pad(beta_weight, ((0, 0), (0, HEAD - heads)))], axis=1)
    attn_in = rms_norm(local_in, first_scale).astype(bf16)
    attn_all = gather(attn_in)
    out_all = gather(out_weight)
    cot_all = gather(cotangent)
    proj = dot(attn_all, qkv_matrix)
    headed, *saved = mixer_fwd(flags, proj, conv, head_scale)
    headed_rows = lax.all_to_all(headed, "tensor", split_axis=0, concat_axis=1, tiled=True)
    hidden_res = local_in + dot(headed_rows, out_all)
    mlp_in = rms_norm(hidden_res, second_scale).astype(bf16)
    gate_w, up_w = gate_up_weight[:, 0], gate_up_weight[:, 1]
    mlp_all, activated, d_gate, d_up, out_parts, d_mlp_in = mlp(mlp_in, cot_all, gate_w, up_w, down_weight)
    d_from_mlp, mlp_gain_part = jax.vjp(rms_norm, hidden_res, second_scale)[1](d_mlp_in)
    d_hidden = cotangent.astype(f32) + d_from_mlp
    d_attn = d_hidden.astype(bf16)
    down_part = dot(activated, cot_all, TN).astype(bf16)
    gate_part = dot(mlp_all, d_gate, TN).astype(bf16)
    up_part = dot(mlp_all, d_up, TN).astype(bf16)
    mlp_out = lax.psum_scatter(out_parts, "tensor", scatter_dimension=0, tiled=True).astype(f32)
    output = (hidden_res + mlp_out).astype(bf16)
    small = jnp.zeros((8, model_width), f32).at[1].set(mlp_gain_part)
    n_dp = lax.axis_size("dp")
    input_grad, small, *sums = backward(
        n_dp, flags, proj, conv, head_scale, saved, headed, attn_all, d_attn, out_weight, qkv_matrix, tokens, d_hidden, first_scale[None], small, gate_part, up_part, down_part)
    if n_dp > RING:
        groups = [list(range(i, n_dp, RING)) for i in range(RING)]
        small, *sums = lax.psum((small, *sums), "dp", axis_index_groups=groups)
    gate_sum, up_sum, down_sum, cat_sum, out_sum = sums
    return (
        output,
        input_grad,
        small[0],
        cat_sum[:, :width].astype(f32).reshape(qkv_weight.shape),
        cat_sum[:, width:width + heads].astype(f32),
        small[3:7, :width].reshape(conv_weight.shape),
        small[2, :HEAD],
        out_sum.astype(f32),
        small[1],
        jnp.stack([gate_sum, up_sum], axis=1).astype(f32),
        down_sum.astype(f32),
    )


def solution(mesh):
    rows = P(("dp", "tensor"), None)
    last = P(None, None, "tensor")
    return jax.shard_map(
        on_device,
        mesh=mesh,
        in_specs=(rows, P("dp", None), P(), last, P(None, "tensor"), last, P(), P("tensor", None), P(), last, P("tensor", None), rows),
        out_specs=(rows, rows, P(), last, P(None, "tensor"), last, P(), P("tensor", None), P(), last, P("tensor", None)),
        check_vma=False,
    )
```

```python
import functools
import jax
import jax.numpy as jnp
from jax import lax
from jax.experimental import pallas as pl
from jax.experimental.pallas import tpu as pltpu
from jax.sharding import PartitionSpec as P

HEAD = 128
STEP = 128
SPAN = 64
STEPS = 4
ROWS = STEP * STEPS
BACK_STEPS = 2
BACK_ROWS = STEP * BACK_STEPS
RING = 8
ROUNDS = 2 * RING - 2
NN = (((1,), (0,)), ((), ()))
NT = (((1,), (1,)), ((), ()))
TN = (((0,), (0,)), ((), ()))
f32 = jnp.float32
bf16 = jnp.bfloat16


def mm(a, b, dims=NN):
    return lax.dot_general(a.astype(bf16), b.astype(bf16), dims, preferred_element_type=f32)


def split(a):
    high = a.astype(bf16)
    return high, (a - high.astype(f32)).astype(bf16)


def stack(x):
    return jnp.concatenate([x[:, :HEAD], x[:, HEAD:]], axis=0)


def unstack(x):
    return jnp.concatenate([x[:STEP], x[STEP:]], axis=1)


def pair_masks():
    i = lax.broadcasted_iota(jnp.int32, (2 * STEP, 2 * STEP), 0)
    j = lax.broadcasted_iota(jnp.int32, (2 * STEP, 2 * STEP), 1)
    same = (i // STEP) == (j // STEP)
    cross = ((i % STEP) >= SPAN) & ((j % STEP) < SPAN)
    levels = []
    size = 1
    while size < STEP:
        levels.append(((i // (2 * size)) == (j // (2 * size))) & ((i // size) % 2 == 1) & ((j // size) % 2 == 0))
        size *= 2
    return same & (i > j), same & (i >= j), cross, levels, i == j


def tri_inverses(systems, levels, eye):
    invs = [jnp.where(eye, 1.0, jnp.where(levels[0], -a, 0.0)) for a in systems]
    for level in levels[1:]:
        lows = [inv.astype(bf16) for inv in invs]
        parts = [mm(low, jnp.where(level, a, 0.0)) for low, a in zip(lows, systems)]
        parts = [mm(part, low) for part, low in zip(parts, lows)]
        invs = [inv - part for inv, part in zip(invs, parts)]
    return invs


def row_masks(start_reset, mid_reset):
    r = lax.broadcasted_iota(jnp.int32, (2 * STEP, HEAD), 0) % STEP
    upper = r < SPAN
    enter = jnp.where(upper, 1.0 - start_reset, (1.0 - start_reset) * (1.0 - mid_reset))
    leave = jnp.where(upper, 1.0 - mid_reset, 1.0)
    keep = (1.0 - start_reset) * (1.0 - mid_reset)
    return enter, leave, keep


def resets(flags, step):
    return flags[2 * step], flags[2 * step + 1]


def sigmoid(x):
    return 0.5 * jnp.tanh(0.5 * x) + 0.5


def span_masks(flags, span, count):
    row = lax.broadcasted_iota(jnp.int32, (8, HEAD), 0)
    heads, tails = [], []
    for i in range(count):
        heads.append([None] + [jnp.where(row >= j, 1.0, 1.0 - flags[span + i]) for j in range(1, 4)])
        tails.append([None] + [jnp.where(row + j < 8, 1.0, 1.0 - flags[span + i + 1]) for j in range(1, 4)])
    return heads, tails


def conv_column(buf, conv_ref, heads, cs):
    out = []
    for i in range(len(heads)):
        at = 8 + i * SPAN
        total = buf[at:at + SPAN, cs] * conv_ref[0:1, cs]
        for j in range(1, 4):
            lead = buf[at - j:at - j + 8, cs] * heads[i][j]
            rest = buf[at - j + 8:at - j + SPAN, cs]
            total = total + jnp.concatenate([lead, rest], axis=0) * conv_ref[j:j + 1, cs]
        out.append(total)
    return jnp.concatenate(out, axis=0)


def conv_column_back(buf, dbuf, conv_ref, tails, cs):
    out, grads = [], [0.0] * 4
    for i in range(len(tails)):
        at = i * SPAN
        x = buf[8 + at:8 + at + SPAN, cs]
        for j in range(4):
            if j == 0:
                grad = dbuf[at:at + SPAN, cs]
                total = grad * conv_ref[0:1, cs]
            else:
                most = dbuf[at + j:at + j + SPAN - 8, cs]
                last = dbuf[at + j + SPAN - 8:at + j + SPAN, cs] * tails[i][j]
                grad = jnp.concatenate([most, last], axis=0)
                total = total + grad * conv_ref[j:j + 1, cs]
            grads[j] = grads[j] + jnp.sum((x * grad).reshape(SPAN // 8, 8, HEAD), axis=0)
        out.append(total)
    return jnp.concatenate(out, axis=0), grads


def mixer_fwd_kernel(flags, proj_ref, conv_ref, gain_ref, headed_ref, mixed_ref, state_out, res_out, wu_out, inv_out, state, buf):
    g = pl.program_id(0)

    @pl.when(g == 0)
    def _():
        state[...] = jnp.zeros_like(state)
        buf[0:8, :] = jnp.zeros((8, buf.shape[1]), f32)

    width = buf.shape[1]
    buf[8:, :] = proj_ref[:, :width]
    heads, _ = span_masks(flags, g * (ROWS // SPAN), ROWS // SPAN)
    cols = []
    for c in range(width // HEAD):
        total = conv_column(buf, conv_ref, heads, slice(c * HEAD, (c + 1) * HEAD))
        cols.append(total * sigmoid(total))
    buf[0:8, :] = buf[ROWS:ROWS + 8, :]
    betas = sigmoid(proj_ref[:, width:])
    strict, causal, cross, levels, eye = pair_masks()
    todo = []
    for s in range(STEPS):
        rs = slice(s * STEP, (s + 1) * STEP)
        start_reset, mid_reset = resets(flags, g * STEPS + s)
        gate = jnp.where(cross, 1.0 - mid_reset, 1.0)
        two = lambda n: jnp.concatenate([cols[2 * n][rs], cols[2 * n + 1][rs]], axis=0)
        q, k, v = two(0), two(1), two(2)
        q = q * lax.rsqrt(jnp.sum(q * q, axis=-1, keepdims=True) + 1e-6)
        k = k * lax.rsqrt(jnp.sum(k * k, axis=-1, keepdims=True) + 1e-6)
        b = jnp.concatenate([betas[rs, 0:1], betas[rs, 1:2]], axis=0)
        gp = mm(jnp.concatenate([k, q], axis=0), k, NT)
        a = jnp.where(strict, gate * gp[:2 * STEP], 0.0) * b
        p = jnp.where(causal, gate * gp[2 * STEP:], 0.0)
        todo.append((q, k, v, b, a, p, row_masks(start_reset, mid_reset)))
    invs = tri_inverses([x[4] for x in todo], levels, eye)
    wus = [mm(inv, jnp.concatenate([x[3] * x[1], x[3] * x[2]], axis=1)) for inv, x in zip(invs, todo)]
    mem = [state[0], state[1]]
    for s in range(STEPS):
        rs = slice(s * STEP, (s + 1) * STEP)
        q, k, v, b, a, p, (enter, leave, keep) = todo[s]
        wu = wus[s]
        inv_out[s] = invs[s].astype(bf16)
        wu_out[s] = wu.astype(bf16)
        state_out[s, :HEAD] = mem[0].astype(bf16)
        state_out[s, HEAD:] = mem[1].astype(bf16)
        w = wu[:, :HEAD] * enter
        qe = q * enter
        ws, qs = [], []
        for h in range(2):
            hs = slice(h * STEP, (h + 1) * STEP)
            both = mm(jnp.concatenate([w[hs], qe[hs]], axis=0), mem[h])
            ws.append(both[:STEP])
            qs.append(both[STEP:])
        res = wu[:, HEAD:] - jnp.concatenate(ws, axis=0)
        res_out[s] = res.astype(bf16)
        ke = k * leave
        for h in range(2):
            hs = slice(h * STEP, (h + 1) * STEP)
            mem[h] = keep * mem[h] + mm(ke[hs], res[hs], TN)
        o = jnp.concatenate(qs, axis=0) + mm(p, res)
        mixed_ref[rs, :] = unstack(o)
        headed = o * lax.rsqrt(jnp.mean(o * o, axis=-1, keepdims=True) + 1e-5) * gain_ref[...]
        headed_ref[rs, :] = unstack(headed).astype(bf16)
    state[0] = mem[0]
    state[1] = mem[1]


def mixer_fwd(flags, proj, conv, gain):
    rows, total = proj.shape
    width = conv.shape[1]
    n = rows // ROWS
    steps = rows // STEP
    return pl.pallas_call(
        mixer_fwd_kernel,
        grid_spec=pltpu.PrefetchScalarGridSpec(
            num_scalar_prefetch=1, grid=(n,),
            in_specs=[pl.BlockSpec((ROWS, total), lambda g, f: (g, 0)), pl.BlockSpec((4, width), lambda g, f: (0, 0)), pl.BlockSpec((1, HEAD), lambda g, f: (0, 0))],
            out_specs=[pl.BlockSpec((ROWS, 2 * HEAD), lambda g, f: (g, 0)), pl.BlockSpec((ROWS, 2 * HEAD), lambda g, f: (g, 0)),
                       pl.BlockSpec((STEPS, 2 * HEAD, HEAD), lambda g, f: (g, 0, 0)), pl.BlockSpec((STEPS, 2 * STEP, HEAD), lambda g, f: (g, 0, 0)),
                       pl.BlockSpec((STEPS, 2 * STEP, 2 * HEAD), lambda g, f: (g, 0, 0)), pl.BlockSpec((STEPS, 2 * STEP, 2 * STEP), lambda g, f: (g, 0, 0))],
            scratch_shapes=[pltpu.VMEM((2, HEAD, HEAD), f32), pltpu.VMEM((ROWS + 8, width), f32)]),
        out_shape=[jax.ShapeDtypeStruct((rows, 2 * HEAD), bf16), jax.ShapeDtypeStruct((rows, 2 * HEAD), f32),
                   jax.ShapeDtypeStruct((steps, 2 * HEAD, HEAD), bf16), jax.ShapeDtypeStruct((steps, 2 * STEP, HEAD), bf16),
                   jax.ShapeDtypeStruct((steps, 2 * STEP, 2 * HEAD), bf16), jax.ShapeDtypeStruct((steps, 2 * STEP, 2 * STEP), bf16)],
        compiler_params=pltpu.CompilerParams(dimension_semantics=("arbitrary",), vmem_limit_bytes=48 * 2**20),
    )(flags, proj, conv, gain)


MESH_ID = pl.DeviceIdType.MESH
HALF = 2


def places():
    d = lax.axis_index("dp")
    t = lax.axis_index("tensor")
    beside = t + 1 - 2 * lax.rem(t, 2)
    across = lax.rem(t + 2, 4)
    corner = lax.rem(beside + 2, 4)
    return d, t, beside, across, corner


def push(src, dst, send, recv, device):
    copy = pltpu.make_async_remote_copy(src_ref=src, dst_ref=dst, send_sem=send, recv_sem=recv, device_id=device, device_id_type=MESH_ID)
    copy.start()
    return copy


def greet(devices):
    barrier = pltpu.get_barrier_semaphore()
    for device in devices:
        pl.semaphore_signal(barrier, inc=1, device_id=device, device_id_type=MESH_ID)
    pl.semaphore_wait(barrier, len(devices))


def row_block(owner, part, owner_rows, part_rows):
    return pl.ds(pl.multiple_of(owner * owner_rows + part * part_rows, part_rows), part_rows)


def mlp_kernel(headed_hbm, out_hbm, tok_hbm, gain_ref, gu_hbm, down_hbm, cot_hbm,
               dhid_hbm, dattn_hbm, gain_out, gu_out, downg_out, own_hbm, across_hbm,
               headed, out_w, tok, gu_w, down_w, cot, hidden, all_rows, act, d_gate, d_up, mine, keep, to_beside, from_beside, to_across, from_across, to_own, from_own,
               out_own, out_keep, from_beside_out, from_own_out, gu_acc, down_acc, gu_sum, down_sum, dattn, load, store, send, recv):
    d, t, beside, across, corner = places()
    rows = tok.shape[0]
    part = rows // HALF
    units = down_w.shape[0]
    loads = [(headed_hbm, headed), (out_hbm, out_w), (tok_hbm, tok), (gu_hbm, gu_w), (down_hbm, down_w), (cot_hbm, cot)]
    stores = [(mine, dhid_hbm), (dattn, dattn_hbm), (gu_sum, gu_out), (down_sum, downg_out), (out_own, own_hbm), (out_keep, across_hbm)]

    def loaded(i):
        return pltpu.make_async_copy(loads[i][0], loads[i][1], load.at[i])

    def stored(i):
        return pltpu.make_async_copy(stores[i][0], stores[i][1], store.at[i])

    def pushed(src, dst, i, s, peer):
        return pltpu.make_async_remote_copy(src_ref=src, dst_ref=dst, send_sem=send.at[i, s], recv_sem=recv.at[i, s], device_id=(d, peer), device_id_type=MESH_ID)

    def half(ref, s):
        return ref.at[pl.ds(s * part, part)]

    def rows_to(i, s, peer):
        block = all_rows.at[row_block(t, s, rows, part)]
        return pushed(block, block, i, s, peer)

    def passed(s):
        block = all_rows.at[row_block(across, s, rows, part)]
        return pushed(block, block, 2, s, beside)

    def handed(s):
        return pushed(half(to_beside, s), half(from_beside, s), 3, s, beside)

    def summed(s):
        return pushed(half(to_across, s), half(from_across, s), 4, s, across)

    def owned(s):
        return pushed(half(to_own, s), half(from_own, s), 5, s, beside)

    def handed_out(s):
        return pushed(half(headed, s), half(from_beside_out, s), 6, s, beside)

    def owned_out(s):
        return pushed(half(dattn, s), half(from_own_out, s), 7, s, beside)

    for i in range(len(loads)):
        loaded(i).start()
    greet([(d, beside), (d, across)])
    for i in range(3):
        loaded(i).wait()
    gain = gain_ref[...]
    for s in range(HALF):
        at = pl.ds(s * part, part)
        x = tok[at, :].astype(f32) + lax.dot_general(headed[at, :], out_w[...], NN, preferred_element_type=f32)
        hidden[at, :] = x
        all_rows[row_block(t, s, rows, part), :] = (x * lax.rsqrt(jnp.mean(x * x, axis=-1, keepdims=True) + 1e-5) * gain).astype(bf16)
        rows_to(0, s, across).start()
        rows_to(1, s, beside).start()
    for i in range(3, len(loads)):
        loaded(i).wait()

    def work(owner, s):
        at = row_block(owner, s, rows, part)
        x = all_rows[at, :]
        gate = lax.dot_general(x, gu_w[:units, :], NT, preferred_element_type=f32)
        up = lax.dot_general(x, gu_w[units:, :], NT, preferred_element_type=f32)
        sig = sigmoid(gate)
        silu = gate * sig
        low = (silu * up).astype(bf16)
        act[at, :] = low
        d_act = lax.dot_general(cot[at, :], down_w[...], NT, preferred_element_type=f32)
        dg = (d_act * up * sig * (1.0 + gate * (1.0 - sig))).astype(bf16)
        du = (d_act * silu).astype(bf16)
        d_gate[at, :] = dg
        d_up[at, :] = du
        out = lax.dot_general(low, down_w[...], NN, preferred_element_type=f32)
        return lax.dot_general(dg, gu_w[:units, :], NN, preferred_element_type=f32) + lax.dot_general(du, gu_w[units:, :], NN, preferred_element_type=f32), out

    def weight_grads(pair, last):
        at = pl.ds(pl.multiple_of(pair * 2 * rows, 2 * rows), 2 * rows)

        def put(acc, total, where, value):
            if last:
                total[where, :] = (acc[where, :] + value).astype(bf16)
            else:
                acc[where, :] = value

        for c in range(0, units, 256):
            size = min(256, units - c)
            put(gu_acc, gu_sum, pl.ds(c, size), lax.dot_general(d_gate[at, c:c + size], all_rows[at, :], TN, preferred_element_type=f32))
            put(gu_acc, gu_sum, pl.ds(units + c, size), lax.dot_general(d_up[at, c:c + size], all_rows[at, :], TN, preferred_element_type=f32))
            put(down_acc, down_sum, pl.ds(c, size), lax.dot_general(act[at, c:c + size], cot[at, :], TN, preferred_element_type=f32))

    for s in range(HALF):
        at = pl.ds(s * part, part)
        mine[at, :], out = work(t, s)
        out_own[at, :] = hidden[at, :] + out
    for s in range(HALF):
        at = pl.ds(s * part, part)
        rows_to(1, s, beside).wait_recv()
        total, out = work(beside, s)
        to_own[at, :] = total.astype(bf16)
        owned(s).start()
        dattn[at, :] = out.astype(bf16)
        owned_out(s).start()
    for s in range(HALF):
        at = pl.ds(s * part, part)
        rows_to(0, s, across).wait_recv()
        passed(s).start()
        keep[...], out = work(across, s)
        out_keep[at, :] = out.astype(bf16)
        passed(s).wait_recv()
        total, out = work(corner, s)
        to_beside[at, :] = total.astype(bf16)
        handed(s).start()
        headed[at, :] = out.astype(bf16)
        handed_out(s).start()
        handed(s).wait_recv()
        to_across[at, :] = (keep[...] + from_beside[at, :].astype(f32)).astype(bf16)
        summed(s).start()
        if s == 0:
            weight_grads(t // 2, False)
    weight_grads(1 - t // 2, True)
    stored(2).start()
    stored(3).start()
    for s in range(HALF):
        at = pl.ds(s * part, part)
        handed_out(s).wait_recv()
        out_keep[at, :] = (out_keep[at, :].astype(f32) + from_beside_out[at, :].astype(f32)).astype(bf16)
        owned_out(s).wait_recv()
        out_own[at, :] = out_own[at, :] + from_own_out[at, :].astype(f32)
        owned_out(s).wait_send()
    stored(4).start()
    stored(5).start()
    gain_out[...] = jnp.zeros_like(gain_out)
    piece = 64
    for s in range(HALF):
        owned(s).wait_recv()
        summed(s).wait_recv()

        def chunk(i, carry, s=s):
            at = pl.ds(pl.multiple_of(s * part + i * piece, piece), piece)
            grad = mine[at, :] + from_own[at, :].astype(f32) + from_across[at, :].astype(f32)
            x = hidden[at, :]
            r = lax.rsqrt(jnp.mean(x * x, axis=-1, keepdims=True) + 1e-5)
            scaled = gain * grad
            cot_rows = cot[pl.ds(pl.multiple_of(t * rows + s * part + i * piece, piece), piece), :].astype(f32)
            full = cot_rows + r * scaled - x * (r * r * r * jnp.mean(x * scaled, axis=-1, keepdims=True))
            mine[at, :] = full
            dattn[at, :] = full.astype(bf16)
            gain_out[...] += jnp.sum((grad * x * r).reshape(piece // 8, 8, grad.shape[1]), axis=0)
            return carry

        lax.fori_loop(0, part // piece, chunk, 0)
    stored(0).start()
    stored(1).start()
    for s in range(HALF):
        for copy in (rows_to(0, s, across), rows_to(1, s, beside), passed(s), handed(s), summed(s), owned(s), handed_out(s)):
            copy.wait_send()
    for i in range(len(stores)):
        stored(i).wait()


def mlp(headed, out_all, tokens, gain, gate_up, down, cot):
    rows, width = tokens.shape
    total = cot.shape[0]
    units = down.shape[0]
    hbm = pl.BlockSpec(memory_space=pl.ANY)
    vmem = pl.BlockSpec(memory_space=pltpu.VMEM)
    like = lambda x: pltpu.VMEM(x.shape, x.dtype)
    half = lambda: pltpu.VMEM((rows, width), bf16)
    wide = lambda: pltpu.VMEM((rows, width), f32)
    unit = lambda: pltpu.VMEM((total, units), bf16)
    out = lambda shape, kind: jax.ShapeDtypeStruct(shape, kind)
    dma = pltpu.SemaphoreType.DMA
    return pl.pallas_call(
        mlp_kernel,
        in_specs=[hbm] * 3 + [vmem] + [hbm] * 3,
        out_specs=[hbm] * 2 + [vmem] + [hbm] * 4,
        out_shape=[out((rows, width), f32), out((rows, width), bf16), out((8, width), f32), out(gate_up.shape, bf16), out(down.shape, bf16), out((rows, width), f32), out((rows, width), bf16)],
        scratch_shapes=[like(headed), like(out_all), like(tokens), like(gate_up), like(down), like(cot), wide(), pltpu.VMEM((total, width), bf16), unit(), unit(), unit(),
                        wide(), pltpu.VMEM((rows // HALF, width), f32), half(), half(), half(), half(), half(), half(), wide(), half(), half(), half(),
                        pltpu.VMEM(gate_up.shape, f32), pltpu.VMEM(down.shape, f32), like(gate_up), like(down), half(), dma((6,)), dma((6,)), dma((8, HALF)), dma((8, HALF))],
        compiler_params=pltpu.CompilerParams(collective_id=1, has_side_effects=True, vmem_limit_bytes=62 * 2**20),
    )(headed, out_all, tokens, gain, gate_up, down, cot)


def mixer_bwd_block(blk, width, flags, proj_ref, prev_ref, conv_ref, gain_ref, mixed_ref, state_in, res_in, wu_in, inv_in, dheaded, dcat, dstate, buf, dbuf, cacc, gacc):
    buf[0:8, :] = prev_ref[:, :width]
    buf[8:, :] = proj_ref[:, :width]
    heads, tails = span_masks(flags, blk * (BACK_ROWS // SPAN), BACK_ROWS // SPAN)
    cols, slopes = [], []
    for c in range(width // HEAD):
        total = conv_column(buf, conv_ref, heads, slice(c * HEAD, (c + 1) * HEAD))
        sig = sigmoid(total)
        cols.append(total * sig)
        slopes.append(sig * (1.0 + total * (1.0 - sig)))
    betas = sigmoid(proj_ref[:, width:])
    strict, causal, cross, _, _ = pair_masks()
    lane = lax.broadcasted_iota(jnp.int32, (STEP, HEAD), 1)
    order = list(reversed(range(BACK_STEPS)))
    hs = [slice(h * STEP, (h + 1) * STEP) for h in range(2)]
    spans = [slice(s * STEP, (s + 1) * STEP) for s in range(BACK_STEPS)]
    edge = [resets(flags, blk * BACK_STEPS + s) for s in range(BACK_STEPS)]
    enter, leave, keep = zip(*[row_masks(*e) for e in edge])
    gate = [jnp.where(cross, 1.0 - e[1], 1.0) for e in edge]
    both = lambda n: [jnp.concatenate([cols[2 * n][rs], cols[2 * n + 1][rs]], axis=0) for rs in spans]
    q, k, v = both(0), both(1), both(2)
    rq = [lax.rsqrt(jnp.sum(x * x, axis=-1, keepdims=True) + 1e-6) for x in q]
    rk = [lax.rsqrt(jnp.sum(x * x, axis=-1, keepdims=True) + 1e-6) for x in k]
    q = [x * r for x, r in zip(q, rq)]
    k = [x * r for x, r in zip(k, rk)]
    q16 = [x.astype(bf16) for x in q]
    k16 = [x.astype(bf16) for x in k]
    b = [jnp.concatenate([betas[rs, 0:1], betas[rs, 1:2]], axis=0) for rs in spans]
    gp = [mm(jnp.concatenate([x, y], axis=0), x, NT) for x, y in zip(k16, q16)]
    gram = [jnp.where(strict, m * x[:2 * STEP], 0.0) for m, x in zip(gate, gp)]
    p = [jnp.where(causal, m * x[2 * STEP:], 0.0).astype(bf16) for m, x in zip(gate, gp)]
    do = []
    for s in range(BACK_STEPS):
        o = stack(mixed_ref[spans[s], :])
        dh = stack(dheaded[pl.ds(pl.multiple_of(blk * BACK_ROWS + s * STEP, STEP), STEP), :].astype(f32))
        ro = lax.rsqrt(jnp.mean(o * o, axis=-1, keepdims=True) + 1e-5)
        on = o * ro
        gacc[...] += jnp.sum((dh * on).reshape(2 * STEP // 8, 8, HEAD), axis=0)
        dn = dh * gain_ref[...]
        do.append(ro * (dn - on * jnp.mean(dn * on, axis=-1, keepdims=True)))
    do16 = [x.astype(bf16) for x in do]
    doe = [(x * e).astype(bf16) for x, e in zip(do, enter)]
    ke16 = [(x * e).astype(bf16) for x, e in zip(k, leave)]
    we = [(wu_in[s][:, :HEAD].astype(f32) * enter[s]).astype(bf16) for s in range(BACK_STEPS)]
    dres = [mm(x, y, TN) for x, y in zip(p, do16)]
    qdo = [[mm(x[r], y[r], TN) for r in hs] for x, y in zip(q16, doe)]
    dmem = [dstate[0], dstate[1]]
    dres16, after = [None] * BACK_STEPS, [None] * BACK_STEPS
    for s in order:
        low = [m.astype(bf16) for m in dmem]
        after[s] = low
        dres[s] = dres[s] + jnp.concatenate([mm(ke16[s][hs[h]], low[h]) for h in range(2)], axis=0)
        dres16[s] = dres[s].astype(bf16)
        for h in range(2):
            dmem[h] = keep[s] * dmem[h] + qdo[s][h] - mm(we[s][hs[h]], dres16[s][hs[h]], TN)
    dp = [mm(do16[s], res_in[s], NT) for s in order]
    dke = [jnp.concatenate([mm(res_in[s, hs[h]], after[s][h], NT) for h in range(2)], axis=0) for s in order]
    ds = [[mm(jnp.concatenate([do16[s][hs[h]], dres16[s][hs[h]]], axis=0), state_in[s, h * HEAD:(h + 1) * HEAD], NT) for h in range(2)] for s in order]
    dp = [jnp.where(causal, gate[s] * x, 0.0).astype(bf16) for s, x in zip(order, dp)]
    dw = [-enter[s] * jnp.concatenate([x[0][STEP:], x[1][STEP:]], axis=0) for s, x in zip(order, ds)]
    db_kv = [mm(inv_in[s], jnp.concatenate([x, dres[s]], axis=1), TN) for s, x in zip(order, dw)]
    dq = [enter[s] * jnp.concatenate([x[0][:STEP], x[1][:STEP]], axis=0) + mm(y, k16[s]) for s, x, y in zip(order, ds, dp)]
    dk = [mm(y, q16[s], TN) + leave[s] * x for s, x, y in zip(order, dke, dp)]
    da = [-jnp.where(strict, gate[s] * mm(x, wu_in[s], NT), 0.0) for s, x in zip(order, db_kv)]
    dg = [(x * b[s]).astype(bf16) for s, x in zip(order, da)]
    dk = [x + mm(y, k16[s]) + mm(y, k16[s], TN) + b[s] * z[:, :HEAD] for s, x, y, z in zip(order, dk, dg, db_kv)]
    for i, s in enumerate(order):
        rs = spans[s]
        dbeta = jnp.sum(da[i] * gram[s], axis=-1, keepdims=True) + jnp.sum(db_kv[i][:, :HEAD] * k[s] + db_kv[i][:, HEAD:] * v[s], axis=-1, keepdims=True)
        dv = b[s] * db_kv[i][:, HEAD:]
        dqs = rq[s] * (dq[i] - q[s] * jnp.sum(dq[i] * q[s], axis=-1, keepdims=True))
        dks = rk[s] * (dk[i] - k[s] * jnp.sum(dk[i] * k[s], axis=-1, keepdims=True))
        dpre = dbeta * b[s] * (1.0 - b[s])
        for n, x in enumerate((dqs, dks, dv)):
            for h in range(2):
                c = 2 * n + h
                dbuf[rs, c * HEAD:(c + 1) * HEAD] = x[hs[h]] * slopes[c][rs]
        dcat[pl.ds(pl.multiple_of(blk * BACK_ROWS + s * STEP, STEP), STEP), width:] = jnp.where(lane == 0, dpre[:STEP], jnp.where(lane == 1, dpre[STEP:], 0.0)).astype(bf16)
    dstate[0] = dmem[0]
    dstate[1] = dmem[1]
    for c in range(width // HEAD):
        cs = slice(c * HEAD, (c + 1) * HEAD)
        total, grads = conv_column_back(buf, dbuf, conv_ref, tails, cs)
        dcat[pl.ds(pl.multiple_of(blk * BACK_ROWS, BACK_ROWS), BACK_ROWS), cs] = total.astype(bf16)
        for j in range(4):
            cacc[j, :, cs] += grads[j]
    dbuf[BACK_ROWS:, :] = dbuf[0:8, :]


class Ring:
    def __init__(self, here, after, before, sources, results, lands, by_rows, send, recv):
        self.here, self.targets = here, (after, before)
        self.sources, self.results, self.lands, self.by_rows, self.send, self.recv = sources, results, lands, by_rows, send, recv

    def shard(self, way, k):
        return lax.rem(self.here + (k if way else 2 * RING - k), RING)

    def view(self, ref, i, way, k):
        shard = self.shard(way, k)
        rows, cols = ref.shape
        if self.by_rows[i]:
            piece = rows // (2 * RING)
            return ref.at[pl.ds(pl.multiple_of((2 * shard + way) * piece, piece), piece)]
        piece = cols // RING
        return ref.at[pl.ds(way * (rows // 2), rows // 2), pl.ds(pl.multiple_of(shard * piece, piece), piece)]

    def copy(self, i, way, r):
        if r == 0:
            src, dst = self.view(self.sources[i], i, way, 0), self.lands[i].at[way, 0]
        elif r < RING - 1:
            src, dst = self.lands[i].at[way, r - 1], self.lands[i].at[way, r]
        else:
            src = dst = self.view(self.results[i], i, way, r)
        return pltpu.make_async_remote_copy(src_ref=src, dst_ref=dst, send_sem=self.send.at[i, way], recv_sem=self.recv.at[i, way, r], device_id=self.targets[way], device_id_type=MESH_ID)

    def round(self, r):
        for i in range(len(self.sources)):
            for way in range(2):
                if r > 0:
                    last = self.copy(i, way, r - 1)
                    last.wait_send()
                    last.wait_recv()
                if 0 < r < RING:
                    land = self.lands[i].at[way, r - 1]
                    total = (land[...].astype(f32) + self.view(self.sources[i], i, way, r)[...].astype(f32)).astype(bf16)
                    if r < RING - 1:
                        land[...] = total
                    else:
                        done = self.view(self.results[i], i, way, r)
                        done[...] = total
                if r < ROUNDS:
                    self.copy(i, way, r).start()


def ring_place(d):
    base = d // RING * RING
    inner = lax.rem(d, RING)
    line = inner // 2
    here = jnp.where(lax.rem(inner, 2) == 0, line, RING - 1 - line)

    def device(place):
        return base + jnp.where(place < RING // 2, 2 * place, 2 * (RING - 1 - place) + 1)

    return here, device(lax.rem(here + 1, RING)), device(lax.rem(here + RING - 1, RING))


def ring_lands(shapes, by_rows):
    pieces = [(s[0] // (2 * RING), s[1]) if rows else (s[0] // 2, s[1] // RING) for s, rows in zip(shapes, by_rows)]
    return [pltpu.VMEM((2, RING - 1) + p, bf16) for p in pieces]


def back_kernel(n_dp, flags, proj_ref, prev_ref, conv_ref, gain_ref, mixed_ref, state_in, res_in, wu_in, inv_in,
                headed_hbm, attn_hbm, dattn_hbm, out_w_hbm, qkv_hbm, beta_hbm, tok_hbm, dhid_hbm, first_gain, second_grad, gu_hbm, down_hbm, across_hbm,
                dx_hbm, small_out, gu_out, down_out, cat_out, outw_out, landed_hbm,
                headed, attn, dattn_all, out_w, w, tok, dhid, gu_src, down_src, cat_src, outw_src,
                gu_res, down_res, cat_res, outw_res, gate_land, up_land, down_land, cat_land, outw_land,
                dheaded, dcat, dstate, buf, dbuf, cacc, gacc, mine, to_beside, from_beside, to_across, from_across, to_own, from_own,
                group_send, group_land, all_send, all_land, gain_acc, beta_grad,
                load, store, send_m, recv_m, send_c, recv_c, send_x, recv_x, send_g, recv_g, send_a, recv_a):
    g = pl.program_id(0)
    n = pl.num_programs(0)
    d, t, beside, across, corner = places()
    here, after, before = ring_place(d)
    rows = tok.shape[0]
    part = rows // HALF
    width = buf.shape[1]
    others = [d // RING * RING + lax.rem(d + k, RING) for k in range(1, RING)]
    units = down_src.shape[0]
    gate_up = lambda ref: [ref.at[pl.ds(0, units)], ref.at[pl.ds(units, units)]]
    mlp_ring = Ring(here, (after, t), (before, t), gate_up(gu_src) + [down_src], gate_up(gu_res) + [down_res], [gate_land, up_land, down_land], [False] * 3, send_m, recv_m)
    cat_ring = Ring(here, (after, t), (before, t), [cat_src, outw_src], [cat_res, outw_res], [cat_land, outw_land], [True, True], send_c, recv_c)
    loads = [(gu_hbm, gu_src), (down_hbm, down_src), (dattn_hbm, dattn_all.at[pl.ds(pl.multiple_of(t * rows, rows), rows)]), (out_w_hbm, out_w), (headed_hbm, headed), (attn_hbm, attn), (tok_hbm, tok), (dhid_hbm, dhid), (beta_hbm, w.at[:, pl.ds(width, HEAD)])]
    loads += [(qkv_hbm.at[i], w.at[:, pl.ds(i * 2 * HEAD, 2 * HEAD)]) for i in range(3)]
    stores = [(gu_res, gu_out), (down_res, down_out), (mine, dx_hbm), (cat_res, cat_out), (outw_res, outw_out)]

    def loaded(i):
        return pltpu.make_async_copy(loads[i][0], loads[i][1], load.at[i])

    def stored(i):
        return pltpu.make_async_copy(stores[i][0], stores[i][1], store.at[i])

    def pushed(src, dst, i, s, peer):
        return pltpu.make_async_remote_copy(src_ref=src, dst_ref=dst, send_sem=send_x.at[i, s], recv_sem=recv_x.at[i, s], device_id=(d, peer), device_id_type=MESH_ID)

    def outward():
        return pushed(across_hbm, landed_hbm, 6, 0, across)

    def block_at(owner, s):
        return row_block(owner, s, rows, part)

    def rows_to(i, s, peer):
        block = dattn_all.at[block_at(t, s)]
        return pushed(block, block, i, s, peer)

    def passed(s):
        block = dattn_all.at[block_at(across, s)]
        return pushed(block, block, 2, s, beside)

    def head_grad(owner, s):
        at = block_at(owner, s)
        dheaded[at, :] = lax.dot_general(dattn_all[at, :], out_w[...], NT, preferred_element_type=f32).astype(bf16)

    @pl.when(g == 0)
    def _():
        for i in range(len(loads)):
            loaded(i).start()
        greet([(d, beside), (d, across), (d, corner)] + [(o, t) for o in others])
        for i in range(3):
            loaded(i).wait()
        for s in range(HALF):
            rows_to(0, s, across).start()
            rows_to(1, s, beside).start()
        mlp_ring.round(0)
        loaded(3).wait()
        dstate[...] = jnp.zeros_like(dstate)
        dbuf[BACK_ROWS:, :] = jnp.zeros((8, width), f32)
        cacc[...] = jnp.zeros_like(cacc)
        gacc[...] = jnp.zeros_like(gacc)
        gain_acc[...] = jnp.zeros_like(gain_acc)
        for s in range(HALF):
            head_grad(t, s)
        for s in range(HALF):
            rows_to(1, s, beside).wait_recv()
            head_grad(beside, s)
        mlp_ring.round(1)
        rows_to(0, 0, across).wait_recv()
        passed(0).start()
        head_grad(across, 0)
        mlp_ring.round(2)
        passed(0).wait_recv()
        head_grad(corner, 0)
        mlp_ring.round(3)
        rows_to(0, 1, across).wait_recv()
        passed(1).start()
        head_grad(across, 1)
        passed(1).wait_recv()
        head_grad(corner, 1)
        outward().start()
        mlp_ring.round(4)

    for at, r in ((1, 5), (3, 6), (5, 7), (6, 8)):
        @pl.when(g == at)
        def _(r=r):
            mlp_ring.round(r)

    blk = n - 1 - g
    mixer_bwd_block(blk, width, flags, proj_ref, prev_ref, conv_ref, gain_ref, mixed_ref, state_in, res_in, wu_in, inv_in, dheaded, dcat, dstate, buf, dbuf, cacc, gacc)

    def work(owner, s):
        return lax.dot_general(dcat[block_at(owner, s), :], w[...], NT, preferred_element_type=f32)

    def handed(s):
        at = pl.ds(s * part, part)
        return pushed(to_beside.at[at], from_beside.at[at], 3, s, beside)

    def summed(s):
        at = pl.ds(s * part, part)
        return pushed(to_across.at[at], from_across.at[at], 4, s, across)

    def owned(s):
        at = pl.ds(s * part, part)
        return pushed(to_own.at[at], from_own.at[at], 5, s, beside)

    def grouped(i, peer):
        return pltpu.make_async_remote_copy(src_ref=group_send, dst_ref=group_land.at[i], send_sem=send_g.at[i], recv_sem=recv_g.at[i], device_id=(d, peer), device_id_type=MESH_ID)

    def spread(i, o):
        return pltpu.make_async_remote_copy(src_ref=all_send, dst_ref=all_land.at[i], send_sem=send_a.at[i], recv_sem=recv_a.at[i], device_id=(o, t), device_id_type=MESH_ID)

    piece = 64

    def finish(s):
        gain = first_gain[...]

        def chunk(i, carry):
            at = pl.ds(pl.multiple_of(s * part + i * piece, piece), piece)
            grad = mine[at, :] + from_own[at, :].astype(f32) + from_across[at, :].astype(f32)
            x = tok[at, :].astype(f32)
            r = lax.rsqrt(jnp.mean(x * x, axis=-1, keepdims=True) + 1e-5)
            scaled = gain * grad
            mine[at, :] = dhid[at, :] + r * scaled - x * (r * r * r * jnp.mean(x * scaled, axis=-1, keepdims=True))
            gain_acc[...] += jnp.sum((grad * x * r).reshape(piece // 8, 8, grad.shape[1]), axis=0)
            return carry

        lax.fori_loop(0, part // piece, chunk, 0)

    @pl.when(g == n - 1)
    def _():
        for i in range(4, len(loads)):
            loaded(i).wait()
        mlp_ring.round(9)

        def cat_chunk(i):
            grad = lax.dot_general(attn[:, i * 256:(i + 1) * 256], dcat[:, :width], TN, preferred_element_type=f32).astype(bf16)
            for j in range(3):
                cat_src[pl.ds(j * attn.shape[1] + i * 256, 256), :] = grad[:, j * 2 * HEAD:(j + 1) * 2 * HEAD]

        count = attn.shape[1] // 256
        for i in range(count):
            cat_chunk(i)
            if i == count // 2 - 1:
                mlp_ring.round(10)
        beta_grad[...] = lax.dot_general(dcat[:, width:], attn[...], TN, preferred_element_type=f32)[:8]
        outw_src[...] = lax.dot_general(headed[...], dattn_all[...], TN, preferred_element_type=f32).astype(bf16)
        cat_ring.round(0)
        mlp_ring.round(11)
        for s in range(HALF):
            at = pl.ds(s * part, part)
            to_beside[at, :] = work(corner, s).astype(bf16)
            handed(s).start()
            total = work(across, s)
            handed(s).wait_recv()
            to_across[at, :] = (total + from_beside[at, :].astype(f32)).astype(bf16)
            summed(s).start()
        cat_ring.round(1)
        mlp_ring.round(12)
        for s in range(HALF):
            at = pl.ds(s * part, part)
            to_own[at, :] = work(beside, s).astype(bf16)
            owned(s).start()
            mine[at, :] = work(t, s)
        cat_ring.round(2)
        mlp_ring.round(13)
        cat_ring.round(3)
        cat_ring.round(4)
        mlp_ring.round(14)
        for i in range(2):
            stored(i).start()
        cat_ring.round(5)
        owned(0).wait_recv()
        summed(0).wait_recv()
        finish(0)
        cat_ring.round(6)
        cat_ring.round(7)
        owned(1).wait_recv()
        summed(1).wait_recv()
        finish(1)
        stored(2).start()
        cat_ring.round(8)
        line = lax.broadcasted_iota(jnp.int32, small_out.shape, 0)
        lane = lax.broadcasted_iota(jnp.int32, small_out.shape, 1)
        shared = (line < 2) | ((line == 3) & (lane >= width))
        group_send[...] = jnp.zeros_like(group_send)
        group_send[0:1, :] = jnp.sum(gain_acc[...], axis=0, keepdims=True)
        group_send[1:2, :] = jnp.sum(second_grad[...], axis=0, keepdims=True)
        group_send[2:3, :] = beta_grad[0:1, :]
        group_send[7:8, :] = beta_grad[1:2, :]
        group_send[3:4, width:width + HEAD] = jnp.sum(gacc[...], axis=0, keepdims=True)
        for j in range(4):
            group_send[3 + j:4 + j, :width] = jnp.sum(cacc[j], axis=0, keepdims=True)
        for i, peer in enumerate((beside, across, corner)):
            grouped(i, peer).start()
        cat_ring.round(9)
        small = group_send[...]
        for i, peer in enumerate((beside, across, corner)):
            grouped(i, peer).wait_recv()
        both = (small + group_land[0]) + (group_land[1] + group_land[2])
        small = jnp.where(shared, both, small)
        all_send[...] = small
        for i, o in enumerate(others):
            spread(i, o).start()
        cat_ring.round(10)
        cat_ring.round(11)
        for i, o in enumerate(others):
            spread(i, o).wait_recv()
            small = small + all_land[i]
        small_out[...] = small
        cat_ring.round(12)
        cat_ring.round(13)
        cat_ring.round(14)
        for i in range(3, 5):
            stored(i).start()
        for s in range(HALF):
            for copy in (rows_to(0, s, across), rows_to(1, s, beside), passed(s), handed(s), summed(s), owned(s)):
                copy.wait_send()
        for i, peer in enumerate((beside, across, corner)):
            grouped(i, peer).wait_send()
        for i, o in enumerate(others):
            spread(i, o).wait_send()
        outward().wait()
        for i in range(len(stores)):
            stored(i).wait()


def backward(n_dp, flags, proj, conv, gain, saved, headed, attn_all, d_attn, out_w, qkv, beta, tokens, d_hidden, first_gain, second_grad, gu_part, down_part, out_across):
    mixed, states, res, wu, inv = saved
    total_rows, total = proj.shape
    width = conv.shape[1]
    rows, model = tokens.shape
    n = total_rows // BACK_ROWS
    m2 = lambda g: (n - 1 - g, 0)
    m3 = lambda g: (n - 1 - g, 0, 0)
    z2 = lambda g: (0, 0)
    hbm = pl.BlockSpec(memory_space=pl.ANY)
    dma = pltpu.SemaphoreType.DMA
    like = lambda x: pltpu.VMEM(x.shape, x.dtype)
    mlp_parts = (gu_part, down_part)
    cat_shapes = [(3 * model, 2 * HEAD), (headed.shape[1], model)]
    half = lambda: pltpu.VMEM((rows, model), bf16)
    line = second_grad.shape
    out = lambda shape, kind: jax.ShapeDtypeStruct(shape, kind)
    return pl.pallas_call(
        functools.partial(back_kernel, n_dp),
        grid=(n,),
        in_specs=[pl.BlockSpec(memory_space=pltpu.SMEM), pl.BlockSpec((BACK_ROWS, total), m2),
                  pl.BlockSpec((8, total), lambda g: (jnp.maximum((n - 1 - g) * (BACK_ROWS // 8) - 1, 0), 0)),
                  pl.BlockSpec((4, width), z2), pl.BlockSpec((1, HEAD), z2), pl.BlockSpec((BACK_ROWS, 2 * HEAD), m2),
                  pl.BlockSpec((BACK_STEPS, 2 * HEAD, HEAD), m3), pl.BlockSpec((BACK_STEPS, 2 * STEP, HEAD), m3),
                  pl.BlockSpec((BACK_STEPS, 2 * STEP, 2 * HEAD), m3), pl.BlockSpec((BACK_STEPS, 2 * STEP, 2 * STEP), m3)]
        + [hbm] * 8 + [pl.BlockSpec((1, model), z2), pl.BlockSpec(line, z2)] + [hbm] * 3,
        out_specs=[hbm, pl.BlockSpec(line, z2)] + [hbm] * 5,
        out_shape=[out((rows, model), f32), out(line, f32)] + [out(x.shape, bf16) for x in mlp_parts] + [out(s, bf16) for s in cat_shapes] + [out((rows, model), bf16)],
        scratch_shapes=[like(headed), like(attn_all), like(attn_all), like(out_w), pltpu.VMEM((model, total), bf16), like(tokens), like(d_hidden)]
        + [like(x) for x in mlp_parts] + [pltpu.VMEM(s, bf16) for s in cat_shapes]
        + [like(x) for x in mlp_parts] + [pltpu.VMEM(s, bf16) for s in cat_shapes]
        + ring_lands([down_part.shape] * 3, [False] * 3) + ring_lands(cat_shapes, [True, True])
        + [pltpu.VMEM((total_rows, 2 * HEAD), bf16), pltpu.VMEM((total_rows, total), bf16), pltpu.VMEM((2, HEAD, HEAD), f32),
           pltpu.VMEM((BACK_ROWS + 8, width), f32), pltpu.VMEM((BACK_ROWS + 8, width), f32), pltpu.VMEM((4, 8, width), f32), pltpu.VMEM((8, HEAD), f32),
           pltpu.VMEM((rows, model), f32), half(), half(), half(), half(), half(), half(),
           pltpu.VMEM(line, f32), pltpu.VMEM((3,) + line, f32), pltpu.VMEM(line, f32), pltpu.VMEM((RING - 1,) + line, f32), pltpu.VMEM((8, model), f32), pltpu.VMEM((8, model), f32),
           dma((13,)), dma((5,)), dma((3, 2)), dma((3, 2, ROUNDS)), dma((2, 2)), dma((2, 2, ROUNDS)), dma((7, HALF)), dma((7, HALF)),
           dma((3,)), dma((3,)), dma((RING - 1,)), dma((RING - 1,))],
        compiler_params=pltpu.CompilerParams(dimension_semantics=("arbitrary",), collective_id=2, has_side_effects=True, vmem_limit_bytes=62 * 2**20),
    )(flags, proj, proj, conv, gain, mixed, states, res, wu, inv, headed, attn_all, d_attn, out_w, qkv, beta, tokens, d_hidden, first_gain, second_grad, gu_part, down_part, out_across)


def rms_norm(values, scales):
    inverse = lax.rsqrt(jnp.mean(values * values, axis=-1, keepdims=True) + 1e-05)
    return values * inverse * scales


def gather(x):
    return lax.all_gather(x, "tensor", axis=0, tiled=True)


def dot(a, b, dims=NN):
    return lax.dot_general(a, b, dims, preferred_element_type=f32)


def on_device(tokens, lengths, attn_gain, qkv_weight, beta_weight, conv_weight, head_gain, out_weight, mlp_gain, gate_up_weight, down_weight, cotangent):
    model_width = tokens.shape[1]
    width = qkv_weight.shape[1] * qkv_weight.shape[2]
    heads = beta_weight.shape[1]
    group_rows = tokens.shape[0] * lax.axis_size("tensor")
    starts = jnp.arange(group_rows // SPAN + 8, dtype=jnp.int32) * SPAN
    flags = jnp.where((starts == 0) | (starts == lengths[0, 0]), 1.0, 0.0).astype(f32)
    local_in = tokens.astype(f32)
    first_scale = attn_gain.astype(f32)
    second_scale = mlp_gain.astype(f32)
    head_scale = head_gain.astype(f32)[None]
    conv = conv_weight.reshape(conv_weight.shape[0], -1).astype(f32)
    qkv = jnp.transpose(qkv_weight, (1, 0, 2))
    beta = jnp.pad(beta_weight, ((0, 0), (0, HEAD - heads)))
    gate_up = jnp.transpose(gate_up_weight, (1, 2, 0)).reshape(-1, model_width)
    attn_in = rms_norm(local_in, first_scale).astype(bf16)
    attn_all = gather(attn_in)
    out_all = gather(out_weight)
    cot_all = gather(cotangent)
    proj = dot(attn_all, jnp.concatenate([qkv[0], qkv[1], qkv[2], beta], axis=1))
    headed, *saved = mixer_fwd(flags, proj, conv, head_scale)
    headed_rows = lax.all_to_all(headed, "tensor", split_axis=0, concat_axis=1, tiled=True)
    d_hidden, d_attn, second_grad, gu_part, down_part, out_own, out_across = mlp(headed_rows, out_all, tokens, second_scale[None], gate_up, down_weight, cot_all)
    n_dp = lax.axis_size("dp")
    input_grad, small, *sums, landed = backward(
        n_dp, flags, proj, conv, head_scale, saved, headed, attn_all, d_attn, out_weight, qkv, beta, tokens, d_hidden, first_scale[None], second_grad, gu_part, down_part, out_across)
    if n_dp > RING:
        groups = [list(range(i, n_dp, RING)) for i in range(RING)]
        small, *sums = lax.psum((small, *sums), "dp", axis_index_groups=groups)
    gu_sum, down_sum, cat_sum, out_sum = sums
    output = (out_own + landed.astype(f32)).astype(bf16)
    return (
        output,
        input_grad,
        small[0],
        jnp.transpose(cat_sum.astype(f32).reshape(3, model_width, -1), (1, 0, 2)),
        jnp.stack([small[2], small[7]], axis=1),
        small[3:7, :width].reshape(conv_weight.shape),
        small[3, width:width + HEAD],
        out_sum.astype(f32),
        small[1],
        jnp.transpose(gu_sum.astype(f32).reshape(2, -1, model_width), (2, 0, 1)),
        down_sum.astype(f32),
    )


def solution(mesh):
    rows = P(("dp", "tensor"), None)
    last = P(None, None, "tensor")
    return jax.shard_map(
        on_device,
        mesh=mesh,
        in_specs=(rows, P("dp", None), P(), last, P(None, "tensor"), last, P(), P("tensor", None), P(), last, P("tensor", None), rows),
        out_specs=(rows, rows, P(), last, P(None, "tensor"), last, P(), P("tensor", None), P(), last, P("tensor", None)),
        check_vma=False,
    )
```

```python
import functools
import jax
import jax.numpy as jnp
from jax import lax
from jax.experimental import pallas as pl
from jax.experimental.pallas import tpu as pltpu
from jax.sharding import PartitionSpec as P

HEAD = 128
STEP = 128
SPAN = 64
STEPS = 4
ROWS = STEP * STEPS
BACK_STEPS = 2
BACK_ROWS = STEP * BACK_STEPS
RING = 8
ROUNDS = 2 * RING - 2
NN = (((1,), (0,)), ((), ()))
NT = (((1,), (1,)), ((), ()))
TN = (((0,), (0,)), ((), ()))
f32 = jnp.float32
bf16 = jnp.bfloat16


def mm(a, b, dims=NN):
    return lax.dot_general(a.astype(bf16), b.astype(bf16), dims, preferred_element_type=f32)


def split(a):
    high = a.astype(bf16)
    return high, (a - high.astype(f32)).astype(bf16)


def stack(x):
    return jnp.concatenate([x[:, :HEAD], x[:, HEAD:]], axis=0)


def unstack(x):
    return jnp.concatenate([x[:STEP], x[STEP:]], axis=1)


def pair_masks():
    i = lax.broadcasted_iota(jnp.int32, (2 * STEP, 2 * STEP), 0)
    j = lax.broadcasted_iota(jnp.int32, (2 * STEP, 2 * STEP), 1)
    same = (i // STEP) == (j // STEP)
    cross = ((i % STEP) >= SPAN) & ((j % STEP) < SPAN)
    levels = []
    size = 1
    while size < STEP:
        levels.append(((i // (2 * size)) == (j // (2 * size))) & ((i // size) % 2 == 1) & ((j // size) % 2 == 0))
        size *= 2
    return same & (i > j), same & (i >= j), cross, levels, i == j


def tri_inverses(systems, levels, eye):
    invs = [jnp.where(eye, 1.0, jnp.where(levels[0], -a, 0.0)) for a in systems]
    for level in levels[1:]:
        lows = [inv.astype(bf16) for inv in invs]
        parts = [mm(low, jnp.where(level, a, 0.0)) for low, a in zip(lows, systems)]
        parts = [mm(part, low) for part, low in zip(parts, lows)]
        invs = [inv - part for inv, part in zip(invs, parts)]
    return invs


def row_masks(start_reset, mid_reset):
    r = lax.broadcasted_iota(jnp.int32, (2 * STEP, HEAD), 0) % STEP
    upper = r < SPAN
    enter = jnp.where(upper, 1.0 - start_reset, (1.0 - start_reset) * (1.0 - mid_reset))
    leave = jnp.where(upper, 1.0 - mid_reset, 1.0)
    keep = (1.0 - start_reset) * (1.0 - mid_reset)
    return enter, leave, keep


def resets(flags, step):
    return flags[2 * step], flags[2 * step + 1]


def sigmoid(x):
    return 0.5 * jnp.tanh(0.5 * x) + 0.5


def span_masks(flags, span, count):
    row = lax.broadcasted_iota(jnp.int32, (8, HEAD), 0)
    heads, tails = [], []
    for i in range(count):
        heads.append([None] + [jnp.where(row >= j, 1.0, 1.0 - flags[span + i]) for j in range(1, 4)])
        tails.append([None] + [jnp.where(row + j < 8, 1.0, 1.0 - flags[span + i + 1]) for j in range(1, 4)])
    return heads, tails


def conv_column(buf, conv_ref, heads, cs):
    out = []
    for i in range(len(heads)):
        at = 8 + i * SPAN
        total = buf[at:at + SPAN, cs] * conv_ref[0:1, cs]
        for j in range(1, 4):
            lead = buf[at - j:at - j + 8, cs] * heads[i][j]
            rest = buf[at - j + 8:at - j + SPAN, cs]
            total = total + jnp.concatenate([lead, rest], axis=0) * conv_ref[j:j + 1, cs]
        out.append(total)
    return jnp.concatenate(out, axis=0)


def conv_column_back(buf, dbuf, conv_ref, tails, cs):
    out, grads = [], [0.0] * 4
    for i in range(len(tails)):
        at = i * SPAN
        x = buf[8 + at:8 + at + SPAN, cs]
        for j in range(4):
            if j == 0:
                grad = dbuf[at:at + SPAN, cs]
                total = grad * conv_ref[0:1, cs]
            else:
                most = dbuf[at + j:at + j + SPAN - 8, cs]
                last = dbuf[at + j + SPAN - 8:at + j + SPAN, cs] * tails[i][j]
                grad = jnp.concatenate([most, last], axis=0)
                total = total + grad * conv_ref[j:j + 1, cs]
            grads[j] = grads[j] + jnp.sum((x * grad).reshape(SPAN // 8, 8, HEAD), axis=0)
        out.append(total)
    return jnp.concatenate(out, axis=0), grads


MESH_ID = pl.DeviceIdType.MESH
HALF = 2


def places():
    d = lax.axis_index("dp")
    t = lax.axis_index("tensor")
    beside = t + 1 - 2 * lax.rem(t, 2)
    across = lax.rem(t + 2, 4)
    corner = lax.rem(beside + 2, 4)
    return d, t, beside, across, corner


def push(src, dst, send, recv, device):
    copy = pltpu.make_async_remote_copy(src_ref=src, dst_ref=dst, send_sem=send, recv_sem=recv, device_id=device, device_id_type=MESH_ID)
    copy.start()
    return copy


def greet(devices):
    barrier = pltpu.get_barrier_semaphore()
    for device in devices:
        pl.semaphore_signal(barrier, inc=1, device_id=device, device_id_type=MESH_ID)
    pl.semaphore_wait(barrier, len(devices))


def row_block(owner, part, owner_rows, part_rows):
    return pl.ds(pl.multiple_of(owner * owner_rows + part * part_rows, part_rows), part_rows)


def mixer_fwd_block(g, width, flags, proj_ref, conv_ref, gain_ref, headed_ref, mixed_ref, state_out, res_out, wu_out, inv_out, state, buf):
    buf[8:, :] = proj_ref[:, :width]
    heads, _ = span_masks(flags, g * (ROWS // SPAN), ROWS // SPAN)
    cols = []
    for c in range(width // HEAD):
        total = conv_column(buf, conv_ref, heads, slice(c * HEAD, (c + 1) * HEAD))
        cols.append(total * sigmoid(total))
    buf[0:8, :] = buf[ROWS:ROWS + 8, :]
    betas = sigmoid(proj_ref[:, width:])
    strict, causal, cross, levels, eye = pair_masks()
    todo = []
    for s in range(STEPS):
        rs = slice(s * STEP, (s + 1) * STEP)
        start_reset, mid_reset = resets(flags, g * STEPS + s)
        gate = jnp.where(cross, 1.0 - mid_reset, 1.0)
        two = lambda n: jnp.concatenate([cols[2 * n][rs], cols[2 * n + 1][rs]], axis=0)
        q, k, v = two(0), two(1), two(2)
        q = q * lax.rsqrt(jnp.sum(q * q, axis=-1, keepdims=True) + 1e-6)
        k = k * lax.rsqrt(jnp.sum(k * k, axis=-1, keepdims=True) + 1e-6)
        b = jnp.concatenate([betas[rs, 0:1], betas[rs, 1:2]], axis=0)
        gp = mm(jnp.concatenate([k, q], axis=0), k, NT)
        a = jnp.where(strict, gate * gp[:2 * STEP], 0.0) * b
        p = jnp.where(causal, gate * gp[2 * STEP:], 0.0)
        todo.append((q, k, v, b, a, p, row_masks(start_reset, mid_reset)))
    invs = tri_inverses([x[4] for x in todo], levels, eye)
    wus = [mm(inv, jnp.concatenate([x[3] * x[1], x[3] * x[2]], axis=1)) for inv, x in zip(invs, todo)]
    mem = [state[0], state[1]]
    for s in range(STEPS):
        rs = slice(s * STEP, (s + 1) * STEP)
        q, k, v, b, a, p, (enter, leave, keep) = todo[s]
        wu = wus[s]
        inv_out[s] = invs[s].astype(bf16)
        wu_out[s] = wu.astype(bf16)
        state_out[s, :HEAD] = mem[0].astype(bf16)
        state_out[s, HEAD:] = mem[1].astype(bf16)
        w = wu[:, :HEAD] * enter
        qe = q * enter
        ws, qs = [], []
        for h in range(2):
            hs = slice(h * STEP, (h + 1) * STEP)
            both = mm(jnp.concatenate([w[hs], qe[hs]], axis=0), mem[h])
            ws.append(both[:STEP])
            qs.append(both[STEP:])
        res = wu[:, HEAD:] - jnp.concatenate(ws, axis=0)
        res_out[s] = res.astype(bf16)
        ke = k * leave
        for h in range(2):
            hs = slice(h * STEP, (h + 1) * STEP)
            mem[h] = keep * mem[h] + mm(ke[hs], res[hs], TN)
        o = jnp.concatenate(qs, axis=0) + mm(p, res)
        mixed_ref[rs, :] = unstack(o)
        headed = o * lax.rsqrt(jnp.mean(o * o, axis=-1, keepdims=True) + 1e-5) * gain_ref[...]
        headed_ref[g, rs, :] = unstack(headed).astype(bf16)
    state[0] = mem[0]
    state[1] = mem[1]


def param_views(params, width):
    return params.at[0:1, :], params.at[1:2, :], params.at[2:3, :HEAD], params.at[3:7, :width]


class Gather:
    def __init__(self, full, rows, send, recv):
        self.full, self.rows, self.send, self.recv = full, rows, send, recv
        self.d, self.t, self.beside, self.across, _ = places()
        self.core = lax.rem(self.t, 2)
        self.base = self.t - self.core
        self.far = lax.rem(self.base + 2, 4)

    def block(self, owner, h):
        part = self.rows // 2
        return self.full.at[pl.ds(pl.multiple_of(owner * self.rows + h * part, part), part)]

    def copy(self, owner, h, i, j, peer):
        block = self.block(owner, h)
        return pltpu.make_async_remote_copy(src_ref=block, dst_ref=block, send_sem=self.send.at[i, j], recv_sem=self.recv.at[i, j], device_id=(self.d, peer), device_id_type=MESH_ID)

    def near(self, h):
        return self.copy(self.t, h, 0, h, self.beside)

    def over(self, i):
        return self.copy(self.base + i, self.core, 1, i, self.across)

    def passed(self, i):
        return self.copy(self.far + i, self.core, 2, i, self.beside)

    def start_near(self):
        self.near(0).start()
        self.near(1).start()

    def start_over(self, first=0):
        @pl.when(self.core == first)
        def _():
            self.over(first).start()

        self.near(self.core).wait_recv()

        @pl.when(self.core != first)
        def _():
            self.over(first).start()

        self.over(1 - first).start()

    def fetch_near(self):
        self.near(1 - self.core).wait_recv()

    def fetch_over(self, i):
        self.over(i).wait_recv()
        self.passed(i).start()

    def sent(self):
        for i in range(2):
            self.near(i).wait_send()
            self.over(i).wait_send()
            self.passed(i).wait_send()


def front_kernel(flags, params, tok_hbm, qkv_hbm, beta_hbm, outw_hbm, cot_hbm,
                 proj_ref, mixed_ref, state_out, res_out, wu_out, inv_out, attn_out, headed_out, heads_hbm, out_hbm, cots_hbm,
                 w, beta_w, tok, attn, headed, out_all, cot_all, state, buf, load, store, send_r, recv_r, send_w, recv_w, send_c, recv_c, send_h, recv_h):
    g = pl.program_id(0)
    n = pl.num_programs(0)
    d, t, beside, across, corner = places()
    rows = tok.shape[0]
    width = buf.shape[1]
    heads = 2 * HEAD
    first_gain, _, gain_ref, conv_ref = param_views(params, width)
    rowset = Gather(attn, rows, send_r, recv_r)
    weights = Gather(out_all, outw_hbm.shape[0], send_w, recv_w)
    cots = Gather(cot_all, rows, send_c, recv_c)
    loads = [(tok_hbm, tok)] + [(qkv_hbm.at[i], w.at[:, pl.ds(i * heads, heads)]) for i in range(3)] + [(beta_hbm, beta_w)]
    loads += [(outw_hbm, out_all.at[pl.ds(pl.multiple_of(t * outw_hbm.shape[0], 16), outw_hbm.shape[0])]), (cot_hbm, cot_all.at[pl.ds(pl.multiple_of(t * rows, rows), rows)])]

    def loaded(i):
        return pltpu.make_async_copy(loads[i][0], loads[i][1], load.at[i])

    def attn_stored():
        return pltpu.make_async_copy(attn, attn_out, store.at[0])

    def head_place(owner):
        return heads_hbm.at[:, pl.ds(pl.multiple_of(owner * heads, heads), heads)]

    def kept(i):
        return pltpu.make_async_copy(headed.at[i], headed_out.at[pl.ds(i * rows, rows)], store.at[1 + i])

    def own_heads():
        return pltpu.make_async_copy(headed.at[t], head_place(t), store.at[1 + n_groups])

    def gathered(i):
        return pltpu.make_async_copy((out_all, cot_all)[i], (out_hbm, cots_hbm)[i], store.at[2 + n_groups + i])

    n_groups = headed.shape[0]

    def heads_to(owner, sender):
        return pltpu.make_async_remote_copy(src_ref=headed.at[owner], dst_ref=head_place(sender), send_sem=send_h.at[owner], recv_sem=recv_h.at[sender], device_id=(d, owner), device_id_type=MESH_ID)

    @pl.when(g == 0)
    def _():
        for i in range(len(loads)):
            loaded(i).start()
        greet([(d, beside), (d, across), (d, corner)])
        loaded(0).wait()
        piece = 64
        gain = first_gain[...]

        def chunk(i, carry):
            x = tok[pl.ds(pl.multiple_of(i * piece, piece), piece), :].astype(f32)
            attn[pl.ds(pl.multiple_of(t * rows + i * piece, piece), piece), :] = (x * lax.rsqrt(jnp.mean(x * x, axis=-1, keepdims=True) + 1e-5) * gain).astype(bf16)
            return carry

        lax.fori_loop(0, rows // piece, chunk, 0)
        rowset.start_near()
        rowset.start_over()
        state[...] = jnp.zeros_like(state)
        buf[0:8, :] = jnp.zeros((8, width), f32)
        for i in range(1, len(loads)):
            loaded(i).wait()
        weights.start_near()
        cots.start_near()

    @pl.when(g == beside)
    def _():
        rowset.fetch_near()

    @pl.when(g // 2 != t // 2)
    def _():
        i = lax.rem(g, 2)
        rowset.fetch_over(i)
        rowset.passed(i).wait_recv()

    @pl.when(g == 2 - t // 2)
    def _():
        weights.start_over()
        cots.start_over()

    @pl.when(g == n - 1)
    def _():
        attn_stored().start()

    now = attn[pl.ds(pl.multiple_of(g * rows, rows), rows), :]
    proj_ref[:, :width] = lax.dot_general(now, w[...], NN, preferred_element_type=f32)
    proj_ref[:, width:] = jnp.zeros((rows, HEAD), f32)
    proj_ref[:, width:width + 16] = lax.dot_general(now, beta_w[...], NT, preferred_element_type=f32)
    mixer_fwd_block(g, width, flags, proj_ref, conv_ref, gain_ref, headed, mixed_ref, state_out, res_out, wu_out, inv_out, state, buf)

    @pl.when(g != t)
    def _():
        heads_to(g, t).start()

    @pl.when(g == t)
    def _():
        own_heads().start()

    @pl.when(g == n - 1)
    def _():
        for i in range(n_groups):
            kept(i).start()
        for gather in (weights, cots):
            gather.fetch_near()
            for i in range(2):
                gather.fetch_over(i)
        for gather in (weights, cots):
            for i in range(2):
                gather.passed(i).wait_recv()
        gathered(0).start()
        gathered(1).start()
        for k in range(1, n_groups):
            other = lax.rem(t + k, n_groups)
            heads_to(other, t).wait_send()
            heads_to(other, other).wait_recv()
        for gather in (rowset, weights, cots):
            gather.sent()
        gathered(0).wait()
        gathered(1).wait()
        own_heads().wait()
        attn_stored().wait()
        for i in range(n_groups):
            kept(i).wait()


def front(flags, params, tokens, qkv, beta, out_weight, cot):
    rows, model = tokens.shape
    groups = 4
    total_rows = rows * groups
    width = 3 * qkv.shape[2]
    total = width + HEAD
    steps = total_rows // STEP
    hbm = pl.BlockSpec(memory_space=pl.ANY)
    z2 = lambda g: (0, 0)
    m2 = lambda g: (g, 0)
    m3 = lambda g: (g, 0, 0)
    dma = pltpu.SemaphoreType.DMA
    out = lambda shape, kind: jax.ShapeDtypeStruct(shape, kind)
    heads = 2 * HEAD
    return pl.pallas_call(
        front_kernel,
        grid=(groups,),
        in_specs=[pl.BlockSpec(memory_space=pltpu.SMEM), pl.BlockSpec(params.shape, z2)] + [hbm] * 5,
        out_specs=[pl.BlockSpec((ROWS, total), m2), pl.BlockSpec((ROWS, heads), m2), pl.BlockSpec((STEPS, heads, HEAD), m3), pl.BlockSpec((STEPS, 2 * STEP, HEAD), m3),
                   pl.BlockSpec((STEPS, 2 * STEP, heads), m3), pl.BlockSpec((STEPS, 2 * STEP, 2 * STEP), m3)] + [hbm] * 5,
        out_shape=[out((total_rows, total), f32), out((total_rows, heads), f32), out((steps, heads, HEAD), bf16), out((steps, 2 * STEP, HEAD), bf16),
                   out((steps, 2 * STEP, heads), bf16), out((steps, 2 * STEP, 2 * STEP), bf16), out((total_rows, model), bf16), out((total_rows, heads), bf16),
                   out((rows, model), bf16), out((groups * out_weight.shape[0], model), bf16), out((total_rows, model), bf16)],
        scratch_shapes=[pltpu.VMEM((model, width), bf16), pltpu.VMEM(beta.shape, bf16), pltpu.VMEM((rows, model), bf16), pltpu.VMEM((total_rows, model), bf16), pltpu.VMEM((groups, rows, heads), bf16),
                        pltpu.VMEM((groups * out_weight.shape[0], model), bf16), pltpu.VMEM((total_rows, model), bf16), pltpu.VMEM((2, HEAD, HEAD), f32), pltpu.VMEM((ROWS + 8, width), f32), dma((7,)), dma((4 + groups,))]
        + [dma((3, 2))] * 6 + [dma((groups,))] * 2,
        compiler_params=pltpu.CompilerParams(dimension_semantics=("arbitrary",), collective_id=3, has_side_effects=True, vmem_limit_bytes=56 * 2**20),
    )(flags, params, tokens, qkv, beta, out_weight, cot)


def mlp_kernel(headed_hbm, out_hbm, tok_hbm, params, gu_hbm, down_hbm, cot_hbm,
               dhid_hbm, dattn_hbm, gain_out, gu_out, downg_out, own_hbm, across_hbm,
               headed, out_w, tok, gu_w, down_w, cot, hidden, all_rows, act, d_gate, d_up, mine, keep, to_beside, from_beside, to_across, from_across, to_own, from_own,
               out_own, out_keep, from_beside_out, from_own_out, gu_acc, down_acc, gu_sum, down_sum, dattn, load, store, send, recv):
    d, t, beside, across, corner = places()
    rows = tok.shape[0]
    part = rows // HALF
    units = down_w.shape[0]
    loads = [(headed_hbm, headed), (out_hbm, out_w), (tok_hbm, tok), (gu_hbm, gu_w), (down_hbm, down_w), (cot_hbm, cot)]
    stores = [(mine, dhid_hbm), (dattn, dattn_hbm), (gu_sum, gu_out), (down_sum, downg_out), (out_own, own_hbm), (out_keep, across_hbm)]

    def loaded(i):
        return pltpu.make_async_copy(loads[i][0], loads[i][1], load.at[i])

    def stored(i):
        return pltpu.make_async_copy(stores[i][0], stores[i][1], store.at[i])

    def pushed(src, dst, i, s, peer):
        return pltpu.make_async_remote_copy(src_ref=src, dst_ref=dst, send_sem=send.at[i, s], recv_sem=recv.at[i, s], device_id=(d, peer), device_id_type=MESH_ID)

    def half(ref, s):
        return ref.at[pl.ds(s * part, part)]

    def rows_to(i, s, peer):
        block = all_rows.at[row_block(t, s, rows, part)]
        return pushed(block, block, i, s, peer)

    def passed(s):
        block = all_rows.at[row_block(across, s, rows, part)]
        return pushed(block, block, 2, s, beside)

    def handed(s):
        return pushed(half(to_beside, s), half(from_beside, s), 3, s, beside)

    def summed(s):
        return pushed(half(to_across, s), half(from_across, s), 4, s, across)

    def owned(s):
        return pushed(half(to_own, s), half(from_own, s), 5, s, beside)

    def handed_out(s):
        return pushed(half(headed, s), half(from_beside_out, s), 6, s, beside)

    def owned_out(s):
        return pushed(half(dattn, s), half(from_own_out, s), 7, s, beside)

    for i in range(len(loads)):
        loaded(i).start()
    greet([(d, beside), (d, across)])
    for i in range(3):
        loaded(i).wait()
    gain = params[1:2, :]
    for s in range(HALF):
        at = pl.ds(s * part, part)
        x = tok[at, :].astype(f32) + lax.dot_general(headed[at, :], out_w[...], NN, preferred_element_type=f32)
        hidden[at, :] = x
        all_rows[row_block(t, s, rows, part), :] = (x * lax.rsqrt(jnp.mean(x * x, axis=-1, keepdims=True) + 1e-5) * gain).astype(bf16)
        rows_to(0, s, across).start()
        rows_to(1, s, beside).start()
    for i in range(3, len(loads)):
        loaded(i).wait()

    def work(owner, s):
        at = row_block(owner, s, rows, part)
        x = all_rows[at, :]
        gate = lax.dot_general(x, gu_w[:units, :], NT, preferred_element_type=f32)
        up = lax.dot_general(x, gu_w[units:, :], NT, preferred_element_type=f32)
        sig = sigmoid(gate)
        silu = gate * sig
        low = (silu * up).astype(bf16)
        act[at, :] = low
        d_act = lax.dot_general(cot[at, :], down_w[...], NT, preferred_element_type=f32)
        dg = (d_act * up * sig * (1.0 + gate * (1.0 - sig))).astype(bf16)
        du = (d_act * silu).astype(bf16)
        d_gate[at, :] = dg
        d_up[at, :] = du
        out = lax.dot_general(low, down_w[...], NN, preferred_element_type=f32)
        return lax.dot_general(dg, gu_w[:units, :], NN, preferred_element_type=f32) + lax.dot_general(du, gu_w[units:, :], NN, preferred_element_type=f32), out

    def weight_grads(pair, last):
        at = pl.ds(pl.multiple_of(pair * 2 * rows, 2 * rows), 2 * rows)

        def put(acc, total, where, value):
            if last:
                total[where, :] = (acc[where, :] + value).astype(bf16)
            else:
                acc[where, :] = value

        for c in range(0, units, 256):
            size = min(256, units - c)
            put(gu_acc, gu_sum, pl.ds(c, size), lax.dot_general(d_gate[at, c:c + size], all_rows[at, :], TN, preferred_element_type=f32))
            put(gu_acc, gu_sum, pl.ds(units + c, size), lax.dot_general(d_up[at, c:c + size], all_rows[at, :], TN, preferred_element_type=f32))
            put(down_acc, down_sum, pl.ds(c, size), lax.dot_general(act[at, c:c + size], cot[at, :], TN, preferred_element_type=f32))

    for s in range(HALF):
        at = pl.ds(s * part, part)
        mine[at, :], out = work(t, s)
        out_own[at, :] = hidden[at, :] + out
    for s in range(HALF):
        at = pl.ds(s * part, part)
        rows_to(1, s, beside).wait_recv()
        total, out = work(beside, s)
        to_own[at, :] = total.astype(bf16)
        owned(s).start()
        dattn[at, :] = out.astype(bf16)
        owned_out(s).start()
    for s in range(HALF):
        at = pl.ds(s * part, part)
        rows_to(0, s, across).wait_recv()
        passed(s).start()
        keep[...], out = work(across, s)
        out_keep[at, :] = out.astype(bf16)
        passed(s).wait_recv()
        total, out = work(corner, s)
        to_beside[at, :] = total.astype(bf16)
        handed(s).start()
        headed[at, :] = out.astype(bf16)
        handed_out(s).start()
        handed(s).wait_recv()
        to_across[at, :] = (keep[...] + from_beside[at, :].astype(f32)).astype(bf16)
        summed(s).start()
        if s == 0:
            weight_grads(t // 2, False)
    weight_grads(1 - t // 2, True)
    stored(2).start()
    stored(3).start()
    for s in range(HALF):
        at = pl.ds(s * part, part)
        handed_out(s).wait_recv()
        out_keep[at, :] = (out_keep[at, :].astype(f32) + from_beside_out[at, :].astype(f32)).astype(bf16)
        owned_out(s).wait_recv()
        out_own[at, :] = out_own[at, :] + from_own_out[at, :].astype(f32)
        owned_out(s).wait_send()
    stored(4).start()
    stored(5).start()
    gain_out[...] = jnp.zeros_like(gain_out)
    piece = 64
    for s in range(HALF):
        owned(s).wait_recv()
        summed(s).wait_recv()

        def chunk(i, carry, s=s):
            at = pl.ds(pl.multiple_of(s * part + i * piece, piece), piece)
            grad = mine[at, :] + from_own[at, :].astype(f32) + from_across[at, :].astype(f32)
            x = hidden[at, :]
            r = lax.rsqrt(jnp.mean(x * x, axis=-1, keepdims=True) + 1e-5)
            scaled = gain * grad
            cot_rows = cot[pl.ds(pl.multiple_of(t * rows + s * part + i * piece, piece), piece), :].astype(f32)
            full = cot_rows + r * scaled - x * (r * r * r * jnp.mean(x * scaled, axis=-1, keepdims=True))
            mine[at, :] = full
            dattn[at, :] = full.astype(bf16)
            gain_out[...] += jnp.sum((grad * x * r).reshape(piece // 8, 8, grad.shape[1]), axis=0)
            return carry

        lax.fori_loop(0, part // piece, chunk, 0)
    stored(0).start()
    stored(1).start()
    for s in range(HALF):
        for copy in (rows_to(0, s, across), rows_to(1, s, beside), passed(s), handed(s), summed(s), owned(s), handed_out(s)):
            copy.wait_send()
    for i in range(len(stores)):
        stored(i).wait()


def mlp(headed, out_all, tokens, gain, gate_up, down, cot):
    rows, width = tokens.shape
    total = cot.shape[0]
    units = down.shape[0]
    hbm = pl.BlockSpec(memory_space=pl.ANY)
    vmem = pl.BlockSpec(memory_space=pltpu.VMEM)
    like = lambda x: pltpu.VMEM(x.shape, x.dtype)
    half = lambda: pltpu.VMEM((rows, width), bf16)
    wide = lambda: pltpu.VMEM((rows, width), f32)
    unit = lambda: pltpu.VMEM((total, units), bf16)
    out = lambda shape, kind: jax.ShapeDtypeStruct(shape, kind)
    dma = pltpu.SemaphoreType.DMA
    return pl.pallas_call(
        mlp_kernel,
        in_specs=[hbm] * 3 + [vmem] + [hbm] * 3,
        out_specs=[hbm] * 2 + [vmem] + [hbm] * 4,
        out_shape=[out((rows, width), f32), out((rows, width), bf16), out((8, width), f32), out(gate_up.shape, bf16), out(down.shape, bf16), out((rows, width), f32), out((rows, width), bf16)],
        scratch_shapes=[like(headed), like(out_all), like(tokens), like(gate_up), like(down), like(cot), wide(), pltpu.VMEM((total, width), bf16), unit(), unit(), unit(),
                        wide(), pltpu.VMEM((rows // HALF, width), f32), half(), half(), half(), half(), half(), half(), wide(), half(), half(), half(),
                        pltpu.VMEM(gate_up.shape, f32), pltpu.VMEM(down.shape, f32), like(gate_up), like(down), half(), dma((6,)), dma((6,)), dma((8, HALF)), dma((8, HALF))],
        compiler_params=pltpu.CompilerParams(collective_id=1, has_side_effects=True, vmem_limit_bytes=62 * 2**20),
    )(headed, out_all, tokens, gain, gate_up, down, cot)


def mixer_bwd_block(blk, width, flags, proj_ref, prev_ref, conv_ref, gain_ref, mixed_ref, state_in, res_in, wu_in, inv_in, dheaded, dcat, dstate, buf, dbuf, cacc, gacc):
    buf[0:8, :] = prev_ref[:, :width]
    buf[8:, :] = proj_ref[:, :width]
    heads, tails = span_masks(flags, blk * (BACK_ROWS // SPAN), BACK_ROWS // SPAN)
    cols, slopes = [], []
    for c in range(width // HEAD):
        total = conv_column(buf, conv_ref, heads, slice(c * HEAD, (c + 1) * HEAD))
        sig = sigmoid(total)
        cols.append(total * sig)
        slopes.append(sig * (1.0 + total * (1.0 - sig)))
    betas = sigmoid(proj_ref[:, width:])
    strict, causal, cross, _, _ = pair_masks()
    lane = lax.broadcasted_iota(jnp.int32, (STEP, HEAD), 1)
    order = list(reversed(range(BACK_STEPS)))
    hs = [slice(h * STEP, (h + 1) * STEP) for h in range(2)]
    spans = [slice(s * STEP, (s + 1) * STEP) for s in range(BACK_STEPS)]
    edge = [resets(flags, blk * BACK_STEPS + s) for s in range(BACK_STEPS)]
    enter, leave, keep = zip(*[row_masks(*e) for e in edge])
    gate = [jnp.where(cross, 1.0 - e[1], 1.0) for e in edge]
    both = lambda n: [jnp.concatenate([cols[2 * n][rs], cols[2 * n + 1][rs]], axis=0) for rs in spans]
    q, k, v = both(0), both(1), both(2)
    rq = [lax.rsqrt(jnp.sum(x * x, axis=-1, keepdims=True) + 1e-6) for x in q]
    rk = [lax.rsqrt(jnp.sum(x * x, axis=-1, keepdims=True) + 1e-6) for x in k]
    q = [x * r for x, r in zip(q, rq)]
    k = [x * r for x, r in zip(k, rk)]
    q16 = [x.astype(bf16) for x in q]
    k16 = [x.astype(bf16) for x in k]
    b = [jnp.concatenate([betas[rs, 0:1], betas[rs, 1:2]], axis=0) for rs in spans]
    gp = [mm(jnp.concatenate([x, y], axis=0), x, NT) for x, y in zip(k16, q16)]
    gram = [jnp.where(strict, m * x[:2 * STEP], 0.0) for m, x in zip(gate, gp)]
    p = [jnp.where(causal, m * x[2 * STEP:], 0.0).astype(bf16) for m, x in zip(gate, gp)]
    do = []
    for s in range(BACK_STEPS):
        o = stack(mixed_ref[spans[s], :])
        dh = stack(dheaded[pl.ds(pl.multiple_of(blk * BACK_ROWS + s * STEP, STEP), STEP), :].astype(f32))
        ro = lax.rsqrt(jnp.mean(o * o, axis=-1, keepdims=True) + 1e-5)
        on = o * ro
        gacc[...] += jnp.sum((dh * on).reshape(2 * STEP // 8, 8, HEAD), axis=0)
        dn = dh * gain_ref[...]
        do.append(ro * (dn - on * jnp.mean(dn * on, axis=-1, keepdims=True)))
    do16 = [x.astype(bf16) for x in do]
    doe = [(x * e).astype(bf16) for x, e in zip(do, enter)]
    ke16 = [(x * e).astype(bf16) for x, e in zip(k, leave)]
    we = [(wu_in[s][:, :HEAD].astype(f32) * enter[s]).astype(bf16) for s in range(BACK_STEPS)]
    dres = [mm(x, y, TN) for x, y in zip(p, do16)]
    qdo = [[mm(x[r], y[r], TN) for r in hs] for x, y in zip(q16, doe)]
    dmem = [dstate[0], dstate[1]]
    dres16, after = [None] * BACK_STEPS, [None] * BACK_STEPS
    for s in order:
        low = [m.astype(bf16) for m in dmem]
        after[s] = low
        dres[s] = dres[s] + jnp.concatenate([mm(ke16[s][hs[h]], low[h]) for h in range(2)], axis=0)
        dres16[s] = dres[s].astype(bf16)
        for h in range(2):
            dmem[h] = keep[s] * dmem[h] + qdo[s][h] - mm(we[s][hs[h]], dres16[s][hs[h]], TN)
    dp = [mm(do16[s], res_in[s], NT) for s in order]
    dke = [jnp.concatenate([mm(res_in[s, hs[h]], after[s][h], NT) for h in range(2)], axis=0) for s in order]
    ds = [[mm(jnp.concatenate([do16[s][hs[h]], dres16[s][hs[h]]], axis=0), state_in[s, h * HEAD:(h + 1) * HEAD], NT) for h in range(2)] for s in order]
    dp = [jnp.where(causal, gate[s] * x, 0.0).astype(bf16) for s, x in zip(order, dp)]
    dw = [-enter[s] * jnp.concatenate([x[0][STEP:], x[1][STEP:]], axis=0) for s, x in zip(order, ds)]
    db_kv = [mm(inv_in[s], jnp.concatenate([x, dres[s]], axis=1), TN) for s, x in zip(order, dw)]
    dq = [enter[s] * jnp.concatenate([x[0][:STEP], x[1][:STEP]], axis=0) + mm(y, k16[s]) for s, x, y in zip(order, ds, dp)]
    dk = [mm(y, q16[s], TN) + leave[s] * x for s, x, y in zip(order, dke, dp)]
    da = [-jnp.where(strict, gate[s] * mm(x, wu_in[s], NT), 0.0) for s, x in zip(order, db_kv)]
    dg = [(x * b[s]).astype(bf16) for s, x in zip(order, da)]
    dk = [x + mm(y, k16[s]) + mm(y, k16[s], TN) + b[s] * z[:, :HEAD] for s, x, y, z in zip(order, dk, dg, db_kv)]
    for i, s in enumerate(order):
        rs = spans[s]
        dbeta = jnp.sum(da[i] * gram[s], axis=-1, keepdims=True) + jnp.sum(db_kv[i][:, :HEAD] * k[s] + db_kv[i][:, HEAD:] * v[s], axis=-1, keepdims=True)
        dv = b[s] * db_kv[i][:, HEAD:]
        dqs = rq[s] * (dq[i] - q[s] * jnp.sum(dq[i] * q[s], axis=-1, keepdims=True))
        dks = rk[s] * (dk[i] - k[s] * jnp.sum(dk[i] * k[s], axis=-1, keepdims=True))
        dpre = dbeta * b[s] * (1.0 - b[s])
        for n, x in enumerate((dqs, dks, dv)):
            for h in range(2):
                c = 2 * n + h
                dbuf[rs, c * HEAD:(c + 1) * HEAD] = x[hs[h]] * slopes[c][rs]
        dcat[pl.ds(pl.multiple_of(blk * BACK_ROWS + s * STEP, STEP), STEP), width:] = jnp.where(lane == 0, dpre[:STEP], jnp.where(lane == 1, dpre[STEP:], 0.0)).astype(bf16)
    dstate[0] = dmem[0]
    dstate[1] = dmem[1]
    for c in range(width // HEAD):
        cs = slice(c * HEAD, (c + 1) * HEAD)
        total, grads = conv_column_back(buf, dbuf, conv_ref, tails, cs)
        dcat[pl.ds(pl.multiple_of(blk * BACK_ROWS, BACK_ROWS), BACK_ROWS), cs] = total.astype(bf16)
        for j in range(4):
            cacc[j, :, cs] += grads[j]
    dbuf[BACK_ROWS:, :] = dbuf[0:8, :]


class Ring:
    def __init__(self, here, after, before, sources, results, lands, by_rows, send, recv):
        self.here, self.targets = here, (after, before)
        self.sources, self.results, self.lands, self.by_rows, self.send, self.recv = sources, results, lands, by_rows, send, recv
        self.visited = 0

    def shard(self, way, k):
        return lax.rem(self.here + (k if way else 2 * RING - k), RING)

    def view(self, ref, i, way, k):
        shard = self.shard(way, k)
        rows, cols = ref.shape
        if self.by_rows[i]:
            piece = rows // (2 * RING)
            return ref.at[pl.ds(pl.multiple_of((2 * shard + way) * piece, piece), piece)]
        piece = cols // RING
        return ref.at[pl.ds(way * (rows // 2), rows // 2), pl.ds(pl.multiple_of(shard * piece, piece), piece)]

    def copy(self, i, way, r):
        if r == 0:
            src, dst = self.view(self.sources[i], i, way, 0), self.lands[i].at[way, 0]
        elif r < RING - 1:
            src, dst = self.lands[i].at[way, r - 1], self.lands[i].at[way, r]
        else:
            src = dst = self.view(self.results[i], i, way, r)
        return pltpu.make_async_remote_copy(src_ref=src, dst_ref=dst, send_sem=self.send.at[i, way], recv_sem=self.recv.at[i, way, r], device_id=self.targets[way], device_id_type=MESH_ID)

    def visit(self, count):
        for _ in range(count):
            if self.visited == len(self.sources) * (ROUNDS + 1):
                return
            r, i = divmod(self.visited, len(self.sources))
            self.visited += 1
            for way in range(2):
                if r > 0:
                    last = self.copy(i, way, r - 1)
                    last.wait_send()
                    last.wait_recv()
                if 0 < r < RING:
                    land = self.lands[i].at[way, r - 1]
                    total = (land[...].astype(f32) + self.view(self.sources[i], i, way, r)[...].astype(f32)).astype(bf16)
                    if r < RING - 1:
                        land[...] = total
                    else:
                        done = self.view(self.results[i], i, way, r)
                        done[...] = total
                if r < ROUNDS:
                    self.copy(i, way, r).start()


def ring_place(d):
    base = d // RING * RING
    inner = lax.rem(d, RING)
    line = inner // 2
    here = jnp.where(lax.rem(inner, 2) == 0, line, RING - 1 - line)

    def device(place):
        return base + jnp.where(place < RING // 2, 2 * place, 2 * (RING - 1 - place) + 1)

    return here, device(lax.rem(here + 1, RING)), device(lax.rem(here + RING - 1, RING))


def ring_lands(shapes, by_rows):
    pieces = [(s[0] // (2 * RING), s[1]) if rows else (s[0] // 2, s[1] // RING) for s, rows in zip(shapes, by_rows)]
    return [pltpu.VMEM((2, RING - 1) + p, bf16) for p in pieces]


def back_kernel(n_dp, flags, proj_ref, prev_ref, params, mixed_ref, state_in, res_in, wu_in, inv_in,
                headed_hbm, attn_hbm, dattn_hbm, out_w_hbm, qkv_hbm, beta_hbm, tok_hbm, dhid_hbm, second_grad, gu_hbm, down_hbm, own_hbm, across_hbm,
                dx_hbm, small_out, output_hbm, gu_out, down_out, cat_out, outw_out, landed_hbm,
                headed, attn, dattn_all, out_w, w, beta_w, tok, dhid, gu_src, down_src, cat_src, outw_src,
                gu_res, down_res, cat_res, outw_res, gate_land, up_land, down_land, q_land, k_land, v_land, outw_land,
                dheaded, dcat, dstate, buf, dbuf, cacc, gacc, mine, to_beside, from_beside, to_across, from_across, to_own, from_own,
                group_send, group_land, all_send, all_land, gain_acc, beta_grad,
                load, store, send_m, recv_m, send_c, recv_c, send_r, recv_r, send_x, recv_x, send_g, recv_g, send_a, recv_a, late_sem):
    g = pl.program_id(0)
    n = pl.num_programs(0)
    d, t, beside, across, corner = places()
    here, after, before = ring_place(d)
    rows = tok.shape[0]
    part = rows // HALF
    width = buf.shape[1]
    others = [d // RING * RING + lax.rem(d + k, RING) for k in range(1, RING)]
    first_gain, _, gain_ref, conv_ref = param_views(params, width)
    units = down_src.shape[0]
    gate_up = lambda ref: [ref.at[pl.ds(0, units)], ref.at[pl.ds(units, units)]]
    mlp_ring = Ring(here, (after, t), (before, t), gate_up(gu_src) + [down_src], gate_up(gu_res) + [down_res], [gate_land, up_land, down_land], [False] * 3, send_m, recv_m)
    model = tok.shape[1]
    thirds = lambda ref: [ref.at[pl.ds(i * model, model)] for i in range(3)]
    cat_ring = Ring(here, (after, t), (before, t), thirds(cat_src) + [outw_src], thirds(cat_res) + [outw_res], [q_land, k_land, v_land, outw_land], [True] * 4, send_c, recv_c)
    rowset = Gather(dattn_all, rows, send_r, recv_r)
    loads = [(gu_hbm, gu_src), (down_hbm, down_src), (dattn_hbm, dattn_all.at[pl.ds(pl.multiple_of(t * rows, rows), rows)]), (out_w_hbm, out_w), (headed_hbm, headed), (attn_hbm, attn), (tok_hbm, tok), (dhid_hbm, dhid), (beta_hbm, beta_w)]
    loads += [(qkv_hbm.at[i], w.at[:, pl.ds(i * 2 * HEAD, 2 * HEAD)]) for i in range(3)]
    stores = [(gu_res, gu_out), (down_res, down_out), (mine, dx_hbm), (cat_res, cat_out), (outw_res, outw_out), (to_own, output_hbm)]

    def loaded(i):
        return pltpu.make_async_copy(loads[i][0], loads[i][1], load.at[i])

    def stored(i):
        return pltpu.make_async_copy(stores[i][0], stores[i][1], store.at[i])

    def pushed(src, dst, i, s, peer):
        return pltpu.make_async_remote_copy(src_ref=src, dst_ref=dst, send_sem=send_x.at[i, s], recv_sem=recv_x.at[i, s], device_id=(d, peer), device_id_type=MESH_ID)

    def outward():
        return pushed(across_hbm, landed_hbm, 6, 0, across)

    def block_at(owner, s):
        return row_block(owner, s, rows, part)

    @pl.when(g == 0)
    def _():
        for i in range(len(loads)):
            loaded(i).start()
        greet([(d, beside), (d, across), (d, corner)] + [(o, t) for o in others])
        loaded(2).wait()
        rowset.start_near()
        loaded(0).wait()
        loaded(1).wait()
        mlp_ring.visit(3)
        rowset.start_over(1)
        dstate[...] = jnp.zeros_like(dstate)
        dbuf[BACK_ROWS:, :] = jnp.zeros((8, width), f32)
        cacc[...] = jnp.zeros_like(cacc)
        gacc[...] = jnp.zeros_like(gacc)
        gain_acc[...] = jnp.zeros_like(gain_acc)
        loaded(3).wait()
        mlp_ring.visit(5)

        @pl.when(t < 2)
        def _():
            rowset.fetch_over(1)

        mlp_ring.visit(1)

    owner = n // 2 - 1 - g // 2
    for k in range(1, n):
        @pl.when(g == k)
        def _(k=k):
            if k == 3:
                outward().start()
            mlp_ring.visit(2)

    @pl.when((lax.rem(g, 2) == 1) & (g < n - 1) & ((owner - 1) // 2 != t // 2))
    def _():
        rowset.fetch_over(lax.rem(owner + 1, 2))

    @pl.when(lax.rem(g, 2) == 0)
    def _():
        @pl.when(owner == beside)
        def _():
            rowset.fetch_near()

        @pl.when(owner // 2 != t // 2)
        def _():
            rowset.passed(lax.rem(owner, 2)).wait_recv()

        at = pl.ds(pl.multiple_of(owner * rows, rows), rows)
        dheaded[at, :] = lax.dot_general(dattn_all[at, :], out_w[...], NT, preferred_element_type=f32).astype(bf16)

    blk = n - 1 - g
    mixer_bwd_block(blk, width, flags, proj_ref, prev_ref, conv_ref, gain_ref, mixed_ref, state_in, res_in, wu_in, inv_in, dheaded, dcat, dstate, buf, dbuf, cacc, gacc)

    def work(owner, s):
        at = block_at(owner, s)
        return lax.dot_general(dcat[at, :width], w[...], NT, preferred_element_type=f32) + lax.dot_general(dcat[at, width:width + 16], beta_w[...], NN, preferred_element_type=f32)

    def handed(s):
        at = pl.ds(s * part, part)
        return pushed(to_beside.at[at], from_beside.at[at], 3, s, beside)

    def summed(s):
        at = pl.ds(s * part, part)
        return pushed(to_across.at[at], from_across.at[at], 4, s, across)

    def owned(s):
        at = pl.ds(s * part, part)
        return pushed(to_own.at[at], from_own.at[at], 5, s, beside)

    def grouped(i, peer):
        return pltpu.make_async_remote_copy(src_ref=group_send, dst_ref=group_land.at[i], send_sem=send_g.at[i], recv_sem=recv_g.at[i], device_id=(d, peer), device_id_type=MESH_ID)

    def spread(i, o):
        return pltpu.make_async_remote_copy(src_ref=all_send, dst_ref=all_land.at[i], send_sem=send_a.at[i], recv_sem=recv_a.at[i], device_id=(o, t), device_id_type=MESH_ID)

    piece = 64

    def finish(s):
        gain = first_gain[...]

        def chunk(i, carry):
            at = pl.ds(pl.multiple_of(s * part + i * piece, piece), piece)
            grad = mine[at, :] + from_own[at, :].astype(f32) + from_across[at, :].astype(f32)
            x = tok[at, :].astype(f32)
            r = lax.rsqrt(jnp.mean(x * x, axis=-1, keepdims=True) + 1e-5)
            scaled = gain * grad
            mine[at, :] = dhid[at, :] + r * scaled - x * (r * r * r * jnp.mean(x * scaled, axis=-1, keepdims=True))
            gain_acc[...] += jnp.sum((grad * x * r).reshape(piece // 8, 8, grad.shape[1]), axis=0)
            return carry

        lax.fori_loop(0, part // piece, chunk, 0)

    @pl.when(g == n - 1)
    def _():
        for i in range(4, len(loads)):
            loaded(i).wait()

        def cat_chunk(i):
            grad = lax.dot_general(attn[:, i * 256:(i + 1) * 256], dcat[:, :width], TN, preferred_element_type=f32).astype(bf16)
            for j in range(3):
                cat_src[pl.ds(j * attn.shape[1] + i * 256, 256), :] = grad[:, j * 2 * HEAD:(j + 1) * 2 * HEAD]

        def turn():
            mlp_ring.visit(1)
            cat_ring.visit(4)

        for i in range(attn.shape[1] // 256):
            cat_chunk(i)
            mlp_ring.visit(1)
        outw_src[...] = lax.dot_general(headed[...], dattn_all[...], TN, preferred_element_type=f32).astype(bf16)
        cat_ring.visit(4)
        for s in range(HALF):
            at = pl.ds(s * part, part)
            to_beside[at, :] = work(corner, s).astype(bf16)
            handed(s).start()
            total = work(across, s)
            handed(s).wait_recv()
            to_across[at, :] = (total + from_beside[at, :].astype(f32)).astype(bf16)
            summed(s).start()
            turn()
        beta_grad[...] = lax.dot_general(dcat[:, width:width + 16], attn[...], TN, preferred_element_type=f32)[:8]
        for s in range(HALF):
            at = pl.ds(s * part, part)
            to_own[at, :] = work(beside, s).astype(bf16)
            owned(s).start()
            mine[at, :] = work(t, s)
            turn()
        turn()
        owned(0).wait_recv()
        summed(0).wait_recv()
        finish(0)
        turn()
        turn()
        owned(1).wait_recv()
        summed(1).wait_recv()
        finish(1)
        stored(2).start()
        for i, copy in enumerate((handed, summed, owned)):
            for s in range(HALF):
                copy(s).wait_send()
        outward().wait_recv()
        late = [pltpu.make_async_copy(own_hbm, dhid, late_sem.at[0]), pltpu.make_async_copy(landed_hbm, to_across, late_sem.at[1])]
        for copy in late:
            copy.start()
        turn()
        for copy in late:
            copy.wait()

        def add(i, carry):
            at = pl.ds(pl.multiple_of(i * piece, piece), piece)
            to_own[at, :] = (dhid[at, :] + to_across[at, :].astype(f32)).astype(bf16)
            return carry

        lax.fori_loop(0, rows // piece, add, 0)
        stored(5).start()
        line = lax.broadcasted_iota(jnp.int32, small_out.shape, 0)
        lane = lax.broadcasted_iota(jnp.int32, small_out.shape, 1)
        shared = (line < 2) | ((line == 3) & (lane >= width))
        group_send[...] = jnp.zeros_like(group_send)
        group_send[0:1, :] = jnp.sum(gain_acc[...], axis=0, keepdims=True)
        group_send[1:2, :] = jnp.sum(second_grad[...], axis=0, keepdims=True)
        group_send[2:3, :] = beta_grad[0:1, :]
        group_send[7:8, :] = beta_grad[1:2, :]
        group_send[3:4, width:width + HEAD] = jnp.sum(gacc[...], axis=0, keepdims=True)
        for j in range(4):
            group_send[3 + j:4 + j, :width] = jnp.sum(cacc[j], axis=0, keepdims=True)
        for i, peer in enumerate((beside, across, corner)):
            grouped(i, peer).start()
        turn()
        small = group_send[...]
        for i, peer in enumerate((beside, across, corner)):
            grouped(i, peer).wait_recv()
        both = (small + group_land[0]) + (group_land[1] + group_land[2])
        small = jnp.where(shared, both, small)
        all_send[...] = small
        for i, o in enumerate(others):
            spread(i, o).start()
        turn()
        turn()
        for i, o in enumerate(others):
            spread(i, o).wait_recv()
            small = small + all_land[i]
        small_out[...] = small
        for _ in range(ROUNDS):
            turn()
        for i in range(2):
            stored(i).start()
        for i in range(3, 5):
            stored(i).start()
        rowset.sent()
        for i, peer in enumerate((beside, across, corner)):
            grouped(i, peer).wait_send()
        for i, o in enumerate(others):
            spread(i, o).wait_send()
        outward().wait_send()
        for i in range(len(stores)):
            stored(i).wait()


def backward(n_dp, flags, proj, params, saved, headed, attn_all, d_attn, out_w, qkv, beta, tokens, d_hidden, second_grad, gu_part, down_part, out_own, out_across):
    mixed, states, res, wu, inv = saved
    total_rows, total = proj.shape
    width = 3 * qkv.shape[2]
    rows, model = tokens.shape
    n = total_rows // BACK_ROWS
    m2 = lambda g: (n - 1 - g, 0)
    m3 = lambda g: (n - 1 - g, 0, 0)
    z2 = lambda g: (0, 0)
    hbm = pl.BlockSpec(memory_space=pl.ANY)
    dma = pltpu.SemaphoreType.DMA
    like = lambda x: pltpu.VMEM(x.shape, x.dtype)
    mlp_parts = (gu_part, down_part)
    cat_shapes = [(3 * model, 2 * HEAD), (headed.shape[1], model)]
    half = lambda: pltpu.VMEM((rows, model), bf16)
    line = second_grad.shape
    out = lambda shape, kind: jax.ShapeDtypeStruct(shape, kind)
    return pl.pallas_call(
        functools.partial(back_kernel, n_dp),
        grid=(n,),
        in_specs=[pl.BlockSpec(memory_space=pltpu.SMEM), pl.BlockSpec((BACK_ROWS, total), m2),
                  pl.BlockSpec((8, total), lambda g: (jnp.maximum((n - 1 - g) * (BACK_ROWS // 8) - 1, 0), 0)),
                  pl.BlockSpec(params.shape, z2), pl.BlockSpec((BACK_ROWS, 2 * HEAD), m2),
                  pl.BlockSpec((BACK_STEPS, 2 * HEAD, HEAD), m3), pl.BlockSpec((BACK_STEPS, 2 * STEP, HEAD), m3),
                  pl.BlockSpec((BACK_STEPS, 2 * STEP, 2 * HEAD), m3), pl.BlockSpec((BACK_STEPS, 2 * STEP, 2 * STEP), m3)]
        + [hbm] * 8 + [pl.BlockSpec(line, z2)] + [hbm] * 4,
        out_specs=[hbm, pl.BlockSpec(line, z2)] + [hbm] * 6,
        out_shape=[out((rows, model), f32), out(line, f32), out((rows, model), bf16)] + [out(x.shape, bf16) for x in mlp_parts] + [out(s, bf16) for s in cat_shapes] + [out((rows, model), bf16)],
        scratch_shapes=[like(headed), like(attn_all), like(attn_all), like(out_w), pltpu.VMEM((model, width), bf16), like(beta), like(tokens), like(d_hidden)]
        + [like(x) for x in mlp_parts] + [pltpu.VMEM(s, bf16) for s in cat_shapes]
        + [like(x) for x in mlp_parts] + [pltpu.VMEM(s, bf16) for s in cat_shapes]
        + ring_lands([down_part.shape] * 3, [False] * 3) + ring_lands([(model, 2 * HEAD)] * 3 + cat_shapes[1:], [True] * 4)
        + [pltpu.VMEM((total_rows, 2 * HEAD), bf16), pltpu.VMEM((total_rows, total), bf16), pltpu.VMEM((2, HEAD, HEAD), f32),
           pltpu.VMEM((BACK_ROWS + 8, width), f32), pltpu.VMEM((BACK_ROWS + 8, width), f32), pltpu.VMEM((4, 8, width), f32), pltpu.VMEM((8, HEAD), f32),
           pltpu.VMEM((rows, model), f32), half(), half(), half(), half(), half(), half(),
           pltpu.VMEM(line, f32), pltpu.VMEM((3,) + line, f32), pltpu.VMEM(line, f32), pltpu.VMEM((RING - 1,) + line, f32), pltpu.VMEM((8, model), f32), pltpu.VMEM((8, model), f32),
           dma((13,)), dma((6,)), dma((3, 2)), dma((3, 2, ROUNDS)), dma((4, 2)), dma((4, 2, ROUNDS)), dma((3, 2)), dma((3, 2)), dma((7, HALF)), dma((7, HALF)),
           dma((3,)), dma((3,)), dma((RING - 1,)), dma((RING - 1,)), dma((2,))],
        compiler_params=pltpu.CompilerParams(dimension_semantics=("arbitrary",), collective_id=2, has_side_effects=True, vmem_limit_bytes=62 * 2**20),
    )(flags, proj, proj, params, mixed, states, res, wu, inv, headed, attn_all, d_attn, out_w, qkv, beta, tokens, d_hidden, second_grad, gu_part, down_part, out_own, out_across)


def on_device(tokens, lengths, attn_gain, qkv_weight, beta_weight, conv_weight, head_gain, out_weight, mlp_gain, gate_up_weight, down_weight, cotangent):
    model_width = tokens.shape[1]
    width = qkv_weight.shape[1] * qkv_weight.shape[2]
    heads = beta_weight.shape[1]
    group_rows = tokens.shape[0] * lax.axis_size("tensor")
    starts = jnp.arange(group_rows // SPAN + 8, dtype=jnp.int32) * SPAN
    flags = jnp.where((starts == 0) | (starts == lengths[0, 0]), 1.0, 0.0).astype(f32)
    qkv = jnp.transpose(qkv_weight, (1, 0, 2))
    beta = jnp.pad(beta_weight.T, ((0, 16 - heads), (0, 0)))
    lines = [attn_gain[None], mlp_gain[None], jnp.pad(head_gain, (0, model_width - HEAD))[None]]
    taps = jnp.concatenate([conv_weight[:, i] for i in range(3)], axis=1)
    lines += [jnp.pad(taps, ((0, 1), (0, model_width - width)))]
    params = jnp.concatenate(lines, axis=0).astype(f32)
    gate_up = jnp.transpose(gate_up_weight, (1, 2, 0)).reshape(-1, model_width)
    proj, mixed, states, res, wu, inv, attn_all, headed, headed_rows, out_all, cot_all = front(
        flags, params, tokens, qkv, beta, out_weight, cotangent)
    saved = (mixed, states, res, wu, inv)
    d_hidden, d_attn, second_grad, gu_part, down_part, out_own, out_across = mlp(headed_rows, out_all, tokens, params, gate_up, down_weight, cot_all)
    n_dp = lax.axis_size("dp")
    input_grad, small, output, *sums, _ = backward(
        n_dp, flags, proj, params, saved, headed, attn_all, d_attn, out_weight, qkv, beta, tokens, d_hidden, second_grad, gu_part, down_part, out_own, out_across)
    if n_dp > RING:
        groups = [list(range(i, n_dp, RING)) for i in range(RING)]
        small, *sums = lax.psum((small, *sums), "dp", axis_index_groups=groups)
    gu_sum, down_sum, cat_sum, out_sum = sums
    return (
        output,
        input_grad,
        small[0],
        jnp.transpose(cat_sum.astype(f32).reshape(3, model_width, -1), (1, 0, 2)),
        jnp.stack([small[2], small[7]], axis=1),
        small[3:7, :width].reshape(conv_weight.shape),
        small[3, width:width + HEAD],
        out_sum.astype(f32),
        small[1],
        jnp.transpose(gu_sum.astype(f32).reshape(2, -1, model_width), (2, 0, 1)),
        down_sum.astype(f32),
    )


def solution(mesh):
    rows = P(("dp", "tensor"), None)
    last = P(None, None, "tensor")
    return jax.shard_map(
        on_device,
        mesh=mesh,
        in_specs=(rows, P("dp", None), P(), last, P(None, "tensor"), last, P(), P("tensor", None), P(), last, P("tensor", None), rows),
        out_specs=(rows, rows, P(), last, P(None, "tensor"), last, P(), P("tensor", None), P(), last, P("tensor", None)),
        check_vma=False,
    )
```

```python
import functools
import jax
import jax.numpy as jnp
from jax import lax
from jax.experimental import pallas as pl
from jax.experimental.pallas import tpu as pltpu
from jax.sharding import PartitionSpec as P

HEAD = 128
STEP = 128
SPAN = 64
STEPS = 4
ROWS = STEP * STEPS
BACK_STEPS = 2
BACK_ROWS = STEP * BACK_STEPS
RING = 8
ROUNDS = 2 * RING - 2
NN = (((1,), (0,)), ((), ()))
NT = (((1,), (1,)), ((), ()))
TN = (((0,), (0,)), ((), ()))
f32 = jnp.float32
bf16 = jnp.bfloat16


def mm(a, b, dims=NN):
    return lax.dot_general(a.astype(bf16), b.astype(bf16), dims, preferred_element_type=f32)


def split(a):
    high = a.astype(bf16)
    return high, (a - high.astype(f32)).astype(bf16)


def stack(x):
    return jnp.concatenate([x[:, :HEAD], x[:, HEAD:]], axis=0)


def unstack(x):
    return jnp.concatenate([x[:STEP], x[STEP:]], axis=1)


def pair_masks():
    i = lax.broadcasted_iota(jnp.int32, (2 * STEP, 2 * STEP), 0)
    j = lax.broadcasted_iota(jnp.int32, (2 * STEP, 2 * STEP), 1)
    same = (i // STEP) == (j // STEP)
    cross = ((i % STEP) >= SPAN) & ((j % STEP) < SPAN)
    levels = []
    size = 1
    while size < STEP:
        levels.append(((i // (2 * size)) == (j // (2 * size))) & ((i // size) % 2 == 1) & ((j // size) % 2 == 0))
        size *= 2
    return same & (i > j), same & (i >= j), cross, levels, i == j


def tri_inverses(systems, levels, eye):
    invs = [jnp.where(eye, 1.0, jnp.where(levels[0], -a, 0.0)) for a in systems]
    for level in levels[1:]:
        lows = [inv.astype(bf16) for inv in invs]
        parts = [mm(low, jnp.where(level, a, 0.0)) for low, a in zip(lows, systems)]
        parts = [mm(part, low) for part, low in zip(parts, lows)]
        invs = [inv - part for inv, part in zip(invs, parts)]
    return invs


def row_masks(start_reset, mid_reset):
    r = lax.broadcasted_iota(jnp.int32, (2 * STEP, HEAD), 0) % STEP
    upper = r < SPAN
    enter = jnp.where(upper, 1.0 - start_reset, (1.0 - start_reset) * (1.0 - mid_reset))
    leave = jnp.where(upper, 1.0 - mid_reset, 1.0)
    keep = (1.0 - start_reset) * (1.0 - mid_reset)
    return enter, leave, keep


def starts(lengths, span):
    return jnp.where((span == 0) | (span * SPAN == lengths[0, 0]), 1.0, 0.0).astype(f32)


def resets(lengths, step):
    return starts(lengths, 2 * step), starts(lengths, 2 * step + 1)


def sigmoid(x):
    return 0.5 * jnp.tanh(0.5 * x) + 0.5


def span_masks(flags, span, count):
    row = lax.broadcasted_iota(jnp.int32, (8, HEAD), 0)
    heads, tails = [], []
    for i in range(count):
        heads.append([None] + [jnp.where(row >= j, 1.0, 1.0 - starts(flags, span + i)) for j in range(1, 4)])
        tails.append([None] + [jnp.where(row + j < 8, 1.0, 1.0 - starts(flags, span + i + 1)) for j in range(1, 4)])
    return heads, tails


def conv_column(buf, conv_ref, heads, cs):
    out = []
    for i in range(len(heads)):
        at = 8 + i * SPAN
        total = buf[at:at + SPAN, cs] * conv_ref[0:1, cs]
        for j in range(1, 4):
            lead = buf[at - j:at - j + 8, cs] * heads[i][j]
            rest = buf[at - j + 8:at - j + SPAN, cs]
            total = total + jnp.concatenate([lead, rest], axis=0) * conv_ref[j:j + 1, cs]
        out.append(total)
    return jnp.concatenate(out, axis=0)


def conv_column_back(buf, dbuf, conv_ref, tails, cs):
    out, grads = [], [0.0] * 4
    for i in range(len(tails)):
        at = i * SPAN
        x = buf[8 + at:8 + at + SPAN, cs]
        for j in range(4):
            if j == 0:
                grad = dbuf[at:at + SPAN, cs]
                total = grad * conv_ref[0:1, cs]
            else:
                most = dbuf[at + j:at + j + SPAN - 8, cs]
                last = dbuf[at + j + SPAN - 8:at + j + SPAN, cs] * tails[i][j]
                grad = jnp.concatenate([most, last], axis=0)
                total = total + grad * conv_ref[j:j + 1, cs]
            grads[j] = grads[j] + jnp.sum((x * grad).reshape(SPAN // 8, 8, HEAD), axis=0)
        out.append(total)
    return jnp.concatenate(out, axis=0), grads


MESH_ID = pl.DeviceIdType.MESH
HALF = 2


def places():
    d = lax.axis_index("dp")
    t = lax.axis_index("tensor")
    beside = t + 1 - 2 * lax.rem(t, 2)
    across = lax.rem(t + 2, 4)
    corner = lax.rem(beside + 2, 4)
    return d, t, beside, across, corner


def push(src, dst, send, recv, device):
    copy = pltpu.make_async_remote_copy(src_ref=src, dst_ref=dst, send_sem=send, recv_sem=recv, device_id=device, device_id_type=MESH_ID)
    copy.start()
    return copy


def greet(devices):
    barrier = pltpu.get_barrier_semaphore()
    for device in devices:
        pl.semaphore_signal(barrier, inc=1, device_id=device, device_id_type=MESH_ID)
    pl.semaphore_wait(barrier, len(devices))


def row_block(owner, part, owner_rows, part_rows):
    return pl.ds(pl.multiple_of(owner * owner_rows + part * part_rows, part_rows), part_rows)


def mixer_fwd_block(g, width, flags, proj_ref, conv_ref, gain_ref, headed_ref, mixed_ref, state_out, res_out, wu_out, inv_out, state, buf):
    buf[8:, :] = proj_ref[:, :width]
    heads, _ = span_masks(flags, g * (ROWS // SPAN), ROWS // SPAN)
    cols = []
    for c in range(width // HEAD):
        total = conv_column(buf, conv_ref, heads, slice(c * HEAD, (c + 1) * HEAD))
        cols.append(total * sigmoid(total))
    buf[0:8, :] = buf[ROWS:ROWS + 8, :]
    betas = sigmoid(proj_ref[:, width:])
    strict, causal, cross, levels, eye = pair_masks()
    todo = []
    for s in range(STEPS):
        rs = slice(s * STEP, (s + 1) * STEP)
        start_reset, mid_reset = resets(flags, g * STEPS + s)
        gate = jnp.where(cross, 1.0 - mid_reset, 1.0)
        two = lambda n: jnp.concatenate([cols[2 * n][rs], cols[2 * n + 1][rs]], axis=0)
        q, k, v = two(0), two(1), two(2)
        q = q * lax.rsqrt(jnp.sum(q * q, axis=-1, keepdims=True) + 1e-6)
        k = k * lax.rsqrt(jnp.sum(k * k, axis=-1, keepdims=True) + 1e-6)
        b = jnp.concatenate([betas[rs, 0:1], betas[rs, 1:2]], axis=0)
        gp = mm(jnp.concatenate([k, q], axis=0), k, NT)
        a = jnp.where(strict, gate * gp[:2 * STEP], 0.0) * b
        p = jnp.where(causal, gate * gp[2 * STEP:], 0.0)
        todo.append((q, k, v, b, a, p, row_masks(start_reset, mid_reset)))
    invs = tri_inverses([x[4] for x in todo], levels, eye)
    wus = [mm(inv, jnp.concatenate([x[3] * x[1], x[3] * x[2]], axis=1)) for inv, x in zip(invs, todo)]
    mem = [state[0], state[1]]
    for s in range(STEPS):
        rs = slice(s * STEP, (s + 1) * STEP)
        q, k, v, b, a, p, (enter, leave, keep) = todo[s]
        wu = wus[s]
        inv_out[s] = invs[s].astype(bf16)
        wu_out[s] = wu.astype(bf16)
        state_out[s, :HEAD] = mem[0].astype(bf16)
        state_out[s, HEAD:] = mem[1].astype(bf16)
        w = wu[:, :HEAD] * enter
        qe = q * enter
        ws, qs = [], []
        for h in range(2):
            hs = slice(h * STEP, (h + 1) * STEP)
            both = mm(jnp.concatenate([w[hs], qe[hs]], axis=0), mem[h])
            ws.append(both[:STEP])
            qs.append(both[STEP:])
        res = wu[:, HEAD:] - jnp.concatenate(ws, axis=0)
        res_out[s] = res.astype(bf16)
        ke = k * leave
        for h in range(2):
            hs = slice(h * STEP, (h + 1) * STEP)
            mem[h] = keep * mem[h] + mm(ke[hs], res[hs], TN)
        o = jnp.concatenate(qs, axis=0) + mm(p, res)
        mixed_ref[rs, :] = unstack(o)
        headed = o * lax.rsqrt(jnp.mean(o * o, axis=-1, keepdims=True) + 1e-5) * gain_ref[...]
        headed_ref[g, rs, :] = unstack(headed).astype(bf16)
    state[0] = mem[0]
    state[1] = mem[1]


def param_views(params, width):
    return params.at[0:1, :], params.at[1:2, :], params.at[2:3, :HEAD], params.at[3:7, :width]


class Gather:
    def __init__(self, full, rows, send, recv):
        self.full, self.rows, self.send, self.recv = full, rows, send, recv
        self.d, self.t, self.beside, self.across, _ = places()
        self.core = lax.rem(self.t, 2)
        self.base = self.t - self.core
        self.far = lax.rem(self.base + 2, 4)

    def block(self, owner, h):
        part = self.rows // 2
        return self.full.at[pl.ds(pl.multiple_of(owner * self.rows + h * part, part), part)]

    def copy(self, owner, h, i, j, peer):
        block = self.block(owner, h)
        return pltpu.make_async_remote_copy(src_ref=block, dst_ref=block, send_sem=self.send.at[i, j], recv_sem=self.recv.at[i, j], device_id=(self.d, peer), device_id_type=MESH_ID)

    def near(self, h):
        return self.copy(self.t, h, 0, h, self.beside)

    def over(self, i):
        return self.copy(self.base + i, self.core, 1, i, self.across)

    def passed(self, i):
        return self.copy(self.far + i, self.core, 2, i, self.beside)

    def start_near(self):
        self.near(0).start()
        self.near(1).start()

    def start_over(self, first=0):
        @pl.when(self.core == first)
        def _():
            self.over(first).start()

        self.near(self.core).wait_recv()

        @pl.when(self.core != first)
        def _():
            self.over(first).start()

        self.over(1 - first).start()

    def fetch_near(self):
        self.near(1 - self.core).wait_recv()

    def fetch_over(self, i):
        self.over(i).wait_recv()
        self.passed(i).start()

    def sent(self):
        for i in range(2):
            self.near(i).wait_send()
            self.over(i).wait_send()
            self.passed(i).wait_send()


def front_kernel(flags, attn_gain, mlp_gain, head_gain, taps, beta_ref, tok_hbm, qkv_hbm, outw_hbm, cot_hbm,
                 params, beta_w, proj_ref, mixed_ref, state_out, res_out, wu_out, inv_out, attn_out, headed_out, heads_hbm, out_hbm, cots_hbm,
                 w, tok, attn, headed, out_all, cot_all, state, buf, load, store, send_r, recv_r, send_w, recv_w, send_c, recv_c, send_h, recv_h, send_s, recv_s):
    g = pl.program_id(0)
    n = pl.num_programs(0)
    d, t, beside, across, corner = places()
    rows = tok.shape[0]
    width = buf.shape[1]
    heads = 2 * HEAD
    first_gain, _, gain_ref, conv_ref = param_views(params, width)
    rowset = Gather(attn, rows, send_r, recv_r)
    weights = Gather(out_all, outw_hbm.shape[0], send_w, recv_w)
    cots = Gather(cot_all, rows, send_c, recv_c)
    loads = [(tok_hbm, tok)] + [(qkv_hbm.at[i], w.at[:, pl.ds(i * heads, heads)]) for i in range(3)]
    loads += [(outw_hbm, out_all.at[pl.ds(pl.multiple_of(t * outw_hbm.shape[0], 16), outw_hbm.shape[0])]), (cot_hbm, cot_all.at[pl.ds(pl.multiple_of(t * rows, rows), rows)])]

    def loaded(i):
        return pltpu.make_async_copy(loads[i][0], loads[i][1], load.at[i])

    def attn_stored():
        return pltpu.make_async_copy(attn, attn_out, store.at[0])

    def head_place(owner):
        return heads_hbm.at[:, pl.ds(pl.multiple_of(owner * heads, heads), heads)]

    def kept(i):
        return pltpu.make_async_copy(headed.at[i], headed_out.at[pl.ds(i * rows, rows)], store.at[1 + i])

    def own_heads():
        return pltpu.make_async_copy(headed.at[t], head_place(t), store.at[1 + n_groups])

    def gathered(i):
        return pltpu.make_async_copy((out_all, cot_all)[i], (out_hbm, cots_hbm)[i], store.at[2 + n_groups + i])

    n_groups = headed.shape[0]

    partners = [d + size - 2 * size * lax.rem(d // size, 2) for size in (1, 2, 4)]
    slot = lax.rem(d, RING)
    cut = outw_hbm.shape[0] // (2 * RING)

    def slice_of(owner, size=1):
        return out_all.at[pl.ds(pl.multiple_of(owner * outw_hbm.shape[0] + (weights.core * RING + slot // size * size) * cut, cut), size * cut)]

    def slice_over(i):
        ref = slice_of(weights.base + i)
        return pltpu.make_async_remote_copy(src_ref=ref, dst_ref=ref, send_sem=send_w.at[1, i], recv_sem=recv_w.at[1, i], device_id=(d, across), device_id_type=MESH_ID)

    def slice_spread(i, k):
        ref = slice_of(weights.far + i, 2 ** k)
        return pltpu.make_async_remote_copy(src_ref=ref, dst_ref=ref, send_sem=send_s.at[i, k], recv_sem=recv_s.at[i, k], device_id=(partners[k], t), device_id_type=MESH_ID)

    def heads_to(owner, sender):
        return pltpu.make_async_remote_copy(src_ref=headed.at[owner], dst_ref=head_place(sender), send_sem=send_h.at[owner], recv_sem=recv_h.at[sender], device_id=(d, owner), device_id_type=MESH_ID)

    @pl.when(g == 0)
    def _():
        for i in range(len(loads)):
            loaded(i).start()
        greet([(d, beside), (d, across), (d, corner)] + [(o, t) for o in partners])
        model = tok.shape[1]
        params[...] = jnp.zeros_like(params)
        params[0:1, :] = attn_gain[...].astype(f32).reshape(1, model)
        params[1:2, :] = mlp_gain[...].astype(f32).reshape(1, model)
        params[2:3, :HEAD] = head_gain[...].astype(f32).reshape(1, HEAD)
        for i in range(3):
            params[3:7, i * heads:(i + 1) * heads] = taps[i].astype(f32)
        beta_w[...] = jnp.concatenate([beta_ref[...].astype(f32), jnp.zeros((14, model), f32)], axis=0).astype(bf16)
        loaded(0).wait()
        piece = 64
        gain = first_gain[...]

        def chunk(i, carry):
            x = tok[pl.ds(pl.multiple_of(i * piece, piece), piece), :].astype(f32)
            attn[pl.ds(pl.multiple_of(t * rows + i * piece, piece), piece), :] = (x * lax.rsqrt(jnp.mean(x * x, axis=-1, keepdims=True) + 1e-5) * gain).astype(bf16)
            return carry

        lax.fori_loop(0, rows // piece, chunk, 0)
        rowset.start_near()
        loaded(4).wait()
        weights.start_near()
        rowset.start_over()
        weights.near(weights.core).wait_recv()
        for i in range(2):
            slice_over(i).start()
        state[...] = jnp.zeros_like(state)
        buf[0:8, :] = jnp.zeros((8, width), f32)
        for i in (1, 2, 3, 5):
            loaded(i).wait()
        cots.start_near()

    @pl.when(g == beside)
    def _():
        rowset.fetch_near()

    @pl.when(g // 2 != t // 2)
    def _():
        i = lax.rem(g, 2)
        rowset.fetch_over(i)
        rowset.passed(i).wait_recv()

    @pl.when(g == 2 - t // 2)
    def _():
        cots.start_over()

    for k in range(2):
        @pl.when(g == k + 2)
        def _(k=k):
            for i in range(2):
                if k == 0:
                    slice_over(i).wait_recv()
                else:
                    slice_spread(i, k - 1).wait_recv()
                slice_spread(i, k).start()

    @pl.when(g == n - 1)
    def _():
        attn_stored().start()

    now = attn[pl.ds(pl.multiple_of(g * rows, rows), rows), :]
    proj_ref[:, :width] = lax.dot_general(now, w[...], NN, preferred_element_type=f32)
    proj_ref[:, width:] = jnp.zeros((rows, HEAD), f32)
    proj_ref[:, width:width + 16] = lax.dot_general(now, beta_w[...], NT, preferred_element_type=f32)
    mixer_fwd_block(g, width, flags, proj_ref, conv_ref, gain_ref, headed, mixed_ref, state_out, res_out, wu_out, inv_out, state, buf)

    @pl.when(g != t)
    def _():
        heads_to(g, t).start()

    @pl.when(g == t)
    def _():
        own_heads().start()

    @pl.when(g == n - 1)
    def _():
        for i in range(n_groups):
            kept(i).start()
        weights.fetch_near()
        for i in range(2):
            slice_spread(i, 1).wait_recv()
            slice_spread(i, 2).start()
        cots.fetch_near()
        cots.fetch_over(0)
        for i in range(2):
            slice_spread(i, 2).wait_recv()
            weights.passed(i).start()
        cots.fetch_over(1)
        for gather in (weights, cots):
            for i in range(2):
                gather.passed(i).wait_recv()
        gathered(0).start()
        gathered(1).start()
        for k in range(1, n_groups):
            other = lax.rem(t + k, n_groups)
            heads_to(other, t).wait_send()
            heads_to(other, other).wait_recv()
        for i in range(2):
            weights.near(i).wait_send()
            weights.passed(i).wait_send()
            slice_over(i).wait_send()
            for k in range(3):
                slice_spread(i, k).wait_send()
        for gather in (rowset, cots):
            gather.sent()
        gathered(0).wait()
        gathered(1).wait()
        own_heads().wait()
        attn_stored().wait()
        for i in range(n_groups):
            kept(i).wait()


def front(lengths, attn_gain, mlp_gain, head_gain, taps, beta, tokens, qkv, out_weight, cot):
    rows, model = tokens.shape
    groups = 4
    total_rows = rows * groups
    width = 3 * qkv.shape[2]
    total = width + HEAD
    steps = total_rows // STEP
    hbm = pl.BlockSpec(memory_space=pl.ANY)
    z2 = lambda g: (0, 0)
    m2 = lambda g: (g, 0)
    m3 = lambda g: (g, 0, 0)
    dma = pltpu.SemaphoreType.DMA
    out = lambda shape, kind: jax.ShapeDtypeStruct(shape, kind)
    heads = 2 * HEAD
    return pl.pallas_call(
        front_kernel,
        grid=(groups,),
        in_specs=[pl.BlockSpec(memory_space=pltpu.SMEM)] + [pl.BlockSpec(memory_space=pltpu.VMEM)] * 5 + [hbm] * 4,
        out_specs=[pl.BlockSpec((8, model), z2), pl.BlockSpec((16, model), z2), pl.BlockSpec((ROWS, total), m2), pl.BlockSpec((ROWS, heads), m2), pl.BlockSpec((STEPS, heads, HEAD), m3), pl.BlockSpec((STEPS, 2 * STEP, HEAD), m3),
                   pl.BlockSpec((STEPS, 2 * STEP, heads), m3), pl.BlockSpec((STEPS, 2 * STEP, 2 * STEP), m3)] + [hbm] * 5,
        out_shape=[out((8, model), f32), out((16, model), bf16), out((total_rows, total), f32), out((total_rows, heads), f32), out((steps, heads, HEAD), bf16), out((steps, 2 * STEP, HEAD), bf16),
                   out((steps, 2 * STEP, heads), bf16), out((steps, 2 * STEP, 2 * STEP), bf16), out((total_rows, model), bf16), out((total_rows, heads), bf16),
                   out((rows, model), bf16), out((groups * out_weight.shape[0], model), bf16), out((total_rows, model), bf16)],
        scratch_shapes=[pltpu.VMEM((model, width), bf16), pltpu.VMEM((rows, model), bf16), pltpu.VMEM((total_rows, model), bf16), pltpu.VMEM((groups, rows, heads), bf16),
                        pltpu.VMEM((groups * out_weight.shape[0], model), bf16), pltpu.VMEM((total_rows, model), bf16), pltpu.VMEM((2, HEAD, HEAD), f32), pltpu.VMEM((ROWS + 8, width), f32), dma((6,)), dma((4 + groups,))]
        + [dma((3, 2))] * 6 + [dma((groups,))] * 2 + [dma((2, 3))] * 2,
        compiler_params=pltpu.CompilerParams(dimension_semantics=("arbitrary",), collective_id=3, has_side_effects=True, vmem_limit_bytes=56 * 2**20),
    )(lengths, attn_gain, mlp_gain, head_gain, taps, beta, tokens, qkv, out_weight, cot)


def mlp_kernel(headed_hbm, out_hbm, tok_hbm, params, gu_hbm, down_hbm, cot_hbm,
               dhid_hbm, dattn_hbm, gain_out, gu_out, downg_out, own_hbm, across_hbm,
               headed, out_w, tok, gu_w, down_w, cot, hidden, all_rows, act, d_gate, d_up, mine, keep, to_beside, from_beside, to_across, from_across, to_own, from_own,
               out_own, out_keep, from_beside_out, from_own_out, gu_acc, down_acc, gu_sum, down_sum, dattn, load, store, send, recv):
    d, t, beside, across, corner = places()
    rows = tok.shape[0]
    part = rows // HALF
    units = down_w.shape[0]
    loads = [(headed_hbm, headed), (out_hbm, out_w), (tok_hbm, tok), (gu_hbm, gu_w), (down_hbm, down_w), (cot_hbm, cot)]
    stores = [(mine, dhid_hbm), (dattn, dattn_hbm), (gu_sum, gu_out), (down_sum, downg_out), (out_own, own_hbm), (out_keep, across_hbm)]

    def loaded(i):
        return pltpu.make_async_copy(loads[i][0], loads[i][1], load.at[i])

    def stored(i):
        return pltpu.make_async_copy(stores[i][0], stores[i][1], store.at[i])

    def pushed(src, dst, i, s, peer):
        return pltpu.make_async_remote_copy(src_ref=src, dst_ref=dst, send_sem=send.at[i, s], recv_sem=recv.at[i, s], device_id=(d, peer), device_id_type=MESH_ID)

    def half(ref, s):
        return ref.at[pl.ds(s * part, part)]

    def rows_to(i, s, peer):
        block = all_rows.at[row_block(t, s, rows, part)]
        return pushed(block, block, i, s, peer)

    def passed(s):
        block = all_rows.at[row_block(across, s, rows, part)]
        return pushed(block, block, 2, s, beside)

    def handed(s):
        return pushed(half(to_beside, s), half(from_beside, s), 3, s, beside)

    def summed(s):
        return pushed(half(to_across, s), half(from_across, s), 4, s, across)

    def owned(s):
        return pushed(half(to_own, s), half(from_own, s), 5, s, beside)

    def handed_out(s):
        return pushed(half(headed, s), half(from_beside_out, s), 6, s, beside)

    def owned_out(s):
        return pushed(half(dattn, s), half(from_own_out, s), 7, s, beside)

    for i in range(len(loads)):
        loaded(i).start()
    greet([(d, beside), (d, across)])
    for i in range(3):
        loaded(i).wait()
    gain = params[1:2, :]
    for s in range(HALF):
        at = pl.ds(s * part, part)
        x = tok[at, :].astype(f32) + lax.dot_general(headed[at, :], out_w[...], NN, preferred_element_type=f32)
        hidden[at, :] = x
        all_rows[row_block(t, s, rows, part), :] = (x * lax.rsqrt(jnp.mean(x * x, axis=-1, keepdims=True) + 1e-5) * gain).astype(bf16)
        rows_to(0, s, across).start()
        rows_to(1, s, beside).start()
    for i in range(3, len(loads)):
        loaded(i).wait()

    def work(owner, s):
        at = row_block(owner, s, rows, part)
        x = all_rows[at, :]
        gate = lax.dot_general(x, gu_w[:units, :], NT, preferred_element_type=f32)
        up = lax.dot_general(x, gu_w[units:, :], NT, preferred_element_type=f32)
        sig = sigmoid(gate)
        silu = gate * sig
        low = (silu * up).astype(bf16)
        act[at, :] = low
        d_act = lax.dot_general(cot[at, :], down_w[...], NT, preferred_element_type=f32)
        dg = (d_act * up * sig * (1.0 + gate * (1.0 - sig))).astype(bf16)
        du = (d_act * silu).astype(bf16)
        d_gate[at, :] = dg
        d_up[at, :] = du
        out = lax.dot_general(low, down_w[...], NN, preferred_element_type=f32)
        return lax.dot_general(dg, gu_w[:units, :], NN, preferred_element_type=f32) + lax.dot_general(du, gu_w[units:, :], NN, preferred_element_type=f32), out

    def weight_grads(pair, last):
        at = pl.ds(pl.multiple_of(pair * 2 * rows, 2 * rows), 2 * rows)

        def put(acc, total, where, value):
            if last:
                total[where, :] = (acc[where, :] + value).astype(bf16)
            else:
                acc[where, :] = value

        for c in range(0, units, 256):
            size = min(256, units - c)
            put(gu_acc, gu_sum, pl.ds(c, size), lax.dot_general(d_gate[at, c:c + size], all_rows[at, :], TN, preferred_element_type=f32))
            put(gu_acc, gu_sum, pl.ds(units + c, size), lax.dot_general(d_up[at, c:c + size], all_rows[at, :], TN, preferred_element_type=f32))
            put(down_acc, down_sum, pl.ds(c, size), lax.dot_general(act[at, c:c + size], cot[at, :], TN, preferred_element_type=f32))

    for s in range(HALF):
        at = pl.ds(s * part, part)
        mine[at, :], out = work(t, s)
        out_own[at, :] = hidden[at, :] + out
    for s in range(HALF):
        at = pl.ds(s * part, part)
        rows_to(1, s, beside).wait_recv()
        total, out = work(beside, s)
        to_own[at, :] = total.astype(bf16)
        owned(s).start()
        dattn[at, :] = out.astype(bf16)
        owned_out(s).start()
    for s in range(HALF):
        at = pl.ds(s * part, part)
        rows_to(0, s, across).wait_recv()
        passed(s).start()
        keep[...], out = work(across, s)
        out_keep[at, :] = out.astype(bf16)
        passed(s).wait_recv()
        total, out = work(corner, s)
        to_beside[at, :] = total.astype(bf16)
        handed(s).start()
        headed[at, :] = out.astype(bf16)
        handed_out(s).start()
        handed(s).wait_recv()
        to_across[at, :] = (keep[...] + from_beside[at, :].astype(f32)).astype(bf16)
        summed(s).start()
        if s == 0:
            weight_grads(t // 2, False)
    weight_grads(1 - t // 2, True)
    stored(2).start()
    stored(3).start()
    for s in range(HALF):
        at = pl.ds(s * part, part)
        handed_out(s).wait_recv()
        out_keep[at, :] = (out_keep[at, :].astype(f32) + from_beside_out[at, :].astype(f32)).astype(bf16)
        owned_out(s).wait_recv()
        out_own[at, :] = out_own[at, :] + from_own_out[at, :].astype(f32)
        owned_out(s).wait_send()
    stored(4).start()
    stored(5).start()
    gain_out[...] = jnp.zeros_like(gain_out)
    piece = 64
    for s in range(HALF):
        owned(s).wait_recv()
        summed(s).wait_recv()

        def chunk(i, carry, s=s):
            at = pl.ds(pl.multiple_of(s * part + i * piece, piece), piece)
            grad = mine[at, :] + from_own[at, :].astype(f32) + from_across[at, :].astype(f32)
            x = hidden[at, :]
            r = lax.rsqrt(jnp.mean(x * x, axis=-1, keepdims=True) + 1e-5)
            scaled = gain * grad
            cot_rows = cot[pl.ds(pl.multiple_of(t * rows + s * part + i * piece, piece), piece), :].astype(f32)
            full = cot_rows + r * scaled - x * (r * r * r * jnp.mean(x * scaled, axis=-1, keepdims=True))
            mine[at, :] = full
            dattn[at, :] = full.astype(bf16)
            gain_out[...] += jnp.sum((grad * x * r).reshape(piece // 8, 8, grad.shape[1]), axis=0)
            return carry

        lax.fori_loop(0, part // piece, chunk, 0)
    stored(0).start()
    stored(1).start()
    for s in range(HALF):
        for copy in (rows_to(0, s, across), rows_to(1, s, beside), passed(s), handed(s), summed(s), owned(s), handed_out(s)):
            copy.wait_send()
    for i in range(len(stores)):
        stored(i).wait()


def mlp(headed, out_all, tokens, gain, gate_up, down, cot):
    rows, width = tokens.shape
    total = cot.shape[0]
    units = down.shape[0]
    hbm = pl.BlockSpec(memory_space=pl.ANY)
    vmem = pl.BlockSpec(memory_space=pltpu.VMEM)
    like = lambda x: pltpu.VMEM(x.shape, x.dtype)
    half = lambda: pltpu.VMEM((rows, width), bf16)
    wide = lambda: pltpu.VMEM((rows, width), f32)
    unit = lambda: pltpu.VMEM((total, units), bf16)
    out = lambda shape, kind: jax.ShapeDtypeStruct(shape, kind)
    dma = pltpu.SemaphoreType.DMA
    return pl.pallas_call(
        mlp_kernel,
        in_specs=[hbm] * 3 + [vmem] + [hbm] * 3,
        out_specs=[hbm] * 2 + [vmem] + [hbm] * 4,
        out_shape=[out((rows, width), f32), out((rows, width), bf16), out((8, width), f32), out(gate_up.shape, bf16), out(down.shape, bf16), out((rows, width), f32), out((rows, width), bf16)],
        scratch_shapes=[like(headed), like(out_all), like(tokens), like(gate_up), like(down), like(cot), wide(), pltpu.VMEM((total, width), bf16), unit(), unit(), unit(),
                        wide(), pltpu.VMEM((rows // HALF, width), f32), half(), half(), half(), half(), half(), half(), wide(), half(), half(), half(),
                        pltpu.VMEM(gate_up.shape, f32), pltpu.VMEM(down.shape, f32), like(gate_up), like(down), half(), dma((6,)), dma((6,)), dma((8, HALF)), dma((8, HALF))],
        compiler_params=pltpu.CompilerParams(collective_id=1, has_side_effects=True, vmem_limit_bytes=62 * 2**20),
    )(headed, out_all, tokens, gain, gate_up, down, cot)


def mixer_bwd_block(blk, width, flags, proj_ref, prev_ref, conv_ref, gain_ref, mixed_ref, state_in, res_in, wu_in, inv_in, dheaded, dcat, dstate, buf, dbuf, cacc, gacc):
    buf[0:8, :] = prev_ref[:, :width]
    buf[8:, :] = proj_ref[:, :width]
    heads, tails = span_masks(flags, blk * (BACK_ROWS // SPAN), BACK_ROWS // SPAN)
    cols, slopes = [], []
    for c in range(width // HEAD):
        total = conv_column(buf, conv_ref, heads, slice(c * HEAD, (c + 1) * HEAD))
        sig = sigmoid(total)
        cols.append(total * sig)
        slopes.append(sig * (1.0 + total * (1.0 - sig)))
    betas = sigmoid(proj_ref[:, width:])
    strict, causal, cross, _, _ = pair_masks()
    lane = lax.broadcasted_iota(jnp.int32, (STEP, HEAD), 1)
    order = list(reversed(range(BACK_STEPS)))
    hs = [slice(h * STEP, (h + 1) * STEP) for h in range(2)]
    spans = [slice(s * STEP, (s + 1) * STEP) for s in range(BACK_STEPS)]
    edge = [resets(flags, blk * BACK_STEPS + s) for s in range(BACK_STEPS)]
    enter, leave, keep = zip(*[row_masks(*e) for e in edge])
    gate = [jnp.where(cross, 1.0 - e[1], 1.0) for e in edge]
    both = lambda n: [jnp.concatenate([cols[2 * n][rs], cols[2 * n + 1][rs]], axis=0) for rs in spans]
    q, k, v = both(0), both(1), both(2)
    rq = [lax.rsqrt(jnp.sum(x * x, axis=-1, keepdims=True) + 1e-6) for x in q]
    rk = [lax.rsqrt(jnp.sum(x * x, axis=-1, keepdims=True) + 1e-6) for x in k]
    q = [x * r for x, r in zip(q, rq)]
    k = [x * r for x, r in zip(k, rk)]
    q16 = [x.astype(bf16) for x in q]
    k16 = [x.astype(bf16) for x in k]
    b = [jnp.concatenate([betas[rs, 0:1], betas[rs, 1:2]], axis=0) for rs in spans]
    gp = [mm(jnp.concatenate([x, y], axis=0), x, NT) for x, y in zip(k16, q16)]
    gram = [jnp.where(strict, m * x[:2 * STEP], 0.0) for m, x in zip(gate, gp)]
    p = [jnp.where(causal, m * x[2 * STEP:], 0.0).astype(bf16) for m, x in zip(gate, gp)]
    do = []
    for s in range(BACK_STEPS):
        o = stack(mixed_ref[spans[s], :])
        dh = stack(dheaded[pl.ds(pl.multiple_of(blk * BACK_ROWS + s * STEP, STEP), STEP), :].astype(f32))
        ro = lax.rsqrt(jnp.mean(o * o, axis=-1, keepdims=True) + 1e-5)
        on = o * ro
        gacc[...] += jnp.sum((dh * on).reshape(2 * STEP // 8, 8, HEAD), axis=0)
        dn = dh * gain_ref[...]
        do.append(ro * (dn - on * jnp.mean(dn * on, axis=-1, keepdims=True)))
    do16 = [x.astype(bf16) for x in do]
    doe = [(x * e).astype(bf16) for x, e in zip(do, enter)]
    ke16 = [(x * e).astype(bf16) for x, e in zip(k, leave)]
    we = [(wu_in[s][:, :HEAD].astype(f32) * enter[s]).astype(bf16) for s in range(BACK_STEPS)]
    dres = [mm(x, y, TN) for x, y in zip(p, do16)]
    qdo = [[mm(x[r], y[r], TN) for r in hs] for x, y in zip(q16, doe)]
    dmem = [dstate[0], dstate[1]]
    dres16, after = [None] * BACK_STEPS, [None] * BACK_STEPS
    for s in order:
        low = [m.astype(bf16) for m in dmem]
        after[s] = low
        dres[s] = dres[s] + jnp.concatenate([mm(ke16[s][hs[h]], low[h]) for h in range(2)], axis=0)
        dres16[s] = dres[s].astype(bf16)
        for h in range(2):
            dmem[h] = keep[s] * dmem[h] + qdo[s][h] - mm(we[s][hs[h]], dres16[s][hs[h]], TN)
    dp = [mm(do16[s], res_in[s], NT) for s in order]
    dke = [jnp.concatenate([mm(res_in[s, hs[h]], after[s][h], NT) for h in range(2)], axis=0) for s in order]
    ds = [[mm(jnp.concatenate([do16[s][hs[h]], dres16[s][hs[h]]], axis=0), state_in[s, h * HEAD:(h + 1) * HEAD], NT) for h in range(2)] for s in order]
    dp = [jnp.where(causal, gate[s] * x, 0.0).astype(bf16) for s, x in zip(order, dp)]
    dw = [-enter[s] * jnp.concatenate([x[0][STEP:], x[1][STEP:]], axis=0) for s, x in zip(order, ds)]
    db_kv = [mm(inv_in[s], jnp.concatenate([x, dres[s]], axis=1), TN) for s, x in zip(order, dw)]
    dq = [enter[s] * jnp.concatenate([x[0][:STEP], x[1][:STEP]], axis=0) + mm(y, k16[s]) for s, x, y in zip(order, ds, dp)]
    dk = [mm(y, q16[s], TN) + leave[s] * x for s, x, y in zip(order, dke, dp)]
    da = [-jnp.where(strict, gate[s] * mm(x, wu_in[s], NT), 0.0) for s, x in zip(order, db_kv)]
    dg = [(x * b[s]).astype(bf16) for s, x in zip(order, da)]
    dk = [x + mm(y, k16[s]) + mm(y, k16[s], TN) + b[s] * z[:, :HEAD] for s, x, y, z in zip(order, dk, dg, db_kv)]
    for i, s in enumerate(order):
        rs = spans[s]
        dbeta = jnp.sum(da[i] * gram[s], axis=-1, keepdims=True) + jnp.sum(db_kv[i][:, :HEAD] * k[s] + db_kv[i][:, HEAD:] * v[s], axis=-1, keepdims=True)
        dv = b[s] * db_kv[i][:, HEAD:]
        dqs = rq[s] * (dq[i] - q[s] * jnp.sum(dq[i] * q[s], axis=-1, keepdims=True))
        dks = rk[s] * (dk[i] - k[s] * jnp.sum(dk[i] * k[s], axis=-1, keepdims=True))
        dpre = dbeta * b[s] * (1.0 - b[s])
        for n, x in enumerate((dqs, dks, dv)):
            for h in range(2):
                c = 2 * n + h
                dbuf[rs, c * HEAD:(c + 1) * HEAD] = x[hs[h]] * slopes[c][rs]
        dcat[pl.ds(pl.multiple_of(blk * BACK_ROWS + s * STEP, STEP), STEP), width:] = jnp.where(lane == 0, dpre[:STEP], jnp.where(lane == 1, dpre[STEP:], 0.0)).astype(bf16)
    dstate[0] = dmem[0]
    dstate[1] = dmem[1]
    for c in range(width // HEAD):
        cs = slice(c * HEAD, (c + 1) * HEAD)
        total, grads = conv_column_back(buf, dbuf, conv_ref, tails, cs)
        dcat[pl.ds(pl.multiple_of(blk * BACK_ROWS, BACK_ROWS), BACK_ROWS), cs] = total.astype(bf16)
        for j in range(4):
            cacc[j, :, cs] += grads[j]
    dbuf[BACK_ROWS:, :] = dbuf[0:8, :]


class Ring:
    def __init__(self, here, after, before, sources, results, lands, by_rows, send, recv):
        self.here, self.targets = here, (after, before)
        self.sources, self.results, self.lands, self.by_rows, self.send, self.recv = sources, results, lands, by_rows, send, recv
        self.visited = 0

    def shard(self, way, k):
        return lax.rem(self.here + (k if way else 2 * RING - k), RING)

    def view(self, ref, i, way, k):
        shard = self.shard(way, k)
        rows, cols = ref.shape
        if self.by_rows[i]:
            piece = rows // (2 * RING)
            return ref.at[pl.ds(pl.multiple_of((2 * shard + way) * piece, piece), piece)]
        piece = cols // RING
        return ref.at[pl.ds(way * (rows // 2), rows // 2), pl.ds(pl.multiple_of(shard * piece, piece), piece)]

    def copy(self, i, way, r):
        if r == 0:
            src, dst = self.view(self.sources[i], i, way, 0), self.lands[i].at[way, 0]
        elif r < RING - 1:
            src, dst = self.lands[i].at[way, r - 1], self.lands[i].at[way, r]
        else:
            src = dst = self.view(self.results[i], i, way, r)
        return pltpu.make_async_remote_copy(src_ref=src, dst_ref=dst, send_sem=self.send.at[i, way], recv_sem=self.recv.at[i, way, r], device_id=self.targets[way], device_id_type=MESH_ID)

    def visit(self, count):
        for _ in range(count):
            if self.visited == len(self.sources) * (ROUNDS + 1):
                return
            r, i = divmod(self.visited, len(self.sources))
            self.visited += 1
            for way in range(2):
                if r > 0:
                    last = self.copy(i, way, r - 1)
                    last.wait_send()
                    last.wait_recv()
                if 0 < r < RING:
                    land = self.lands[i].at[way, r - 1]
                    total = (land[...].astype(f32) + self.view(self.sources[i], i, way, r)[...].astype(f32)).astype(bf16)
                    if r < RING - 1:
                        land[...] = total
                    else:
                        done = self.view(self.results[i], i, way, r)
                        done[...] = total
                if r < ROUNDS:
                    self.copy(i, way, r).start()


def ring_place(d):
    base = d // RING * RING
    inner = lax.rem(d, RING)
    line = inner // 2
    here = jnp.where(lax.rem(inner, 2) == 0, line, RING - 1 - line)

    def device(place):
        return base + jnp.where(place < RING // 2, 2 * place, 2 * (RING - 1 - place) + 1)

    return here, device(lax.rem(here + 1, RING)), device(lax.rem(here + RING - 1, RING))


def ring_lands(shapes, by_rows):
    pieces = [(s[0] // (2 * RING), s[1]) if rows else (s[0] // 2, s[1] // RING) for s, rows in zip(shapes, by_rows)]
    return [pltpu.VMEM((2, RING - 1) + p, bf16) for p in pieces]


def back_kernel(n_dp, flags, proj_ref, prev_ref, params, mixed_ref, state_in, res_in, wu_in, inv_in,
                headed_hbm, attn_hbm, dattn_hbm, out_w_hbm, qkv_hbm, beta_hbm, tok_hbm, dhid_hbm, second_grad, gu_hbm, down_hbm, own_hbm, across_hbm,
                dx_hbm, small_out, output_hbm, gu_out, down_out, cat_out, outw_out, landed_hbm,
                headed, attn, dattn_all, out_w, w, beta_w, tok, dhid, gu_src, down_src, cat_src, outw_src,
                gu_res, down_res, cat_res, outw_res, gate_land, up_land, down_land, q_land, k_land, v_land, outw_land,
                dheaded, dcat, dstate, buf, dbuf, cacc, gacc, mine, to_beside, from_beside, to_across, from_across, to_own, from_own,
                group_send, group_land, all_send, all_land, gain_acc, beta_grad,
                load, store, send_m, recv_m, send_c, recv_c, send_r, recv_r, send_x, recv_x, send_g, recv_g, send_a, recv_a, late_sem):
    g = pl.program_id(0)
    n = pl.num_programs(0)
    d, t, beside, across, corner = places()
    here, after, before = ring_place(d)
    rows = tok.shape[0]
    part = rows // HALF
    width = buf.shape[1]
    others = [d // RING * RING + lax.rem(d + k, RING) for k in range(1, RING)]
    first_gain, _, gain_ref, conv_ref = param_views(params, width)
    units = down_src.shape[0]
    gate_up = lambda ref: [ref.at[pl.ds(0, units)], ref.at[pl.ds(units, units)]]
    mlp_ring = Ring(here, (after, t), (before, t), gate_up(gu_src) + [down_src], gate_up(gu_res) + [down_res], [gate_land, up_land, down_land], [False] * 3, send_m, recv_m)
    model = tok.shape[1]
    thirds = lambda ref: [ref.at[pl.ds(i * model, model)] for i in range(3)]
    cat_ring = Ring(here, (after, t), (before, t), thirds(cat_src) + [outw_src], thirds(cat_res) + [outw_res], [q_land, k_land, v_land, outw_land], [True] * 4, send_c, recv_c)
    rowset = Gather(dattn_all, rows, send_r, recv_r)
    loads = [(gu_hbm, gu_src), (down_hbm, down_src), (dattn_hbm, dattn_all.at[pl.ds(pl.multiple_of(t * rows, rows), rows)]), (out_w_hbm, out_w), (headed_hbm, headed), (attn_hbm, attn), (tok_hbm, tok), (dhid_hbm, dhid), (beta_hbm, beta_w)]
    loads += [(qkv_hbm.at[i], w.at[:, pl.ds(i * 2 * HEAD, 2 * HEAD)]) for i in range(3)]
    stores = [(gu_res, gu_out), (down_res, down_out), (mine, dx_hbm), (cat_res, cat_out), (outw_res, outw_out), (to_own, output_hbm)]

    def loaded(i):
        return pltpu.make_async_copy(loads[i][0], loads[i][1], load.at[i])

    def stored(i):
        return pltpu.make_async_copy(stores[i][0], stores[i][1], store.at[i])

    def pushed(src, dst, i, s, peer):
        return pltpu.make_async_remote_copy(src_ref=src, dst_ref=dst, send_sem=send_x.at[i, s], recv_sem=recv_x.at[i, s], device_id=(d, peer), device_id_type=MESH_ID)

    def outward():
        return pushed(across_hbm, landed_hbm, 6, 0, across)

    def block_at(owner, s):
        return row_block(owner, s, rows, part)

    @pl.when(g == 0)
    def _():
        for i in range(len(loads)):
            loaded(i).start()
        greet([(d, beside), (d, across), (d, corner)] + [(o, t) for o in others])
        loaded(2).wait()
        rowset.start_near()
        loaded(0).wait()
        loaded(1).wait()
        mlp_ring.visit(3)
        rowset.start_over(1)
        dstate[...] = jnp.zeros_like(dstate)
        dbuf[BACK_ROWS:, :] = jnp.zeros((8, width), f32)
        cacc[...] = jnp.zeros_like(cacc)
        gacc[...] = jnp.zeros_like(gacc)
        gain_acc[...] = jnp.zeros_like(gain_acc)
        loaded(3).wait()
        mlp_ring.visit(7)

        @pl.when(t < 2)
        def _():
            rowset.fetch_over(1)

        mlp_ring.visit(2)

    owner = n // 2 - 1 - g // 2
    for k in range(1, n):
        @pl.when(g == k)
        def _(k=k):
            if k == 3:
                outward().start()
            mlp_ring.visit(2)

    @pl.when((lax.rem(g, 2) == 1) & (g < n - 1) & ((owner - 1) // 2 != t // 2))
    def _():
        rowset.fetch_over(lax.rem(owner + 1, 2))

    @pl.when(lax.rem(g, 2) == 0)
    def _():
        @pl.when(owner == beside)
        def _():
            rowset.fetch_near()

        @pl.when(owner // 2 != t // 2)
        def _():
            rowset.passed(lax.rem(owner, 2)).wait_recv()

        at = pl.ds(pl.multiple_of(owner * rows, rows), rows)
        dheaded[at, :] = lax.dot_general(dattn_all[at, :], out_w[...], NT, preferred_element_type=f32).astype(bf16)

    blk = n - 1 - g
    mixer_bwd_block(blk, width, flags, proj_ref, prev_ref, conv_ref, gain_ref, mixed_ref, state_in, res_in, wu_in, inv_in, dheaded, dcat, dstate, buf, dbuf, cacc, gacc)

    def work(owner, s):
        at = block_at(owner, s)
        return lax.dot_general(dcat[at, :width], w[...], NT, preferred_element_type=f32) + lax.dot_general(dcat[at, width:width + 16], beta_w[...], NN, preferred_element_type=f32)

    def handed(s):
        at = pl.ds(s * part, part)
        return pushed(to_beside.at[at], from_beside.at[at], 3, s, beside)

    def summed(s):
        at = pl.ds(s * part, part)
        return pushed(to_across.at[at], from_across.at[at], 4, s, across)

    def owned(s):
        at = pl.ds(s * part, part)
        return pushed(to_own.at[at], from_own.at[at], 5, s, beside)

    def grouped(i, peer):
        return pltpu.make_async_remote_copy(src_ref=group_send, dst_ref=group_land.at[i], send_sem=send_g.at[i], recv_sem=recv_g.at[i], device_id=(d, peer), device_id_type=MESH_ID)

    def spread(i, o):
        return pltpu.make_async_remote_copy(src_ref=all_send, dst_ref=all_land.at[i], send_sem=send_a.at[i], recv_sem=recv_a.at[i], device_id=(o, t), device_id_type=MESH_ID)

    piece = 64

    def finish(s):
        gain = first_gain[...]

        def chunk(i, carry):
            at = pl.ds(pl.multiple_of(s * part + i * piece, piece), piece)
            grad = mine[at, :] + from_own[at, :].astype(f32) + from_across[at, :].astype(f32)
            x = tok[at, :].astype(f32)
            r = lax.rsqrt(jnp.mean(x * x, axis=-1, keepdims=True) + 1e-5)
            scaled = gain * grad
            mine[at, :] = dhid[at, :] + r * scaled - x * (r * r * r * jnp.mean(x * scaled, axis=-1, keepdims=True))
            gain_acc[...] += jnp.sum((grad * x * r).reshape(piece // 8, 8, grad.shape[1]), axis=0)
            return carry

        lax.fori_loop(0, part // piece, chunk, 0)

    @pl.when(g == n - 1)
    def _():
        for i in range(4, len(loads)):
            loaded(i).wait()

        def cat_chunk(i):
            grad = lax.dot_general(attn[:, i * 256:(i + 1) * 256], dcat[:, :width], TN, preferred_element_type=f32).astype(bf16)
            for j in range(3):
                cat_src[pl.ds(j * attn.shape[1] + i * 256, 256), :] = grad[:, j * 2 * HEAD:(j + 1) * 2 * HEAD]

        def turn():
            mlp_ring.visit(1)
            cat_ring.visit(4)

        for i in range(attn.shape[1] // 256):
            cat_chunk(i)
            mlp_ring.visit(1)
        outw_src[...] = lax.dot_general(headed[...], dattn_all[...], TN, preferred_element_type=f32).astype(bf16)
        cat_ring.visit(4)
        for s in range(HALF):
            at = pl.ds(s * part, part)
            to_beside[at, :] = work(corner, s).astype(bf16)
            handed(s).start()
            total = work(across, s)
            handed(s).wait_recv()
            to_across[at, :] = (total + from_beside[at, :].astype(f32)).astype(bf16)
            summed(s).start()
            turn()
        beta_grad[...] = lax.dot_general(dcat[:, width:width + 16], attn[...], TN, preferred_element_type=f32)[:8]
        for s in range(HALF):
            at = pl.ds(s * part, part)
            to_own[at, :] = work(beside, s).astype(bf16)
            owned(s).start()
            mine[at, :] = work(t, s)
            turn()
        turn()
        owned(0).wait_recv()
        summed(0).wait_recv()
        finish(0)
        turn()
        turn()
        owned(1).wait_recv()
        summed(1).wait_recv()
        finish(1)
        stored(2).start()
        for i, copy in enumerate((handed, summed, owned)):
            for s in range(HALF):
                copy(s).wait_send()
        outward().wait_recv()
        late = [pltpu.make_async_copy(own_hbm, dhid, late_sem.at[0]), pltpu.make_async_copy(landed_hbm, to_across, late_sem.at[1])]
        for copy in late:
            copy.start()
        turn()
        for copy in late:
            copy.wait()

        def add(i, carry):
            at = pl.ds(pl.multiple_of(i * piece, piece), piece)
            to_own[at, :] = (dhid[at, :] + to_across[at, :].astype(f32)).astype(bf16)
            return carry

        lax.fori_loop(0, rows // piece, add, 0)
        stored(5).start()
        line = lax.broadcasted_iota(jnp.int32, small_out.shape, 0)
        lane = lax.broadcasted_iota(jnp.int32, small_out.shape, 1)
        shared = (line < 2) | ((line == 3) & (lane >= width))
        group_send[...] = jnp.zeros_like(group_send)
        group_send[0:1, :] = jnp.sum(gain_acc[...], axis=0, keepdims=True)
        group_send[1:2, :] = jnp.sum(second_grad[...], axis=0, keepdims=True)
        group_send[2:3, :] = beta_grad[0:1, :]
        group_send[7:8, :] = beta_grad[1:2, :]
        group_send[3:4, width:width + HEAD] = jnp.sum(gacc[...], axis=0, keepdims=True)
        for j in range(4):
            group_send[3 + j:4 + j, :width] = jnp.sum(cacc[j], axis=0, keepdims=True)
        for i, peer in enumerate((beside, across, corner)):
            grouped(i, peer).start()
        turn()
        small = group_send[...]
        for i, peer in enumerate((beside, across, corner)):
            grouped(i, peer).wait_recv()
        both = (small + group_land[0]) + (group_land[1] + group_land[2])
        small = jnp.where(shared, both, small)
        all_send[...] = small
        for i, o in enumerate(others):
            spread(i, o).start()
        turn()
        turn()
        for i, o in enumerate(others):
            spread(i, o).wait_recv()
            small = small + all_land[i]
        small_out[...] = small
        for _ in range(ROUNDS):
            turn()
        for i in range(2):
            stored(i).start()
        for i in range(3, 5):
            stored(i).start()
        rowset.sent()
        for i, peer in enumerate((beside, across, corner)):
            grouped(i, peer).wait_send()
        for i, o in enumerate(others):
            spread(i, o).wait_send()
        outward().wait_send()
        for i in range(len(stores)):
            stored(i).wait()


def backward(n_dp, flags, proj, params, saved, headed, attn_all, d_attn, out_w, qkv, beta, tokens, d_hidden, second_grad, gu_part, down_part, out_own, out_across):
    mixed, states, res, wu, inv = saved
    total_rows, total = proj.shape
    width = 3 * qkv.shape[2]
    rows, model = tokens.shape
    n = total_rows // BACK_ROWS
    m2 = lambda g: (n - 1 - g, 0)
    m3 = lambda g: (n - 1 - g, 0, 0)
    z2 = lambda g: (0, 0)
    hbm = pl.BlockSpec(memory_space=pl.ANY)
    dma = pltpu.SemaphoreType.DMA
    like = lambda x: pltpu.VMEM(x.shape, x.dtype)
    mlp_parts = (gu_part, down_part)
    cat_shapes = [(3 * model, 2 * HEAD), (headed.shape[1], model)]
    half = lambda: pltpu.VMEM((rows, model), bf16)
    line = second_grad.shape
    out = lambda shape, kind: jax.ShapeDtypeStruct(shape, kind)
    return pl.pallas_call(
        functools.partial(back_kernel, n_dp),
        grid=(n,),
        in_specs=[pl.BlockSpec(memory_space=pltpu.SMEM), pl.BlockSpec((BACK_ROWS, total), m2),
                  pl.BlockSpec((8, total), lambda g: (jnp.maximum((n - 1 - g) * (BACK_ROWS // 8) - 1, 0), 0)),
                  pl.BlockSpec(params.shape, z2), pl.BlockSpec((BACK_ROWS, 2 * HEAD), m2),
                  pl.BlockSpec((BACK_STEPS, 2 * HEAD, HEAD), m3), pl.BlockSpec((BACK_STEPS, 2 * STEP, HEAD), m3),
                  pl.BlockSpec((BACK_STEPS, 2 * STEP, 2 * HEAD), m3), pl.BlockSpec((BACK_STEPS, 2 * STEP, 2 * STEP), m3)]
        + [hbm] * 8 + [pl.BlockSpec(line, z2)] + [hbm] * 4,
        out_specs=[hbm, pl.BlockSpec(line, z2)] + [hbm] * 6,
        out_shape=[out((rows, model), f32), out(line, f32), out((rows, model), bf16)] + [out(x.shape, bf16) for x in mlp_parts] + [out(s, bf16) for s in cat_shapes] + [out((rows, model), bf16)],
        scratch_shapes=[like(headed), like(attn_all), like(attn_all), like(out_w), pltpu.VMEM((model, width), bf16), like(beta), like(tokens), like(d_hidden)]
        + [like(x) for x in mlp_parts] + [pltpu.VMEM(s, bf16) for s in cat_shapes]
        + [like(x) for x in mlp_parts] + [pltpu.VMEM(s, bf16) for s in cat_shapes]
        + ring_lands([down_part.shape] * 3, [False] * 3) + ring_lands([(model, 2 * HEAD)] * 3 + cat_shapes[1:], [True] * 4)
        + [pltpu.VMEM((total_rows, 2 * HEAD), bf16), pltpu.VMEM((total_rows, total), bf16), pltpu.VMEM((2, HEAD, HEAD), f32),
           pltpu.VMEM((BACK_ROWS + 8, width), f32), pltpu.VMEM((BACK_ROWS + 8, width), f32), pltpu.VMEM((4, 8, width), f32), pltpu.VMEM((8, HEAD), f32),
           pltpu.VMEM((rows, model), f32), half(), half(), half(), half(), half(), half(),
           pltpu.VMEM(line, f32), pltpu.VMEM((3,) + line, f32), pltpu.VMEM(line, f32), pltpu.VMEM((RING - 1,) + line, f32), pltpu.VMEM((8, model), f32), pltpu.VMEM((8, model), f32),
           dma((13,)), dma((6,)), dma((3, 2)), dma((3, 2, ROUNDS)), dma((4, 2)), dma((4, 2, ROUNDS)), dma((3, 2)), dma((3, 2)), dma((7, HALF)), dma((7, HALF)),
           dma((3,)), dma((3,)), dma((RING - 1,)), dma((RING - 1,)), dma((2,))],
        compiler_params=pltpu.CompilerParams(dimension_semantics=("arbitrary",), collective_id=2, has_side_effects=True, vmem_limit_bytes=62 * 2**20),
    )(flags, proj, proj, params, mixed, states, res, wu, inv, headed, attn_all, d_attn, out_w, qkv, beta, tokens, d_hidden, second_grad, gu_part, down_part, out_own, out_across)


def cast_kernel(small, gu, down, cat, outw, dx, out, attn_grad, mlp_grad, head_grad, taps_grad, beta_grad, gu_out, down_out, cat_out, outw_out, dx_out, out_out):
    gu_out[...] = gu[...].astype(f32)
    down_out[...] = down[...].astype(f32)
    cat_out[...] = cat[...].astype(f32)
    outw_out[...] = outw[...].astype(f32)
    dx_out[...] = dx[...]
    out_out[...] = out[...]
    width = 3 * taps_grad.shape[2]
    attn_grad[...] = small[0, :]
    mlp_grad[...] = small[1, :]
    head_grad[...] = small[3, width:width + HEAD]
    for i in range(3):
        taps_grad[i] = small[3:7, i * width // 3:(i + 1) * width // 3]
    beta_grad[0:1, :] = small[2:3, :]
    beta_grad[1:2, :] = small[7:8, :]


def cast(small, gu, down, cat, outw, dx, out):
    steps = 4
    model = small.shape[1]
    arrays = (gu, down, cat, outw, dx, out)
    kinds = [f32] * 5 + [out.dtype]
    spec = lambda x: pl.BlockSpec((x.shape[0] // steps, x.shape[1]), lambda g: (g, 0))
    shapes = [(model,), (model,), (HEAD,), (3, 4, cat.shape[1]), (2, model)]
    whole = lambda s: pl.BlockSpec(s, lambda g: (0,) * len(s))
    return pl.pallas_call(
        cast_kernel,
        grid=(steps,),
        in_specs=[whole(small.shape)] + [spec(x) for x in arrays],
        out_specs=[whole(s) for s in shapes] + [spec(x) for x in arrays],
        out_shape=[jax.ShapeDtypeStruct(s, f32) for s in shapes] + [jax.ShapeDtypeStruct(x.shape, k) for x, k in zip(arrays, kinds)],
        compiler_params=pltpu.CompilerParams(dimension_semantics=("arbitrary",), vmem_limit_bytes=62 * 2**20),
    )(small, *arrays)


def on_device(tokens, lengths, attn_gain, qkv_weight, beta_weight, conv_weight, head_gain, out_weight, mlp_gain, gate_up_weight, down_weight, cotangent):
    model_width = tokens.shape[1]
    qkv = jnp.transpose(qkv_weight, (1, 0, 2))
    gate_up = jnp.transpose(gate_up_weight, (1, 2, 0)).reshape(-1, model_width)
    params, beta, proj, mixed, states, res, wu, inv, attn_all, headed, headed_rows, out_all, cot_all = front(
        lengths, attn_gain, mlp_gain, head_gain, jnp.transpose(conv_weight, (1, 0, 2)), beta_weight.T, tokens, qkv, out_weight, cotangent)
    saved = (mixed, states, res, wu, inv)
    d_hidden, d_attn, second_grad, gu_part, down_part, out_own, out_across = mlp(headed_rows, out_all, tokens, params, gate_up, down_weight, cot_all)
    n_dp = lax.axis_size("dp")
    input_grad, small, output, *sums, _ = backward(
        n_dp, lengths, proj, params, saved, headed, attn_all, d_attn, out_weight, qkv, beta, tokens, d_hidden, second_grad, gu_part, down_part, out_own, out_across)
    if n_dp > RING:
        groups = [list(range(i, n_dp, RING)) for i in range(RING)]
        small, *sums = lax.psum((small, *sums), "dp", axis_index_groups=groups)
    attn_gain_grad, mlp_gain_grad, head_gain_grad, taps_grad, beta_grad, gu_sum, down_sum, cat_sum, out_sum, input_grad, output = cast(small, *sums, input_grad, output)
    return (
        output,
        input_grad,
        attn_gain_grad,
        jnp.transpose(cat_sum.reshape(3, model_width, -1), (1, 0, 2)),
        beta_grad.T,
        jnp.transpose(taps_grad, (1, 0, 2)),
        head_gain_grad,
        out_sum,
        mlp_gain_grad,
        jnp.transpose(gu_sum.reshape(2, -1, model_width), (2, 0, 1)),
        down_sum,
    )


def solution(mesh):
    rows = P(("dp", "tensor"), None)
    last = P(None, None, "tensor")
    return jax.shard_map(
        on_device,
        mesh=mesh,
        in_specs=(rows, P("dp", None), P(), last, P(None, "tensor"), last, P(), P("tensor", None), P(), last, P("tensor", None), rows),
        out_specs=(rows, rows, P(), last, P(None, "tensor"), last, P(), P("tensor", None), P(), last, P("tensor", None)),
        check_vma=False,
    )
```

```python
import functools
import jax
import jax.numpy as jnp
from jax import lax
from jax.experimental import pallas as pl
from jax.experimental.pallas import tpu as pltpu
from jax.sharding import PartitionSpec as P

HEAD = 128
STEP = 128
SPAN = 64
STEPS = 4
ROWS = STEP * STEPS
BACK_STEPS = 2
BACK_ROWS = STEP * BACK_STEPS
RING = 8
ROUNDS = 2 * RING - 2
NN = (((1,), (0,)), ((), ()))
NT = (((1,), (1,)), ((), ()))
TN = (((0,), (0,)), ((), ()))
f32 = jnp.float32
bf16 = jnp.bfloat16


def mm(a, b, dims=NN):
    return lax.dot_general(a.astype(bf16), b.astype(bf16), dims, preferred_element_type=f32)


def split(a):
    high = a.astype(bf16)
    return high, (a - high.astype(f32)).astype(bf16)


def stack(x):
    return jnp.concatenate([x[:, :HEAD], x[:, HEAD:]], axis=0)


def unstack(x):
    return jnp.concatenate([x[:STEP], x[STEP:]], axis=1)


def pair_masks():
    i = lax.broadcasted_iota(jnp.int32, (2 * STEP, 2 * STEP), 0)
    j = lax.broadcasted_iota(jnp.int32, (2 * STEP, 2 * STEP), 1)
    same = (i // STEP) == (j // STEP)
    cross = ((i % STEP) >= SPAN) & ((j % STEP) < SPAN)
    levels = []
    size = 1
    while size < STEP:
        levels.append(((i // (2 * size)) == (j // (2 * size))) & ((i // size) % 2 == 1) & ((j // size) % 2 == 0))
        size *= 2
    return same & (i > j), same & (i >= j), cross, levels, i == j


def tri_inverses(systems, levels, eye):
    invs = [jnp.where(eye, 1.0, jnp.where(levels[0], -a, 0.0)) for a in systems]
    for level in levels[1:]:
        lows = [inv.astype(bf16) for inv in invs]
        parts = [mm(low, jnp.where(level, a, 0.0)) for low, a in zip(lows, systems)]
        parts = [mm(part, low) for part, low in zip(parts, lows)]
        invs = [inv - part for inv, part in zip(invs, parts)]
    return invs


def row_masks(start_reset, mid_reset):
    r = lax.broadcasted_iota(jnp.int32, (2 * STEP, HEAD), 0) % STEP
    upper = r < SPAN
    enter = jnp.where(upper, 1.0 - start_reset, (1.0 - start_reset) * (1.0 - mid_reset))
    leave = jnp.where(upper, 1.0 - mid_reset, 1.0)
    keep = (1.0 - start_reset) * (1.0 - mid_reset)
    return enter, leave, keep


def starts(lengths, span):
    return jnp.where((span == 0) | (span * SPAN == lengths[0, 0]), 1.0, 0.0).astype(f32)


def resets(lengths, step):
    return starts(lengths, 2 * step), starts(lengths, 2 * step + 1)


def sigmoid(x):
    return 0.5 * jnp.tanh(0.5 * x) + 0.5


def span_masks(flags, span, count):
    row = lax.broadcasted_iota(jnp.int32, (8, HEAD), 0)
    heads, tails = [], []
    for i in range(count):
        heads.append([None] + [jnp.where(row >= j, 1.0, 1.0 - starts(flags, span + i)) for j in range(1, 4)])
        tails.append([None] + [jnp.where(row + j < 8, 1.0, 1.0 - starts(flags, span + i + 1)) for j in range(1, 4)])
    return heads, tails


def conv_column(buf, conv_ref, heads, cs):
    out = []
    for i in range(len(heads)):
        at = 8 + i * SPAN
        total = buf[at:at + SPAN, cs] * conv_ref[0:1, cs]
        for j in range(1, 4):
            lead = buf[at - j:at - j + 8, cs] * heads[i][j]
            rest = buf[at - j + 8:at - j + SPAN, cs]
            total = total + jnp.concatenate([lead, rest], axis=0) * conv_ref[j:j + 1, cs]
        out.append(total)
    return jnp.concatenate(out, axis=0)


def conv_column_back(buf, dbuf, conv_ref, tails, cs):
    out, grads = [], [0.0] * 4
    for i in range(len(tails)):
        at = i * SPAN
        x = buf[8 + at:8 + at + SPAN, cs]
        for j in range(4):
            if j == 0:
                grad = dbuf[at:at + SPAN, cs]
                total = grad * conv_ref[0:1, cs]
            else:
                most = dbuf[at + j:at + j + SPAN - 8, cs]
                last = dbuf[at + j + SPAN - 8:at + j + SPAN, cs] * tails[i][j]
                grad = jnp.concatenate([most, last], axis=0)
                total = total + grad * conv_ref[j:j + 1, cs]
            grads[j] = grads[j] + jnp.sum((x * grad).reshape(SPAN // 8, 8, HEAD), axis=0)
        out.append(total)
    return jnp.concatenate(out, axis=0), grads


MESH_ID = pl.DeviceIdType.MESH
HALF = 2
EARLY_A, EARLY_B, EARLY_C = 5, 6, 5


def places():
    d = lax.axis_index("dp")
    t = lax.axis_index("tensor")
    beside = t + 1 - 2 * lax.rem(t, 2)
    across = lax.rem(t + 2, 4)
    corner = lax.rem(beside + 2, 4)
    return d, t, beside, across, corner


def push(src, dst, send, recv, device):
    copy = pltpu.make_async_remote_copy(src_ref=src, dst_ref=dst, send_sem=send, recv_sem=recv, device_id=device, device_id_type=MESH_ID)
    copy.start()
    return copy


def greet(devices):
    barrier = pltpu.get_barrier_semaphore()
    for device in devices:
        pl.semaphore_signal(barrier, inc=1, device_id=device, device_id_type=MESH_ID)
    pl.semaphore_wait(barrier, len(devices))


def row_block(owner, part, owner_rows, part_rows):
    return pl.ds(pl.multiple_of(owner * owner_rows + part * part_rows, part_rows), part_rows)


def mixer_fwd_block(g, width, flags, proj_ref, conv_ref, gain_ref, headed_ref, mixed_ref, state_out, res_out, wu_out, inv_out, state, buf):
    buf[8:, :] = proj_ref[:, :width]
    heads, _ = span_masks(flags, g * (ROWS // SPAN), ROWS // SPAN)
    cols = []
    for c in range(width // HEAD):
        total = conv_column(buf, conv_ref, heads, slice(c * HEAD, (c + 1) * HEAD))
        cols.append(total * sigmoid(total))
    buf[0:8, :] = buf[ROWS:ROWS + 8, :]
    betas = sigmoid(proj_ref[:, width:])
    strict, causal, cross, levels, eye = pair_masks()
    todo = []
    for s in range(STEPS):
        rs = slice(s * STEP, (s + 1) * STEP)
        start_reset, mid_reset = resets(flags, g * STEPS + s)
        gate = jnp.where(cross, 1.0 - mid_reset, 1.0)
        two = lambda n: jnp.concatenate([cols[2 * n][rs], cols[2 * n + 1][rs]], axis=0)
        q, k, v = two(0), two(1), two(2)
        q = q * lax.rsqrt(jnp.sum(q * q, axis=-1, keepdims=True) + 1e-6)
        k = k * lax.rsqrt(jnp.sum(k * k, axis=-1, keepdims=True) + 1e-6)
        b = jnp.concatenate([betas[rs, 0:1], betas[rs, 1:2]], axis=0)
        gp = mm(jnp.concatenate([k, q], axis=0), k, NT)
        a = jnp.where(strict, gate * gp[:2 * STEP], 0.0) * b
        p = jnp.where(causal, gate * gp[2 * STEP:], 0.0)
        todo.append((q, k, v, b, a, p, row_masks(start_reset, mid_reset)))
    invs = tri_inverses([x[4] for x in todo], levels, eye)
    wus = [mm(inv, jnp.concatenate([x[3] * x[1], x[3] * x[2]], axis=1)) for inv, x in zip(invs, todo)]
    mem = [state[0], state[1]]
    for s in range(STEPS):
        rs = slice(s * STEP, (s + 1) * STEP)
        q, k, v, b, a, p, (enter, leave, keep) = todo[s]
        wu = wus[s]
        inv_out[s] = invs[s].astype(bf16)
        wu_out[s] = wu.astype(bf16)
        state_out[s, :HEAD] = mem[0].astype(bf16)
        state_out[s, HEAD:] = mem[1].astype(bf16)
        w = wu[:, :HEAD] * enter
        qe = q * enter
        ws, qs = [], []
        for h in range(2):
            hs = slice(h * STEP, (h + 1) * STEP)
            both = mm(jnp.concatenate([w[hs], qe[hs]], axis=0), mem[h])
            ws.append(both[:STEP])
            qs.append(both[STEP:])
        res = wu[:, HEAD:] - jnp.concatenate(ws, axis=0)
        res_out[s] = res.astype(bf16)
        ke = k * leave
        for h in range(2):
            hs = slice(h * STEP, (h + 1) * STEP)
            mem[h] = keep * mem[h] + mm(ke[hs], res[hs], TN)
        o = jnp.concatenate(qs, axis=0) + mm(p, res)
        mixed_ref[rs, :] = unstack(o)
        headed = o * lax.rsqrt(jnp.mean(o * o, axis=-1, keepdims=True) + 1e-5) * gain_ref[...]
        headed_ref[g, rs, :] = unstack(headed).astype(bf16)
    state[0] = mem[0]
    state[1] = mem[1]


def param_views(params, width):
    return params.at[0:1, :], params.at[1:2, :], params.at[2:3, :HEAD], params.at[3:7, :width]


class Gather:
    def __init__(self, full, rows, send, recv):
        self.full, self.rows, self.send, self.recv = full, rows, send, recv
        self.d, self.t, self.beside, self.across, _ = places()
        self.core = lax.rem(self.t, 2)
        self.base = self.t - self.core
        self.far = lax.rem(self.base + 2, 4)

    def block(self, owner, h):
        part = self.rows // 2
        return self.full.at[pl.ds(pl.multiple_of(owner * self.rows + h * part, part), part)]

    def copy(self, owner, h, i, j, peer):
        block = self.block(owner, h)
        return pltpu.make_async_remote_copy(src_ref=block, dst_ref=block, send_sem=self.send.at[i, j], recv_sem=self.recv.at[i, j], device_id=(self.d, peer), device_id_type=MESH_ID)

    def near(self, h):
        return self.copy(self.t, h, 0, h, self.beside)

    def over(self, i):
        return self.copy(self.base + i, self.core, 1, i, self.across)

    def passed(self, i):
        return self.copy(self.far + i, self.core, 2, i, self.beside)

    def start_near(self):
        self.near(0).start()
        self.near(1).start()

    def start_over(self, first=0):
        @pl.when(self.core == first)
        def _():
            self.over(first).start()

        self.near(self.core).wait_recv()

        @pl.when(self.core != first)
        def _():
            self.over(first).start()

        self.over(1 - first).start()

    def fetch_near(self):
        self.near(1 - self.core).wait_recv()

    def fetch_over(self, i):
        self.over(i).wait_recv()
        self.passed(i).start()

    def sent(self):
        for i in range(2):
            self.near(i).wait_send()
            self.over(i).wait_send()
            self.passed(i).wait_send()


def front_kernel(flags, attn_gain, mlp_gain, head_gain, taps, beta_ref, tok_hbm, qkv_hbm, outw_hbm, cot_hbm,
                 params, beta_w, proj_ref, mixed_ref, state_out, res_out, wu_out, inv_out, attn_out, headed_out, heads_hbm, out_hbm, cots_hbm,
                 w, tok, attn, headed, out_all, cot_all, state, buf, load, store, send_r, recv_r, send_w, recv_w, send_c, recv_c, send_h, recv_h, send_s, recv_s):
    g = pl.program_id(0)
    n = pl.num_programs(0)
    d, t, beside, across, corner = places()
    rows = tok.shape[0]
    width = buf.shape[1]
    heads = 2 * HEAD
    first_gain, _, gain_ref, conv_ref = param_views(params, width)
    rowset = Gather(attn, rows, send_r, recv_r)
    weights = Gather(out_all, outw_hbm.shape[0], send_w, recv_w)
    cots = Gather(cot_all, rows, send_c, recv_c)
    loads = [(tok_hbm, tok)] + [(qkv_hbm.at[i], w.at[:, pl.ds(i * heads, heads)]) for i in range(3)]
    loads += [(outw_hbm, out_all.at[pl.ds(pl.multiple_of(t * outw_hbm.shape[0], 16), outw_hbm.shape[0])]), (cot_hbm, cot_all.at[pl.ds(pl.multiple_of(t * rows, rows), rows)])]

    def loaded(i):
        return pltpu.make_async_copy(loads[i][0], loads[i][1], load.at[i])

    def attn_stored():
        return pltpu.make_async_copy(attn, attn_out, store.at[0])

    def head_place(owner):
        return heads_hbm.at[:, pl.ds(pl.multiple_of(owner * heads, heads), heads)]

    def kept(i):
        return pltpu.make_async_copy(headed.at[i], headed_out.at[pl.ds(i * rows, rows)], store.at[1 + i])

    def own_heads():
        return pltpu.make_async_copy(headed.at[t], head_place(t), store.at[1 + n_groups])

    def gathered(i):
        return pltpu.make_async_copy((out_all, cot_all)[i], (out_hbm, cots_hbm)[i], store.at[2 + n_groups + i])

    n_groups = headed.shape[0]

    partners = [d + size - 2 * size * lax.rem(d // size, 2) for size in (1, 2, 4)]
    slot = lax.rem(d, RING)
    cut = outw_hbm.shape[0] // (2 * RING)

    def slice_of(owner, size=1):
        return out_all.at[pl.ds(pl.multiple_of(owner * outw_hbm.shape[0] + (weights.core * RING + slot // size * size) * cut, cut), size * cut)]

    def slice_over(i):
        ref = slice_of(weights.base + i)
        return pltpu.make_async_remote_copy(src_ref=ref, dst_ref=ref, send_sem=send_w.at[1, i], recv_sem=recv_w.at[1, i], device_id=(d, across), device_id_type=MESH_ID)

    def slice_spread(i, k):
        ref = slice_of(weights.far + i, 2 ** k)
        return pltpu.make_async_remote_copy(src_ref=ref, dst_ref=ref, send_sem=send_s.at[i, k], recv_sem=recv_s.at[i, k], device_id=(partners[k], t), device_id_type=MESH_ID)

    def heads_to(owner, sender):
        return pltpu.make_async_remote_copy(src_ref=headed.at[owner], dst_ref=head_place(sender), send_sem=send_h.at[owner], recv_sem=recv_h.at[sender], device_id=(d, owner), device_id_type=MESH_ID)

    @pl.when(g == 0)
    def _():
        for i in range(len(loads)):
            loaded(i).start()
        greet([(d, beside), (d, across), (d, corner)] + [(o, t) for o in partners])
        model = tok.shape[1]
        params[...] = jnp.zeros_like(params)
        params[0:1, :] = attn_gain[...].astype(f32).reshape(1, model)
        params[1:2, :] = mlp_gain[...].astype(f32).reshape(1, model)
        params[2:3, :HEAD] = head_gain[...].astype(f32).reshape(1, HEAD)
        for i in range(3):
            params[3:7, i * heads:(i + 1) * heads] = taps[i].astype(f32)
        beta_w[...] = jnp.concatenate([beta_ref[...].astype(f32), jnp.zeros((14, model), f32)], axis=0).astype(bf16)
        loaded(0).wait()
        piece = 64
        gain = first_gain[...]

        def chunk(i, carry):
            x = tok[pl.ds(pl.multiple_of(i * piece, piece), piece), :].astype(f32)
            attn[pl.ds(pl.multiple_of(t * rows + i * piece, piece), piece), :] = (x * lax.rsqrt(jnp.mean(x * x, axis=-1, keepdims=True) + 1e-5) * gain).astype(bf16)
            return carry

        lax.fori_loop(0, rows // piece, chunk, 0)
        rowset.start_near()
        loaded(4).wait()
        weights.start_near()
        rowset.start_over()
        weights.near(weights.core).wait_recv()
        for i in range(2):
            slice_over(i).start()
        state[...] = jnp.zeros_like(state)
        buf[0:8, :] = jnp.zeros((8, width), f32)
        for i in (1, 2, 3, 5):
            loaded(i).wait()
        cots.start_near()

    @pl.when(g == beside)
    def _():
        rowset.fetch_near()

    @pl.when(g // 2 != t // 2)
    def _():
        i = lax.rem(g, 2)
        rowset.fetch_over(i)
        rowset.passed(i).wait_recv()

    @pl.when(g == 2 - t // 2)
    def _():
        cots.start_over()

    for k in range(2):
        @pl.when(g == k + 2)
        def _(k=k):
            for i in range(2):
                if k == 0:
                    slice_over(i).wait_recv()
                else:
                    slice_spread(i, k - 1).wait_recv()
                slice_spread(i, k).start()

    @pl.when(g == n - 1)
    def _():
        attn_stored().start()

    now = attn[pl.ds(pl.multiple_of(g * rows, rows), rows), :]
    proj_ref[:, :width] = lax.dot_general(now, w[...], NN, preferred_element_type=f32)
    proj_ref[:, width:] = jnp.zeros((rows, HEAD), f32)
    proj_ref[:, width:width + 16] = lax.dot_general(now, beta_w[...], NT, preferred_element_type=f32)
    mixer_fwd_block(g, width, flags, proj_ref, conv_ref, gain_ref, headed, mixed_ref, state_out, res_out, wu_out, inv_out, state, buf)

    @pl.when(g != t)
    def _():
        heads_to(g, t).start()

    @pl.when(g == t)
    def _():
        own_heads().start()

    @pl.when(g == n - 1)
    def _():
        for i in range(n_groups):
            kept(i).start()
        weights.fetch_near()
        for i in range(2):
            slice_spread(i, 1).wait_recv()
            slice_spread(i, 2).start()
        cots.fetch_near()
        cots.fetch_over(0)
        for i in range(2):
            slice_spread(i, 2).wait_recv()
            weights.passed(i).start()
        cots.fetch_over(1)
        for gather in (weights, cots):
            for i in range(2):
                gather.passed(i).wait_recv()
        gathered(0).start()
        gathered(1).start()
        for k in range(1, n_groups):
            other = lax.rem(t + k, n_groups)
            heads_to(other, t).wait_send()
            heads_to(other, other).wait_recv()
        for i in range(2):
            weights.near(i).wait_send()
            weights.passed(i).wait_send()
            slice_over(i).wait_send()
            for k in range(3):
                slice_spread(i, k).wait_send()
        for gather in (rowset, cots):
            gather.sent()
        gathered(0).wait()
        gathered(1).wait()
        own_heads().wait()
        attn_stored().wait()
        for i in range(n_groups):
            kept(i).wait()


def front(lengths, attn_gain, mlp_gain, head_gain, taps, beta, tokens, qkv, out_weight, cot):
    rows, model = tokens.shape
    groups = 4
    total_rows = rows * groups
    width = 3 * qkv.shape[2]
    total = width + HEAD
    steps = total_rows // STEP
    hbm = pl.BlockSpec(memory_space=pl.ANY)
    z2 = lambda g: (0, 0)
    m2 = lambda g: (g, 0)
    m3 = lambda g: (g, 0, 0)
    dma = pltpu.SemaphoreType.DMA
    out = lambda shape, kind: jax.ShapeDtypeStruct(shape, kind)
    heads = 2 * HEAD
    return pl.pallas_call(
        front_kernel,
        grid=(groups,),
        in_specs=[pl.BlockSpec(memory_space=pltpu.SMEM)] + [pl.BlockSpec(memory_space=pltpu.VMEM)] * 5 + [hbm] * 4,
        out_specs=[pl.BlockSpec((8, model), z2), pl.BlockSpec((16, model), z2), pl.BlockSpec((ROWS, total), m2), pl.BlockSpec((ROWS, heads), m2), pl.BlockSpec((STEPS, heads, HEAD), m3), pl.BlockSpec((STEPS, 2 * STEP, HEAD), m3),
                   pl.BlockSpec((STEPS, 2 * STEP, heads), m3), pl.BlockSpec((STEPS, 2 * STEP, 2 * STEP), m3)] + [hbm] * 5,
        out_shape=[out((8, model), f32), out((16, model), bf16), out((total_rows, total), f32), out((total_rows, heads), f32), out((steps, heads, HEAD), bf16), out((steps, 2 * STEP, HEAD), bf16),
                   out((steps, 2 * STEP, heads), bf16), out((steps, 2 * STEP, 2 * STEP), bf16), out((total_rows, model), bf16), out((total_rows, heads), bf16),
                   out((rows, model), bf16), out((groups * out_weight.shape[0], model), bf16), out((total_rows, model), bf16)],
        scratch_shapes=[pltpu.VMEM((model, width), bf16), pltpu.VMEM((rows, model), bf16), pltpu.VMEM((total_rows, model), bf16), pltpu.VMEM((groups, rows, heads), bf16),
                        pltpu.VMEM((groups * out_weight.shape[0], model), bf16), pltpu.VMEM((total_rows, model), bf16), pltpu.VMEM((2, HEAD, HEAD), f32), pltpu.VMEM((ROWS + 8, width), f32), dma((6,)), dma((4 + groups,))]
        + [dma((3, 2))] * 6 + [dma((groups,))] * 2 + [dma((2, 3))] * 2,
        compiler_params=pltpu.CompilerParams(dimension_semantics=("arbitrary",), collective_id=3, has_side_effects=True, vmem_limit_bytes=56 * 2**20),
    )(lengths, attn_gain, mlp_gain, head_gain, taps, beta, tokens, qkv, out_weight, cot)


def norm_back(grad, x, gain, through):
    r = lax.rsqrt(jnp.mean(x * x, axis=-1, keepdims=True) + 1e-5)
    scaled = gain * grad
    full = through + r * scaled - x * (r * r * r * jnp.mean(x * scaled, axis=-1, keepdims=True))
    return full, jnp.sum((grad * x * r).reshape(x.shape[0] // 8, 8, x.shape[1]), axis=0)


def mlp_kernel(headed_hbm, out_hbm, tok_hbm, params, gu_hbm, down_hbm, cot_hbm,
               dhid_hbm, dattn_hbm, gain_out, gu_out, downg_out, own_hbm, across_hbm, late_hbm, hidden_hbm,
               headed, out_w, tok, gu_w, down_w, cot, hidden, all_rows, act, d_gate, d_up, mine, keep, to_beside, from_beside, to_across, from_across, to_own, from_own,
               out_own, out_keep, from_beside_out, from_own_out, gu_acc, down_acc, gu_sum, down_sum, dattn, load, store, send, recv):
    d, t, beside, across, corner = places()
    rows = tok.shape[0]
    part = rows // HALF
    units = down_w.shape[0]
    def half(ref, s):
        return ref.at[pl.ds(s * part, part)]

    loads = [(headed_hbm, headed), (out_hbm, out_w), (tok_hbm, tok), (gu_hbm, gu_w), (down_hbm, down_w), (cot_hbm, cot)]
    stores = [(mine, dhid_hbm), (dattn, dattn_hbm), (gu_sum, gu_out), (down_sum, downg_out), (out_own, own_hbm), (out_keep, across_hbm), (half(to_across, 1), late_hbm), (half(hidden, 1), hidden_hbm)]

    def loaded(i):
        return pltpu.make_async_copy(loads[i][0], loads[i][1], load.at[i])

    def stored(i):
        return pltpu.make_async_copy(stores[i][0], stores[i][1], store.at[i])

    def pushed(src, dst, i, s, peer):
        return pltpu.make_async_remote_copy(src_ref=src, dst_ref=dst, send_sem=send.at[i, s], recv_sem=recv.at[i, s], device_id=(d, peer), device_id_type=MESH_ID)

    def rows_to(i, s, peer):
        block = all_rows.at[row_block(t, s, rows, part)]
        return pushed(block, block, i, s, peer)

    def passed(s):
        block = all_rows.at[row_block(across, s, rows, part)]
        return pushed(block, block, 2, s, beside)

    def handed(s):
        return pushed(half(to_beside, s), half(from_beside, s), 3, s, beside)

    def summed(s):
        return pushed(half(to_across, s), half(from_across, s), 4, s, across)

    def owned(s):
        return pushed(half(to_own, s), half(from_own, s), 5, s, beside)

    def handed_out(s):
        return pushed(half(headed, s), half(from_beside_out, s), 6, s, beside)

    def owned_out(s):
        return pushed(half(dattn, s), half(from_own_out, s), 7, s, beside)

    for i in range(len(loads)):
        loaded(i).start()
    greet([(d, beside), (d, across)])
    for i in range(3):
        loaded(i).wait()
    gain = params[1:2, :]
    for s in range(HALF):
        at = pl.ds(s * part, part)
        x = tok[at, :].astype(f32) + lax.dot_general(headed[at, :], out_w[...], NN, preferred_element_type=f32)
        hidden[at, :] = x
        all_rows[row_block(t, s, rows, part), :] = (x * lax.rsqrt(jnp.mean(x * x, axis=-1, keepdims=True) + 1e-5) * gain).astype(bf16)
        rows_to(0, s, across).start()
        rows_to(1, s, beside).start()
    for i in range(3, len(loads)):
        loaded(i).wait()

    def work(owner, s):
        at = row_block(owner, s, rows, part)
        x = all_rows[at, :]
        gate = lax.dot_general(x, gu_w[:units, :], NT, preferred_element_type=f32)
        up = lax.dot_general(x, gu_w[units:, :], NT, preferred_element_type=f32)
        sig = sigmoid(gate)
        silu = gate * sig
        low = (silu * up).astype(bf16)
        act[at, :] = low
        d_act = lax.dot_general(cot[at, :], down_w[...], NT, preferred_element_type=f32)
        dg = (d_act * up * sig * (1.0 + gate * (1.0 - sig))).astype(bf16)
        du = (d_act * silu).astype(bf16)
        d_gate[at, :] = dg
        d_up[at, :] = du
        out = lax.dot_general(low, down_w[...], NN, preferred_element_type=f32)
        return lax.dot_general(dg, gu_w[:units, :], NN, preferred_element_type=f32) + lax.dot_general(du, gu_w[units:, :], NN, preferred_element_type=f32), out

    def weight_grads(pair, last):
        at = pl.ds(pl.multiple_of(pair * 2 * rows, 2 * rows), 2 * rows)

        def put(acc, total, where, value):
            if last:
                total[where, :] = (acc[where, :] + value).astype(bf16)
            else:
                acc[where, :] = value

        for c in range(0, units, 256):
            size = min(256, units - c)
            put(gu_acc, gu_sum, pl.ds(c, size), lax.dot_general(d_gate[at, c:c + size], all_rows[at, :], TN, preferred_element_type=f32))
            put(gu_acc, gu_sum, pl.ds(units + c, size), lax.dot_general(d_up[at, c:c + size], all_rows[at, :], TN, preferred_element_type=f32))
            put(down_acc, down_sum, pl.ds(c, size), lax.dot_general(act[at, c:c + size], cot[at, :], TN, preferred_element_type=f32))

    for s in range(HALF):
        at = pl.ds(s * part, part)
        mine[at, :], out = work(t, s)
        out_own[at, :] = hidden[at, :] + out
    for s in range(HALF):
        at = pl.ds(s * part, part)
        rows_to(1, s, beside).wait_recv()
        total, out = work(beside, s)
        to_own[at, :] = total.astype(bf16)
        owned(s).start()
        dattn[at, :] = out.astype(bf16)
        owned_out(s).start()
    for s in range(HALF):
        at = pl.ds(s * part, part)
        rows_to(0, s, across).wait_recv()
        passed(s).start()
        keep[...], out = work(across, s)
        out_keep[at, :] = out.astype(bf16)
        passed(s).wait_recv()
        total, out = work(corner, s)
        to_beside[at, :] = total.astype(bf16)
        handed(s).start()
        headed[at, :] = out.astype(bf16)
        handed_out(s).start()
        handed(s).wait_recv()
        to_across[at, :] = (keep[...] + from_beside[at, :].astype(f32)).astype(bf16)
        if s == 0:
            summed(s).start()
            weight_grads(t // 2, False)
        else:
            stored(6).start()
            stored(7).start()
    weight_grads(1 - t // 2, True)
    stored(2).start()
    stored(3).start()
    for s in range(HALF):
        at = pl.ds(s * part, part)
        handed_out(s).wait_recv()
        out_keep[at, :] = (out_keep[at, :].astype(f32) + from_beside_out[at, :].astype(f32)).astype(bf16)
        owned_out(s).wait_recv()
        out_own[at, :] = out_own[at, :] + from_own_out[at, :].astype(f32)
        owned_out(s).wait_send()
    stored(4).start()
    stored(5).start()
    gain_out[...] = jnp.zeros_like(gain_out)
    piece = 64
    owned(0).wait_recv()
    summed(0).wait_recv()

    def chunk(i, carry):
        at = pl.ds(pl.multiple_of(i * piece, piece), piece)
        grad = mine[at, :] + from_own[at, :].astype(f32) + from_across[at, :].astype(f32)
        cot_rows = cot[pl.ds(pl.multiple_of(t * rows + i * piece, piece), piece), :].astype(f32)
        full, part_gain = norm_back(grad, hidden[at, :], gain, cot_rows)
        mine[at, :] = full
        dattn[at, :] = full.astype(bf16)
        gain_out[...] += part_gain
        return carry

    lax.fori_loop(0, part // piece, chunk, 0)
    owned(1).wait_recv()
    mine[pl.ds(part, part), :] = mine[pl.ds(part, part), :] + from_own[pl.ds(part, part), :].astype(f32)
    stored(0).start()
    stored(1).start()
    for s in range(HALF):
        for copy in (rows_to(0, s, across), rows_to(1, s, beside), passed(s), handed(s), owned(s), handed_out(s)):
            copy.wait_send()
    summed(0).wait_send()
    for i in range(len(stores)):
        stored(i).wait()


def mlp(headed, out_all, tokens, gain, gate_up, down, cot):
    rows, width = tokens.shape
    total = cot.shape[0]
    units = down.shape[0]
    hbm = pl.BlockSpec(memory_space=pl.ANY)
    vmem = pl.BlockSpec(memory_space=pltpu.VMEM)
    like = lambda x: pltpu.VMEM(x.shape, x.dtype)
    half = lambda: pltpu.VMEM((rows, width), bf16)
    wide = lambda: pltpu.VMEM((rows, width), f32)
    unit = lambda: pltpu.VMEM((total, units), bf16)
    out = lambda shape, kind: jax.ShapeDtypeStruct(shape, kind)
    dma = pltpu.SemaphoreType.DMA
    return pl.pallas_call(
        mlp_kernel,
        in_specs=[hbm] * 3 + [vmem] + [hbm] * 3,
        out_specs=[hbm] * 2 + [vmem] + [hbm] * 6,
        out_shape=[out((rows, width), f32), out((rows, width), bf16), out((8, width), f32), out(gate_up.shape, bf16), out(down.shape, bf16), out((rows, width), f32), out((rows, width), bf16), out((rows // HALF, width), bf16), out((rows // HALF, width), f32)],
        scratch_shapes=[like(headed), like(out_all), like(tokens), like(gate_up), like(down), like(cot), wide(), pltpu.VMEM((total, width), bf16), unit(), unit(), unit(),
                        wide(), pltpu.VMEM((rows // HALF, width), f32), half(), half(), half(), half(), half(), half(), wide(), half(), half(), half(),
                        pltpu.VMEM(gate_up.shape, f32), pltpu.VMEM(down.shape, f32), like(gate_up), like(down), half(), dma((6,)), dma((8,)), dma((8, HALF)), dma((8, HALF))],
        compiler_params=pltpu.CompilerParams(collective_id=1, has_side_effects=True, vmem_limit_bytes=62 * 2**20),
    )(headed, out_all, tokens, gain, gate_up, down, cot)


def mixer_bwd_block(blk, width, flags, proj_ref, prev_ref, conv_ref, gain_ref, mixed_ref, state_in, res_in, wu_in, inv_in, dheaded, dcat, dstate, buf, dbuf, cacc, gacc):
    buf[0:8, :] = prev_ref[:, :width]
    buf[8:, :] = proj_ref[:, :width]
    heads, tails = span_masks(flags, blk * (BACK_ROWS // SPAN), BACK_ROWS // SPAN)
    cols, slopes = [], []
    for c in range(width // HEAD):
        total = conv_column(buf, conv_ref, heads, slice(c * HEAD, (c + 1) * HEAD))
        sig = sigmoid(total)
        cols.append(total * sig)
        slopes.append(sig * (1.0 + total * (1.0 - sig)))
    betas = sigmoid(proj_ref[:, width:])
    strict, causal, cross, _, _ = pair_masks()
    lane = lax.broadcasted_iota(jnp.int32, (STEP, HEAD), 1)
    order = list(reversed(range(BACK_STEPS)))
    hs = [slice(h * STEP, (h + 1) * STEP) for h in range(2)]
    spans = [slice(s * STEP, (s + 1) * STEP) for s in range(BACK_STEPS)]
    edge = [resets(flags, blk * BACK_STEPS + s) for s in range(BACK_STEPS)]
    enter, leave, keep = zip(*[row_masks(*e) for e in edge])
    gate = [jnp.where(cross, 1.0 - e[1], 1.0) for e in edge]
    both = lambda n: [jnp.concatenate([cols[2 * n][rs], cols[2 * n + 1][rs]], axis=0) for rs in spans]
    q, k, v = both(0), both(1), both(2)
    rq = [lax.rsqrt(jnp.sum(x * x, axis=-1, keepdims=True) + 1e-6) for x in q]
    rk = [lax.rsqrt(jnp.sum(x * x, axis=-1, keepdims=True) + 1e-6) for x in k]
    q = [x * r for x, r in zip(q, rq)]
    k = [x * r for x, r in zip(k, rk)]
    q16 = [x.astype(bf16) for x in q]
    k16 = [x.astype(bf16) for x in k]
    b = [jnp.concatenate([betas[rs, 0:1], betas[rs, 1:2]], axis=0) for rs in spans]
    gp = [mm(jnp.concatenate([x, y], axis=0), x, NT) for x, y in zip(k16, q16)]
    gram = [jnp.where(strict, m * x[:2 * STEP], 0.0) for m, x in zip(gate, gp)]
    p = [jnp.where(causal, m * x[2 * STEP:], 0.0).astype(bf16) for m, x in zip(gate, gp)]
    do = []
    for s in range(BACK_STEPS):
        o = stack(mixed_ref[spans[s], :])
        dh = stack(dheaded[pl.ds(pl.multiple_of(blk * BACK_ROWS + s * STEP, STEP), STEP), :].astype(f32))
        ro = lax.rsqrt(jnp.mean(o * o, axis=-1, keepdims=True) + 1e-5)
        on = o * ro
        gacc[...] += jnp.sum((dh * on).reshape(2 * STEP // 8, 8, HEAD), axis=0)
        dn = dh * gain_ref[...]
        do.append(ro * (dn - on * jnp.mean(dn * on, axis=-1, keepdims=True)))
    do16 = [x.astype(bf16) for x in do]
    doe = [(x * e).astype(bf16) for x, e in zip(do, enter)]
    ke16 = [(x * e).astype(bf16) for x, e in zip(k, leave)]
    we = [(wu_in[s][:, :HEAD].astype(f32) * enter[s]).astype(bf16) for s in range(BACK_STEPS)]
    dres = [mm(x, y, TN) for x, y in zip(p, do16)]
    qdo = [[mm(x[r], y[r], TN) for r in hs] for x, y in zip(q16, doe)]
    dmem = [dstate[0], dstate[1]]
    dres16, after = [None] * BACK_STEPS, [None] * BACK_STEPS
    for s in order:
        low = [m.astype(bf16) for m in dmem]
        after[s] = low
        dres[s] = dres[s] + jnp.concatenate([mm(ke16[s][hs[h]], low[h]) for h in range(2)], axis=0)
        dres16[s] = dres[s].astype(bf16)
        for h in range(2):
            dmem[h] = keep[s] * dmem[h] + qdo[s][h] - mm(we[s][hs[h]], dres16[s][hs[h]], TN)
    dp = [mm(do16[s], res_in[s], NT) for s in order]
    dke = [jnp.concatenate([mm(res_in[s, hs[h]], after[s][h], NT) for h in range(2)], axis=0) for s in order]
    ds = [[mm(jnp.concatenate([do16[s][hs[h]], dres16[s][hs[h]]], axis=0), state_in[s, h * HEAD:(h + 1) * HEAD], NT) for h in range(2)] for s in order]
    dp = [jnp.where(causal, gate[s] * x, 0.0).astype(bf16) for s, x in zip(order, dp)]
    dw = [-enter[s] * jnp.concatenate([x[0][STEP:], x[1][STEP:]], axis=0) for s, x in zip(order, ds)]
    db_kv = [mm(inv_in[s], jnp.concatenate([x, dres[s]], axis=1), TN) for s, x in zip(order, dw)]
    dq = [enter[s] * jnp.concatenate([x[0][:STEP], x[1][:STEP]], axis=0) + mm(y, k16[s]) for s, x, y in zip(order, ds, dp)]
    dk = [mm(y, q16[s], TN) + leave[s] * x for s, x, y in zip(order, dke, dp)]
    da = [-jnp.where(strict, gate[s] * mm(x, wu_in[s], NT), 0.0) for s, x in zip(order, db_kv)]
    dg = [(x * b[s]).astype(bf16) for s, x in zip(order, da)]
    dk = [x + mm(y, k16[s]) + mm(y, k16[s], TN) + b[s] * z[:, :HEAD] for s, x, y, z in zip(order, dk, dg, db_kv)]
    for i, s in enumerate(order):
        rs = spans[s]
        dbeta = jnp.sum(da[i] * gram[s], axis=-1, keepdims=True) + jnp.sum(db_kv[i][:, :HEAD] * k[s] + db_kv[i][:, HEAD:] * v[s], axis=-1, keepdims=True)
        dv = b[s] * db_kv[i][:, HEAD:]
        dqs = rq[s] * (dq[i] - q[s] * jnp.sum(dq[i] * q[s], axis=-1, keepdims=True))
        dks = rk[s] * (dk[i] - k[s] * jnp.sum(dk[i] * k[s], axis=-1, keepdims=True))
        dpre = dbeta * b[s] * (1.0 - b[s])
        for n, x in enumerate((dqs, dks, dv)):
            for h in range(2):
                c = 2 * n + h
                dbuf[rs, c * HEAD:(c + 1) * HEAD] = x[hs[h]] * slopes[c][rs]
        dcat[pl.ds(pl.multiple_of(blk * BACK_ROWS + s * STEP, STEP), STEP), width:] = jnp.where(lane == 0, dpre[:STEP], jnp.where(lane == 1, dpre[STEP:], 0.0)).astype(bf16)
    dstate[0] = dmem[0]
    dstate[1] = dmem[1]
    for c in range(width // HEAD):
        cs = slice(c * HEAD, (c + 1) * HEAD)
        total, grads = conv_column_back(buf, dbuf, conv_ref, tails, cs)
        dcat[pl.ds(pl.multiple_of(blk * BACK_ROWS, BACK_ROWS), BACK_ROWS), cs] = total.astype(bf16)
        for j in range(4):
            cacc[j, :, cs] += grads[j]
    dbuf[BACK_ROWS:, :] = dbuf[0:8, :]


class Ring:
    def __init__(self, here, after, before, sources, results, lands, by_rows, send, recv):
        self.here, self.targets = here, (after, before)
        self.sources, self.results, self.lands, self.by_rows, self.send, self.recv = sources, results, lands, by_rows, send, recv
        self.visited = 0

    def shard(self, way, k):
        return lax.rem(self.here + (k if way else 2 * RING - k), RING)

    def view(self, ref, i, way, k):
        shard = self.shard(way, k)
        rows, cols = ref.shape
        if self.by_rows[i]:
            piece = rows // (2 * RING)
            return ref.at[pl.ds(pl.multiple_of((2 * shard + way) * piece, piece), piece)]
        piece = cols // RING
        return ref.at[pl.ds(way * (rows // 2), rows // 2), pl.ds(pl.multiple_of(shard * piece, piece), piece)]

    def copy(self, i, way, r):
        if r == 0:
            src, dst = self.view(self.sources[i], i, way, 0), self.lands[i].at[way, 0]
        elif r < RING - 1:
            src, dst = self.lands[i].at[way, r - 1], self.lands[i].at[way, r]
        else:
            src = dst = self.view(self.results[i], i, way, r)
        return pltpu.make_async_remote_copy(src_ref=src, dst_ref=dst, send_sem=self.send.at[i, way], recv_sem=self.recv.at[i, way, r], device_id=self.targets[way], device_id_type=MESH_ID)

    def visit(self, count):
        for _ in range(count):
            if self.visited == len(self.sources) * (ROUNDS + 1):
                return
            r, i = divmod(self.visited, len(self.sources))
            self.visited += 1
            for way in range(2):
                if r > 0:
                    last = self.copy(i, way, r - 1)
                    last.wait_send()
                    last.wait_recv()
                if 0 < r < RING:
                    land = self.lands[i].at[way, r - 1]
                    total = (land[...].astype(f32) + self.view(self.sources[i], i, way, r)[...].astype(f32)).astype(bf16)
                    if r < RING - 1:
                        land[...] = total
                    else:
                        done = self.view(self.results[i], i, way, r)
                        done[...] = total
                if r < ROUNDS:
                    self.copy(i, way, r).start()


def ring_place(d):
    base = d // RING * RING
    inner = lax.rem(d, RING)
    line = inner // 2
    here = jnp.where(lax.rem(inner, 2) == 0, line, RING - 1 - line)

    def device(place):
        return base + jnp.where(place < RING // 2, 2 * place, 2 * (RING - 1 - place) + 1)

    return here, device(lax.rem(here + 1, RING)), device(lax.rem(here + RING - 1, RING))


def ring_lands(shapes, by_rows):
    pieces = [(s[0] // (2 * RING), s[1]) if rows else (s[0] // 2, s[1] // RING) for s, rows in zip(shapes, by_rows)]
    return [pltpu.VMEM((2, RING - 1) + p, bf16) for p in pieces]


def back_kernel(n_dp, flags, proj_ref, prev_ref, params, mixed_ref, state_in, res_in, wu_in, inv_in,
                headed_hbm, attn_hbm, dattn_hbm, out_w_hbm, qkv_hbm, beta_hbm, tok_hbm, dhid_hbm, second_grad, gu_hbm, down_hbm, own_hbm, across_hbm, late_hbm, hidden_hbm, cot_hbm,
                dx_hbm, small_out, output_hbm, gu_out, down_out, cat_out, outw_out, landed_hbm,
                headed, attn, dattn_all, out_w, w, beta_w, tok, dhid, gu_src, down_src, cat_src, outw_src,
                gu_res, down_res, cat_res, outw_res, gate_land, up_land, down_land, q_land, k_land, v_land, outw_land,
                dheaded, dcat, dstate, buf, dbuf, cacc, gacc, mine, to_beside, from_beside, to_across, from_across, to_own, from_own,
                group_send, group_land, all_send, all_land, gain_acc, beta_grad, second_acc, late_land,
                load, store, send_m, recv_m, send_c, recv_c, send_r, recv_r, send_x, recv_x, send_g, recv_g, send_a, recv_a, late_sem):
    g = pl.program_id(0)
    n = pl.num_programs(0)
    d, t, beside, across, corner = places()
    here, after, before = ring_place(d)
    rows = tok.shape[0]
    part = rows // HALF
    width = buf.shape[1]
    others = [d // RING * RING + lax.rem(d + k, RING) for k in range(1, RING)]
    first_gain, second_gain, gain_ref, conv_ref = param_views(params, width)
    units = down_src.shape[0]
    gate_up = lambda ref: [ref.at[pl.ds(0, units)], ref.at[pl.ds(units, units)]]
    mlp_ring = Ring(here, (after, t), (before, t), gate_up(gu_src) + [down_src], gate_up(gu_res) + [down_res], [gate_land, up_land, down_land], [False] * 3, send_m, recv_m)
    model = tok.shape[1]
    thirds = lambda ref: [ref.at[pl.ds(i * model, model)] for i in range(3)]
    cat_ring = Ring(here, (after, t), (before, t), thirds(cat_src) + [outw_src], thirds(cat_res) + [outw_res], [q_land, k_land, v_land, outw_land], [True] * 4, send_c, recv_c)
    rowset = Gather(dattn_all, rows, send_r, recv_r)
    loads = [(gu_hbm, gu_src), (down_hbm, down_src), (dattn_hbm, dattn_all.at[pl.ds(pl.multiple_of(t * rows, rows), rows)]), (out_w_hbm, out_w), (headed_hbm, headed), (attn_hbm, attn), (tok_hbm, tok), (dhid_hbm, dhid), (beta_hbm, beta_w)]
    loads += [(qkv_hbm.at[i], w.at[:, pl.ds(i * 2 * HEAD, 2 * HEAD)]) for i in range(3)]
    early = len(loads)
    dhid_load = 7
    loads += [(hidden_hbm, mine.at[pl.ds(0, part)]), (cot_hbm.at[pl.ds(pl.multiple_of(t * rows + part, part), part)], to_own.at[pl.ds(0, part)])]
    stores = [(gu_res, gu_out), (down_res, down_out), (mine, dx_hbm), (cat_res, cat_out), (outw_res, outw_out), (to_own, output_hbm)]

    def loaded(i):
        return pltpu.make_async_copy(loads[i][0], loads[i][1], load.at[i])

    def stored(i):
        return pltpu.make_async_copy(stores[i][0], stores[i][1], store.at[i])

    def pushed(src, dst, i, s, peer):
        return pltpu.make_async_remote_copy(src_ref=src, dst_ref=dst, send_sem=send_x.at[i, s], recv_sem=recv_x.at[i, s], device_id=(d, peer), device_id_type=MESH_ID)

    def outward():
        return pushed(across_hbm, landed_hbm, 6, 0, across)

    def late():
        return pushed(late_hbm, late_land, 6, 1, across)

    def block_at(owner, s):
        return row_block(owner, s, rows, part)

    @pl.when(g == 0)
    def _():
        for i in range(len(loads)):
            loaded(i).start()
        greet([(d, beside), (d, across), (d, corner)] + [(o, t) for o in others])
        late().start()
        loaded(2).wait()
        rowset.near(0).start()
        loaded(0).wait()
        loaded(1).wait()
        mlp_ring.visit(3)
        dstate[...] = jnp.zeros_like(dstate)
        dbuf[BACK_ROWS:, :] = jnp.zeros((8, width), f32)
        cacc[...] = jnp.zeros_like(cacc)
        gacc[...] = jnp.zeros_like(gacc)
        gain_acc[...] = jnp.zeros_like(gain_acc)
        second_acc[...] = jnp.zeros_like(second_acc)
        for i in (3, dhid_load, early, early + 1):
            loaded(i).wait()
        mlp_ring.visit(EARLY_A)
        late().wait_recv()

        def last(i, carry):
            here_at = pl.ds(pl.multiple_of(i * 64, 64), 64)
            at = pl.ds(pl.multiple_of(part + i * 64, 64), 64)
            full, part_gain = norm_back(dhid[at, :] + late_land[here_at, :].astype(f32), mine[here_at, :], second_gain[...], to_own[here_at, :].astype(f32))
            dhid[at, :] = full
            dattn_all[pl.ds(pl.multiple_of(t * rows + part + i * 64, 64), 64), :] = full.astype(bf16)
            second_acc[...] += part_gain
            return carry

        lax.fori_loop(0, part // 64, last, 0)
        rowset.near(1).start()
        rowset.start_over(1)
        mlp_ring.visit(EARLY_B)

        @pl.when(t < 2)
        def _():
            rowset.fetch_over(1)

        mlp_ring.visit(EARLY_C)

    owner = n // 2 - 1 - g // 2
    for k in range(1, n):
        @pl.when(g == k)
        def _(k=k):
            if k == 3:
                outward().start()
            mlp_ring.visit(2)

    @pl.when((lax.rem(g, 2) == 1) & (g < n - 1) & ((owner - 1) // 2 != t // 2))
    def _():
        rowset.fetch_over(lax.rem(owner + 1, 2))

    @pl.when(lax.rem(g, 2) == 0)
    def _():
        @pl.when(owner == beside)
        def _():
            rowset.fetch_near()

        @pl.when(owner // 2 != t // 2)
        def _():
            rowset.passed(lax.rem(owner, 2)).wait_recv()

        at = pl.ds(pl.multiple_of(owner * rows, rows), rows)
        dheaded[at, :] = lax.dot_general(dattn_all[at, :], out_w[...], NT, preferred_element_type=f32).astype(bf16)

    blk = n - 1 - g
    mixer_bwd_block(blk, width, flags, proj_ref, prev_ref, conv_ref, gain_ref, mixed_ref, state_in, res_in, wu_in, inv_in, dheaded, dcat, dstate, buf, dbuf, cacc, gacc)

    def work(owner, s):
        at = block_at(owner, s)
        return lax.dot_general(dcat[at, :width], w[...], NT, preferred_element_type=f32) + lax.dot_general(dcat[at, width:width + 16], beta_w[...], NN, preferred_element_type=f32)

    def handed(s):
        at = pl.ds(s * part, part)
        return pushed(to_beside.at[at], from_beside.at[at], 3, s, beside)

    def summed(s):
        at = pl.ds(s * part, part)
        return pushed(to_across.at[at], from_across.at[at], 4, s, across)

    def owned(s):
        at = pl.ds(s * part, part)
        return pushed(to_own.at[at], from_own.at[at], 5, s, beside)

    def grouped(i, peer):
        return pltpu.make_async_remote_copy(src_ref=group_send, dst_ref=group_land.at[i], send_sem=send_g.at[i], recv_sem=recv_g.at[i], device_id=(d, peer), device_id_type=MESH_ID)

    def spread(i, o):
        return pltpu.make_async_remote_copy(src_ref=all_send, dst_ref=all_land.at[i], send_sem=send_a.at[i], recv_sem=recv_a.at[i], device_id=(o, t), device_id_type=MESH_ID)

    piece = 64

    def finish(s):
        gain = first_gain[...]

        def chunk(i, carry):
            at = pl.ds(pl.multiple_of(s * part + i * piece, piece), piece)
            grad = mine[at, :] + from_own[at, :].astype(f32) + from_across[at, :].astype(f32)
            x = tok[at, :].astype(f32)
            r = lax.rsqrt(jnp.mean(x * x, axis=-1, keepdims=True) + 1e-5)
            scaled = gain * grad
            mine[at, :] = dhid[at, :] + r * scaled - x * (r * r * r * jnp.mean(x * scaled, axis=-1, keepdims=True))
            gain_acc[...] += jnp.sum((grad * x * r).reshape(piece // 8, 8, grad.shape[1]), axis=0)
            return carry

        lax.fori_loop(0, part // piece, chunk, 0)

    @pl.when(g == n - 1)
    def _():
        for i in range(4, early):
            if i != dhid_load:
                loaded(i).wait()

        def cat_chunk(i):
            grad = lax.dot_general(attn[:, i * 256:(i + 1) * 256], dcat[:, :width], TN, preferred_element_type=f32).astype(bf16)
            for j in range(3):
                cat_src[pl.ds(j * attn.shape[1] + i * 256, 256), :] = grad[:, j * 2 * HEAD:(j + 1) * 2 * HEAD]

        def turn():
            mlp_ring.visit(1)
            cat_ring.visit(4)

        for i in range(attn.shape[1] // 256):
            cat_chunk(i)
            mlp_ring.visit(1)
        outw_src[...] = lax.dot_general(headed[...], dattn_all[...], TN, preferred_element_type=f32).astype(bf16)
        cat_ring.visit(4)
        for s in range(HALF):
            at = pl.ds(s * part, part)
            to_beside[at, :] = work(corner, s).astype(bf16)
            handed(s).start()
            total = work(across, s)
            handed(s).wait_recv()
            to_across[at, :] = (total + from_beside[at, :].astype(f32)).astype(bf16)
            summed(s).start()
            turn()
        beta_grad[...] = lax.dot_general(dcat[:, width:width + 16], attn[...], TN, preferred_element_type=f32)[:8]
        for s in range(HALF):
            at = pl.ds(s * part, part)
            to_own[at, :] = work(beside, s).astype(bf16)
            owned(s).start()
            mine[at, :] = work(t, s)
            turn()
        turn()
        owned(0).wait_recv()
        summed(0).wait_recv()
        finish(0)
        turn()
        turn()
        owned(1).wait_recv()
        summed(1).wait_recv()
        finish(1)
        stored(2).start()
        for i, copy in enumerate((handed, summed, owned)):
            for s in range(HALF):
                copy(s).wait_send()
        outward().wait_recv()
        ends = [pltpu.make_async_copy(own_hbm, dhid, late_sem.at[0]), pltpu.make_async_copy(landed_hbm, to_across, late_sem.at[1])]
        for copy in ends:
            copy.start()
        turn()
        for copy in ends:
            copy.wait()

        def add(i, carry):
            at = pl.ds(pl.multiple_of(i * piece, piece), piece)
            to_own[at, :] = (dhid[at, :] + to_across[at, :].astype(f32)).astype(bf16)
            return carry

        lax.fori_loop(0, rows // piece, add, 0)
        stored(5).start()
        line = lax.broadcasted_iota(jnp.int32, small_out.shape, 0)
        lane = lax.broadcasted_iota(jnp.int32, small_out.shape, 1)
        shared = (line < 2) | ((line == 3) & (lane >= width))
        group_send[...] = jnp.zeros_like(group_send)
        group_send[0:1, :] = jnp.sum(gain_acc[...], axis=0, keepdims=True)
        group_send[1:2, :] = jnp.sum(second_grad[...] + second_acc[...], axis=0, keepdims=True)
        group_send[2:3, :] = beta_grad[0:1, :]
        group_send[7:8, :] = beta_grad[1:2, :]
        group_send[3:4, width:width + HEAD] = jnp.sum(gacc[...], axis=0, keepdims=True)
        for j in range(4):
            group_send[3 + j:4 + j, :width] = jnp.sum(cacc[j], axis=0, keepdims=True)
        for i, peer in enumerate((beside, across, corner)):
            grouped(i, peer).start()
        turn()
        small = group_send[...]
        for i, peer in enumerate((beside, across, corner)):
            grouped(i, peer).wait_recv()
        both = (small + group_land[0]) + (group_land[1] + group_land[2])
        small = jnp.where(shared, both, small)
        all_send[...] = small
        for i, o in enumerate(others):
            spread(i, o).start()
        turn()
        turn()
        for i, o in enumerate(others):
            spread(i, o).wait_recv()
            small = small + all_land[i]
        small_out[...] = small
        for _ in range(ROUNDS):
            turn()
        for i in range(2):
            stored(i).start()
        for i in range(3, 5):
            stored(i).start()
        rowset.sent()
        for i, peer in enumerate((beside, across, corner)):
            grouped(i, peer).wait_send()
        for i, o in enumerate(others):
            spread(i, o).wait_send()
        outward().wait_send()
        late().wait_send()
        for i in range(len(stores)):
            stored(i).wait()


def backward(n_dp, flags, proj, params, saved, headed, attn_all, d_attn, out_w, qkv, beta, tokens, d_hidden, second_grad, gu_part, down_part, out_own, out_across, late, hidden_late, cot_all):
    mixed, states, res, wu, inv = saved
    total_rows, total = proj.shape
    width = 3 * qkv.shape[2]
    rows, model = tokens.shape
    n = total_rows // BACK_ROWS
    m2 = lambda g: (n - 1 - g, 0)
    m3 = lambda g: (n - 1 - g, 0, 0)
    z2 = lambda g: (0, 0)
    hbm = pl.BlockSpec(memory_space=pl.ANY)
    dma = pltpu.SemaphoreType.DMA
    like = lambda x: pltpu.VMEM(x.shape, x.dtype)
    mlp_parts = (gu_part, down_part)
    cat_shapes = [(3 * model, 2 * HEAD), (headed.shape[1], model)]
    half = lambda: pltpu.VMEM((rows, model), bf16)
    line = second_grad.shape
    out = lambda shape, kind: jax.ShapeDtypeStruct(shape, kind)
    return pl.pallas_call(
        functools.partial(back_kernel, n_dp),
        grid=(n,),
        in_specs=[pl.BlockSpec(memory_space=pltpu.SMEM), pl.BlockSpec((BACK_ROWS, total), m2),
                  pl.BlockSpec((8, total), lambda g: (jnp.maximum((n - 1 - g) * (BACK_ROWS // 8) - 1, 0), 0)),
                  pl.BlockSpec(params.shape, z2), pl.BlockSpec((BACK_ROWS, 2 * HEAD), m2),
                  pl.BlockSpec((BACK_STEPS, 2 * HEAD, HEAD), m3), pl.BlockSpec((BACK_STEPS, 2 * STEP, HEAD), m3),
                  pl.BlockSpec((BACK_STEPS, 2 * STEP, 2 * HEAD), m3), pl.BlockSpec((BACK_STEPS, 2 * STEP, 2 * STEP), m3)]
        + [hbm] * 8 + [pl.BlockSpec(line, z2)] + [hbm] * 7,
        out_specs=[hbm, pl.BlockSpec(line, z2)] + [hbm] * 6,
        out_shape=[out((rows, model), f32), out(line, f32), out((rows, model), bf16)] + [out(x.shape, bf16) for x in mlp_parts] + [out(s, bf16) for s in cat_shapes] + [out((rows, model), bf16)],
        scratch_shapes=[like(headed), like(attn_all), like(attn_all), like(out_w), pltpu.VMEM((model, width), bf16), like(beta), like(tokens), like(d_hidden)]
        + [like(x) for x in mlp_parts] + [pltpu.VMEM(s, bf16) for s in cat_shapes]
        + [like(x) for x in mlp_parts] + [pltpu.VMEM(s, bf16) for s in cat_shapes]
        + ring_lands([down_part.shape] * 3, [False] * 3) + ring_lands([(model, 2 * HEAD)] * 3 + cat_shapes[1:], [True] * 4)
        + [pltpu.VMEM((total_rows, 2 * HEAD), bf16), pltpu.VMEM((total_rows, total), bf16), pltpu.VMEM((2, HEAD, HEAD), f32),
           pltpu.VMEM((BACK_ROWS + 8, width), f32), pltpu.VMEM((BACK_ROWS + 8, width), f32), pltpu.VMEM((4, 8, width), f32), pltpu.VMEM((8, HEAD), f32),
           pltpu.VMEM((rows, model), f32), half(), half(), half(), half(), half(), half(),
           pltpu.VMEM(line, f32), pltpu.VMEM((3,) + line, f32), pltpu.VMEM(line, f32), pltpu.VMEM((RING - 1,) + line, f32), pltpu.VMEM((8, model), f32), pltpu.VMEM((8, model), f32), pltpu.VMEM((8, model), f32), like(late),
           dma((15,)), dma((6,)), dma((3, 2)), dma((3, 2, ROUNDS)), dma((4, 2)), dma((4, 2, ROUNDS)), dma((3, 2)), dma((3, 2)), dma((7, HALF)), dma((7, HALF)),
           dma((3,)), dma((3,)), dma((RING - 1,)), dma((RING - 1,)), dma((2,))],
        compiler_params=pltpu.CompilerParams(dimension_semantics=("arbitrary",), collective_id=2, has_side_effects=True, vmem_limit_bytes=62 * 2**20),
    )(flags, proj, proj, params, mixed, states, res, wu, inv, headed, attn_all, d_attn, out_w, qkv, beta, tokens, d_hidden, second_grad, gu_part, down_part, out_own, out_across, late, hidden_late, cot_all)


def cast_kernel(small, gu, down, cat, outw, dx, out, attn_grad, mlp_grad, head_grad, taps_grad, beta_grad, gu_out, down_out, cat_out, outw_out, dx_out, out_out):
    gu_out[...] = gu[...].astype(f32)
    down_out[...] = down[...].astype(f32)
    cat_out[...] = cat[...].astype(f32)
    outw_out[...] = outw[...].astype(f32)
    dx_out[...] = dx[...]
    out_out[...] = out[...]
    width = 3 * taps_grad.shape[2]
    attn_grad[...] = small[0, :]
    mlp_grad[...] = small[1, :]
    head_grad[...] = small[3, width:width + HEAD]
    for i in range(3):
        taps_grad[i] = small[3:7, i * width // 3:(i + 1) * width // 3]
    beta_grad[0:1, :] = small[2:3, :]
    beta_grad[1:2, :] = small[7:8, :]


def cast(small, gu, down, cat, outw, dx, out):
    steps = 4
    model = small.shape[1]
    arrays = (gu, down, cat, outw, dx, out)
    kinds = [f32] * 5 + [out.dtype]
    spec = lambda x: pl.BlockSpec((x.shape[0] // steps, x.shape[1]), lambda g: (g, 0))
    shapes = [(model,), (model,), (HEAD,), (3, 4, cat.shape[1]), (2, model)]
    whole = lambda s: pl.BlockSpec(s, lambda g: (0,) * len(s))
    return pl.pallas_call(
        cast_kernel,
        grid=(steps,),
        in_specs=[whole(small.shape)] + [spec(x) for x in arrays],
        out_specs=[whole(s) for s in shapes] + [spec(x) for x in arrays],
        out_shape=[jax.ShapeDtypeStruct(s, f32) for s in shapes] + [jax.ShapeDtypeStruct(x.shape, k) for x, k in zip(arrays, kinds)],
        compiler_params=pltpu.CompilerParams(dimension_semantics=("arbitrary",), vmem_limit_bytes=62 * 2**20),
    )(small, *arrays)


def on_device(tokens, lengths, attn_gain, qkv_weight, beta_weight, conv_weight, head_gain, out_weight, mlp_gain, gate_up_weight, down_weight, cotangent):
    model_width = tokens.shape[1]
    qkv = jnp.transpose(qkv_weight, (1, 0, 2))
    gate_up = jnp.transpose(gate_up_weight, (1, 2, 0)).reshape(-1, model_width)
    params, beta, proj, mixed, states, res, wu, inv, attn_all, headed, headed_rows, out_all, cot_all = front(
        lengths, attn_gain, mlp_gain, head_gain, jnp.transpose(conv_weight, (1, 0, 2)), beta_weight.T, tokens, qkv, out_weight, cotangent)
    saved = (mixed, states, res, wu, inv)
    d_hidden, d_attn, second_grad, gu_part, down_part, out_own, out_across, late, hidden_late = mlp(headed_rows, out_all, tokens, params, gate_up, down_weight, cot_all)
    n_dp = lax.axis_size("dp")
    input_grad, small, output, *sums, _ = backward(
        n_dp, lengths, proj, params, saved, headed, attn_all, d_attn, out_weight, qkv, beta, tokens, d_hidden, second_grad, gu_part, down_part, out_own, out_across, late, hidden_late, cot_all)
    if n_dp > RING:
        groups = [list(range(i, n_dp, RING)) for i in range(RING)]
        small, *sums = lax.psum((small, *sums), "dp", axis_index_groups=groups)
    attn_gain_grad, mlp_gain_grad, head_gain_grad, taps_grad, beta_grad, gu_sum, down_sum, cat_sum, out_sum, input_grad, output = cast(small, *sums, input_grad, output)
    return (
        output,
        input_grad,
        attn_gain_grad,
        jnp.transpose(cat_sum.reshape(3, model_width, -1), (1, 0, 2)),
        beta_grad.T,
        jnp.transpose(taps_grad, (1, 0, 2)),
        head_gain_grad,
        out_sum,
        mlp_gain_grad,
        jnp.transpose(gu_sum.reshape(2, -1, model_width), (2, 0, 1)),
        down_sum,
    )


def solution(mesh):
    rows = P(("dp", "tensor"), None)
    last = P(None, None, "tensor")
    return jax.shard_map(
        on_device,
        mesh=mesh,
        in_specs=(rows, P("dp", None), P(), last, P(None, "tensor"), last, P(), P("tensor", None), P(), last, P("tensor", None), rows),
        out_specs=(rows, rows, P(), last, P(None, "tensor"), last, P(), P("tensor", None), P(), last, P("tensor", None)),
        check_vma=False,
    )
```

```python
import functools
import jax
import jax.numpy as jnp
from jax import lax
from jax.experimental import pallas as pl
from jax.experimental.pallas import tpu as pltpu
from jax.sharding import PartitionSpec as P

HEAD = 128
STEP = 128
SPAN = 64
STEPS = 4
ROWS = STEP * STEPS
BACK_STEPS = 2
BACK_ROWS = STEP * BACK_STEPS
RING = 8
ROUNDS = 2 * RING - 2
NN = (((1,), (0,)), ((), ()))
NT = (((1,), (1,)), ((), ()))
TN = (((0,), (0,)), ((), ()))
f32 = jnp.float32
bf16 = jnp.bfloat16


def mm(a, b, dims=NN):
    return lax.dot_general(a.astype(bf16), b.astype(bf16), dims, preferred_element_type=f32)


def split(a):
    high = a.astype(bf16)
    return high, (a - high.astype(f32)).astype(bf16)


def stack(x):
    return jnp.concatenate([x[:, :HEAD], x[:, HEAD:]], axis=0)


def unstack(x):
    return jnp.concatenate([x[:STEP], x[STEP:]], axis=1)


def pair_masks():
    i = lax.broadcasted_iota(jnp.int32, (2 * STEP, 2 * STEP), 0)
    j = lax.broadcasted_iota(jnp.int32, (2 * STEP, 2 * STEP), 1)
    same = (i // STEP) == (j // STEP)
    cross = ((i % STEP) >= SPAN) & ((j % STEP) < SPAN)
    levels = []
    size = 1
    while size < STEP:
        levels.append(((i // (2 * size)) == (j // (2 * size))) & ((i // size) % 2 == 1) & ((j // size) % 2 == 0))
        size *= 2
    return same & (i > j), same & (i >= j), cross, levels, i == j


def tri_inverses(systems, levels, eye):
    invs = [jnp.where(eye, 1.0, jnp.where(levels[0], -a, 0.0)) for a in systems]
    for level in levels[1:]:
        lows = [inv.astype(bf16) for inv in invs]
        parts = [mm(low, jnp.where(level, a, 0.0)) for low, a in zip(lows, systems)]
        parts = [mm(part, low) for part, low in zip(parts, lows)]
        invs = [inv - part for inv, part in zip(invs, parts)]
    return invs


def row_masks(start_reset, mid_reset):
    r = lax.broadcasted_iota(jnp.int32, (2 * STEP, HEAD), 0) % STEP
    upper = r < SPAN
    enter = jnp.where(upper, 1.0 - start_reset, (1.0 - start_reset) * (1.0 - mid_reset))
    leave = jnp.where(upper, 1.0 - mid_reset, 1.0)
    keep = (1.0 - start_reset) * (1.0 - mid_reset)
    return enter, leave, keep


def starts(lengths, span):
    return jnp.where((span == 0) | (span * SPAN == lengths[0, 0]), 1.0, 0.0).astype(f32)


def resets(lengths, step):
    return starts(lengths, 2 * step), starts(lengths, 2 * step + 1)


def sigmoid(x):
    return 0.5 * jnp.tanh(0.5 * x) + 0.5


def span_masks(flags, span, count):
    row = lax.broadcasted_iota(jnp.int32, (8, HEAD), 0)
    heads, tails = [], []
    for i in range(count):
        heads.append([None] + [jnp.where(row >= j, 1.0, 1.0 - starts(flags, span + i)) for j in range(1, 4)])
        tails.append([None] + [jnp.where(row + j < 8, 1.0, 1.0 - starts(flags, span + i + 1)) for j in range(1, 4)])
    return heads, tails


def conv_column(buf, conv_ref, heads, cs):
    out = []
    for i in range(len(heads)):
        at = 8 + i * SPAN
        total = buf[at:at + SPAN, cs] * conv_ref[0:1, cs]
        for j in range(1, 4):
            lead = buf[at - j:at - j + 8, cs] * heads[i][j]
            rest = buf[at - j + 8:at - j + SPAN, cs]
            total = total + jnp.concatenate([lead, rest], axis=0) * conv_ref[j:j + 1, cs]
        out.append(total)
    return jnp.concatenate(out, axis=0)


def conv_column_back(buf, dbuf, conv_ref, tails, cs):
    out, grads = [], [0.0] * 4
    for i in range(len(tails)):
        at = i * SPAN
        x = buf[8 + at:8 + at + SPAN, cs]
        for j in range(4):
            if j == 0:
                grad = dbuf[at:at + SPAN, cs]
                total = grad * conv_ref[0:1, cs]
            else:
                most = dbuf[at + j:at + j + SPAN - 8, cs]
                last = dbuf[at + j + SPAN - 8:at + j + SPAN, cs] * tails[i][j]
                grad = jnp.concatenate([most, last], axis=0)
                total = total + grad * conv_ref[j:j + 1, cs]
            grads[j] = grads[j] + jnp.sum((x * grad).reshape(SPAN // 8, 8, HEAD), axis=0)
        out.append(total)
    return jnp.concatenate(out, axis=0), grads


MESH_ID = pl.DeviceIdType.MESH
HALF = 2
EARLY_A, EARLY_B, EARLY_C = 5, 6, 5


def places():
    d = lax.axis_index("dp")
    t = lax.axis_index("tensor")
    beside = t + 1 - 2 * lax.rem(t, 2)
    across = lax.rem(t + 2, 4)
    corner = lax.rem(beside + 2, 4)
    return d, t, beside, across, corner


def push(src, dst, send, recv, device):
    copy = pltpu.make_async_remote_copy(src_ref=src, dst_ref=dst, send_sem=send, recv_sem=recv, device_id=device, device_id_type=MESH_ID)
    copy.start()
    return copy


def greet(devices):
    barrier = pltpu.get_barrier_semaphore()
    for device in devices:
        pl.semaphore_signal(barrier, inc=1, device_id=device, device_id_type=MESH_ID)
    pl.semaphore_wait(barrier, len(devices))


def row_block(owner, part, owner_rows, part_rows):
    return pl.ds(pl.multiple_of(owner * owner_rows + part * part_rows, part_rows), part_rows)


def mixer_fwd_block(g, width, flags, proj_ref, conv_ref, gain_ref, headed_ref, mixed_ref, state_out, res_out, wu_out, inv_out, state, buf):
    buf[8:, :] = proj_ref[:, :width]
    heads, _ = span_masks(flags, g * (ROWS // SPAN), ROWS // SPAN)
    cols = []
    for c in range(width // HEAD):
        total = conv_column(buf, conv_ref, heads, slice(c * HEAD, (c + 1) * HEAD))
        cols.append(total * sigmoid(total))
    buf[0:8, :] = buf[ROWS:ROWS + 8, :]
    betas = sigmoid(proj_ref[:, width:])
    strict, causal, cross, levels, eye = pair_masks()
    todo = []
    for s in range(STEPS):
        rs = slice(s * STEP, (s + 1) * STEP)
        start_reset, mid_reset = resets(flags, g * STEPS + s)
        gate = jnp.where(cross, 1.0 - mid_reset, 1.0)
        two = lambda n: jnp.concatenate([cols[2 * n][rs], cols[2 * n + 1][rs]], axis=0)
        q, k, v = two(0), two(1), two(2)
        q = q * lax.rsqrt(jnp.sum(q * q, axis=-1, keepdims=True) + 1e-6)
        k = k * lax.rsqrt(jnp.sum(k * k, axis=-1, keepdims=True) + 1e-6)
        b = jnp.concatenate([betas[rs, 0:1], betas[rs, 1:2]], axis=0)
        gp = mm(jnp.concatenate([k, q], axis=0), k, NT)
        a = jnp.where(strict, gate * gp[:2 * STEP], 0.0) * b
        p = jnp.where(causal, gate * gp[2 * STEP:], 0.0)
        todo.append((q, k, v, b, a, p, row_masks(start_reset, mid_reset)))
    invs = tri_inverses([x[4] for x in todo], levels, eye)
    wus = [mm(inv, jnp.concatenate([x[3] * x[1], x[3] * x[2]], axis=1)) for inv, x in zip(invs, todo)]
    mem = [state[0], state[1]]
    for s in range(STEPS):
        rs = slice(s * STEP, (s + 1) * STEP)
        q, k, v, b, a, p, (enter, leave, keep) = todo[s]
        wu = wus[s]
        inv_out[s] = invs[s].astype(bf16)
        wu_out[s] = wu.astype(bf16)
        state_out[s, :HEAD] = mem[0].astype(bf16)
        state_out[s, HEAD:] = mem[1].astype(bf16)
        w = wu[:, :HEAD] * enter
        qe = q * enter
        ws, qs = [], []
        for h in range(2):
            hs = slice(h * STEP, (h + 1) * STEP)
            both = mm(jnp.concatenate([w[hs], qe[hs]], axis=0), mem[h])
            ws.append(both[:STEP])
            qs.append(both[STEP:])
        res = wu[:, HEAD:] - jnp.concatenate(ws, axis=0)
        res_out[s] = res.astype(bf16)
        ke = k * leave
        for h in range(2):
            hs = slice(h * STEP, (h + 1) * STEP)
            mem[h] = keep * mem[h] + mm(ke[hs], res[hs], TN)
        o = jnp.concatenate(qs, axis=0) + mm(p, res)
        mixed_ref[rs, :] = unstack(o)
        headed = o * lax.rsqrt(jnp.mean(o * o, axis=-1, keepdims=True) + 1e-5) * gain_ref[...]
        headed_ref[g, rs, :] = unstack(headed).astype(bf16)
    state[0] = mem[0]
    state[1] = mem[1]


def param_views(params, width):
    return params.at[0:1, :], params.at[1:2, :], params.at[2:3, :HEAD], params.at[3:7, :width]


class Gather:
    def __init__(self, full, rows, send, recv):
        self.full, self.rows, self.send, self.recv = full, rows, send, recv
        self.d, self.t, self.beside, self.across, _ = places()
        self.core = lax.rem(self.t, 2)
        self.base = self.t - self.core
        self.far = lax.rem(self.base + 2, 4)

    def block(self, owner, h):
        part = self.rows // 2
        return self.full.at[pl.ds(pl.multiple_of(owner * self.rows + h * part, part), part)]

    def copy(self, owner, h, i, j, peer):
        block = self.block(owner, h)
        return pltpu.make_async_remote_copy(src_ref=block, dst_ref=block, send_sem=self.send.at[i, j], recv_sem=self.recv.at[i, j], device_id=(self.d, peer), device_id_type=MESH_ID)

    def near(self, h):
        return self.copy(self.t, h, 0, h, self.beside)

    def over(self, i):
        return self.copy(self.base + i, self.core, 1, i, self.across)

    def passed(self, i):
        return self.copy(self.far + i, self.core, 2, i, self.beside)

    def start_near(self):
        self.near(0).start()
        self.near(1).start()

    def start_over(self, first=0):
        @pl.when(self.core == first)
        def _():
            self.over(first).start()

        self.near(self.core).wait_recv()

        @pl.when(self.core != first)
        def _():
            self.over(first).start()

        self.over(1 - first).start()

    def fetch_near(self):
        self.near(1 - self.core).wait_recv()

    def fetch_over(self, i):
        self.over(i).wait_recv()
        self.passed(i).start()

    def sent(self):
        for i in range(2):
            self.near(i).wait_send()
            self.over(i).wait_send()
            self.passed(i).wait_send()


def front_kernel(flags, attn_gain, mlp_gain, head_gain, taps, beta_ref, tok_hbm, qkv_hbm, outw_hbm, cot_hbm,
                 params, beta_w, proj_ref, mixed_ref, state_out, res_out, wu_out, inv_out, attn_out, headed_out, heads_hbm, out_hbm, cots_hbm,
                 w, tok, attn, headed, out_all, cot_all, state, buf, load, store, send_r, recv_r, send_w, recv_w, send_c, recv_c, send_h, recv_h, send_s, recv_s):
    g = pl.program_id(0)
    n = pl.num_programs(0)
    d, t, beside, across, corner = places()
    rows = tok.shape[0]
    width = buf.shape[1]
    heads = 2 * HEAD
    first_gain, _, gain_ref, conv_ref = param_views(params, width)
    rowset = Gather(attn, rows, send_r, recv_r)
    weights = Gather(out_all, outw_hbm.shape[0], send_w, recv_w)
    cots = Gather(cot_all, rows, send_c, recv_c)
    loads = [(tok_hbm, tok)] + [(qkv_hbm.at[i], w.at[:, pl.ds(i * heads, heads)]) for i in range(3)]
    loads += [(outw_hbm, out_all.at[pl.ds(pl.multiple_of(t * outw_hbm.shape[0], 16), outw_hbm.shape[0])]), (cot_hbm, cot_all.at[pl.ds(pl.multiple_of(t * rows, rows), rows)])]

    def loaded(i):
        return pltpu.make_async_copy(loads[i][0], loads[i][1], load.at[i])

    def attn_stored():
        return pltpu.make_async_copy(attn, attn_out, store.at[0])

    def head_place(owner):
        return heads_hbm.at[:, pl.ds(pl.multiple_of(owner * heads, heads), heads)]

    def kept(i):
        return pltpu.make_async_copy(headed.at[i], headed_out.at[pl.ds(i * rows, rows)], store.at[1 + i])

    def own_heads():
        return pltpu.make_async_copy(headed.at[t], head_place(t), store.at[1 + n_groups])

    def gathered(i):
        return pltpu.make_async_copy((out_all, cot_all)[i], (out_hbm, cots_hbm)[i], store.at[2 + n_groups + i])

    n_groups = headed.shape[0]

    partners = [d + size - 2 * size * lax.rem(d // size, 2) for size in (1, 2, 4)]
    slot = lax.rem(d, RING)
    cut = outw_hbm.shape[0] // (2 * RING)

    def slice_of(owner, size=1):
        return out_all.at[pl.ds(pl.multiple_of(owner * outw_hbm.shape[0] + (weights.core * RING + slot // size * size) * cut, cut), size * cut)]

    def slice_over(i):
        ref = slice_of(weights.base + i)
        return pltpu.make_async_remote_copy(src_ref=ref, dst_ref=ref, send_sem=send_w.at[1, i], recv_sem=recv_w.at[1, i], device_id=(d, across), device_id_type=MESH_ID)

    def slice_spread(i, k):
        ref = slice_of(weights.far + i, 2 ** k)
        return pltpu.make_async_remote_copy(src_ref=ref, dst_ref=ref, send_sem=send_s.at[i, k], recv_sem=recv_s.at[i, k], device_id=(partners[k], t), device_id_type=MESH_ID)

    def heads_to(owner, sender):
        return pltpu.make_async_remote_copy(src_ref=headed.at[owner], dst_ref=head_place(sender), send_sem=send_h.at[owner], recv_sem=recv_h.at[sender], device_id=(d, owner), device_id_type=MESH_ID)

    @pl.when(g == 0)
    def _():
        for i in range(len(loads)):
            loaded(i).start()
        greet([(d, beside), (d, across), (d, corner)] + [(o, t) for o in partners])
        model = tok.shape[1]
        params[...] = jnp.zeros_like(params)
        params[0:1, :] = attn_gain[...].astype(f32).reshape(1, model)
        params[1:2, :] = mlp_gain[...].astype(f32).reshape(1, model)
        params[2:3, :HEAD] = head_gain[...].astype(f32).reshape(1, HEAD)
        for i in range(3):
            params[3:7, i * heads:(i + 1) * heads] = taps[i].astype(f32)
        beta_w[...] = jnp.concatenate([beta_ref[...].astype(f32), jnp.zeros((14, model), f32)], axis=0).astype(bf16)
        loaded(0).wait()
        piece = 64
        gain = first_gain[...]

        def chunk(i, carry):
            x = tok[pl.ds(pl.multiple_of(i * piece, piece), piece), :].astype(f32)
            attn[pl.ds(pl.multiple_of(t * rows + i * piece, piece), piece), :] = (x * lax.rsqrt(jnp.mean(x * x, axis=-1, keepdims=True) + 1e-5) * gain).astype(bf16)
            return carry

        lax.fori_loop(0, rows // piece, chunk, 0)
        rowset.start_near()
        loaded(4).wait()
        weights.start_near()
        rowset.start_over()
        weights.near(weights.core).wait_recv()
        for i in range(2):
            slice_over(i).start()
        state[...] = jnp.zeros_like(state)
        buf[0:8, :] = jnp.zeros((8, width), f32)
        for i in (1, 2, 3, 5):
            loaded(i).wait()
        cots.start_near()

    @pl.when(g == beside)
    def _():
        rowset.fetch_near()

    @pl.when(g // 2 != t // 2)
    def _():
        i = lax.rem(g, 2)
        rowset.fetch_over(i)
        rowset.passed(i).wait_recv()

    @pl.when(g == 2 - t // 2)
    def _():
        cots.start_over()

    for k in range(2):
        @pl.when(g == k + 2)
        def _(k=k):
            for i in range(2):
                if k == 0:
                    slice_over(i).wait_recv()
                else:
                    slice_spread(i, k - 1).wait_recv()
                slice_spread(i, k).start()

    @pl.when(g == n - 1)
    def _():
        attn_stored().start()

    now = attn[pl.ds(pl.multiple_of(g * rows, rows), rows), :]
    proj_ref[:, :width] = lax.dot_general(now, w[...], NN, preferred_element_type=f32)
    proj_ref[:, width:] = jnp.zeros((rows, HEAD), f32)
    proj_ref[:, width:width + 16] = lax.dot_general(now, beta_w[...], NT, preferred_element_type=f32)
    mixer_fwd_block(g, width, flags, proj_ref, conv_ref, gain_ref, headed, mixed_ref, state_out, res_out, wu_out, inv_out, state, buf)

    @pl.when(g != t)
    def _():
        heads_to(g, t).start()

    @pl.when(g == t)
    def _():
        own_heads().start()

    @pl.when(g == n - 1)
    def _():
        for i in range(n_groups):
            kept(i).start()
        weights.fetch_near()
        for i in range(2):
            slice_spread(i, 1).wait_recv()
            slice_spread(i, 2).start()
        cots.fetch_near()
        cots.fetch_over(0)
        for i in range(2):
            slice_spread(i, 2).wait_recv()
            weights.passed(i).start()
        cots.fetch_over(1)
        for gather in (weights, cots):
            for i in range(2):
                gather.passed(i).wait_recv()
        gathered(0).start()
        gathered(1).start()
        for k in range(1, n_groups):
            other = lax.rem(t + k, n_groups)
            heads_to(other, t).wait_send()
            heads_to(other, other).wait_recv()
        for i in range(2):
            weights.near(i).wait_send()
            weights.passed(i).wait_send()
            slice_over(i).wait_send()
            for k in range(3):
                slice_spread(i, k).wait_send()
        for gather in (rowset, cots):
            gather.sent()
        gathered(0).wait()
        gathered(1).wait()
        own_heads().wait()
        attn_stored().wait()
        for i in range(n_groups):
            kept(i).wait()


def front(lengths, attn_gain, mlp_gain, head_gain, taps, beta, tokens, qkv, out_weight, cot):
    rows, model = tokens.shape
    groups = 4
    total_rows = rows * groups
    width = 3 * qkv.shape[2]
    total = width + HEAD
    steps = total_rows // STEP
    hbm = pl.BlockSpec(memory_space=pl.ANY)
    z2 = lambda g: (0, 0)
    m2 = lambda g: (g, 0)
    m3 = lambda g: (g, 0, 0)
    dma = pltpu.SemaphoreType.DMA
    out = lambda shape, kind: jax.ShapeDtypeStruct(shape, kind)
    heads = 2 * HEAD
    return pl.pallas_call(
        front_kernel,
        grid=(groups,),
        in_specs=[pl.BlockSpec(memory_space=pltpu.SMEM)] + [pl.BlockSpec(memory_space=pltpu.VMEM)] * 5 + [hbm] * 4,
        out_specs=[pl.BlockSpec((8, model), z2), pl.BlockSpec((16, model), z2), pl.BlockSpec((ROWS, total), m2), pl.BlockSpec((ROWS, heads), m2), pl.BlockSpec((STEPS, heads, HEAD), m3), pl.BlockSpec((STEPS, 2 * STEP, HEAD), m3),
                   pl.BlockSpec((STEPS, 2 * STEP, heads), m3), pl.BlockSpec((STEPS, 2 * STEP, 2 * STEP), m3)] + [hbm] * 5,
        out_shape=[out((8, model), f32), out((16, model), bf16), out((total_rows, total), f32), out((total_rows, heads), f32), out((steps, heads, HEAD), bf16), out((steps, 2 * STEP, HEAD), bf16),
                   out((steps, 2 * STEP, heads), bf16), out((steps, 2 * STEP, 2 * STEP), bf16), out((total_rows, model), bf16), out((total_rows, heads), bf16),
                   out((rows, model), bf16), out((groups * out_weight.shape[0], model), bf16), out((total_rows, model), bf16)],
        scratch_shapes=[pltpu.VMEM((model, width), bf16), pltpu.VMEM((rows, model), bf16), pltpu.VMEM((total_rows, model), bf16), pltpu.VMEM((groups, rows, heads), bf16),
                        pltpu.VMEM((groups * out_weight.shape[0], model), bf16), pltpu.VMEM((total_rows, model), bf16), pltpu.VMEM((2, HEAD, HEAD), f32), pltpu.VMEM((ROWS + 8, width), f32), dma((6,)), dma((4 + groups,))]
        + [dma((3, 2))] * 6 + [dma((groups,))] * 2 + [dma((2, 3))] * 2,
        compiler_params=pltpu.CompilerParams(dimension_semantics=("arbitrary",), collective_id=3, has_side_effects=True, vmem_limit_bytes=56 * 2**20),
    )(lengths, attn_gain, mlp_gain, head_gain, taps, beta, tokens, qkv, out_weight, cot)


def norm_back(grad, x, gain, through):
    r = lax.rsqrt(jnp.mean(x * x, axis=-1, keepdims=True) + 1e-5)
    scaled = gain * grad
    full = through + r * scaled - x * (r * r * r * jnp.mean(x * scaled, axis=-1, keepdims=True))
    return full, jnp.sum((grad * x * r).reshape(x.shape[0] // 8, 8, x.shape[1]), axis=0)


def mlp_kernel(headed_hbm, out_hbm, tok_hbm, params, gu_hbm, down_hbm, cot_hbm,
               dhid_hbm, dattn_hbm, gain_out, gu_out, downg_out, own_hbm, across_hbm, late_hbm, hidden_hbm,
               headed, out_w, tok, gu_w, down_w, cot, hidden, all_rows, act, d_gate, d_up, mine, keep, to_beside, from_beside, to_across, from_across, to_own, from_own,
               out_own, out_keep, from_beside_out, from_own_out, gu_acc, down_acc, gu_sum, down_sum, dattn, load, store, send, recv):
    d, t, beside, across, corner = places()
    rows = tok.shape[0]
    part = rows // HALF
    units = down_w.shape[0]
    def half(ref, s):
        return ref.at[pl.ds(s * part, part)]

    loads = [(headed_hbm, headed), (out_hbm, out_w), (tok_hbm, tok), (gu_hbm, gu_w), (down_hbm, down_w), (cot_hbm, cot)]
    stores = [(mine, dhid_hbm), (dattn, dattn_hbm), (gu_sum, gu_out), (down_sum, downg_out), (out_own, own_hbm), (out_keep, across_hbm), (half(to_across, 1), late_hbm), (half(hidden, 1), hidden_hbm)]

    def loaded(i):
        return pltpu.make_async_copy(loads[i][0], loads[i][1], load.at[i])

    def stored(i):
        return pltpu.make_async_copy(stores[i][0], stores[i][1], store.at[i])

    def pushed(src, dst, i, s, peer):
        return pltpu.make_async_remote_copy(src_ref=src, dst_ref=dst, send_sem=send.at[i, s], recv_sem=recv.at[i, s], device_id=(d, peer), device_id_type=MESH_ID)

    def rows_to(i, s, peer):
        block = all_rows.at[row_block(t, s, rows, part)]
        return pushed(block, block, i, s, peer)

    def passed(s):
        block = all_rows.at[row_block(across, s, rows, part)]
        return pushed(block, block, 2, s, beside)

    def handed(s):
        return pushed(half(to_beside, s), half(from_beside, s), 3, s, beside)

    def summed(s):
        return pushed(half(to_across, s), half(from_across, s), 4, s, across)

    def owned(s):
        return pushed(half(to_own, s), half(from_own, s), 5, s, beside)

    def handed_out(s):
        return pushed(half(headed, s), half(from_beside_out, s), 6, s, beside)

    def owned_out(s):
        return pushed(half(dattn, s), half(from_own_out, s), 7, s, beside)

    for i in range(len(loads)):
        loaded(i).start()
    greet([(d, beside), (d, across)])
    for i in range(3):
        loaded(i).wait()
    gain = params[1:2, :]
    for s in range(HALF):
        at = pl.ds(s * part, part)
        x = tok[at, :].astype(f32) + lax.dot_general(headed[at, :], out_w[...], NN, preferred_element_type=f32)
        hidden[at, :] = x
        all_rows[row_block(t, s, rows, part), :] = (x * lax.rsqrt(jnp.mean(x * x, axis=-1, keepdims=True) + 1e-5) * gain).astype(bf16)
        rows_to(0, s, across).start()
        rows_to(1, s, beside).start()
    for i in range(3, len(loads)):
        loaded(i).wait()

    def work(owner, s):
        at = row_block(owner, s, rows, part)
        x = all_rows[at, :]
        gate = lax.dot_general(x, gu_w[:units, :], NT, preferred_element_type=f32)
        up = lax.dot_general(x, gu_w[units:, :], NT, preferred_element_type=f32)
        sig = sigmoid(gate)
        silu = gate * sig
        low = (silu * up).astype(bf16)
        act[at, :] = low
        d_act = lax.dot_general(cot[at, :], down_w[...], NT, preferred_element_type=f32)
        dg = (d_act * up * sig * (1.0 + gate * (1.0 - sig))).astype(bf16)
        du = (d_act * silu).astype(bf16)
        d_gate[at, :] = dg
        d_up[at, :] = du
        out = lax.dot_general(low, down_w[...], NN, preferred_element_type=f32)
        return lax.dot_general(dg, gu_w[:units, :], NN, preferred_element_type=f32) + lax.dot_general(du, gu_w[units:, :], NN, preferred_element_type=f32), out

    def weight_grads(pair, last):
        at = pl.ds(pl.multiple_of(pair * 2 * rows, 2 * rows), 2 * rows)

        def put(acc, total, where, value):
            if last:
                total[where, :] = (acc[where, :] + value).astype(bf16)
            else:
                acc[where, :] = value

        for c in range(0, units, 256):
            size = min(256, units - c)
            put(gu_acc, gu_sum, pl.ds(c, size), lax.dot_general(d_gate[at, c:c + size], all_rows[at, :], TN, preferred_element_type=f32))
            put(gu_acc, gu_sum, pl.ds(units + c, size), lax.dot_general(d_up[at, c:c + size], all_rows[at, :], TN, preferred_element_type=f32))
            put(down_acc, down_sum, pl.ds(c, size), lax.dot_general(act[at, c:c + size], cot[at, :], TN, preferred_element_type=f32))

    for s in range(HALF):
        at = pl.ds(s * part, part)
        mine[at, :], out = work(t, s)
        out_own[at, :] = hidden[at, :] + out
    for s in range(HALF):
        at = pl.ds(s * part, part)
        rows_to(1, s, beside).wait_recv()
        total, out = work(beside, s)
        to_own[at, :] = total.astype(bf16)
        owned(s).start()
        dattn[at, :] = out.astype(bf16)
        owned_out(s).start()
    for s in range(HALF):
        at = pl.ds(s * part, part)
        rows_to(0, s, across).wait_recv()
        passed(s).start()
        keep[...], out = work(across, s)
        out_keep[at, :] = out.astype(bf16)
        passed(s).wait_recv()
        total, out = work(corner, s)
        to_beside[at, :] = total.astype(bf16)
        handed(s).start()
        headed[at, :] = out.astype(bf16)
        handed_out(s).start()
        handed(s).wait_recv()
        to_across[at, :] = (keep[...] + from_beside[at, :].astype(f32)).astype(bf16)
        if s == 0:
            summed(s).start()
            weight_grads(t // 2, False)
        else:
            stored(6).start()
            stored(7).start()
    weight_grads(1 - t // 2, True)
    stored(2).start()
    stored(3).start()
    for s in range(HALF):
        at = pl.ds(s * part, part)
        handed_out(s).wait_recv()
        out_keep[at, :] = (out_keep[at, :].astype(f32) + from_beside_out[at, :].astype(f32)).astype(bf16)
        owned_out(s).wait_recv()
        out_own[at, :] = out_own[at, :] + from_own_out[at, :].astype(f32)
        owned_out(s).wait_send()
    stored(4).start()
    stored(5).start()
    gain_out[...] = jnp.zeros_like(gain_out)
    piece = 64
    owned(0).wait_recv()
    summed(0).wait_recv()

    def chunk(i, carry):
        at = pl.ds(pl.multiple_of(i * piece, piece), piece)
        grad = mine[at, :] + from_own[at, :].astype(f32) + from_across[at, :].astype(f32)
        cot_rows = cot[pl.ds(pl.multiple_of(t * rows + i * piece, piece), piece), :].astype(f32)
        full, part_gain = norm_back(grad, hidden[at, :], gain, cot_rows)
        mine[at, :] = full
        dattn[at, :] = full.astype(bf16)
        gain_out[...] += part_gain
        return carry

    lax.fori_loop(0, part // piece, chunk, 0)
    owned(1).wait_recv()
    mine[pl.ds(part, part), :] = mine[pl.ds(part, part), :] + from_own[pl.ds(part, part), :].astype(f32)
    stored(0).start()
    stored(1).start()
    for s in range(HALF):
        for copy in (rows_to(0, s, across), rows_to(1, s, beside), passed(s), handed(s), owned(s), handed_out(s)):
            copy.wait_send()
    summed(0).wait_send()
    for i in range(len(stores)):
        stored(i).wait()


def mlp(headed, out_all, tokens, gain, gate_up, down, cot):
    rows, width = tokens.shape
    total = cot.shape[0]
    units = down.shape[0]
    hbm = pl.BlockSpec(memory_space=pl.ANY)
    vmem = pl.BlockSpec(memory_space=pltpu.VMEM)
    like = lambda x: pltpu.VMEM(x.shape, x.dtype)
    half = lambda: pltpu.VMEM((rows, width), bf16)
    wide = lambda: pltpu.VMEM((rows, width), f32)
    unit = lambda: pltpu.VMEM((total, units), bf16)
    out = lambda shape, kind: jax.ShapeDtypeStruct(shape, kind)
    dma = pltpu.SemaphoreType.DMA
    return pl.pallas_call(
        mlp_kernel,
        in_specs=[hbm] * 3 + [vmem] + [hbm] * 3,
        out_specs=[hbm] * 2 + [vmem] + [hbm] * 6,
        out_shape=[out((rows, width), f32), out((rows, width), bf16), out((8, width), f32), out(gate_up.shape, bf16), out(down.shape, bf16), out((rows, width), f32), out((rows, width), bf16), out((rows // HALF, width), bf16), out((rows // HALF, width), f32)],
        scratch_shapes=[like(headed), like(out_all), like(tokens), like(gate_up), like(down), like(cot), wide(), pltpu.VMEM((total, width), bf16), unit(), unit(), unit(),
                        wide(), pltpu.VMEM((rows // HALF, width), f32), half(), half(), half(), half(), half(), half(), wide(), half(), half(), half(),
                        pltpu.VMEM(gate_up.shape, f32), pltpu.VMEM(down.shape, f32), like(gate_up), like(down), half(), dma((6,)), dma((8,)), dma((8, HALF)), dma((8, HALF))],
        compiler_params=pltpu.CompilerParams(collective_id=1, has_side_effects=True, vmem_limit_bytes=62 * 2**20),
    )(headed, out_all, tokens, gain, gate_up, down, cot)


def mixer_bwd_block(blk, width, flags, proj_ref, prev_ref, conv_ref, gain_ref, mixed_ref, state_in, res_in, wu_in, inv_in, dheaded, dcat, dstate, buf, dbuf, cacc, gacc):
    buf[0:8, :] = prev_ref[:, :width]
    buf[8:, :] = proj_ref[:, :width]
    heads, tails = span_masks(flags, blk * (BACK_ROWS // SPAN), BACK_ROWS // SPAN)
    cols, slopes = [], []
    for c in range(width // HEAD):
        total = conv_column(buf, conv_ref, heads, slice(c * HEAD, (c + 1) * HEAD))
        sig = sigmoid(total)
        cols.append(total * sig)
        slopes.append(sig * (1.0 + total * (1.0 - sig)))
    betas = sigmoid(proj_ref[:, width:])
    strict, causal, cross, _, _ = pair_masks()
    lane = lax.broadcasted_iota(jnp.int32, (STEP, HEAD), 1)
    order = list(reversed(range(BACK_STEPS)))
    hs = [slice(h * STEP, (h + 1) * STEP) for h in range(2)]
    spans = [slice(s * STEP, (s + 1) * STEP) for s in range(BACK_STEPS)]
    edge = [resets(flags, blk * BACK_STEPS + s) for s in range(BACK_STEPS)]
    enter, leave, keep = zip(*[row_masks(*e) for e in edge])
    gate = [jnp.where(cross, 1.0 - e[1], 1.0) for e in edge]
    both = lambda n: [jnp.concatenate([cols[2 * n][rs], cols[2 * n + 1][rs]], axis=0) for rs in spans]
    q, k, v = both(0), both(1), both(2)
    rq = [lax.rsqrt(jnp.sum(x * x, axis=-1, keepdims=True) + 1e-6) for x in q]
    rk = [lax.rsqrt(jnp.sum(x * x, axis=-1, keepdims=True) + 1e-6) for x in k]
    q = [x * r for x, r in zip(q, rq)]
    k = [x * r for x, r in zip(k, rk)]
    q16 = [x.astype(bf16) for x in q]
    k16 = [x.astype(bf16) for x in k]
    b = [jnp.concatenate([betas[rs, 0:1], betas[rs, 1:2]], axis=0) for rs in spans]
    gp = [mm(jnp.concatenate([x, y], axis=0), x, NT) for x, y in zip(k16, q16)]
    gram = [jnp.where(strict, m * x[:2 * STEP], 0.0) for m, x in zip(gate, gp)]
    p = [jnp.where(causal, m * x[2 * STEP:], 0.0).astype(bf16) for m, x in zip(gate, gp)]
    do = []
    for s in range(BACK_STEPS):
        o = stack(mixed_ref[spans[s], :])
        dh = stack(dheaded[pl.ds(pl.multiple_of(blk * BACK_ROWS + s * STEP, STEP), STEP), :].astype(f32))
        ro = lax.rsqrt(jnp.mean(o * o, axis=-1, keepdims=True) + 1e-5)
        on = o * ro
        gacc[...] += jnp.sum((dh * on).reshape(2 * STEP // 8, 8, HEAD), axis=0)
        dn = dh * gain_ref[...]
        do.append(ro * (dn - on * jnp.mean(dn * on, axis=-1, keepdims=True)))
    do16 = [x.astype(bf16) for x in do]
    doe = [(x * e).astype(bf16) for x, e in zip(do, enter)]
    ke16 = [(x * e).astype(bf16) for x, e in zip(k, leave)]
    we = [(wu_in[s][:, :HEAD].astype(f32) * enter[s]).astype(bf16) for s in range(BACK_STEPS)]
    dres = [mm(x, y, TN) for x, y in zip(p, do16)]
    qdo = [[mm(x[r], y[r], TN) for r in hs] for x, y in zip(q16, doe)]
    dmem = [dstate[0], dstate[1]]
    dres16, after = [None] * BACK_STEPS, [None] * BACK_STEPS
    for s in order:
        low = [m.astype(bf16) for m in dmem]
        after[s] = low
        dres[s] = dres[s] + jnp.concatenate([mm(ke16[s][hs[h]], low[h]) for h in range(2)], axis=0)
        dres16[s] = dres[s].astype(bf16)
        for h in range(2):
            dmem[h] = keep[s] * dmem[h] + qdo[s][h] - mm(we[s][hs[h]], dres16[s][hs[h]], TN)
    dp = [mm(do16[s], res_in[s], NT) for s in order]
    dke = [jnp.concatenate([mm(res_in[s, hs[h]], after[s][h], NT) for h in range(2)], axis=0) for s in order]
    ds = [[mm(jnp.concatenate([do16[s][hs[h]], dres16[s][hs[h]]], axis=0), state_in[s, h * HEAD:(h + 1) * HEAD], NT) for h in range(2)] for s in order]
    dp = [jnp.where(causal, gate[s] * x, 0.0).astype(bf16) for s, x in zip(order, dp)]
    dw = [-enter[s] * jnp.concatenate([x[0][STEP:], x[1][STEP:]], axis=0) for s, x in zip(order, ds)]
    db_kv = [mm(inv_in[s], jnp.concatenate([x, dres[s]], axis=1), TN) for s, x in zip(order, dw)]
    dq = [enter[s] * jnp.concatenate([x[0][:STEP], x[1][:STEP]], axis=0) + mm(y, k16[s]) for s, x, y in zip(order, ds, dp)]
    dk = [mm(y, q16[s], TN) + leave[s] * x for s, x, y in zip(order, dke, dp)]
    da = [-jnp.where(strict, gate[s] * mm(x, wu_in[s], NT), 0.0) for s, x in zip(order, db_kv)]
    dg = [(x * b[s]).astype(bf16) for s, x in zip(order, da)]
    dk = [x + mm(y, k16[s]) + mm(y, k16[s], TN) + b[s] * z[:, :HEAD] for s, x, y, z in zip(order, dk, dg, db_kv)]
    for i, s in enumerate(order):
        rs = spans[s]
        dbeta = jnp.sum(da[i] * gram[s], axis=-1, keepdims=True) + jnp.sum(db_kv[i][:, :HEAD] * k[s] + db_kv[i][:, HEAD:] * v[s], axis=-1, keepdims=True)
        dv = b[s] * db_kv[i][:, HEAD:]
        dqs = rq[s] * (dq[i] - q[s] * jnp.sum(dq[i] * q[s], axis=-1, keepdims=True))
        dks = rk[s] * (dk[i] - k[s] * jnp.sum(dk[i] * k[s], axis=-1, keepdims=True))
        dpre = dbeta * b[s] * (1.0 - b[s])
        for n, x in enumerate((dqs, dks, dv)):
            for h in range(2):
                c = 2 * n + h
                dbuf[rs, c * HEAD:(c + 1) * HEAD] = x[hs[h]] * slopes[c][rs]
        dcat[pl.ds(pl.multiple_of(blk * BACK_ROWS + s * STEP, STEP), STEP), width:] = jnp.where(lane == 0, dpre[:STEP], jnp.where(lane == 1, dpre[STEP:], 0.0)).astype(bf16)
    dstate[0] = dmem[0]
    dstate[1] = dmem[1]
    for c in range(width // HEAD):
        cs = slice(c * HEAD, (c + 1) * HEAD)
        total, grads = conv_column_back(buf, dbuf, conv_ref, tails, cs)
        dcat[pl.ds(pl.multiple_of(blk * BACK_ROWS, BACK_ROWS), BACK_ROWS), cs] = total.astype(bf16)
        for j in range(4):
            cacc[j, :, cs] += grads[j]
    dbuf[BACK_ROWS:, :] = dbuf[0:8, :]


class Ring:
    def __init__(self, here, after, before, sources, results, lands, by_rows, send, recv):
        self.here, self.targets = here, (after, before)
        self.sources, self.results, self.lands, self.by_rows, self.send, self.recv = sources, results, lands, by_rows, send, recv
        self.visited = 0

    def shard(self, way, k):
        return lax.rem(self.here + (k if way else 2 * RING - k), RING)

    def view(self, ref, i, way, k):
        shard = self.shard(way, k)
        rows, cols = ref.shape
        if self.by_rows[i]:
            piece = rows // (2 * RING)
            return ref.at[pl.ds(pl.multiple_of((2 * shard + way) * piece, piece), piece)]
        piece = cols // RING
        return ref.at[pl.ds(way * (rows // 2), rows // 2), pl.ds(pl.multiple_of(shard * piece, piece), piece)]

    def copy(self, i, way, r):
        if r == 0:
            src, dst = self.view(self.sources[i], i, way, 0), self.lands[i].at[way, 0]
        elif r < RING - 1:
            src, dst = self.lands[i].at[way, r - 1], self.lands[i].at[way, r]
        else:
            src = dst = self.view(self.results[i], i, way, r)
        return pltpu.make_async_remote_copy(src_ref=src, dst_ref=dst, send_sem=self.send.at[i, way], recv_sem=self.recv.at[i, way, r], device_id=self.targets[way], device_id_type=MESH_ID)

    def visit(self, count):
        for _ in range(count):
            if self.visited == len(self.sources) * (ROUNDS + 1):
                return
            r, i = divmod(self.visited, len(self.sources))
            self.visited += 1
            for way in range(2):
                if r > 0:
                    last = self.copy(i, way, r - 1)
                    last.wait_send()
                    last.wait_recv()
                if 0 < r < RING:
                    land = self.lands[i].at[way, r - 1]
                    total = (land[...].astype(f32) + self.view(self.sources[i], i, way, r)[...].astype(f32)).astype(bf16)
                    if r < RING - 1:
                        land[...] = total
                    else:
                        done = self.view(self.results[i], i, way, r)
                        done[...] = total
                if r < ROUNDS:
                    self.copy(i, way, r).start()


def ring_place(d):
    base = d // RING * RING
    inner = lax.rem(d, RING)
    line = inner // 2
    here = jnp.where(lax.rem(inner, 2) == 0, line, RING - 1 - line)

    def device(place):
        return base + jnp.where(place < RING // 2, 2 * place, 2 * (RING - 1 - place) + 1)

    return here, device(lax.rem(here + 1, RING)), device(lax.rem(here + RING - 1, RING))


def ring_lands(shapes, by_rows):
    pieces = [(s[0] // (2 * RING), s[1]) if rows else (s[0] // 2, s[1] // RING) for s, rows in zip(shapes, by_rows)]
    return [pltpu.VMEM((2, RING - 1) + p, bf16) for p in pieces]


def back_kernel(n_dp, flags, proj_ref, prev_ref, params, mixed_ref, state_in, res_in, wu_in, inv_in,
                headed_hbm, attn_hbm, dattn_hbm, out_w_hbm, qkv_hbm, beta_hbm, tok_hbm, dhid_hbm, second_grad, gu_hbm, down_hbm, own_hbm, across_hbm, late_hbm, hidden_hbm, cot_hbm,
                dx_hbm, small_out, output_hbm, gu_out, down_out, cat_out, outw_out, landed_hbm,
                headed, attn, dattn_all, out_w, w, beta_w, tok, dhid, gu_src, down_src, cat_src, outw_src,
                gu_res, down_res, cat_res, outw_res, gate_land, up_land, down_land, q_land, k_land, v_land, outw_land,
                dheaded, dcat, dstate, buf, dbuf, cacc, gacc, mine, to_beside, from_beside, to_across, from_across, to_own, from_own,
                group_send, group_land, all_send, all_land, gain_acc, beta_grad, second_acc, late_land,
                load, store, send_m, recv_m, send_c, recv_c, send_r, recv_r, send_x, recv_x, send_g, recv_g, send_a, recv_a, late_sem):
    g = pl.program_id(0)
    n = pl.num_programs(0)
    d, t, beside, across, corner = places()
    here, after, before = ring_place(d)
    rows = tok.shape[0]
    part = rows // HALF
    width = buf.shape[1]
    others = [d // RING * RING + lax.rem(d + k, RING) for k in range(1, RING)]
    first_gain, second_gain, gain_ref, conv_ref = param_views(params, width)
    units = down_src.shape[0]
    gate_up = lambda ref: [ref.at[pl.ds(0, units)], ref.at[pl.ds(units, units)]]
    mlp_ring = Ring(here, (after, t), (before, t), gate_up(gu_src) + [down_src], gate_up(gu_res) + [down_res], [gate_land, up_land, down_land], [False] * 3, send_m, recv_m)
    model = tok.shape[1]
    thirds = lambda ref: [ref.at[pl.ds(i * model, model)] for i in range(3)]
    cat_ring = Ring(here, (after, t), (before, t), thirds(cat_src) + [outw_src], thirds(cat_res) + [outw_res], [q_land, k_land, v_land, outw_land], [True] * 4, send_c, recv_c)
    rowset = Gather(dattn_all, rows, send_r, recv_r)
    loads = [(gu_hbm, gu_src), (down_hbm, down_src), (dattn_hbm, dattn_all.at[pl.ds(pl.multiple_of(t * rows, rows), rows)]), (out_w_hbm, out_w), (headed_hbm, headed), (attn_hbm, attn), (tok_hbm, tok), (dhid_hbm, dhid), (beta_hbm, beta_w)]
    loads += [(qkv_hbm.at[i], w.at[:, pl.ds(i * 2 * HEAD, 2 * HEAD)]) for i in range(3)]
    early = len(loads)
    dhid_load = 7
    loads += [(hidden_hbm, mine.at[pl.ds(0, part)]), (cot_hbm.at[pl.ds(pl.multiple_of(t * rows + part, part), part)], to_own.at[pl.ds(0, part)])]
    stores = [(gu_res, gu_out), (down_res, down_out), (mine, dx_hbm), (cat_res, cat_out), (outw_res, outw_out), (to_own, output_hbm)]

    def loaded(i):
        return pltpu.make_async_copy(loads[i][0], loads[i][1], load.at[i])

    def stored(i):
        return pltpu.make_async_copy(stores[i][0], stores[i][1], store.at[i])

    def pushed(src, dst, i, s, peer):
        return pltpu.make_async_remote_copy(src_ref=src, dst_ref=dst, send_sem=send_x.at[i, s], recv_sem=recv_x.at[i, s], device_id=(d, peer), device_id_type=MESH_ID)

    def outward():
        return pushed(across_hbm, landed_hbm, 6, 0, across)

    def late():
        return pushed(late_hbm, late_land, 6, 1, across)

    def block_at(owner, s):
        return row_block(owner, s, rows, part)

    @pl.when(g == 0)
    def _():
        for i in range(len(loads)):
            loaded(i).start()
        greet([(d, beside), (d, across), (d, corner)] + [(o, t) for o in others])
        late().start()
        loaded(2).wait()
        rowset.near(0).start()
        loaded(0).wait()
        loaded(1).wait()
        mlp_ring.visit(3)
        dstate[...] = jnp.zeros_like(dstate)
        dbuf[BACK_ROWS:, :] = jnp.zeros((8, width), f32)
        cacc[...] = jnp.zeros_like(cacc)
        gacc[...] = jnp.zeros_like(gacc)
        gain_acc[...] = jnp.zeros_like(gain_acc)
        second_acc[...] = jnp.zeros_like(second_acc)
        for i in (3, dhid_load, early, early + 1):
            loaded(i).wait()
        mlp_ring.visit(EARLY_A)
        late().wait_recv()

        def last(i, carry):
            here_at = pl.ds(pl.multiple_of(i * 64, 64), 64)
            at = pl.ds(pl.multiple_of(part + i * 64, 64), 64)
            full, part_gain = norm_back(dhid[at, :] + late_land[here_at, :].astype(f32), mine[here_at, :], second_gain[...], to_own[here_at, :].astype(f32))
            dhid[at, :] = full
            dattn_all[pl.ds(pl.multiple_of(t * rows + part + i * 64, 64), 64), :] = full.astype(bf16)
            second_acc[...] += part_gain
            return carry

        lax.fori_loop(0, part // 64, last, 0)
        rowset.near(1).start()
        rowset.start_over(1)
        mlp_ring.visit(EARLY_B)

        @pl.when(t < 2)
        def _():
            rowset.fetch_over(1)

        mlp_ring.visit(EARLY_C)

    owner = n // 2 - 1 - g // 2
    for k in range(1, n):
        @pl.when(g == k)
        def _(k=k):
            if k == 3:
                outward().start()
            mlp_ring.visit(2)

    @pl.when((lax.rem(g, 2) == 1) & (g < n - 1) & ((owner - 1) // 2 != t // 2))
    def _():
        rowset.fetch_over(lax.rem(owner + 1, 2))

    @pl.when(lax.rem(g, 2) == 0)
    def _():
        @pl.when(owner == beside)
        def _():
            rowset.fetch_near()

        @pl.when(owner // 2 != t // 2)
        def _():
            rowset.passed(lax.rem(owner, 2)).wait_recv()

        at = pl.ds(pl.multiple_of(owner * rows, rows), rows)
        dheaded[at, :] = lax.dot_general(dattn_all[at, :], out_w[...], NT, preferred_element_type=f32).astype(bf16)

    blk = n - 1 - g
    mixer_bwd_block(blk, width, flags, proj_ref, prev_ref, conv_ref, gain_ref, mixed_ref, state_in, res_in, wu_in, inv_in, dheaded, dcat, dstate, buf, dbuf, cacc, gacc)

    def work(owner, s):
        at = block_at(owner, s)
        return lax.dot_general(dcat[at, :width], w[...], NT, preferred_element_type=f32) + lax.dot_general(dcat[at, width:width + 16], beta_w[...], NN, preferred_element_type=f32)

    def handed(s):
        at = pl.ds(s * part, part)
        return pushed(to_beside.at[at], from_beside.at[at], 3, s, beside)

    def summed(s):
        at = pl.ds(s * part, part)
        return pushed(to_across.at[at], from_across.at[at], 4, s, across)

    def owned(s):
        at = pl.ds(s * part, part)
        return pushed(to_own.at[at], from_own.at[at], 5, s, beside)

    def grouped(i, peer):
        return pltpu.make_async_remote_copy(src_ref=group_send, dst_ref=group_land.at[i], send_sem=send_g.at[i], recv_sem=recv_g.at[i], device_id=(d, peer), device_id_type=MESH_ID)

    def spread(i, o):
        return pltpu.make_async_remote_copy(src_ref=all_send, dst_ref=all_land.at[i], send_sem=send_a.at[i], recv_sem=recv_a.at[i], device_id=(o, t), device_id_type=MESH_ID)

    piece = 64

    def finish(s):
        gain = first_gain[...]

        def chunk(i, carry):
            at = pl.ds(pl.multiple_of(s * part + i * piece, piece), piece)
            grad = mine[at, :] + from_own[at, :].astype(f32) + from_across[at, :].astype(f32)
            x = tok[at, :].astype(f32)
            r = lax.rsqrt(jnp.mean(x * x, axis=-1, keepdims=True) + 1e-5)
            scaled = gain * grad
            mine[at, :] = dhid[at, :] + r * scaled - x * (r * r * r * jnp.mean(x * scaled, axis=-1, keepdims=True))
            gain_acc[...] += jnp.sum((grad * x * r).reshape(piece // 8, 8, grad.shape[1]), axis=0)
            return carry

        lax.fori_loop(0, part // piece, chunk, 0)

    @pl.when(g == n - 1)
    def _():
        for i in range(4, early):
            if i != dhid_load:
                loaded(i).wait()

        def cat_chunk(i):
            grad = lax.dot_general(attn[:, i * 256:(i + 1) * 256], dcat[:, :width], TN, preferred_element_type=f32).astype(bf16)
            for j in range(3):
                cat_src[pl.ds(j * attn.shape[1] + i * 256, 256), :] = grad[:, j * 2 * HEAD:(j + 1) * 2 * HEAD]

        def turn():
            mlp_ring.visit(1)
            cat_ring.visit(4)

        for i in range(attn.shape[1] // 256):
            cat_chunk(i)
            mlp_ring.visit(1)
        outw_src[...] = lax.dot_general(headed[...], dattn_all[...], TN, preferred_element_type=f32).astype(bf16)
        cat_ring.visit(4)
        for s in range(HALF):
            at = pl.ds(s * part, part)
            to_beside[at, :] = work(corner, s).astype(bf16)
            handed(s).start()
            total = work(across, s)
            handed(s).wait_recv()
            to_across[at, :] = (total + from_beside[at, :].astype(f32)).astype(bf16)
            summed(s).start()
            turn()
        beta_grad[...] = lax.dot_general(dcat[:, width:width + 16], attn[...], TN, preferred_element_type=f32)[:8]
        for s in range(HALF):
            at = pl.ds(s * part, part)
            to_own[at, :] = work(beside, s).astype(bf16)
            owned(s).start()
            mine[at, :] = work(t, s)
            turn()
        turn()
        owned(0).wait_recv()
        summed(0).wait_recv()
        finish(0)
        turn()
        turn()
        owned(1).wait_recv()
        summed(1).wait_recv()
        finish(1)
        stored(2).start()
        for i, copy in enumerate((handed, summed, owned)):
            for s in range(HALF):
                copy(s).wait_send()
        outward().wait_recv()
        ends = [pltpu.make_async_copy(own_hbm, dhid, late_sem.at[0]), pltpu.make_async_copy(landed_hbm, to_across, late_sem.at[1])]
        for copy in ends:
            copy.start()
        turn()
        for copy in ends:
            copy.wait()

        def add(i, carry):
            at = pl.ds(pl.multiple_of(i * piece, piece), piece)
            to_own[at, :] = (dhid[at, :] + to_across[at, :].astype(f32)).astype(bf16)
            return carry

        lax.fori_loop(0, rows // piece, add, 0)
        stored(5).start()
        line = lax.broadcasted_iota(jnp.int32, small_out.shape, 0)
        lane = lax.broadcasted_iota(jnp.int32, small_out.shape, 1)
        shared = (line < 2) | ((line == 3) & (lane >= width))
        group_send[...] = jnp.zeros_like(group_send)
        group_send[0:1, :] = jnp.sum(gain_acc[...], axis=0, keepdims=True)
        group_send[1:2, :] = jnp.sum(second_grad[...] + second_acc[...], axis=0, keepdims=True)
        group_send[2:3, :] = beta_grad[0:1, :]
        group_send[7:8, :] = beta_grad[1:2, :]
        group_send[3:4, width:width + HEAD] = jnp.sum(gacc[...], axis=0, keepdims=True)
        for j in range(4):
            group_send[3 + j:4 + j, :width] = jnp.sum(cacc[j], axis=0, keepdims=True)
        for i, peer in enumerate((beside, across, corner)):
            grouped(i, peer).start()
        turn()
        small = group_send[...]
        for i, peer in enumerate((beside, across, corner)):
            grouped(i, peer).wait_recv()
        both = (small + group_land[0]) + (group_land[1] + group_land[2])
        small = jnp.where(shared, both, small)
        all_send[...] = small
        for i, o in enumerate(others):
            spread(i, o).start()
        turn()
        turn()
        for i, o in enumerate(others):
            spread(i, o).wait_recv()
            small = small + all_land[i]
        small_out[...] = small
        for _ in range(ROUNDS):
            turn()
        for i in range(2):
            stored(i).start()
        for i in range(3, 5):
            stored(i).start()
        rowset.sent()
        for i, peer in enumerate((beside, across, corner)):
            grouped(i, peer).wait_send()
        for i, o in enumerate(others):
            spread(i, o).wait_send()
        outward().wait_send()
        late().wait_send()
        for i in range(len(stores)):
            stored(i).wait()


def backward(n_dp, flags, proj, params, saved, headed, attn_all, d_attn, out_w, qkv, beta, tokens, d_hidden, second_grad, gu_part, down_part, out_own, out_across, late, hidden_late, cot_all):
    mixed, states, res, wu, inv = saved
    total_rows, total = proj.shape
    width = 3 * qkv.shape[2]
    rows, model = tokens.shape
    n = total_rows // BACK_ROWS
    m2 = lambda g: (n - 1 - g, 0)
    m3 = lambda g: (n - 1 - g, 0, 0)
    z2 = lambda g: (0, 0)
    hbm = pl.BlockSpec(memory_space=pl.ANY)
    dma = pltpu.SemaphoreType.DMA
    like = lambda x: pltpu.VMEM(x.shape, x.dtype)
    mlp_parts = (gu_part, down_part)
    cat_shapes = [(3 * model, 2 * HEAD), (headed.shape[1], model)]
    half = lambda: pltpu.VMEM((rows, model), bf16)
    line = second_grad.shape
    out = lambda shape, kind: jax.ShapeDtypeStruct(shape, kind)
    return pl.pallas_call(
        functools.partial(back_kernel, n_dp),
        grid=(n,),
        in_specs=[pl.BlockSpec(memory_space=pltpu.SMEM), pl.BlockSpec((BACK_ROWS, total), m2),
                  pl.BlockSpec((8, total), lambda g: (jnp.maximum((n - 1 - g) * (BACK_ROWS // 8) - 1, 0), 0)),
                  pl.BlockSpec(params.shape, z2), pl.BlockSpec((BACK_ROWS, 2 * HEAD), m2),
                  pl.BlockSpec((BACK_STEPS, 2 * HEAD, HEAD), m3), pl.BlockSpec((BACK_STEPS, 2 * STEP, HEAD), m3),
                  pl.BlockSpec((BACK_STEPS, 2 * STEP, 2 * HEAD), m3), pl.BlockSpec((BACK_STEPS, 2 * STEP, 2 * STEP), m3)]
        + [hbm] * 8 + [pl.BlockSpec(line, z2)] + [hbm] * 7,
        out_specs=[hbm, pl.BlockSpec(line, z2)] + [hbm] * 6,
        out_shape=[out((rows, model), f32), out(line, f32), out((rows, model), bf16)] + [out(x.shape, bf16) for x in mlp_parts] + [out(s, bf16) for s in cat_shapes] + [out((rows, model), bf16)],
        scratch_shapes=[like(headed), like(attn_all), like(attn_all), like(out_w), pltpu.VMEM((model, width), bf16), like(beta), like(tokens), like(d_hidden)]
        + [like(x) for x in mlp_parts] + [pltpu.VMEM(s, bf16) for s in cat_shapes]
        + [like(x) for x in mlp_parts] + [pltpu.VMEM(s, bf16) for s in cat_shapes]
        + ring_lands([down_part.shape] * 3, [False] * 3) + ring_lands([(model, 2 * HEAD)] * 3 + cat_shapes[1:], [True] * 4)
        + [pltpu.VMEM((total_rows, 2 * HEAD), bf16), pltpu.VMEM((total_rows, total), bf16), pltpu.VMEM((2, HEAD, HEAD), f32),
           pltpu.VMEM((BACK_ROWS + 8, width), f32), pltpu.VMEM((BACK_ROWS + 8, width), f32), pltpu.VMEM((4, 8, width), f32), pltpu.VMEM((8, HEAD), f32),
           pltpu.VMEM((rows, model), f32), half(), half(), half(), half(), half(), half(),
           pltpu.VMEM(line, f32), pltpu.VMEM((3,) + line, f32), pltpu.VMEM(line, f32), pltpu.VMEM((RING - 1,) + line, f32), pltpu.VMEM((8, model), f32), pltpu.VMEM((8, model), f32), pltpu.VMEM((8, model), f32), like(late),
           dma((15,)), dma((6,)), dma((3, 2)), dma((3, 2, ROUNDS)), dma((4, 2)), dma((4, 2, ROUNDS)), dma((3, 2)), dma((3, 2)), dma((7, HALF)), dma((7, HALF)),
           dma((3,)), dma((3,)), dma((RING - 1,)), dma((RING - 1,)), dma((2,))],
        compiler_params=pltpu.CompilerParams(dimension_semantics=("arbitrary",), collective_id=2, has_side_effects=True, vmem_limit_bytes=62 * 2**20),
    )(flags, proj, proj, params, mixed, states, res, wu, inv, headed, attn_all, d_attn, out_w, qkv, beta, tokens, d_hidden, second_grad, gu_part, down_part, out_own, out_across, late, hidden_late, cot_all)


def cast_kernel(small, gu, down, cat, outw, dx, out, attn_grad, mlp_grad, head_grad, taps_grad, beta_grad, gu_out, down_out, cat_out, outw_out, dx_out, out_out):
    gu_out[...] = gu[...].astype(f32)
    down_out[...] = down[...].astype(f32)
    cat_out[...] = cat[...].astype(f32)
    outw_out[...] = outw[...].astype(f32)
    dx_out[...] = dx[...]
    out_out[...] = out[...]
    width = 3 * taps_grad.shape[2]
    attn_grad[...] = small[0, :]
    mlp_grad[...] = small[1, :]
    head_grad[...] = small[3, width:width + HEAD]
    for i in range(3):
        taps_grad[i] = small[3:7, i * width // 3:(i + 1) * width // 3]
    beta_grad[0:1, :] = small[2:3, :]
    beta_grad[1:2, :] = small[7:8, :]


def cast(small, gu, down, cat, outw, dx, out):
    steps = 8
    model = small.shape[1]
    arrays = (gu, down, cat, outw, dx, out)
    kinds = [f32] * 5 + [out.dtype]
    def spec(x):
        if x is down:
            return pl.BlockSpec((x.shape[0], x.shape[1] // steps), lambda g: (0, g))
        return pl.BlockSpec((x.shape[0] // steps, x.shape[1]), lambda g: (g, 0))

    shapes = [(model,), (model,), (HEAD,), (3, 4, cat.shape[1]), (2, model)]
    whole = lambda s: pl.BlockSpec(s, lambda g: (0,) * len(s))
    return pl.pallas_call(
        cast_kernel,
        grid=(steps,),
        in_specs=[whole(small.shape)] + [spec(x) for x in arrays],
        out_specs=[whole(s) for s in shapes] + [spec(x) for x in arrays],
        out_shape=[jax.ShapeDtypeStruct(s, f32) for s in shapes] + [jax.ShapeDtypeStruct(x.shape, k) for x, k in zip(arrays, kinds)],
        compiler_params=pltpu.CompilerParams(dimension_semantics=("arbitrary",), vmem_limit_bytes=62 * 2**20),
    )(small, *arrays)


def on_device(tokens, lengths, attn_gain, qkv_weight, beta_weight, conv_weight, head_gain, out_weight, mlp_gain, gate_up_weight, down_weight, cotangent):
    model_width = tokens.shape[1]
    qkv = jnp.transpose(qkv_weight, (1, 0, 2))
    gate_up = jnp.transpose(gate_up_weight, (1, 2, 0)).reshape(-1, model_width)
    params, beta, proj, mixed, states, res, wu, inv, attn_all, headed, headed_rows, out_all, cot_all = front(
        lengths, attn_gain, mlp_gain, head_gain, jnp.transpose(conv_weight, (1, 0, 2)), beta_weight.T, tokens, qkv, out_weight, cotangent)
    saved = (mixed, states, res, wu, inv)
    d_hidden, d_attn, second_grad, gu_part, down_part, out_own, out_across, late, hidden_late = mlp(headed_rows, out_all, tokens, params, gate_up, down_weight, cot_all)
    n_dp = lax.axis_size("dp")
    input_grad, small, output, *sums, _ = backward(
        n_dp, lengths, proj, params, saved, headed, attn_all, d_attn, out_weight, qkv, beta, tokens, d_hidden, second_grad, gu_part, down_part, out_own, out_across, late, hidden_late, cot_all)
    if n_dp > RING:
        groups = [list(range(i, n_dp, RING)) for i in range(RING)]
        small, *sums = lax.psum((small, *sums), "dp", axis_index_groups=groups)
    attn_gain_grad, mlp_gain_grad, head_gain_grad, taps_grad, beta_grad, gu_sum, down_sum, cat_sum, out_sum, input_grad, output = cast(small, *sums, input_grad, output)
    return (
        output,
        input_grad,
        attn_gain_grad,
        jnp.transpose(cat_sum.reshape(3, model_width, -1), (1, 0, 2)),
        beta_grad.T,
        jnp.transpose(taps_grad, (1, 0, 2)),
        head_gain_grad,
        out_sum,
        mlp_gain_grad,
        jnp.transpose(gu_sum.reshape(2, -1, model_width), (2, 0, 1)),
        down_sum,
    )


def solution(mesh):
    rows = P(("dp", "tensor"), None)
    last = P(None, None, "tensor")
    return jax.shard_map(
        on_device,
        mesh=mesh,
        in_specs=(rows, P("dp", None), P(), last, P(None, "tensor"), last, P(), P("tensor", None), P(), last, P("tensor", None), rows),
        out_specs=(rows, rows, P(), last, P(None, "tensor"), last, P(), P("tensor", None), P(), last, P("tensor", None)),
        check_vma=False,
    )
```
